32 devices in a mesh: section: 4 (over y, x), dp: 8 (over z, core).
Axes of the slice: x: 2, y: 2, z: 4, core: 2. Of those that a mesh axis runs over, the one named last changes fastest.
Arguments:
- inputs: bfloat16 [2, 640, 4096], P(None, 'dp'), may hold values from -36 to 36
- target: bfloat16 [2, 640, 4096], P(None, 'dp'), may hold values from -8 to 8
- blocks: bfloat16 [4, 64, 8, 4096], P('section', 'dp'), may hold values from -0.25 to 0.25
- columns: int32 [4, 64, 8], P('section', 'dp'), may hold values from 0 to 63, as said below
- counts: int32 [4, 64], P('section', 'dp'), may hold values from 4 to 8, as said below
Outputs:
- block_grads: bfloat16 [4, 64, 8, 4096], P('section', 'dp')
The draws below stay inside these ranges and needn't reach their ends.
Inputs may be any that keep to these rules, and one draw needn't show every extreme that they name: Each block row lists 8 different block columns; only its first counts entries are kept blocks, the rest are padding. `counts`: every layer has a block row with exactly 8 kept blocks.
All inputs are finite; a program needn't handle non-finite values.
Results may differ from the reference program's by a relative error of at most 0.015.
Values may be sent and summed in bfloat16 or wider, within the bound.
No kernel may reach another device: no remote copies, remote signals or barrier semaphores. Data moves between devices by JAX's collectives and lax.ppermute only.
A program may use at most 128 MiB of HBM per device.

```python
import jax
import jax.numpy as jnp
from jax import lax

DW = 4096
BLK = 64
KEEP = 8
MB = 2
TOK_MB = 80
LAYERS = 4
BR = 64
TOKENS = 640
N_DP = 8


def draw_inputs(key, part):
    subkeys = jax.random.split(key, 3)
    log_low = jnp.log(0.3)
    log_high = jnp.log(3.0)
    row_scale = jnp.exp(jax.random.uniform(subkeys[1], (MB, TOKENS, 1), jnp.float32, log_low, log_high))
    col_scale = jnp.exp(jax.random.uniform(subkeys[2], (DW,), jnp.float32, log_low, log_high))
    base_vals = jnp.clip(jax.random.normal(subkeys[0], (MB, TOKENS, DW), jnp.float32), -4.0, 4.0)
    return (base_vals * row_scale * col_scale).astype(jnp.bfloat16)


def draw_counts(key, part):
    key_counts, key_rows = jax.random.split(key)
    drawn = jax.random.randint(key_counts, (LAYERS, BR), KEEP // 2, KEEP + 1, dtype=jnp.int32)
    full_row = jax.random.randint(key_rows, (LAYERS, 1), 0, BR, dtype=jnp.int32)
    row_ids = jnp.arange(BR, dtype=jnp.int32)[None, :]
    return jnp.where(row_ids == full_row, KEEP, drawn).astype(jnp.int32)


def draw_columns(key, part):
    scores = jax.random.randint(key, (LAYERS, BR, BR), 0, 2 ** 20, dtype=jnp.int32) * BR
    scores = scores + jnp.arange(BR, dtype=jnp.int32)
    ranking = jnp.argsort(scores, axis=-1)
    return ranking[:, :, :KEEP].astype(jnp.int32)


def block_scale(key, extent, shards, least, largest):
    level, own = 1.0, jax.random.fold_in(key, 6)
    for dim, blocks in shards:
        heights = jnp.exp(jax.random.uniform(jax.random.fold_in(own, dim), (blocks,), jnp.float32, least / len(shards), largest / len(shards)))
        level = level * jnp.repeat(heights, extent[dim] // blocks).reshape([-1 if axis == dim else 1 for axis in range(len(extent))])
    return level


def noise(key, extent, deviation, limit, cuts=(), kind=jnp.bfloat16):
    entries = deviation * jax.random.normal(key, extent, jnp.float32)
    if cuts:
        entries = entries * block_scale(key, extent, cuts, -0.22, 0.18)
    return jnp.clip(entries, -limit, limit).astype(kind)


def setup_inputs(seed: int = 0) -> dict:
    arg_keys = jax.random.split(jax.random.key(seed), 6)
    inputs = draw_inputs(jax.random.fold_in(arg_keys[5], 71), 0)
    target = noise(arg_keys[1], (MB, TOKENS, DW), 1.5, 8.0, ((1, 8),))
    blocks = noise(arg_keys[2], (LAYERS, BR, KEEP, BLK * BLK), (KEEP * BLK) ** -0.5, 0.25, ((0, 4), (1, 8)))
    columns = draw_columns(jax.random.fold_in(arg_keys[5], 71), 0)
    counts = draw_counts(jax.random.fold_in(arg_keys[5], 71), 0)
    return dict(inputs=inputs, target=target, blocks=blocks, columns=columns, counts=counts)


EPSILON = 1e-05

def row_stats(hidden):
    widened = hidden.astype(jnp.float32)
    inv_rms = lax.rsqrt(lax.optimization_barrier(jnp.mean(widened * widened, axis=-1, keepdims=True)) + EPSILON)
    return (widened, inv_rms)

def group_of(row_count):
    if row_count % 16 == 0:
        return 16
    return 8 if row_count % 8 == 0 else row_count

def sparse_apply(normed, blocks, columns, live_mask):
    tok_count = normed.shape[0]
    feat_count = normed.shape[1]
    row_count = columns.shape[0]
    slot_count = columns.shape[1]
    group_rows = group_of(row_count)
    sweeps = row_count // group_rows
    in_parts = normed.astype(jnp.float32).reshape(tok_count, sweeps, group_rows, BLK).transpose(1, 0, 2, 3)
    weight_parts = blocks.astype(jnp.float32).reshape(sweeps, group_rows, slot_count, BLK, BLK)
    col_parts = columns.reshape(sweeps, group_rows * slot_count).astype(jnp.int32)
    live_parts = live_mask.astype(jnp.float32).reshape(sweeps, group_rows, slot_count)

    def visit_group(summed, pieces):
        in_part, weight_part, col_part, live_part = pieces
        products = jnp.einsum('mgi,gkij->gkmj', in_part, weight_part)
        products = products * live_part[:, :, None, None]
        products = products.reshape(group_rows * slot_count, tok_count, BLK)
        return (summed + jax.ops.segment_sum(products, col_part, num_segments=feat_count // BLK), None)
    start_sum = jnp.zeros((feat_count // BLK, tok_count, BLK), jnp.float32)
    summed, unused = lax.scan(visit_group, start_sum, (in_parts, weight_parts, col_parts, live_parts))
    return summed.transpose(1, 0, 2).reshape(tok_count, feat_count)

def sparse_back(cotangent, blocks, columns, live_mask):
    tok_count = cotangent.shape[0]
    feat_count = cotangent.shape[1]
    row_count = columns.shape[0]
    slot_count = columns.shape[1]
    group_rows = group_of(row_count)
    sweeps = row_count // group_rows
    by_column = cotangent.astype(jnp.float32).reshape(tok_count, feat_count // BLK, BLK)
    masked = blocks.astype(jnp.float32) * live_mask.astype(jnp.float32)[:, :, None]
    weight_parts = masked.reshape(sweeps, group_rows, slot_count, BLK, BLK)
    col_parts = columns.reshape(sweeps, group_rows * slot_count).astype(jnp.int32)

    def one_group(pieces):
        weight_part, col_part = pieces
        picked = jnp.take(by_column, col_part, axis=1).reshape(tok_count, group_rows, slot_count, BLK)
        return jnp.einsum('mgkj,gkij->gmi', picked, weight_part)
    outputs = lax.map(one_group, (weight_parts, col_parts))
    return outputs.transpose(2, 0, 1, 3).reshape(tok_count, feat_count)

def grad_rows(normed_rows, cotangent, col_part, live_part):
    tok_count = normed_rows.shape[0]
    row_count = normed_rows.shape[1]
    slot_count = col_part.shape[1]
    group_rows = group_of(row_count)
    sweeps = row_count // group_rows
    by_column = cotangent.astype(jnp.float32).reshape(tok_count, cotangent.shape[1] // BLK, BLK)
    in_parts = normed_rows.astype(jnp.float32).reshape(tok_count, sweeps, group_rows, BLK).transpose(1, 0, 2, 3)
    col_parts = col_part.reshape(sweeps, group_rows * slot_count).astype(jnp.int32)
    live_parts = live_part.astype(jnp.float32).reshape(sweeps, group_rows, slot_count)

    def one_group(pieces):
        in_one, col_one, live_one = pieces
        picked = jnp.take(by_column, col_one, axis=1).reshape(tok_count, group_rows, slot_count, BLK)
        gradient = jnp.einsum('mgi,mgkj->gkij', in_one, picked)
        return gradient * live_one[:, :, None, None]
    outputs = lax.map(one_group, (in_parts, col_parts, live_parts))
    return outputs.reshape(row_count, slot_count, BLK * BLK)

def dp_partials(normed, cotangent, columns, live_mask):
    per_in = normed.reshape(MB, N_DP, TOK_MB, DW).transpose(1, 0, 2, 3).reshape(N_DP, MB * TOK_MB, DW)
    per_cot = cotangent.reshape(MB, N_DP, TOK_MB, DW).transpose(1, 0, 2, 3).reshape(N_DP, MB * TOK_MB, DW)

    def add_group(summed, pieces):
        in_dev, cot_dev = pieces
        partial_sum = grad_rows(in_dev.reshape(MB * TOK_MB, BR, BLK), cot_dev, columns, live_mask)
        rounded = lax.optimization_barrier(partial_sum.astype(jnp.bfloat16))
        return (summed + rounded.astype(jnp.float32), None)
    start_sum = jnp.zeros((BR, KEEP, BLK * BLK), jnp.float32)
    summed, unused = lax.scan(add_group, start_sum, (per_in, per_cot))
    return summed.astype(jnp.bfloat16)

def reference(inputs, target, blocks, columns, counts):
    slot_ids = jnp.arange(KEEP, dtype=jnp.int32)
    live_all = slot_ids[None, None, :] < counts[:, :, None]
    hidden = inputs.reshape(MB * TOKENS, DW)
    stashed = []
    for layer_id in range(LAYERS):
        stashed.append(hidden)
        widened, inv_rms = row_stats(hidden)
        normed = (widened * inv_rms).astype(jnp.bfloat16)
        branch = sparse_apply(normed, blocks[layer_id], columns[layer_id], live_all[layer_id])
        hidden = (widened + branch).astype(jnp.bfloat16)
    loss_scale = (MB * TOKENS) ** (-0.5)
    goal = target.reshape(MB * TOKENS, DW).astype(jnp.float32)
    cotangent = ((hidden.astype(jnp.float32) - goal) * loss_scale).astype(jnp.bfloat16)
    gradients = [None] * LAYERS
    for layer_id in reversed(range(LAYERS)):
        widened, inv_rms = row_stats(stashed[layer_id])
        exact_norm = widened * inv_rms
        normed = exact_norm.astype(jnp.bfloat16)
        gradients[layer_id] = dp_partials(normed, cotangent, columns[layer_id], live_all[layer_id])
        back_sum = sparse_back(cotangent, blocks[layer_id], columns[layer_id], live_all[layer_id])
        centred = back_sum - exact_norm * lax.optimization_barrier(jnp.mean(back_sum * exact_norm, axis=-1, keepdims=True))
        cotangent = (cotangent.astype(jnp.float32) + inv_rms * centred).astype(jnp.bfloat16)
    return jnp.stack(gradients)
```

```python
import functools

import jax
import jax.numpy as jnp
from jax import lax
from jax.experimental import pallas as pl
from jax.experimental.pallas import tpu as pltpu
from jax.sharding import PartitionSpec as P

BLK = 64
LANES = 128
EPSILON = 1e-05
VMEM_LIMIT = 40 * 1024 * 1024


def chunk_rows(row_count):
    for size in (8, 4, 2):
        if row_count % size == 0:
            return size
    return 1


def lane_ids(rows):
    return lax.broadcasted_iota(jnp.int32, (rows, LANES), 1)


def inv_rms_of(hidden):
    return lax.rsqrt(jnp.mean(hidden * hidden, axis=-1, keepdims=True) + EPSILON)


def forward_kernel(rows_per, chunks, cols, start, weights, outs, current, normed, even, odd):
    layer = pl.program_id(0)
    chunk = pl.program_id(1)
    tokens, feats = current.shape
    pairs = feats // LANES

    @pl.when((layer == 0) & (chunk == 0))
    def _():
        current[...] = start[...]

    @pl.when(chunk == 0)
    def _():
        hidden = current[...].astype(jnp.float32)
        unit = (hidden * inv_rms_of(hidden)).astype(jnp.bfloat16)
        for block in range(feats // BLK):
            normed[block] = unit[:, block * BLK : (block + 1) * BLK]
        even[...] = jnp.zeros_like(even)
        odd[...] = jnp.zeros_like(odd)

    def visit(row, carry):
        whole_row = chunk * rows_per + row
        product = jnp.dot(
            normed[whole_row], weights[0, row], preferred_element_type=jnp.float32
        )
        halves = product.shape[1] // LANES
        for total, side in ((even, 0), (odd, 1)):
            places = [cols[layer, whole_row, 2 * half + side] for half in range(halves)]
            sums = [
                total[places[half]] + product[:, half * LANES : (half + 1) * LANES]
                for half in range(halves)
            ]
            for half in range(halves):
                total[places[half]] = sums[half]
        return carry

    lax.fori_loop(0, rows_per, visit, 0, unroll=True)

    @pl.when(chunk == chunks - 1)
    def _():
        low = lane_ids(tokens) < BLK
        for pair in range(pairs):
            first = even[2 * pair] + pltpu.roll(odd[2 * pair], BLK, 1)
            second = pltpu.roll(even[2 * pair + 1], BLK, 1) + odd[2 * pair + 1]
            lanes = slice(pair * LANES, (pair + 1) * LANES)
            added = current[:, lanes].astype(jnp.float32) + jnp.where(low, first, second)
            current[:, lanes] = added.astype(jnp.bfloat16)
        outs[0] = current[...]


def forward_pass(start, weights, cols):
    layers, row_count, _, width = weights.shape
    tokens, feats = start.shape
    rows_per = chunk_rows(row_count)
    chunks = row_count // rows_per
    blocks = feats // BLK
    return pl.pallas_call(
        functools.partial(forward_kernel, rows_per, chunks),
        grid_spec=pltpu.PrefetchScalarGridSpec(
            num_scalar_prefetch=1,
            grid=(layers, chunks),
            in_specs=[
                pl.BlockSpec((tokens, feats), lambda i, j, c: (0, 0)),
                pl.BlockSpec((1, rows_per, BLK, width), lambda i, j, c: (i, j, 0, 0)),
            ],
            out_specs=pl.BlockSpec((1, tokens, feats), lambda i, j, c: (i, 0, 0)),
            scratch_shapes=[
                pltpu.VMEM((tokens, feats), jnp.bfloat16),
                pltpu.VMEM((blocks, tokens, BLK), jnp.bfloat16),
                pltpu.VMEM((blocks, tokens, LANES), jnp.float32),
                pltpu.VMEM((blocks, tokens, LANES), jnp.float32),
            ],
        ),
        out_shape=jax.ShapeDtypeStruct((layers, tokens, feats), jnp.bfloat16),
        compiler_params=pltpu.CompilerParams(vmem_limit_bytes=VMEM_LIMIT),
        name="forward_layers",
    )(cols, start, weights)


def backward_kernel(
    rows_per, chunks, scale, cols, hidden_in, last, goal, weights, grads, cotangent, flipped, lows, highs, back
):
    step = pl.program_id(0)
    layers = pl.num_programs(0)
    layer = layers - 1 - step
    chunk = pl.program_id(1)
    tokens, feats = cotangent.shape
    pairs = feats // LANES

    @pl.when((step == 0) & (chunk == 0))
    def _():
        residue = last[...].astype(jnp.float32) - goal[...].astype(jnp.float32)
        cotangent[...] = (residue * scale).astype(jnp.bfloat16)

    @pl.when(chunk == 0)
    def _():
        hidden = hidden_in[0].astype(jnp.float32)
        unit = hidden * inv_rms_of(hidden)
        low = lane_ids(tokens) < BLK
        for pair in range(pairs):
            lanes = slice(pair * LANES, (pair + 1) * LANES)
            turned = unit[:, lanes].T.astype(jnp.bfloat16)
            flipped[2 * pair] = turned[:BLK]
            flipped[2 * pair + 1] = turned[BLK:]
            both = cotangent[:, lanes].astype(jnp.float32)
            moved = pltpu.roll(both, BLK, 1)
            lows[2 * pair] = jnp.where(low, both, 0.0).astype(jnp.bfloat16)
            highs[2 * pair] = jnp.where(low, 0.0, moved).astype(jnp.bfloat16)
            lows[2 * pair + 1] = jnp.where(low, moved, 0.0).astype(jnp.bfloat16)
            highs[2 * pair + 1] = jnp.where(low, 0.0, both).astype(jnp.bfloat16)

    def visit(row, carry):
        whole_row = chunk * rows_per + row
        halves = weights.shape[3] // LANES
        picked = jnp.concatenate(
            [
                lows[cols[layer, whole_row, 2 * half]] + highs[cols[layer, whole_row, 2 * half + 1]]
                for half in range(halves)
            ],
            axis=1,
        )
        gradient = jnp.dot(flipped[whole_row], picked, preferred_element_type=jnp.float32)
        grads[0, row] = gradient.astype(jnp.bfloat16)
        back[whole_row] = lax.dot_general(
            picked, weights[0, row], (((1,), (1,)), ((), ())), preferred_element_type=jnp.float32
        )
        return carry

    lax.fori_loop(0, rows_per, visit, 0, unroll=True)

    @pl.when((chunk == chunks - 1) & (step < layers - 1))
    def _():
        hidden = hidden_in[0].astype(jnp.float32)
        inv_rms = inv_rms_of(hidden)
        unit = hidden * inv_rms
        joined = jnp.concatenate([back[block] for block in range(feats // BLK)], axis=1)
        centred = joined - unit * jnp.mean(joined * unit, axis=-1, keepdims=True)
        cotangent[...] = (cotangent[...].astype(jnp.float32) + inv_rms * centred).astype(jnp.bfloat16)


def backward_pass(stash, last, goal, scale, weights, cols):
    layers, row_count, _, width = weights.shape
    tokens, feats = last.shape
    rows_per = chunk_rows(row_count)
    chunks = row_count // rows_per
    blocks = feats // BLK
    return pl.pallas_call(
        functools.partial(backward_kernel, rows_per, chunks, scale),
        grid_spec=pltpu.PrefetchScalarGridSpec(
            num_scalar_prefetch=1,
            grid=(layers, chunks),
            in_specs=[
                pl.BlockSpec((1, tokens, feats), lambda i, j, c: (layers - 1 - i, 0, 0)),
                pl.BlockSpec((tokens, feats), lambda i, j, c: (0, 0)),
                pl.BlockSpec((tokens, feats), lambda i, j, c: (0, 0)),
                pl.BlockSpec((1, rows_per, BLK, width), lambda i, j, c: (layers - 1 - i, j, 0, 0)),
            ],
            out_specs=pl.BlockSpec(
                (1, rows_per, BLK, width), lambda i, j, c: (layers - 1 - i, j, 0, 0)
            ),
            scratch_shapes=[
                pltpu.VMEM((tokens, feats), jnp.bfloat16),
                pltpu.VMEM((blocks, BLK, tokens), jnp.bfloat16),
                pltpu.VMEM((blocks, tokens, LANES), jnp.bfloat16),
                pltpu.VMEM((blocks, tokens, LANES), jnp.bfloat16),
                pltpu.VMEM((blocks, tokens, BLK), jnp.float32),
            ],
        ),
        out_shape=jax.ShapeDtypeStruct((layers, row_count, BLK, width), jnp.bfloat16),
        compiler_params=pltpu.CompilerParams(vmem_limit_bytes=VMEM_LIMIT),
        name="backward_layers",
    )(cols, stash, last, goal, weights)


def to_rows(blocks):
    rows, slots, _ = blocks.shape
    split = blocks.reshape(rows, slots, BLK, BLK)
    return split.transpose(0, 2, 1, 3).reshape(rows, BLK, slots * BLK)


def from_rows(matrix, slots):
    rows = matrix.shape[0]
    split = matrix.reshape(rows, BLK, slots, BLK)
    return split.transpose(0, 2, 1, 3).reshape(rows, slots, BLK * BLK)


def body(inputs, target, blocks, columns, counts):
    everyone = ("section", "dp")
    section_id = lax.axis_index("section")
    section_count = lax.axis_size("section")
    dp_count = lax.axis_size("dp")
    mb_count, tok_local, feats = inputs.shape
    own_rows, slots = columns.shape[1:]
    loss_scale = (mb_count * tok_local * dp_count) ** (-0.5)
    share = mb_count * tok_local // section_count
    padded = -(-share // 16) * 16

    live = jnp.arange(slots, dtype=jnp.int32)[None, :] < counts[0][:, None]
    kept = jnp.where(live[:, :, None], blocks[0], jnp.zeros_like(blocks[0]))
    own = to_rows(kept)
    weights = lax.all_gather(own, everyone, axis=0, tiled=True)
    weights = weights.reshape(section_count, dp_count * own_rows, BLK, slots * BLK)
    cols = lax.all_gather(columns[0], everyone, axis=0, tiled=True)
    cols = cols.reshape(section_count, dp_count * own_rows, slots)

    def my_rows(array):
        flat = array.reshape(mb_count * tok_local, feats)
        mine = lax.dynamic_slice_in_dim(flat, section_id * share, share, 0)
        return jnp.pad(mine, ((0, padded - share), (0, 0)))

    start = my_rows(inputs)
    goal = my_rows(target)
    outs = forward_pass(start, weights, cols)
    stash = jnp.concatenate([start[None], outs[:-1]], axis=0)
    grads = backward_pass(stash, outs[-1], goal, loss_scale, weights, cols)
    grads = grads.reshape(section_count * dp_count * own_rows, BLK, slots * BLK)
    summed = lax.psum_scatter(grads, everyone, scatter_dimension=0, tiled=True)
    result = from_rows(summed, slots)
    return jnp.where(live[:, :, None], result, jnp.zeros_like(result))[None]


def solution(mesh):
    return jax.shard_map(
        body,
        mesh=mesh,
        in_specs=(
            P(None, "dp", None),
            P(None, "dp", None),
            P("section", "dp", None, None),
            P("section", "dp", None),
            P("section", "dp"),
        ),
        out_specs=P("section", "dp", None, None),
        check_vma=False,
    )
```

```python
import functools

import jax
import jax.numpy as jnp
from jax import lax
from jax.experimental import pallas as pl
from jax.experimental.pallas import tpu as pltpu
from jax.sharding import PartitionSpec as P

BLK = 64
LANES = 128
EPSILON = 1e-05
VMEM_LIMIT = 48 * 1024 * 1024
CHUNK_ROWS = 16


def chunk_units(units, rows):
    size = max(1, CHUNK_ROWS // rows)
    while units % size:
        size -= 1
    return size


def lane_ids(rows):
    return lax.broadcasted_iota(jnp.int32, (rows, LANES), 1)


def inv_rms_of(hidden):
    return lax.rsqrt(jnp.mean(hidden * hidden, axis=-1, keepdims=True) + EPSILON)


def row_places(bases, chunk, per_chunk, rows):
    places = []
    for unit in range(per_chunk):
        base = bases[chunk * per_chunk + unit]
        for row in range(rows):
            places.append((unit, row, base + row))
    return places


def column_of(cols, layer, chunk, per_chunk, rows, slots, total_rows, index, slot):
    flat = layer * total_rows + chunk * per_chunk * rows + index
    return cols[flat * slots + slot]


def spread_halves(values, low, lows, highs, pair):
    both = values.astype(jnp.float32)
    moved = pltpu.roll(both, BLK, 1)
    lows[2 * pair] = jnp.where(low, both, 0.0).astype(jnp.bfloat16)
    highs[2 * pair] = jnp.where(low, 0.0, moved).astype(jnp.bfloat16)
    lows[2 * pair + 1] = jnp.where(low, moved, 0.0).astype(jnp.bfloat16)
    highs[2 * pair + 1] = jnp.where(low, 0.0, both).astype(jnp.bfloat16)


def forward_kernel(per_chunk, chunks, slots, cols, bases, start, weights, stash, final, current, normed, even, odd):
    layer = pl.program_id(0)
    chunk = pl.program_id(1)
    tokens, feats = current.shape
    pairs = feats // LANES
    rows = weights.shape[2]
    total_rows = chunks * per_chunk * rows

    @pl.when((layer == 0) & (chunk == 0))
    def _():
        current[...] = start[...]

    @pl.when(chunk == 0)
    def _():
        stash[0] = current[...]
        hidden = current[...].astype(jnp.float32)
        unit = (hidden * inv_rms_of(hidden)).astype(jnp.bfloat16)
        for block in range(feats // BLK):
            normed[block] = unit[:, block * BLK : (block + 1) * BLK]
        even[...] = jnp.zeros_like(even)
        odd[...] = jnp.zeros_like(odd)

    places = row_places(bases, chunk, per_chunk, rows)

    def product_of(index):
        unit, row, place = places[index]
        return jnp.dot(normed[place], weights[0, unit, row], preferred_element_type=jnp.float32)

    upcoming = product_of(0)
    for index in range(len(places)):
        product = upcoming
        if index + 1 < len(places):
            upcoming = product_of(index + 1)
        halves = slots // 2
        for total, side in ((even, 0), (odd, 1)):
            at = [
                column_of(cols, layer, chunk, per_chunk, rows, slots, total_rows, index, 2 * half + side)
                for half in range(halves)
            ]
            sums = [
                total[at[half]] + product[:, half * LANES : (half + 1) * LANES] for half in range(halves)
            ]
            for half in range(halves):
                total[at[half]] = sums[half]

    @pl.when(chunk == chunks - 1)
    def _():
        low = lane_ids(tokens) < BLK
        for pair in range(pairs):
            first = even[2 * pair] + pltpu.roll(odd[2 * pair], BLK, 1)
            second = pltpu.roll(even[2 * pair + 1], BLK, 1) + odd[2 * pair + 1]
            lanes = slice(pair * LANES, (pair + 1) * LANES)
            added = current[:, lanes].astype(jnp.float32) + jnp.where(low, first, second)
            current[:, lanes] = added.astype(jnp.bfloat16)
        final[...] = current[...]


def forward_pass(start, weights, cols, bases):
    layers, units, rows, _, width = weights.shape
    tokens, feats = start.shape
    per_chunk = chunk_units(units, rows)
    chunks = units // per_chunk
    blocks = feats // BLK
    return pl.pallas_call(
        functools.partial(forward_kernel, per_chunk, chunks, width // BLK),
        grid_spec=pltpu.PrefetchScalarGridSpec(
            num_scalar_prefetch=2,
            grid=(layers, chunks),
            in_specs=[
                pl.BlockSpec((tokens, feats), lambda i, j, c, b: (0, 0)),
                pl.BlockSpec((1, per_chunk, rows, BLK, width), lambda i, j, c, b: (i, j, 0, 0, 0)),
            ],
            out_specs=[
                pl.BlockSpec((1, tokens, feats), lambda i, j, c, b: (i, 0, 0)),
                pl.BlockSpec((tokens, feats), lambda i, j, c, b: (0, 0)),
            ],
            scratch_shapes=[
                pltpu.VMEM((tokens, feats), jnp.bfloat16),
                pltpu.VMEM((blocks, tokens, BLK), jnp.bfloat16),
                pltpu.VMEM((blocks, tokens, LANES), jnp.float32),
                pltpu.VMEM((blocks, tokens, LANES), jnp.float32),
            ],
        ),
        out_shape=[
            jax.ShapeDtypeStruct((layers, tokens, feats), jnp.bfloat16),
            jax.ShapeDtypeStruct((tokens, feats), jnp.bfloat16),
        ],
        compiler_params=pltpu.CompilerParams(vmem_limit_bytes=VMEM_LIMIT),
        name="forward_layers",
    )(cols, bases, start, weights)


def pick_columns(lows, highs, at):
    return jnp.concatenate(
        [lows[at[2 * half]] + highs[at[2 * half + 1]] for half in range(len(at) // 2)], axis=1
    )


def input_grad_kernel(
    per_chunk, chunks, slots, top, cols, bases, stash, start, weights, final, cotangent, lows, highs, back
):
    layer = top - pl.program_id(0)
    chunk = pl.program_id(1)
    tokens, feats = cotangent.shape
    pairs = feats // LANES
    rows = weights.shape[2]
    total_rows = chunks * per_chunk * rows

    @pl.when((pl.program_id(0) == 0) & (chunk == 0))
    def _():
        cotangent[...] = start[...]

    @pl.when(chunk == 0)
    def _():
        low = lane_ids(tokens) < BLK
        for pair in range(pairs):
            spread_halves(cotangent[:, pair * LANES : (pair + 1) * LANES], low, lows, highs, pair)

    places = row_places(bases, chunk, per_chunk, rows)

    def picked_at(index):
        at = [
            column_of(cols, layer, chunk, per_chunk, rows, slots, total_rows, index, slot)
            for slot in range(slots)
        ]
        return pick_columns(lows, highs, at)

    upcoming = picked_at(0)
    waiting = None
    for index in range(len(places)):
        unit, row, place = places[index]
        picked = upcoming
        if index + 1 < len(places):
            upcoming = picked_at(index + 1)
        result = lax.dot_general(
            picked, weights[0, unit, row], (((1,), (1,)), ((), ())), preferred_element_type=jnp.float32
        )
        if waiting is not None:
            back[waiting[0]] = waiting[1]
        waiting = (place, result)
    back[waiting[0]] = waiting[1]

    @pl.when(chunk == chunks - 1)
    def _():
        hidden = stash[0].astype(jnp.float32)
        inv_rms = inv_rms_of(hidden)
        unit = hidden * inv_rms
        joined = jnp.concatenate([back[block] for block in range(feats // BLK)], axis=1)
        centred = joined - unit * jnp.mean(joined * unit, axis=-1, keepdims=True)
        cotangent[...] = (cotangent[...].astype(jnp.float32) + inv_rms * centred).astype(jnp.bfloat16)
        final[...] = cotangent[...]


def input_grad_pass(stash, start, weights, cols, bases, count):
    layers, units, rows, _, width = weights.shape
    tokens, feats = start.shape
    per_chunk = chunk_units(units, rows)
    chunks = units // per_chunk
    blocks = feats // BLK
    top = layers - 1
    return pl.pallas_call(
        functools.partial(input_grad_kernel, per_chunk, chunks, width // BLK, top),
        grid_spec=pltpu.PrefetchScalarGridSpec(
            num_scalar_prefetch=2,
            grid=(count, chunks),
            in_specs=[
                pl.BlockSpec((1, tokens, feats), lambda i, j, c, b: (top - i, 0, 0)),
                pl.BlockSpec((tokens, feats), lambda i, j, c, b: (0, 0)),
                pl.BlockSpec((1, per_chunk, rows, BLK, width), lambda i, j, c, b: (top - i, j, 0, 0, 0)),
            ],
            out_specs=pl.BlockSpec((tokens, feats), lambda i, j, c, b: (0, 0)),
            scratch_shapes=[
                pltpu.VMEM((tokens, feats), jnp.bfloat16),
                pltpu.VMEM((blocks, tokens, LANES), jnp.bfloat16),
                pltpu.VMEM((blocks, tokens, LANES), jnp.bfloat16),
                pltpu.VMEM((blocks, tokens, BLK), jnp.float32),
            ],
        ),
        out_shape=jax.ShapeDtypeStruct((tokens, feats), jnp.bfloat16),
        compiler_params=pltpu.CompilerParams(vmem_limit_bytes=VMEM_LIMIT),
        name="input_grad_layers",
    )(cols, bases, stash, start, weights)


def block_grad_kernel(
    per_chunk, chunks, slots, cols, bases, stash, cotangents, grads, flipped, lows, highs
):
    layer = pl.program_id(0)
    chunk = pl.program_id(1)
    tokens, feats = stash.shape[1:]
    pairs = feats // LANES
    rows = grads.shape[2]
    total_rows = chunks * per_chunk * rows

    @pl.when(chunk == 0)
    def _():
        hidden = stash[0].astype(jnp.float32)
        unit = hidden * inv_rms_of(hidden)
        low = lane_ids(tokens) < BLK
        for pair in range(pairs):
            lanes = slice(pair * LANES, (pair + 1) * LANES)
            turned = unit[:, lanes].T.astype(jnp.bfloat16)
            flipped[2 * pair] = turned[:BLK]
            flipped[2 * pair + 1] = turned[BLK:]
            spread_halves(cotangents[0, :, lanes], low, lows, highs, pair)

    places = row_places(bases, chunk, per_chunk, rows)

    def operands(index):
        at = [
            column_of(cols, layer, chunk, per_chunk, rows, slots, total_rows, index, slot)
            for slot in range(slots)
        ]
        return flipped[places[index][2]], pick_columns(lows, highs, at)

    upcoming = operands(0)
    waiting = None
    for index in range(len(places)):
        turned, picked = upcoming
        if index + 1 < len(places):
            upcoming = operands(index + 1)
        result = jnp.dot(turned, picked, preferred_element_type=jnp.float32)
        if waiting is not None:
            grads[0, waiting[0], waiting[1]] = waiting[2].astype(jnp.bfloat16)
        waiting = (places[index][0], places[index][1], result)
    grads[0, waiting[0], waiting[1]] = waiting[2].astype(jnp.bfloat16)


def block_grad_pass(stash, cotangents, cols, bases, rows, slots):
    layers, tokens, feats = stash.shape
    units = bases.shape[0]
    width = slots * BLK
    per_chunk = chunk_units(units, rows)
    chunks = units // per_chunk
    blocks = feats // BLK
    return pl.pallas_call(
        functools.partial(block_grad_kernel, per_chunk, chunks, slots),
        grid_spec=pltpu.PrefetchScalarGridSpec(
            num_scalar_prefetch=2,
            grid=(layers, chunks),
            in_specs=[
                pl.BlockSpec((1, tokens, feats), lambda i, j, c, b: (i, 0, 0)),
                pl.BlockSpec((1, tokens, feats), lambda i, j, c, b: (i, 0, 0)),
            ],
            out_specs=pl.BlockSpec(
                (1, per_chunk, rows, BLK, width), lambda i, j, c, b: (i, j, 0, 0, 0)
            ),
            scratch_shapes=[
                pltpu.VMEM((blocks, BLK, tokens), jnp.bfloat16),
                pltpu.VMEM((blocks, tokens, LANES), jnp.bfloat16),
                pltpu.VMEM((blocks, tokens, LANES), jnp.bfloat16),
            ],
        ),
        out_shape=jax.ShapeDtypeStruct((layers, units, rows, BLK, width), jnp.bfloat16),
        compiler_params=pltpu.CompilerParams(vmem_limit_bytes=VMEM_LIMIT),
        name="block_grads",
    )(cols, bases, stash, cotangents)


def to_rows(blocks):
    rows, slots, _ = blocks.shape
    split = blocks.reshape(rows, slots, BLK, BLK)
    return split.transpose(0, 2, 1, 3).reshape(rows, BLK, slots * BLK)


def from_rows(matrix, slots):
    rows = matrix.shape[0]
    split = matrix.reshape(rows, BLK, slots, BLK)
    return split.transpose(0, 2, 1, 3).reshape(rows, slots, BLK * BLK)


def add_rounded(left, right):
    return (left.astype(jnp.float32) + right.astype(jnp.float32)).astype(jnp.bfloat16)


def body(inputs, target, blocks, columns, counts):
    section_id = lax.axis_index("section")
    section_count = lax.axis_size("section")
    dp_id = lax.axis_index("dp")
    dp_count = lax.axis_size("dp")
    mb_count, tok_local, feats = inputs.shape
    own_rows, slots = columns.shape[1:]
    loss_scale = (mb_count * tok_local * dp_count) ** (-0.5)
    places = dp_count // 2
    place = dp_id // 2
    core = dp_id % 2
    side = section_id % 2
    stage = section_id // 2
    stages = section_count // 2
    share = mb_count * tok_local // 2

    def ring(array):
        return lax.ppermute(array, "dp", [(i, (i + 2) % dp_count) for i in range(dp_count)])

    def sibling(array):
        return lax.ppermute(array, "dp", [(i, i ^ 1) for i in range(dp_count)])

    def partner(array):
        return lax.ppermute(array, "section", [(i, i ^ 1) for i in range(section_count)])

    live = jnp.arange(slots, dtype=jnp.int32)[None, :] < counts[0][:, None]
    kept = jnp.where(live[:, :, None], blocks[0], jnp.zeros_like(blocks[0]))
    own = to_rows(kept)

    weights = jnp.zeros((2, 2 * places) + own.shape, own.dtype)

    def put(weights, piece, layer, unit):
        return lax.dynamic_update_slice(weights, piece[None, None], (layer, unit, 0, 0, 0))

    for slot in range(places):
        other = partner(own)
        following = ring(own) if slot + 1 < places else None
        weights = put(weights, own, side, slot)
        weights = put(weights, other, 1 - side, slot)
        weights = put(weights, sibling(own), side, places + slot)
        weights = put(weights, sibling(other), 1 - side, places + slot)
        own = following

    all_cols = lax.all_gather(columns[0], ("section", "dp"), axis=0, tiled=True)
    all_cols = all_cols.reshape(section_count, dp_count, own_rows, slots)
    order = [
        ((place - slot) % places) * 2 + (core if kind == 0 else 1 - core)
        for kind in range(2)
        for slot in range(places)
    ]
    order = jnp.stack(order).astype(jnp.int32)
    pair_cols = lax.dynamic_slice_in_dim(all_cols, stage * 2, 2, 0)
    cols = jnp.take(pair_cols, order, axis=1).reshape(-1)
    bases = order * own_rows

    def my_rows(array):
        flat = array.reshape(mb_count * tok_local, feats)
        return lax.dynamic_slice_in_dim(flat, side * share, share, 0)

    start = my_rows(inputs)
    goal = my_rows(target)
    layer_in = start
    for step in range(stages):
        stash, final = forward_pass(layer_in, weights, cols, bases)
        if step + 1 < stages:
            moved = lax.ppermute(
                final, "section", [(i, i + 2) for i in range(section_count - 2)]
            )
            layer_in = jnp.where(stage == 0, start, moved)

    residue = final.astype(jnp.float32) - goal.astype(jnp.float32)
    from_loss = (residue * loss_scale).astype(jnp.bfloat16)
    cotangent = from_loss
    for step in range(stages - 1):
        result = input_grad_pass(stash, cotangent, weights, cols, bases, 2)
        moved = lax.ppermute(result, "section", [(i + 2, i) for i in range(section_count - 2)])
        cotangent = jnp.where(stage == stages - 1, from_loss, moved)
    middle = input_grad_pass(stash, cotangent, weights, cols, bases, 1)
    cotangents = jnp.stack([middle, cotangent])
    grads = block_grad_pass(stash, cotangents, cols, bases, own_rows, slots)

    travelling = None
    for slot in list(range(1, places)) + [0]:
        mine = grads[:, slot]
        both = add_rounded(mine, sibling(grads[:, places + slot]))
        outgoing = lax.dynamic_index_in_dim(both, 1 - side, 0, keepdims=False)
        kept_here = lax.dynamic_index_in_dim(both, side, 0, keepdims=False)
        total = kept_here.astype(jnp.float32) + partner(outgoing).astype(jnp.float32)
        if travelling is not None:
            total = total + ring(travelling).astype(jnp.float32)
        travelling = total.astype(jnp.bfloat16)
    result = from_rows(travelling, slots)
    return jnp.where(live[:, :, None], result, jnp.zeros_like(result))[None]


def solution(mesh):
    return jax.shard_map(
        body,
        mesh=mesh,
        in_specs=(
            P(None, "dp", None),
            P(None, "dp", None),
            P("section", "dp", None, None),
            P("section", "dp", None),
            P("section", "dp"),
        ),
        out_specs=P("section", "dp", None, None),
        check_vma=False,
    )
```

```python
import functools

import jax
import jax.numpy as jnp
from jax import lax
from jax.experimental import pallas as pl
from jax.experimental.pallas import tpu as pltpu
from jax.sharding import PartitionSpec as P

BLK = 64
LANES = 128
EPSILON = 1e-05
VMEM_LIMIT = 50 * 1024 * 1024
TAIL = 16
STEP_ROWS = 8

IN_VMEM = pl.BlockSpec(memory_space=pltpu.VMEM)
IN_SMEM = pl.BlockSpec(memory_space=pltpu.SMEM)
IN_HBM = pl.BlockSpec(memory_space=pl.ANY)


def step_units(units, rows):
    size = max(1, STEP_ROWS // rows)
    while units % size:
        size -= 1
    return size


def lane_ids(rows):
    return lax.broadcasted_iota(jnp.int32, (rows, LANES), 1)


def inv_rms_of(hidden):
    return lax.rsqrt(jnp.mean(hidden * hidden, axis=-1, keepdims=True) + EPSILON)


def spread_halves(values, low, lows, highs, pair):
    both = values.astype(jnp.float32)
    moved = pltpu.roll(both, BLK, 1)
    lows[2 * pair] = jnp.where(low, both, 0.0).astype(jnp.bfloat16)
    highs[2 * pair] = jnp.where(low, 0.0, moved).astype(jnp.bfloat16)
    lows[2 * pair + 1] = jnp.where(low, moved, 0.0).astype(jnp.bfloat16)
    highs[2 * pair + 1] = jnp.where(low, 0.0, both).astype(jnp.bfloat16)


def start_loads(side, pieces, held, arrived, wanted):
    units = len(pieces) // 2
    for unit in range(units):
        own, other = pieces[2 * unit], pieces[2 * unit + 1]
        for piece, layer in ((own, side), (other, 1 - side)):
            copy = pltpu.make_async_copy(piece, held.at[layer, unit], arrived.at[layer, unit])
            if wanted is None:
                copy.start()
            else:
                pl.when(layer == wanted)(copy.start)


def wait_load(pieces, held, arrived, layer, unit):
    pltpu.make_async_copy(pieces[0], held.at[layer, unit], arrived.at[layer, unit]).wait()


def forward_kernel(rows, slots, count, cols, bases, sides, start, *rest):
    pieces = rest[:count]
    stash, final, held, current, normed, even, odd, arrived = rest[count:]
    units = count // 2
    tokens, feats = current.shape
    pairs = feats // LANES
    halves = slots // 2
    per_step = step_units(units, rows)
    total_rows = units * rows

    start_loads(sides[0], pieces, held, arrived, None)
    current[...] = start[...]

    def run_layer(layer, carry):
        stash[layer] = current[...]
        hidden = current[...].astype(jnp.float32)
        unit_rows = (hidden * inv_rms_of(hidden)).astype(jnp.bfloat16)
        for block in range(feats // BLK):
            normed[block] = unit_rows[:, block * BLK : (block + 1) * BLK]
        even[...] = jnp.zeros_like(even)
        odd[...] = jnp.zeros_like(odd)

        def run_step(step, carry):
            for inner in range(per_step):
                wait_load(pieces, held, arrived, layer, step * per_step + inner)
            items = [(inner, row) for inner in range(per_step) for row in range(rows)]

            def product_of(index):
                inner, row = items[index]
                unit = step * per_step + inner
                return jnp.dot(
                    normed[bases[unit] + row],
                    held[layer, unit, row * BLK : (row + 1) * BLK],
                    preferred_element_type=jnp.float32,
                )

            upcoming = product_of(0)
            for index in range(len(items)):
                product = upcoming
                if index + 1 < len(items):
                    upcoming = product_of(index + 1)
                flat = (layer * total_rows + step * per_step * rows + index) * slots
                for total, part in ((even, 0), (odd, 1)):
                    at = [cols[flat + 2 * half + part] for half in range(halves)]
                    sums = [
                        total[at[half]] + product[:, half * LANES : (half + 1) * LANES]
                        for half in range(halves)
                    ]
                    for half in range(halves):
                        total[at[half]] = sums[half]
            return carry

        lax.fori_loop(0, units // per_step, run_step, 0)

        low = lane_ids(tokens) < BLK
        for pair in range(pairs):
            first = even[2 * pair] + pltpu.roll(odd[2 * pair], BLK, 1)
            second = pltpu.roll(even[2 * pair + 1], BLK, 1) + odd[2 * pair + 1]
            lanes = slice(pair * LANES, (pair + 1) * LANES)
            added = current[:, lanes].astype(jnp.float32) + jnp.where(low, first, second)
            current[:, lanes] = added.astype(jnp.bfloat16)
        return carry

    lax.fori_loop(0, 2, run_layer, 0)
    final[...] = current[...]


def forward_pass(start, pieces, cols, bases, sides, rows, slots):
    tokens, feats = start.shape
    blocks = feats // BLK
    units = len(pieces) // 2
    return pl.pallas_call(
        functools.partial(forward_kernel, rows, slots, len(pieces)),
        in_specs=[IN_SMEM] * 3 + [IN_VMEM] + [IN_HBM] * len(pieces),
        out_specs=[IN_VMEM, IN_VMEM],
        out_shape=[
            jax.ShapeDtypeStruct((2, tokens, feats), jnp.bfloat16),
            jax.ShapeDtypeStruct((tokens, feats), jnp.bfloat16),
        ],
        scratch_shapes=[
            pltpu.VMEM((2, units) + pieces[0].shape, jnp.bfloat16),
            pltpu.VMEM((tokens, feats), jnp.bfloat16),
            pltpu.VMEM((blocks, tokens, BLK), jnp.bfloat16),
            pltpu.VMEM((blocks, tokens, LANES), jnp.float32),
            pltpu.VMEM((blocks, tokens, LANES), jnp.float32),
            pltpu.SemaphoreType.DMA((2, units)),
        ],
        compiler_params=pltpu.CompilerParams(vmem_limit_bytes=VMEM_LIMIT),
        name="forward_layers",
    )(cols, bases, sides, start, *pieces)


def pick_columns(lows, highs, cols, flat, slots):
    return jnp.concatenate(
        [
            lows[cols[flat + 2 * half]] + highs[cols[flat + 2 * half + 1]]
            for half in range(slots // 2)
        ],
        axis=1,
    )


def input_grad_kernel(rows, slots, count, depth, cols, bases, sides, stash, start, *rest):
    pieces = rest[:count]
    final, held, lows, highs, back, arrived = rest[count:]
    units = count // 2
    tokens, feats = final.shape
    pairs = feats // LANES
    per_step = step_units(units, rows)
    total_rows = units * rows

    start_loads(sides[0], pieces, held, arrived, 1 if depth == 1 else None)
    final[...] = start[...]

    def run_layer(turn, carry):
        layer = 1 - turn
        low = lane_ids(tokens) < BLK
        for pair in range(pairs):
            spread_halves(final[:, pair * LANES : (pair + 1) * LANES], low, lows, highs, pair)

        def run_step(step, carry):
            for inner in range(per_step):
                wait_load(pieces, held, arrived, layer, step * per_step + inner)
            items = [(inner, row) for inner in range(per_step) for row in range(rows)]

            def picked_at(index):
                flat = (layer * total_rows + step * per_step * rows + index) * slots
                return pick_columns(lows, highs, cols, flat, slots)

            upcoming = picked_at(0)
            waiting = []
            for index in range(len(items)):
                inner, row = items[index]
                unit = step * per_step + inner
                picked = upcoming
                if index + 1 < len(items):
                    upcoming = picked_at(index + 1)
                result = lax.dot_general(
                    picked,
                    held[layer, unit, row * BLK : (row + 1) * BLK],
                    (((1,), (1,)), ((), ())),
                    preferred_element_type=jnp.float32,
                )
                waiting.append((bases[unit] + row, result))
                if len(waiting) > 1:
                    place, ready = waiting.pop(0)
                    back[place] = ready
            place, ready = waiting.pop(0)
            back[place] = ready
            return carry

        lax.fori_loop(0, units // per_step, run_step, 0)

        hidden = stash[layer].astype(jnp.float32)
        inv_rms = inv_rms_of(hidden)
        unit_rows = hidden * inv_rms
        joined = jnp.concatenate([back[block] for block in range(feats // BLK)], axis=1)
        centred = joined - unit_rows * jnp.mean(joined * unit_rows, axis=-1, keepdims=True)
        final[...] = (final[...].astype(jnp.float32) + inv_rms * centred).astype(jnp.bfloat16)
        return carry

    lax.fori_loop(0, depth, run_layer, 0)


def input_grad_pass(stash, start, pieces, cols, bases, sides, rows, slots, depth):
    tokens, feats = start.shape
    blocks = feats // BLK
    units = len(pieces) // 2
    return pl.pallas_call(
        functools.partial(input_grad_kernel, rows, slots, len(pieces), depth),
        in_specs=[IN_SMEM] * 3 + [IN_VMEM] * 2 + [IN_HBM] * len(pieces),
        out_specs=IN_VMEM,
        out_shape=jax.ShapeDtypeStruct((tokens, feats), jnp.bfloat16),
        scratch_shapes=[
            pltpu.VMEM((2, units) + pieces[0].shape, jnp.bfloat16),
            pltpu.VMEM((blocks, tokens, LANES), jnp.bfloat16),
            pltpu.VMEM((blocks, tokens, LANES), jnp.bfloat16),
            pltpu.VMEM((blocks, tokens, BLK), jnp.float32),
            pltpu.SemaphoreType.DMA((2, units)),
        ],
        compiler_params=pltpu.CompilerParams(vmem_limit_bytes=VMEM_LIMIT),
        name="input_grad_layers",
    )(cols, bases, sides, stash, start, *pieces)


def block_grad_kernel(rows, slots, chosen, units, cols, bases, stash, *rest):
    cotangents = rest[:2]
    outs = rest[2:-3]
    flipped, lows, highs = rest[-3:]
    tokens, feats = stash.shape[1:]
    pairs = feats // LANES
    total_rows = units * rows

    for layer in range(2):
        hidden = stash[layer].astype(jnp.float32)
        unit_rows = hidden * inv_rms_of(hidden)
        low = lane_ids(tokens) < BLK
        for pair in range(pairs):
            lanes = slice(pair * LANES, (pair + 1) * LANES)
            turned = unit_rows[:, lanes].T.astype(jnp.bfloat16)
            flipped[2 * pair] = turned[:BLK]
            flipped[2 * pair + 1] = turned[BLK:]
            spread_halves(cotangents[layer][:, lanes], low, lows, highs, pair)

        items = [(which, row) for which in range(len(chosen)) for row in range(rows)]

        def operands(index):
            which, row = items[index]
            unit = chosen[which]
            flat = (layer * total_rows + unit * rows + row) * slots
            return flipped[bases[unit] + row], pick_columns(lows, highs, cols, flat, slots)

        upcoming = operands(0)
        waiting = []
        for index in range(len(items)):
            which, row = items[index]
            turned, picked = upcoming
            if index + 1 < len(items):
                upcoming = operands(index + 1)
            result = jnp.dot(turned, picked, preferred_element_type=jnp.float32)
            waiting.append((which, row, result))
            if len(waiting) > 1 or index + 1 == len(items):
                for which, row, ready in waiting if index + 1 == len(items) else waiting[:1]:
                    outs[which][layer, row * BLK : (row + 1) * BLK] = ready.astype(jnp.bfloat16)
                waiting = waiting[1:]


def block_grad_pass(stash, cotangents, cols, bases, rows, slots, chosen):
    _, tokens, feats = stash.shape
    blocks = feats // BLK
    units = bases.shape[0]
    return pl.pallas_call(
        functools.partial(block_grad_kernel, rows, slots, tuple(chosen), units),
        in_specs=[IN_SMEM] * 2 + [IN_VMEM] * 3,
        out_specs=[IN_VMEM] * len(chosen),
        out_shape=[
            jax.ShapeDtypeStruct((2, rows * BLK, slots * BLK), jnp.bfloat16) for _ in chosen
        ],
        scratch_shapes=[
            pltpu.VMEM((blocks, BLK, tokens), jnp.bfloat16),
            pltpu.VMEM((blocks, tokens, LANES), jnp.bfloat16),
            pltpu.VMEM((blocks, tokens, LANES), jnp.bfloat16),
        ],
        compiler_params=pltpu.CompilerParams(vmem_limit_bytes=VMEM_LIMIT),
        name="block_grads",
    )(cols, bases, stash, *cotangents)


def to_rows(blocks):
    rows, slots, _ = blocks.shape
    split = blocks.reshape(rows, slots, BLK, BLK)
    return split.transpose(0, 2, 1, 3).reshape(rows * BLK, slots * BLK)


def from_rows(matrix, slots):
    rows = matrix.shape[0] // BLK
    split = matrix.reshape(rows, BLK, slots, BLK)
    return split.transpose(0, 2, 1, 3).reshape(rows, slots, BLK * BLK)


def add_rounded(left, right):
    return (left.astype(jnp.float32) + right.astype(jnp.float32)).astype(jnp.bfloat16)


def body(inputs, target, blocks, columns, counts):
    section_id = lax.axis_index("section")
    section_count = lax.axis_size("section")
    dp_id = lax.axis_index("dp")
    dp_count = lax.axis_size("dp")
    mb_count, tok_local, feats = inputs.shape
    rows, slots = columns.shape[1:]
    width = slots * BLK
    loss_scale = (mb_count * tok_local * dp_count) ** (-0.5)
    places = dp_count // 2
    place = dp_id // 2
    core = dp_id % 2
    side = section_id % 2
    stage = section_id // 2
    stages = section_count // 2
    share = mb_count * tok_local // 2

    def ring(array):
        return lax.ppermute(array, "dp", [(i, (i + 2) % dp_count) for i in range(dp_count)])

    def sibling(array):
        return lax.ppermute(array, "dp", [(i, i ^ 1) for i in range(dp_count)])

    def partner(array):
        return lax.ppermute(array, "section", [(i, i ^ 1) for i in range(section_count)])

    live = jnp.arange(slots, dtype=jnp.int32)[None, :] < counts[0][:, None]
    kept = jnp.where(live[:, :, None], blocks[0], jnp.zeros_like(blocks[0]))
    listed = columns[0].reshape(1, rows * slots).astype(jnp.bfloat16)
    tail = jnp.pad(listed, ((0, TAIL - 1), (0, width - rows * slots)))
    own = jnp.concatenate([to_rows(kept), tail], axis=0)

    near = []
    far = []
    for slot in range(places):
        following = ring(own) if slot + 1 < places else None
        other = partner(own)
        near += [own, other]
        far += [sibling(own), sibling(other)]
        own = following
    pieces = near + far

    by_role = jnp.stack(
        [
            jnp.stack([piece[rows * BLK, : rows * slots] for piece in pieces[role::2]])
            for role in range(2)
        ]
    )
    by_layer = jnp.where(side == 0, by_role, by_role[::-1])
    cols = by_layer.astype(jnp.int32).reshape(-1)
    bases = [
        (((place - slot) % places) * 2 + (core if kind == 0 else 1 - core)) * rows
        for kind in range(2)
        for slot in range(places)
    ]
    bases = jnp.stack(bases).astype(jnp.int32)
    sides = side.reshape(1).astype(jnp.int32)

    def my_rows(array):
        flat = array.reshape(mb_count * tok_local, feats)
        return lax.dynamic_slice_in_dim(flat, side * share, share, 0)

    start = my_rows(inputs)
    goal = my_rows(target)
    layer_in = start
    for step in range(stages):
        stash, final = forward_pass(layer_in, pieces, cols, bases, sides, rows, slots)
        if step + 1 < stages:
            moved = lax.ppermute(
                final, "section", [(i, i + 2) for i in range(section_count - 2)]
            )
            layer_in = jnp.where(stage == 0, start, moved)

    residue = final.astype(jnp.float32) - goal.astype(jnp.float32)
    from_loss = (residue * loss_scale).astype(jnp.bfloat16)
    cotangent = from_loss
    for step in range(stages - 1):
        result = input_grad_pass(stash, cotangent, pieces, cols, bases, sides, rows, slots, 2)
        moved = lax.ppermute(result, "section", [(i + 2, i) for i in range(section_count - 2)])
        cotangent = jnp.where(stage == stages - 1, from_loss, moved)
    middle = input_grad_pass(stash, cotangent, pieces, cols, bases, sides, rows, slots, 1)

    order = list(range(1, places)) + [0]
    grads = {}
    for group in (order[:1], order[1:]):
        chosen = [unit for slot in group for unit in (slot, places + slot)]
        outs = block_grad_pass(stash, [middle, cotangent], cols, bases, rows, slots, chosen)
        grads.update(zip(chosen, outs))

    travelling = None
    for slot in order:
        both = add_rounded(grads[slot], sibling(grads[places + slot]))
        outgoing = lax.dynamic_index_in_dim(both, 1 - side, 0, keepdims=False)
        kept_here = lax.dynamic_index_in_dim(both, side, 0, keepdims=False)
        total = kept_here.astype(jnp.float32) + partner(outgoing).astype(jnp.float32)
        if travelling is not None:
            total = total + ring(travelling).astype(jnp.float32)
        travelling = total.astype(jnp.bfloat16)
    result = from_rows(travelling, slots)
    return jnp.where(live[:, :, None], result, jnp.zeros_like(result))[None]


def solution(mesh):
    return jax.shard_map(
        body,
        mesh=mesh,
        in_specs=(
            P(None, "dp", None),
            P(None, "dp", None),
            P("section", "dp", None, None),
            P("section", "dp", None),
            P("section", "dp"),
        ),
        out_specs=P("section", "dp", None, None),
        check_vma=False,
    )
```

```python
import functools

import jax
import jax.numpy as jnp
from jax import lax
from jax.experimental import pallas as pl
from jax.experimental.pallas import tpu as pltpu
from jax.sharding import PartitionSpec as P

BLK = 64
LANES = 128
EPSILON = 1e-05
VMEM_LIMIT = 50 * 1024 * 1024
STEP_ROWS = 8

IN_VMEM = pl.BlockSpec(memory_space=pltpu.VMEM)
IN_SMEM = pl.BlockSpec(memory_space=pltpu.SMEM)
IN_HBM = pl.BlockSpec(memory_space=pl.ANY)


def step_units(units, rows):
    size = max(1, STEP_ROWS // rows)
    while units % size:
        size -= 1
    return size


def low_half(rows):
    return lax.broadcasted_iota(jnp.int32, (rows, LANES), 1) < BLK


def tile(pair):
    return pl.ds(pl.multiple_of(pair * LANES, LANES), LANES)


def over_pairs(feats, visit, carry):
    return lax.fori_loop(0, feats // LANES, visit, carry, unroll=4)


def inv_rms_of(ref):
    tokens, feats = ref.shape

    def visit(pair, total):
        values = ref[:, tile(pair)].astype(jnp.float32)
        return total + values * values

    total = over_pairs(feats, visit, jnp.zeros((tokens, LANES), jnp.float32))
    return lax.rsqrt(jnp.sum(total, axis=-1, keepdims=True) / feats + EPSILON)


def start_loads(side, pieces, held, arrived, wanted):
    for unit in range(len(pieces) // 2):
        own, other = pieces[2 * unit], pieces[2 * unit + 1]
        for piece, layer in ((own, side), (other, 1 - side)):
            copy = pltpu.make_async_copy(piece, held.at[layer, unit], arrived.at[layer, unit])
            if wanted is None:
                copy.start()
            else:
                pl.when(layer == wanted)(copy.start)


def wait_load(pieces, held, arrived, layer, unit):
    pltpu.make_async_copy(pieces[0], held.at[layer, unit], arrived.at[layer, unit]).wait()


def forward_layer(layer, wait, cols, bases, current, held, parts, sums, rows, slots):
    tokens, feats = current.shape
    units = held.shape[1]
    per_step = step_units(units, rows)
    low = low_half(tokens)
    inv_rms = inv_rms_of(current)

    def normalise(pair, carry):
        lanes = tile(pair)
        unit_rows = current[:, lanes].astype(jnp.float32) * inv_rms
        parts[2 * pair] = jnp.where(low, unit_rows, 0.0).astype(jnp.bfloat16)
        parts[2 * pair + 1] = jnp.where(low, 0.0, unit_rows).astype(jnp.bfloat16)
        sums[2 * pair] = jnp.zeros((tokens, LANES), jnp.float32)
        sums[2 * pair + 1] = jnp.zeros((tokens, LANES), jnp.float32)
        return carry

    over_pairs(feats, normalise, 0)

    def run_step(step, carry):
        for inner in range(per_step):
            wait(layer, step * per_step + inner)
        items = [(inner, row) for inner in range(per_step) for row in range(0, rows, 2)]

        def product_of(index):
            inner, row = items[index]
            unit = step * per_step + inner
            place = bases[unit] + row
            left = jnp.concatenate([parts[place], parts[place + 1]], axis=0)
            right = held[layer, unit, row * BLK : (row + 2) * BLK]
            return jnp.dot(left, right, preferred_element_type=jnp.float32)

        upcoming = product_of(0)
        for index, (inner, row) in enumerate(items):
            product = upcoming
            if index + 1 < len(items):
                upcoming = product_of(index + 1)
            for which in range(2):
                flat = ((layer * units + step * per_step + inner) * rows + row + which) * slots
                for begin in range(0, slots, 4):
                    at = [cols[flat + slot] for slot in range(begin, min(begin + 4, slots))]
                    added = []
                    for offset in range(len(at)):
                        slot = begin + offset
                        lanes = slice((slot // 2) * LANES, (slot // 2 + 1) * LANES)
                        piece = product[which * tokens : (which + 1) * tokens, lanes]
                        piece = jnp.where(low, piece, 0.0) if slot % 2 == 0 else jnp.where(low, 0.0, piece)
                        added.append(sums[at[offset]] + piece)
                    for offset in range(len(at)):
                        sums[at[offset]] = added[offset]
        return carry

    lax.fori_loop(0, units // per_step, run_step, 0)

    def finish(pair, carry):
        lanes = tile(pair)
        first, second = sums[2 * pair], sums[2 * pair + 1]
        branch = jnp.where(low, first, second) + pltpu.roll(jnp.where(low, second, first), BLK, 1)
        current[:, lanes] = (current[:, lanes].astype(jnp.float32) + branch).astype(jnp.bfloat16)
        return carry

    over_pairs(feats, finish, 0)


def spread(source, lows, highs):
    tokens, feats = source.shape
    low = low_half(tokens)

    def visit(pair, carry):
        both = source[:, tile(pair)].astype(jnp.float32)
        moved = pltpu.roll(both, BLK, 1)
        lows[2 * pair] = jnp.where(low, both, 0.0).astype(jnp.bfloat16)
        highs[2 * pair] = jnp.where(low, 0.0, moved).astype(jnp.bfloat16)
        lows[2 * pair + 1] = jnp.where(low, moved, 0.0).astype(jnp.bfloat16)
        highs[2 * pair + 1] = jnp.where(low, 0.0, both).astype(jnp.bfloat16)
        return carry

    over_pairs(feats, visit, 0)


def pick_columns(lows, highs, cols, flat, slots):
    return jnp.concatenate(
        [
            lows[cols[flat + 2 * half]] + highs[cols[flat + 2 * half + 1]]
            for half in range(slots // 2)
        ],
        axis=1,
    )


def input_grad_layer(layer, wait, cols, bases, hidden, cotangent, out, held, lows, highs, back, rows, slots):
    tokens, feats = cotangent.shape
    units = held.shape[1]
    per_step = step_units(units, rows)
    low = low_half(tokens)

    def run_step(step, carry):
        for inner in range(per_step):
            wait(layer, step * per_step + inner)
        items = [(inner, row) for inner in range(per_step) for row in range(0, rows, 2)]

        def picked_at(index):
            inner, row = items[index]
            flat = ((layer * units + step * per_step + inner) * rows + row) * slots
            return jnp.concatenate(
                [pick_columns(lows, highs, cols, flat + which * slots, slots) for which in range(2)],
                axis=0,
            )

        upcoming = picked_at(0)
        for index, (inner, row) in enumerate(items):
            unit = step * per_step + inner
            picked = upcoming
            if index + 1 < len(items):
                upcoming = picked_at(index + 1)
            result = lax.dot_general(
                picked,
                held[layer, unit, row * BLK : (row + 2) * BLK],
                (((1,), (1,)), ((), ())),
                preferred_element_type=jnp.float32,
            )
            place = (bases[unit] + row) // 2
            back[place] = jnp.where(low, result[:tokens], result[tokens:])
        return carry

    lax.fori_loop(0, units // per_step, run_step, 0)
    inv_rms = inv_rms_of(hidden)

    def correlate(pair, total):
        unit_rows = hidden[:, tile(pair)].astype(jnp.float32) * inv_rms
        return total + back[pair] * unit_rows

    total = over_pairs(feats, correlate, jnp.zeros((tokens, LANES), jnp.float32))
    mean = jnp.sum(total, axis=-1, keepdims=True) / feats

    def finish(pair, carry):
        lanes = tile(pair)
        unit_rows = hidden[:, lanes].astype(jnp.float32) * inv_rms
        centred = back[pair] - unit_rows * mean
        out[:, lanes] = (cotangent[:, lanes].astype(jnp.float32) + inv_rms * centred).astype(jnp.bfloat16)
        return carry

    over_pairs(feats, finish, 0)


def flip(hidden, flipped):
    tokens, feats = hidden.shape
    inv_rms = inv_rms_of(hidden)

    def visit(pair, carry):
        turned = (hidden[:, tile(pair)].astype(jnp.float32) * inv_rms).T.astype(jnp.bfloat16)
        flipped[2 * pair] = turned[:BLK]
        flipped[2 * pair + 1] = turned[BLK:]
        return carry

    over_pairs(feats, visit, 0)


def block_grad_layer(layer, cols, bases, flipped, lows, highs, outs, chosen, units, rows, slots):
    items = [(which, row) for which in range(len(chosen)) for row in range(rows)]

    def operands(index):
        which, row = items[index]
        unit = chosen[which]
        flat = ((layer * units + unit) * rows + row) * slots
        return flipped[bases[unit] + row], pick_columns(lows, highs, cols, flat, slots)

    upcoming = operands(0)
    for index, (which, row) in enumerate(items):
        turned, picked = upcoming
        if index + 1 < len(items):
            upcoming = operands(index + 1)
        result = jnp.dot(turned, picked, preferred_element_type=jnp.float32)
        outs[which][layer, row * BLK : (row + 1) * BLK] = result.astype(jnp.bfloat16)


def choose(flag, first, second, target):
    @pl.when(flag == 1)
    def _():
        target[...] = first[...]

    @pl.when(flag != 1)
    def _():
        target[...] = second[...]


def forward_kernel(rows, slots, count, scale, cols, bases, flags, *rest):
    turning = scale is not None
    start, moved = rest[:2]
    rest = rest[2:]
    if turning:
        goal, rest = rest[0], rest[1:]
    pieces, rest = rest[:count], rest[count:]
    if turning:
        stash, loss_grad, final, held, parts, sums, arrived, lows, highs, back = rest
    else:
        final, held, parts, sums, arrived = rest
    start_loads(flags[0], pieces, held, arrived, None)
    choose(flags[1], start, moved, final)
    wait = functools.partial(wait_load, pieces, held, arrived)

    def run_forward(layer, carry):
        if turning:
            stash[layer] = final[...]
        forward_layer(layer, wait, cols, bases, final, held, parts, sums, rows, slots)
        return carry

    lax.fori_loop(0, 2, run_forward, 0)
    if not turning:
        return
    tokens, feats = final.shape

    def residue(pair, carry):
        lanes = tile(pair)
        gap = final[:, lanes].astype(jnp.float32) - goal[:, lanes].astype(jnp.float32)
        loss_grad[:, lanes] = (gap * scale).astype(jnp.bfloat16)
        return carry

    over_pairs(feats, residue, 0)
    final[...] = loss_grad[...]

    def run_back(turn, carry):
        layer = 1 - turn
        spread(final, lows, highs)
        input_grad_layer(
            layer,
            lambda *_: None,
            cols,
            bases,
            stash.at[layer],
            final,
            final,
            held,
            lows,
            highs,
            back,
            rows,
            slots,
        )
        return carry

    lax.fori_loop(0, 2, run_back, 0)


def state_of(tokens, feats):
    return jax.ShapeDtypeStruct((tokens, feats), jnp.bfloat16)


def forward_pass(start, moved, goal, scale, pieces, meta, rows, slots):
    tokens, feats = start.shape
    blocks = feats // BLK
    units = len(pieces) // 2
    stack = jax.ShapeDtypeStruct((2, tokens, feats), jnp.bfloat16)
    scratch = [
        pltpu.VMEM((2, units) + pieces[0].shape, jnp.bfloat16),
        pltpu.VMEM((blocks, tokens, LANES), jnp.bfloat16),
        pltpu.VMEM((blocks, tokens, LANES), jnp.float32),
        pltpu.SemaphoreType.DMA((2, units)),
    ]
    outs = [state_of(tokens, feats)]
    ins = [start, moved]
    if goal is not None:
        ins.append(goal)
        outs = [stack, state_of(tokens, feats)] + outs
        scratch += [
            pltpu.VMEM((blocks, tokens, LANES), jnp.bfloat16),
            pltpu.VMEM((blocks, tokens, LANES), jnp.bfloat16),
            pltpu.VMEM((blocks // 2, tokens, LANES), jnp.float32),
        ]
    return pl.pallas_call(
        functools.partial(forward_kernel, rows, slots, len(pieces), None if goal is None else scale),
        in_specs=[IN_SMEM] * 3 + [IN_VMEM] * len(ins) + [IN_HBM] * len(pieces),
        out_specs=[IN_VMEM] * len(outs),
        out_shape=outs,
        scratch_shapes=scratch,
        compiler_params=pltpu.CompilerParams(vmem_limit_bytes=VMEM_LIMIT),
        name="forward_layers" if goal is None else "turning_layers",
    )(*meta, *ins, *pieces)


def backward_kernel(rows, slots, count, depth, chosen, cols, bases, flags, stash, loss_grad, moved, *rest):
    pieces, rest = rest[:count], rest[count:]
    if depth == 1:
        cotangents, outs = rest[0], rest[1 : 1 + len(chosen)]
        first, second = cotangents.at[1], cotangents.at[0]
    else:
        first = second = rest[0]
    held, lows, highs, back, arrived = rest[-6:-1]
    flipped = rest[-1]
    units = count // 2
    start_loads(flags[0], pieces, held, arrived, 1 if depth == 1 else None)
    choose(flags[2], loss_grad, moved, first)
    wait = functools.partial(wait_load, pieces, held, arrived)

    def run_back(layer):
        spread(first, lows, highs)
        input_grad_layer(
            layer, wait, cols, bases, stash.at[layer], first, second, held, lows, highs, back, rows, slots
        )

    run_back(1)
    if depth == 2:
        run_back(0)
        return
    for layer in (1, 0):
        if layer == 0:
            spread(second, lows, highs)
        flip(stash.at[layer], flipped)
        block_grad_layer(layer, cols, bases, flipped, lows, highs, outs, chosen, units, rows, slots)


def backward_pass(stash, loss_grad, moved, pieces, meta, rows, slots, depth, chosen):
    _, tokens, feats = stash.shape
    blocks = feats // BLK
    units = len(pieces) // 2
    if depth == 1:
        outs = [jax.ShapeDtypeStruct((2, tokens, feats), jnp.bfloat16)]
        outs += [grad_shape(rows, slots) for _ in chosen]
    else:
        outs = [state_of(tokens, feats)]
    return pl.pallas_call(
        functools.partial(backward_kernel, rows, slots, len(pieces), depth, tuple(chosen)),
        in_specs=[IN_SMEM] * 3 + [IN_VMEM] * 3 + [IN_HBM] * len(pieces),
        out_specs=[IN_VMEM] * len(outs),
        out_shape=outs,
        scratch_shapes=[
            pltpu.VMEM((2, units) + pieces[0].shape, jnp.bfloat16),
            pltpu.VMEM((blocks, tokens, LANES), jnp.bfloat16),
            pltpu.VMEM((blocks, tokens, LANES), jnp.bfloat16),
            pltpu.VMEM((blocks // 2, tokens, LANES), jnp.float32),
            pltpu.SemaphoreType.DMA((2, units)),
            pltpu.VMEM((blocks, BLK, tokens), jnp.bfloat16),
        ],
        compiler_params=pltpu.CompilerParams(vmem_limit_bytes=VMEM_LIMIT),
        name="backward_layers",
    )(*meta, stash, loss_grad, moved, *pieces)


def grad_shape(rows, slots):
    return jax.ShapeDtypeStruct((2, rows * BLK, slots * BLK), jnp.bfloat16)


def block_grad_kernel(rows, slots, chosen, units, cols, bases, stash, cotangents, *rest):
    outs, (flipped, lows, highs) = rest[:-3], rest[-3:]

    def run(layer, carry):
        spread(cotangents.at[layer], lows, highs)
        flip(stash.at[layer], flipped)
        block_grad_layer(layer, cols, bases, flipped, lows, highs, outs, chosen, units, rows, slots)
        return carry

    lax.fori_loop(0, 2, run, 0)


def block_grad_pass(stash, cotangents, meta, rows, slots, chosen):
    _, tokens, feats = stash.shape
    blocks = feats // BLK
    cols, bases, _ = meta
    return pl.pallas_call(
        functools.partial(block_grad_kernel, rows, slots, tuple(chosen), bases.shape[0]),
        in_specs=[IN_SMEM] * 2 + [IN_VMEM] * 2,
        out_specs=[IN_VMEM] * len(chosen),
        out_shape=[grad_shape(rows, slots) for _ in chosen],
        scratch_shapes=[
            pltpu.VMEM((blocks, BLK, tokens), jnp.bfloat16),
            pltpu.VMEM((blocks, tokens, LANES), jnp.bfloat16),
            pltpu.VMEM((blocks, tokens, LANES), jnp.bfloat16),
        ],
        compiler_params=pltpu.CompilerParams(vmem_limit_bytes=VMEM_LIMIT),
        name="block_grads",
    )(cols, bases, stash, cotangents)


def to_rows(blocks):
    rows, slots, _ = blocks.shape
    split = blocks.reshape(rows, slots, BLK, BLK)
    return split.transpose(0, 2, 1, 3).reshape(rows * BLK, slots * BLK)


def from_rows(matrix, slots):
    rows = matrix.shape[0] // BLK
    split = matrix.reshape(rows, BLK, slots, BLK)
    return split.transpose(0, 2, 1, 3).reshape(rows, slots, BLK * BLK)


def folded(count):
    return list(range(0, 1)) + list(range(1, count, 2)) + list(range(2, count, 2))[::-1]


def body(inputs, target, blocks, columns, counts):
    section_id = lax.axis_index("section")
    section_count = lax.axis_size("section")
    dp_id = lax.axis_index("dp")
    dp_count = lax.axis_size("dp")
    mb_count, tok_local, feats = inputs.shape
    rows, slots = columns.shape[1:]
    loss_scale = (mb_count * tok_local * dp_count) ** (-0.5)
    places = dp_count // 2
    place = dp_id // 2
    core = dp_id % 2
    side = section_id % 2
    stage = section_id // 2
    stages = section_count // 2
    share = mb_count * tok_local // 2

    around = folded(places)
    ranks = [around.index(spot) for spot in range(places)]
    rank = jnp.array(ranks, jnp.int32)[place]
    hops = [
        (2 * around[i] + half, 2 * around[(i + 1) % places] + half)
        for i in range(places)
        for half in range(2)
    ]

    def ring(array):
        return lax.ppermute(array, "dp", hops)

    def sibling(array):
        return lax.ppermute(array, "dp", [(i, i ^ 1) for i in range(dp_count)])

    def partner(array):
        return lax.ppermute(array, "section", [(i, i ^ 1) for i in range(section_count)])

    def partner_sibling(array):
        pairs = [
            (s * dp_count + d, (s ^ 1) * dp_count + (d ^ 1))
            for s in range(section_count)
            for d in range(dp_count)
        ]
        return lax.ppermute(array, ("section", "dp"), pairs)

    live = jnp.arange(slots, dtype=jnp.int32)[None, :] < counts[0][:, None]
    kept = jnp.where(live[:, :, None], blocks[0], jnp.zeros_like(blocks[0]))
    own = to_rows(kept)
    listed = columns[0]

    owns, others, far_owns, far_others, lists = [own], [], [], [], [listed]
    for slot in range(places):
        more = slot + 1 < places
        moving = {"other": partner(owns[slot]), "far_own": sibling(owns[slot])}
        if more:
            moving["own"] = ring(owns[slot])
            moving["list"] = ring(lists[slot])
        if slot:
            moving["far_other"] = sibling(others[slot - 1])
        if not more:
            all_lists = jnp.stack(lists)
            moving["lists"] = (partner(all_lists), sibling(all_lists), partner_sibling(all_lists))
        moving = lax.optimization_barrier(moving)
        others.append(moving["other"])
        far_owns.append(moving["far_own"])
        if more:
            owns.append(moving["own"])
            lists.append(moving["list"])
        if slot:
            far_others.append(moving["far_other"])
    far_others.append(sibling(others[-1]))
    pieces = [piece for pair in zip(owns, others) for piece in pair]
    pieces += [piece for pair in zip(far_owns, far_others) for piece in pair]

    other_lists, far_lists, far_other_lists = moving["lists"]
    by_role = jnp.stack(
        [jnp.stack([all_lists, far_lists]), jnp.stack([other_lists, far_other_lists])]
    )
    cols = jnp.where(side == 0, by_role, by_role[::-1]).reshape(-1)
    spots = jnp.array(around, jnp.int32)[(rank - jnp.arange(places)) % places]
    bases = jnp.concatenate([spots * 2 + core, spots * 2 + 1 - core]).astype(jnp.int32) * rows
    flags = jnp.stack([side, stage == 0, stage == stages - 1]).astype(jnp.int32)
    meta = (cols, bases, flags)

    def my_rows(array):
        flat = array.reshape(mb_count * tok_local, feats)
        return lax.dynamic_slice_in_dim(flat, side * share, share, 0)

    start = my_rows(inputs)
    goal = my_rows(target)
    moved = start
    for step in range(stages - 1):
        (final,) = forward_pass(start, moved, None, None, pieces, meta, rows, slots)
        moved = lax.ppermute(final, "section", [(i, i + 2) for i in range(section_count - 2)])
    stash, loss_grad, result = forward_pass(start, moved, goal, loss_scale, pieces, meta, rows, slots)
    moved = loss_grad
    for step in range(stages - 1):
        if step:
            (result,) = backward_pass(stash, loss_grad, moved, pieces, meta, rows, slots, 2, [])
        moved = lax.ppermute(result, "section", [(i + 2, i) for i in range(section_count - 2)])

    order = list(range(1, places)) + [0]

    def units_of(group):
        return [unit for slot in group for unit in (slot, places + slot)]

    def fold(slot, near, far):
        both = add_rounded(near, sibling(far))
        outgoing = lax.dynamic_index_in_dim(both, 1 - side, 0, keepdims=False)
        return lax.dynamic_index_in_dim(both, side, 0, keepdims=False), outgoing

    early, late = order[:1], order[1:]
    cotangents, near, far = backward_pass(
        stash, loss_grad, moved, pieces, meta, rows, slots, 1, units_of(early)
    )
    kept_here, outgoing = fold(early[0], near, far)
    cotangents, outgoing = lax.optimization_barrier((cotangents, outgoing))
    coming = partner(outgoing)
    grads = block_grad_pass(stash, cotangents, meta, rows, slots, units_of(late))
    folds = [fold(slot, grads[2 * i], grads[2 * i + 1]) for i, slot in enumerate(late)]
    coming, folds = lax.optimization_barrier((coming, folds))
    travelling = add_rounded(kept_here, coming)
    for kept_here, outgoing in folds:
        passed, coming = lax.optimization_barrier((ring(travelling), partner(outgoing)))
        total = kept_here.astype(jnp.float32) + coming.astype(jnp.float32) + passed.astype(jnp.float32)
        travelling = total.astype(jnp.bfloat16)
    result = from_rows(travelling, slots)
    return jnp.where(live[:, :, None], result, jnp.zeros_like(result))[None]


def add_rounded(left, right):
    return (left.astype(jnp.float32) + right.astype(jnp.float32)).astype(jnp.bfloat16)


def solution(mesh):
    return jax.shard_map(
        body,
        mesh=mesh,
        in_specs=(
            P(None, "dp", None),
            P(None, "dp", None),
            P("section", "dp", None, None),
            P("section", "dp", None),
            P("section", "dp"),
        ),
        out_specs=P("section", "dp", None, None),
        check_vma=False,
    )
```

```python
import functools

import jax
import jax.numpy as jnp
from jax import lax
from jax.experimental import pallas as pl
from jax.experimental.pallas import tpu as pltpu
from jax.sharding import PartitionSpec as P

BLK = 64
LANES = 128
EPSILON = 1e-05
VMEM_LIMIT = 32 * 1024 * 1024
STEP_ROWS = 8

TAIL = 16

IN_VMEM = pl.BlockSpec(memory_space=pltpu.VMEM)
IN_SMEM = pl.BlockSpec(memory_space=pltpu.SMEM)
IN_HBM = pl.BlockSpec(memory_space=pl.ANY)


def about(microseconds):
    return pl.CostEstimate(
        flops=int(microseconds * 1.1e9), bytes_accessed=1 << 20, transcendentals=0
    )


def step_units(units, rows):
    size = max(1, STEP_ROWS // rows)
    while units % size:
        size -= 1
    return size


def low_half(rows):
    return lax.broadcasted_iota(jnp.int32, (rows, LANES), 1) < BLK


def tile(pair):
    return pl.ds(pl.multiple_of(pair * LANES, LANES), LANES)


def over_pairs(feats, visit, carry):
    return lax.fori_loop(0, feats // LANES, visit, carry, unroll=4)


def inv_rms_of(ref):
    tokens, feats = ref.shape

    def visit(pair, total):
        values = ref[:, tile(pair)].astype(jnp.float32)
        return total + values * values

    total = over_pairs(feats, visit, jnp.zeros((tokens, LANES), jnp.float32))
    return lax.rsqrt(jnp.sum(total, axis=-1, keepdims=True) / feats + EPSILON)


def start_loads(side, pieces, held, arrived, wanted):
    for unit in range(len(pieces) // 2):
        own, other = pieces[2 * unit], pieces[2 * unit + 1]
        for piece, layer in ((own, side), (other, 1 - side)):
            copy = pltpu.make_async_copy(piece, held.at[layer, unit], arrived.at[layer, unit])
            if wanted is None:
                copy.start()
            else:
                pl.when(layer == wanted)(copy.start)


def wait_load(pieces, held, arrived, layer, unit):
    pltpu.make_async_copy(pieces[0], held.at[layer, unit], arrived.at[layer, unit]).wait()


def forward_layer(layer, wait, cols, bases, current, held, parts, sums, rows, slots):
    tokens, feats = current.shape
    units = held.shape[1]
    per_step = step_units(units, rows)
    low = low_half(tokens)
    inv_rms = inv_rms_of(current)

    def normalise(pair, carry):
        lanes = tile(pair)
        unit_rows = current[:, lanes].astype(jnp.float32) * inv_rms
        parts[2 * pair] = jnp.where(low, unit_rows, 0.0).astype(jnp.bfloat16)
        parts[2 * pair + 1] = jnp.where(low, 0.0, unit_rows).astype(jnp.bfloat16)
        sums[2 * pair] = jnp.zeros((tokens, LANES), jnp.float32)
        sums[2 * pair + 1] = jnp.zeros((tokens, LANES), jnp.float32)
        return carry

    over_pairs(feats, normalise, 0)

    def run_step(step, carry):
        for inner in range(per_step):
            wait(layer, step * per_step + inner)
        items = [(inner, row) for inner in range(per_step) for row in range(0, rows, 2)]

        def product_of(index):
            inner, row = items[index]
            unit = step * per_step + inner
            place = bases[unit] + row
            left = jnp.concatenate([parts[place], parts[place + 1]], axis=0)
            right = held[layer, unit, row * BLK : (row + 2) * BLK]
            return jnp.dot(left, right, preferred_element_type=jnp.float32)

        upcoming = product_of(0)
        for index, (inner, row) in enumerate(items):
            product = upcoming
            if index + 1 < len(items):
                upcoming = product_of(index + 1)
            for which in range(2):
                line = layer * units + step * per_step + inner
                flat = (row + which) * slots
                for begin in range(0, slots, 4):
                    at = [cols[line, flat + slot] for slot in range(begin, min(begin + 4, slots))]
                    added = []
                    for offset in range(len(at)):
                        slot = begin + offset
                        lanes = slice((slot // 2) * LANES, (slot // 2 + 1) * LANES)
                        piece = product[which * tokens : (which + 1) * tokens, lanes]
                        piece = jnp.where(low, piece, 0.0) if slot % 2 == 0 else jnp.where(low, 0.0, piece)
                        added.append(sums[at[offset]] + piece)
                    for offset in range(len(at)):
                        sums[at[offset]] = added[offset]
        return carry

    lax.fori_loop(0, units // per_step, run_step, 0)

    def finish(pair, carry):
        lanes = tile(pair)
        first, second = sums[2 * pair], sums[2 * pair + 1]
        branch = jnp.where(low, first, second) + pltpu.roll(jnp.where(low, second, first), BLK, 1)
        current[:, lanes] = (current[:, lanes].astype(jnp.float32) + branch).astype(jnp.bfloat16)
        return carry

    over_pairs(feats, finish, 0)


def spread(source, lows, highs):
    tokens, feats = source.shape
    low = low_half(tokens)

    def visit(pair, carry):
        both = source[:, tile(pair)].astype(jnp.float32)
        moved = pltpu.roll(both, BLK, 1)
        lows[2 * pair] = jnp.where(low, both, 0.0).astype(jnp.bfloat16)
        highs[2 * pair] = jnp.where(low, 0.0, moved).astype(jnp.bfloat16)
        lows[2 * pair + 1] = jnp.where(low, moved, 0.0).astype(jnp.bfloat16)
        highs[2 * pair + 1] = jnp.where(low, 0.0, both).astype(jnp.bfloat16)
        return carry

    over_pairs(feats, visit, 0)


def pick_columns(lows, highs, cols, line, flat, slots):
    return jnp.concatenate(
        [
            lows[cols[line, flat + 2 * half]] + highs[cols[line, flat + 2 * half + 1]]
            for half in range(slots // 2)
        ],
        axis=1,
    )


def input_grad_layer(layer, wait, cols, bases, hidden, cotangent, out, held, lows, highs, back, rows, slots):
    tokens, feats = cotangent.shape
    units = held.shape[1]
    per_step = step_units(units, rows)
    low = low_half(tokens)

    def run_step(step, carry):
        for inner in range(per_step):
            wait(layer, step * per_step + inner)
        items = [(inner, row) for inner in range(per_step) for row in range(0, rows, 2)]

        def picked_at(index):
            inner, row = items[index]
            line = layer * units + step * per_step + inner
            return jnp.concatenate(
                [
                    pick_columns(lows, highs, cols, line, (row + which) * slots, slots)
                    for which in range(2)
                ],
                axis=0,
            )

        upcoming = picked_at(0)
        for index, (inner, row) in enumerate(items):
            unit = step * per_step + inner
            picked = upcoming
            if index + 1 < len(items):
                upcoming = picked_at(index + 1)
            result = lax.dot_general(
                picked,
                held[layer, unit, row * BLK : (row + 2) * BLK],
                (((1,), (1,)), ((), ())),
                preferred_element_type=jnp.float32,
            )
            place = (bases[unit] + row) // 2
            back[place] = jnp.where(low, result[:tokens], result[tokens:])
        return carry

    lax.fori_loop(0, units // per_step, run_step, 0)
    inv_rms = inv_rms_of(hidden)

    def correlate(pair, total):
        unit_rows = hidden[:, tile(pair)].astype(jnp.float32) * inv_rms
        return total + back[pair] * unit_rows

    total = over_pairs(feats, correlate, jnp.zeros((tokens, LANES), jnp.float32))
    mean = jnp.sum(total, axis=-1, keepdims=True) / feats

    def finish(pair, carry):
        lanes = tile(pair)
        unit_rows = hidden[:, lanes].astype(jnp.float32) * inv_rms
        centred = back[pair] - unit_rows * mean
        out[:, lanes] = (cotangent[:, lanes].astype(jnp.float32) + inv_rms * centred).astype(jnp.bfloat16)
        return carry

    over_pairs(feats, finish, 0)


def block_grad_layer(layer, cols, bases, flipped, lows, highs, outs, chosen, units, rows, slots):
    items = [(which, row) for which in range(len(chosen)) for row in range(rows)]

    def operands(index):
        which, row = items[index]
        unit = chosen[which]
        picked = pick_columns(lows, highs, cols, layer * units + unit, row * slots, slots)
        return flipped[layer, which * rows + row], picked

    upcoming = operands(0)
    for index, (which, row) in enumerate(items):
        turned, picked = upcoming
        if index + 1 < len(items):
            upcoming = operands(index + 1)
        result = jnp.dot(turned, picked, preferred_element_type=jnp.float32)
        outs[which][layer, row * BLK : (row + 1) * BLK] = result.astype(jnp.bfloat16)


def choose(flag, first, second, target):
    @pl.when(flag == 1)
    def _():
        target[...] = first[...]

    @pl.when(flag != 1)
    def _():
        target[...] = second[...]


def forward_kernel(rows, slots, count, scale, cols, bases, flags, *rest):
    turning = scale is not None
    start, moved = rest[:2]
    rest = rest[2:]
    if turning:
        goal, rest = rest[0], rest[1:]
    pieces, rest = rest[:count], rest[count:]
    if turning:
        stash, loss_grad, final, held, parts, sums, arrived, lows, highs, back = rest
    else:
        final, held, parts, sums, arrived = rest
    start_loads(flags[0], pieces, held, arrived, None)
    choose(flags[1], start, moved, final)
    wait = functools.partial(wait_load, pieces, held, arrived)

    def run_forward(layer, carry):
        if turning:
            stash[layer] = final[...]
        forward_layer(layer, wait, cols, bases, final, held, parts, sums, rows, slots)
        return carry

    lax.fori_loop(0, 2, run_forward, 0)
    if not turning:
        return
    tokens, feats = final.shape

    def residue(pair, carry):
        lanes = tile(pair)
        gap = final[:, lanes].astype(jnp.float32) - goal[:, lanes].astype(jnp.float32)
        loss_grad[:, lanes] = (gap * scale).astype(jnp.bfloat16)
        return carry

    over_pairs(feats, residue, 0)
    final[...] = loss_grad[...]

    def run_back(turn, carry):
        layer = 1 - turn
        spread(final, lows, highs)
        input_grad_layer(
            layer,
            lambda *_: None,
            cols,
            bases,
            stash.at[layer],
            final,
            final,
            held,
            lows,
            highs,
            back,
            rows,
            slots,
        )
        return carry

    lax.fori_loop(0, 2, run_back, 0)


def state_of(tokens, feats):
    return jax.ShapeDtypeStruct((tokens, feats), jnp.bfloat16)


def forward_pass(start, moved, goal, scale, pieces, meta, rows, slots):
    tokens, feats = start.shape
    blocks = feats // BLK
    units = len(pieces) // 2
    stack = jax.ShapeDtypeStruct((2, tokens, feats), jnp.bfloat16)
    scratch = [
        pltpu.VMEM((2, units) + pieces[0].shape, jnp.bfloat16),
        pltpu.VMEM((blocks, tokens, LANES), jnp.bfloat16),
        pltpu.VMEM((blocks, tokens, LANES), jnp.float32),
        pltpu.SemaphoreType.DMA((2, units)),
    ]
    outs = [state_of(tokens, feats)]
    ins = [start, moved]
    if goal is not None:
        ins.append(goal)
        outs = [stack, state_of(tokens, feats)] + outs
        scratch += [
            pltpu.VMEM((blocks, tokens, LANES), jnp.bfloat16),
            pltpu.VMEM((blocks, tokens, LANES), jnp.bfloat16),
            pltpu.VMEM((blocks // 2, tokens, LANES), jnp.float32),
        ]
    return pl.pallas_call(
        functools.partial(forward_kernel, rows, slots, len(pieces), None if goal is None else scale),
        in_specs=[IN_SMEM] * 3 + [IN_VMEM] * len(ins) + [IN_HBM] * len(pieces),
        out_specs=[IN_VMEM] * len(outs),
        out_shape=outs,
        scratch_shapes=scratch,
        compiler_params=pltpu.CompilerParams(vmem_limit_bytes=VMEM_LIMIT),
        cost_estimate=about(8 if goal is None else 14),
        name="forward_layers" if goal is None else "turning_layers",
    )(*meta, *ins, *pieces)


def backward_kernel(rows, slots, count, depth, cols, bases, flags, stash, loss_grad, moved, *rest):
    pieces, rest = rest[:count], rest[count:]
    outs, held, lows, highs, back, arrived = rest
    if depth == 1:
        first, second = outs.at[1], outs.at[0]
    else:
        first = second = outs
    start_loads(flags[0], pieces, held, arrived, 1 if depth == 1 else None)
    choose(flags[2], loss_grad, moved, first)
    wait = functools.partial(wait_load, pieces, held, arrived)

    def run_back(layer):
        spread(first, lows, highs)
        input_grad_layer(
            layer, wait, cols, bases, stash.at[layer], first, second, held, lows, highs, back, rows, slots
        )

    run_back(1)
    if depth == 2:
        run_back(0)


def backward_pass(stash, loss_grad, moved, pieces, meta, rows, slots, depth):
    _, tokens, feats = stash.shape
    blocks = feats // BLK
    units = len(pieces) // 2
    if depth == 1:
        out = jax.ShapeDtypeStruct((2, tokens, feats), jnp.bfloat16)
    else:
        out = state_of(tokens, feats)
    return pl.pallas_call(
        functools.partial(backward_kernel, rows, slots, len(pieces), depth),
        in_specs=[IN_SMEM] * 3 + [IN_VMEM] * 3 + [IN_HBM] * len(pieces),
        out_specs=IN_VMEM,
        out_shape=out,
        scratch_shapes=[
            pltpu.VMEM((2, units) + pieces[0].shape, jnp.bfloat16),
            pltpu.VMEM((blocks, tokens, LANES), jnp.bfloat16),
            pltpu.VMEM((blocks, tokens, LANES), jnp.bfloat16),
            pltpu.VMEM((blocks // 2, tokens, LANES), jnp.float32),
            pltpu.SemaphoreType.DMA((2, units)),
        ],
        compiler_params=pltpu.CompilerParams(vmem_limit_bytes=VMEM_LIMIT),
        cost_estimate=about(4 * depth),
        name="backward_layers",
    )(*meta, stash, loss_grad, moved, *pieces)


def join_tokens(sources, joined, arrived):
    copies = []
    begin = 0
    for index, source in enumerate(sources):
        span = pl.ds(begin, source.shape[1])
        copies.append(pltpu.make_async_copy(source, joined.at[:, span], arrived.at[index]))
        begin += source.shape[1]
    for copy in copies:
        copy.start()
    for copy in copies:
        copy.wait()


def flip_kernel(*refs):
    *sources, flipped, joined, arrived = refs
    join_tokens(sources, joined, arrived)

    def run(layer, carry):
        hidden = joined.at[layer]
        inv_rms = inv_rms_of(hidden)

        def visit(pair, carry):
            turned = (hidden[:, tile(pair)].astype(jnp.float32) * inv_rms).T.astype(jnp.bfloat16)
            flipped[layer, 2 * pair] = turned[:BLK]
            flipped[layer, 2 * pair + 1] = turned[BLK:]
            return carry

        over_pairs(hidden.shape[1], visit, 0)
        return carry

    lax.fori_loop(0, 2, run, 0)


def flip_pass(stashes):
    tokens = sum(stash.shape[1] for stash in stashes)
    feats = stashes[0].shape[2]
    return pl.pallas_call(
        flip_kernel,
        in_specs=[IN_HBM] * len(stashes),
        out_specs=IN_VMEM,
        out_shape=jax.ShapeDtypeStruct((2, feats // BLK, BLK, tokens), jnp.bfloat16),
        scratch_shapes=[
            pltpu.VMEM((2, tokens, feats), jnp.bfloat16),
            pltpu.SemaphoreType.DMA((len(stashes),)),
        ],
        compiler_params=pltpu.CompilerParams(vmem_limit_bytes=VMEM_LIMIT),
        cost_estimate=about(4),
        name="flip_rows",
    )(*stashes)


def grad_shape(rows, slots):
    return jax.ShapeDtypeStruct((2, rows * BLK, slots * BLK), jnp.bfloat16)


def block_grad_kernel(rows, slots, chosen, units, parts, cols, bases, turned, *rest):
    sources, rest = rest[:parts], rest[parts:]
    outs = rest[: len(chosen)]
    joined, flipped, lows, highs, arrived, fetched = rest[len(chosen) :]
    fetches = [
        pltpu.make_async_copy(
            turned.at[:, pl.ds(bases[unit], rows)],
            flipped.at[:, pl.ds(which * rows, rows)],
            fetched.at[which],
        )
        for which, unit in enumerate(chosen)
    ]
    for fetch in fetches:
        fetch.start()
    join_tokens(sources, joined, arrived)
    for fetch in fetches:
        fetch.wait()

    def run(layer, carry):
        spread(joined.at[layer], lows, highs)
        block_grad_layer(layer, cols, bases, flipped, lows, highs, outs, chosen, units, rows, slots)
        return carry

    lax.fori_loop(0, 2, run, 0)


def block_grad_pass(turned, cotangents, meta, rows, slots, chosen):
    _, blocks, _, tokens = turned.shape
    feats = blocks * BLK
    cols, bases, _ = meta
    return pl.pallas_call(
        functools.partial(
            block_grad_kernel, rows, slots, tuple(chosen), bases.shape[0], len(cotangents)
        ),
        in_specs=[IN_SMEM] * 2 + [IN_HBM] * (1 + len(cotangents)),
        out_specs=[IN_VMEM] * len(chosen),
        out_shape=[grad_shape(rows, slots) for _ in chosen],
        scratch_shapes=[
            pltpu.VMEM((2, tokens, feats), jnp.bfloat16),
            pltpu.VMEM((2, len(chosen) * rows, BLK, tokens), jnp.bfloat16),
            pltpu.VMEM((blocks, tokens, LANES), jnp.bfloat16),
            pltpu.VMEM((blocks, tokens, LANES), jnp.bfloat16),
            pltpu.SemaphoreType.DMA((len(cotangents),)),
            pltpu.SemaphoreType.DMA((len(chosen),)),
        ],
        compiler_params=pltpu.CompilerParams(vmem_limit_bytes=VMEM_LIMIT),
        cost_estimate=about(2 + len(chosen)),
        name="block_grads",
    )(cols, bases, turned, *cotangents)


def list_kernel(rows, slots, count, flags, *rest):
    pieces, (listed, tails, arrived) = rest[:count], rest[count:]
    units = count // 2
    copies = [
        pltpu.make_async_copy(pieces[i].at[pl.ds(rows * BLK, TAIL)], tails.at[i], arrived.at[i])
        for i in range(count)
    ]
    for copy in copies:
        copy.start()
    for i, copy in enumerate(copies):
        copy.wait()
        layer = flags[0] if i % 2 == 0 else 1 - flags[0]
        line = tails[i].astype(jnp.float32)[:1, : listed.shape[1]]
        listed[pl.ds(layer * units + i // 2, 1), :] = line.astype(jnp.int32)


def list_pass(pieces, flags, rows, slots):
    count = len(pieces)
    width = -(-rows * slots // LANES) * LANES
    return pl.pallas_call(
        functools.partial(list_kernel, rows, slots, count),
        in_specs=[IN_SMEM] + [IN_HBM] * count,
        out_specs=IN_VMEM,
        out_shape=jax.ShapeDtypeStruct((count, width), jnp.int32),
        scratch_shapes=[
            pltpu.VMEM((count, TAIL, slots * BLK), jnp.bfloat16),
            pltpu.SemaphoreType.DMA((count,)),
        ],
        cost_estimate=about(2),
        name="list_columns",
    )(flags, *pieces)


def to_rows(blocks):
    rows, slots, _ = blocks.shape
    split = blocks.reshape(rows, slots, BLK, BLK)
    return split.transpose(0, 2, 1, 3).reshape(rows * BLK, slots * BLK)


def from_rows(matrix, slots):
    rows = matrix.shape[0] // BLK
    split = matrix.reshape(rows, BLK, slots, BLK)
    return split.transpose(0, 2, 1, 3).reshape(rows, slots, BLK * BLK)


def token_cuts(tokens):
    if tokens % 16 or tokens < 32:
        return [(0, tokens)]
    first = -(-tokens // 32) * 16
    return [(0, first), (first, tokens)]


def folded(count):
    return list(range(0, 1)) + list(range(1, count, 2)) + list(range(2, count, 2))[::-1]


def body(inputs, target, blocks, columns, counts):
    section_id = lax.axis_index("section")
    section_count = lax.axis_size("section")
    dp_id = lax.axis_index("dp")
    dp_count = lax.axis_size("dp")
    mb_count, tok_local, feats = inputs.shape
    rows, slots = columns.shape[1:]
    loss_scale = (mb_count * tok_local * dp_count) ** (-0.5)
    places = dp_count // 2
    place = dp_id // 2
    core = dp_id % 2
    side = section_id % 2
    stage = section_id // 2
    stages = section_count // 2
    share = mb_count * tok_local // 2

    around = folded(places)
    ranks = [around.index(spot) for spot in range(places)]
    rank = jnp.array(ranks, jnp.int32)[place]
    hops = [
        (2 * around[i] + half, 2 * around[(i + 1) % places] + half)
        for i in range(places)
        for half in range(2)
    ]

    def ring(array):
        return lax.ppermute(array, "dp", hops)

    def sibling(array):
        return lax.ppermute(array, "dp", [(i, i ^ 1) for i in range(dp_count)])

    def partner(array):
        return lax.ppermute(array, "section", [(i, i ^ 1) for i in range(section_count)])

    live = jnp.arange(slots, dtype=jnp.int32)[None, :] < counts[0][:, None]
    kept = jnp.where(live[:, :, None], blocks[0], jnp.zeros_like(blocks[0]))
    listed = columns[0].reshape(1, rows * slots).astype(jnp.bfloat16)
    tail = jnp.pad(listed, ((0, TAIL - 1), (0, slots * BLK - rows * slots)))
    own = jnp.concatenate([to_rows(kept), tail], axis=0)

    owns, others, far_owns, far_others = [own], [], [], []
    for slot in range(places):
        moving = {"other": partner(owns[slot]), "far_own": sibling(owns[slot])}
        if slot + 1 < places:
            moving["own"] = ring(owns[slot])
        if slot:
            moving["far_other"] = sibling(others[slot - 1])
        moving = lax.optimization_barrier(moving)
        others.append(moving["other"])
        far_owns.append(moving["far_own"])
        if slot + 1 < places:
            owns.append(moving["own"])
        if slot:
            far_others.append(moving["far_other"])
    far_others.append(sibling(others[-1]))
    pieces = [piece for pair in zip(owns, others) for piece in pair]
    pieces += [piece for pair in zip(far_owns, far_others) for piece in pair]

    spots = jnp.array(around, jnp.int32)[(rank - jnp.arange(places)) % places]
    bases = jnp.concatenate([spots * 2 + core, spots * 2 + 1 - core]).astype(jnp.int32) * rows
    flags = jnp.stack([side, stage == 0, stage == stages - 1]).astype(jnp.int32)
    cols = list_pass(pieces, flags, rows, slots)
    meta = (cols, bases, flags)

    def my_rows(array):
        flat = array.reshape(mb_count * tok_local, feats)
        return lax.dynamic_slice_in_dim(flat, side * share, share, 0)

    def hop(array, distance):
        route = [(i, i + distance) for i in range(section_count) if 0 <= i + distance < section_count]
        return lax.ppermute(array, "section", route)

    cuts = token_cuts(share)
    ways = range(len(cuts))
    whole_start, whole_goal = my_rows(inputs), my_rows(target)
    start = [whole_start[begin:end] for begin, end in cuts]
    goal = [whole_goal[begin:end] for begin, end in cuts]
    moved = list(start)
    for step in range(stages - 1):
        final = [
            forward_pass(start[i], moved[i], None, None, pieces, meta, rows, slots)[0] for i in ways
        ]
        moved = [hop(final[i], 2) for i in ways]
    turned = [
        forward_pass(start[i], moved[i], goal[i], loss_scale, pieces, meta, rows, slots) for i in ways
    ]
    stashes, loss_grads, result = [list(column) for column in zip(*turned)]
    moved = loss_grads
    for step in range(stages - 1):
        if step:
            result = [
                backward_pass(stashes[i], loss_grads[i], moved[i], pieces, meta, rows, slots, 2)
                for i in ways
            ]
        moved = [hop(result[i], -2) for i in ways]
    flipped = flip_pass(stashes)
    cotangents = [
        backward_pass(stashes[i], loss_grads[i], moved[i], pieces, meta, rows, slots, 1) for i in ways
    ]

    order = list(range(1, places)) + [0]

    def units_of(group):
        return [unit for slot in group for unit in (slot, places + slot)]

    def fold(near, far):
        both = add_rounded(near, sibling(far))
        outgoing = lax.dynamic_index_in_dim(both, 1 - side, 0, keepdims=False)
        return lax.dynamic_index_in_dim(both, side, 0, keepdims=False), outgoing

    early, late = order[:1], order[1:]
    near, far = block_grad_pass(flipped, cotangents, meta, rows, slots, units_of(early))
    kept_here, outgoing = fold(near, far)
    cotangents, outgoing = lax.optimization_barrier((cotangents, outgoing))
    coming = partner(outgoing)
    grads = block_grad_pass(flipped, cotangents, meta, rows, slots, units_of(late))
    folds = [fold(grads[2 * i], grads[2 * i + 1]) for i in range(len(late))]
    coming, folds = lax.optimization_barrier((coming, folds))
    travelling = add_rounded(kept_here, coming)
    for kept_here, outgoing in folds:
        passed, coming = lax.optimization_barrier((ring(travelling), partner(outgoing)))
        total = kept_here.astype(jnp.float32) + coming.astype(jnp.float32) + passed.astype(jnp.float32)
        travelling = total.astype(jnp.bfloat16)
    result = from_rows(travelling, slots)
    return jnp.where(live[:, :, None], result, jnp.zeros_like(result))[None]


def add_rounded(left, right):
    return (left.astype(jnp.float32) + right.astype(jnp.float32)).astype(jnp.bfloat16)


def solution(mesh):
    return jax.shard_map(
        body,
        mesh=mesh,
        in_specs=(
            P(None, "dp", None),
            P(None, "dp", None),
            P("section", "dp", None, None),
            P("section", "dp", None),
            P("section", "dp"),
        ),
        out_specs=P("section", "dp", None, None),
        check_vma=False,
    )
```

```python
import functools

import jax
import jax.numpy as jnp
from jax import lax
from jax.experimental import pallas as pl
from jax.experimental.pallas import tpu as pltpu
from jax.sharding import PartitionSpec as P

BLK = 64
LANES = 128
EPSILON = 1e-05
VMEM_LIMIT = 32 * 1024 * 1024
STEP_ROWS = 8

TAIL = 16

IN_VMEM = pl.BlockSpec(memory_space=pltpu.VMEM)
IN_SMEM = pl.BlockSpec(memory_space=pltpu.SMEM)
IN_HBM = pl.BlockSpec(memory_space=pl.ANY)


def about(microseconds):
    return pl.CostEstimate(
        flops=int(microseconds * 1.1e9), bytes_accessed=1 << 20, transcendentals=0
    )


def step_units(units, rows):
    size = max(1, STEP_ROWS // rows)
    while units % size:
        size -= 1
    return size


def low_half(rows):
    return lax.broadcasted_iota(jnp.int32, (rows, LANES), 1) < BLK


def tile(pair):
    return pl.ds(pl.multiple_of(pair * LANES, LANES), LANES)


def over_pairs(feats, visit, carry):
    return lax.fori_loop(0, feats // LANES, visit, carry, unroll=4)


def inv_rms_of(ref):
    tokens, feats = ref.shape

    def visit(pair, total):
        values = ref[:, tile(pair)].astype(jnp.float32)
        return total + values * values

    total = over_pairs(feats, visit, jnp.zeros((tokens, LANES), jnp.float32))
    return lax.rsqrt(jnp.sum(total, axis=-1, keepdims=True) / feats + EPSILON)


def start_loads(pieces, held, arrived, layers):
    for layer in layers:
        for unit in range(held.shape[1]):
            pltpu.make_async_copy(
                pieces.at[layer, unit], held.at[layer, unit], arrived.at[layer, unit]
            ).start()


def wait_load(pieces, held, arrived, layer, unit):
    pltpu.make_async_copy(
        pieces.at[layer, unit], held.at[layer, unit], arrived.at[layer, unit]
    ).wait()


def group_of(rows):
    return 4 if rows % 4 == 0 else 2


def forward_layer(layer, wait, cols, bases, current, held, parts, sums, rows, slots):
    tokens, feats = current.shape
    units = held.shape[1]
    per_step = step_units(units, rows)
    low = low_half(tokens)
    inv_rms = inv_rms_of(current)

    def normalise(pair, carry):
        lanes = tile(pair)
        unit_rows = current[:, lanes].astype(jnp.float32) * inv_rms
        parts[2 * pair] = jnp.where(low, unit_rows, 0.0).astype(jnp.bfloat16)
        parts[2 * pair + 1] = jnp.where(low, 0.0, unit_rows).astype(jnp.bfloat16)
        sums[2 * pair] = jnp.zeros((tokens, LANES), jnp.float32)
        sums[2 * pair + 1] = jnp.zeros((tokens, LANES), jnp.float32)
        return carry

    over_pairs(feats, normalise, 0)

    def run_step(step, carry):
        for inner in range(per_step):
            wait(layer, step * per_step + inner)
        group = group_of(rows)
        items = [(inner, row) for inner in range(per_step) for row in range(0, rows, group)]

        def product_of(index):
            inner, row = items[index]
            unit = step * per_step + inner
            place = bases[unit] + row
            empty = jnp.zeros((tokens, LANES), jnp.bfloat16)
            lines = []
            for which in range(group):
                line = [empty] * (group // 2)
                line[which // 2] = parts[place + which]
                lines.append(jnp.concatenate(line, axis=1))
            left = jnp.concatenate(lines, axis=0)
            right = held[layer, unit, row * BLK : (row + group) * BLK]
            return jnp.dot(left, right, preferred_element_type=jnp.float32)

        upcoming = product_of(0)
        for index, (inner, row) in enumerate(items):
            product = upcoming
            if index + 1 < len(items):
                upcoming = product_of(index + 1)
            for which in range(group):
                line = layer * units + step * per_step + inner
                flat = (row + which) * slots
                for begin in range(0, slots, 4):
                    at = [cols[line, flat + slot] for slot in range(begin, min(begin + 4, slots))]
                    added = []
                    for offset in range(len(at)):
                        slot = begin + offset
                        lanes = slice((slot // 2) * LANES, (slot // 2 + 1) * LANES)
                        piece = product[which * tokens : (which + 1) * tokens, lanes]
                        piece = jnp.where(low, piece, 0.0) if slot % 2 == 0 else jnp.where(low, 0.0, piece)
                        added.append(sums[at[offset]] + piece)
                    for offset in range(len(at)):
                        sums[at[offset]] = added[offset]
        return carry

    lax.fori_loop(0, units // per_step, run_step, 0)

    def finish(pair, carry):
        lanes = tile(pair)
        first, second = sums[2 * pair], sums[2 * pair + 1]
        branch = jnp.where(low, first, second) + pltpu.roll(jnp.where(low, second, first), BLK, 1)
        current[:, lanes] = (current[:, lanes].astype(jnp.float32) + branch).astype(jnp.bfloat16)
        return carry

    over_pairs(feats, finish, 0)


def spread(source, lows, highs):
    tokens, feats = source.shape
    low = low_half(tokens)

    def visit(pair, carry):
        both = source[:, tile(pair)].astype(jnp.float32)
        moved = pltpu.roll(both, BLK, 1)
        lows[2 * pair] = jnp.where(low, both, 0.0).astype(jnp.bfloat16)
        highs[2 * pair] = jnp.where(low, 0.0, moved).astype(jnp.bfloat16)
        lows[2 * pair + 1] = jnp.where(low, moved, 0.0).astype(jnp.bfloat16)
        highs[2 * pair + 1] = jnp.where(low, 0.0, both).astype(jnp.bfloat16)
        return carry

    over_pairs(feats, visit, 0)


def pick_columns(lows, highs, cols, line, flat, slots):
    return jnp.concatenate(
        [
            lows[cols[line, flat + 2 * half]] + highs[cols[line, flat + 2 * half + 1]]
            for half in range(slots // 2)
        ],
        axis=1,
    )


def input_grad_layer(layer, wait, cols, bases, hidden, cotangent, out, held, lows, highs, back, rows, slots):
    tokens, feats = cotangent.shape
    units = held.shape[1]
    per_step = step_units(units, rows)
    low = low_half(tokens)

    def run_step(step, carry):
        for inner in range(per_step):
            wait(layer, step * per_step + inner)
        group = group_of(rows)
        items = [(inner, row) for inner in range(per_step) for row in range(0, rows, group)]

        def picked_at(index):
            inner, row = items[index]
            line = layer * units + step * per_step + inner
            return jnp.concatenate(
                [
                    pick_columns(lows, highs, cols, line, (row + which) * slots, slots)
                    for which in range(group)
                ],
                axis=0,
            )

        upcoming = picked_at(0)
        for index, (inner, row) in enumerate(items):
            unit = step * per_step + inner
            picked = upcoming
            if index + 1 < len(items):
                upcoming = picked_at(index + 1)
            result = lax.dot_general(
                picked,
                held[layer, unit, row * BLK : (row + group) * BLK],
                (((1,), (1,)), ((), ())),
                preferred_element_type=jnp.float32,
            )
            for half in range(group // 2):
                lanes = slice(half * LANES, (half + 1) * LANES)
                first = result[2 * half * tokens : (2 * half + 1) * tokens, lanes]
                second = result[(2 * half + 1) * tokens : (2 * half + 2) * tokens, lanes]
                back[(bases[unit] + row) // 2 + half] = jnp.where(low, first, second)
        return carry

    lax.fori_loop(0, units // per_step, run_step, 0)
    inv_rms = inv_rms_of(hidden)

    def correlate(pair, total):
        unit_rows = hidden[:, tile(pair)].astype(jnp.float32) * inv_rms
        return total + back[pair] * unit_rows

    total = over_pairs(feats, correlate, jnp.zeros((tokens, LANES), jnp.float32))
    mean = jnp.sum(total, axis=-1, keepdims=True) / feats

    def finish(pair, carry):
        lanes = tile(pair)
        unit_rows = hidden[:, lanes].astype(jnp.float32) * inv_rms
        centred = back[pair] - unit_rows * mean
        out[:, lanes] = (cotangent[:, lanes].astype(jnp.float32) + inv_rms * centred).astype(jnp.bfloat16)
        return carry

    over_pairs(feats, finish, 0)


def block_grad_layer(layer, role, cols, spots, flipped, lows, highs, outs, chosen, units, rows, slots):
    items = [(which, row) for which in range(len(chosen)) for row in range(0, rows, 2)]
    tokens = flipped.shape[3]

    def operands(index):
        which, row = items[index]
        line = layer * units + spots[chosen[which]]
        first, second = flipped[layer, which * rows + row], flipped[layer, which * rows + row + 1]
        picked = [pick_columns(lows, highs, cols, line, (row + i) * slots, slots) for i in range(2)]
        empty = jnp.zeros((BLK, tokens), jnp.bfloat16)
        left = jnp.concatenate(
            [jnp.concatenate([first, empty], axis=1), jnp.concatenate([empty, second], axis=1)], axis=0
        )
        return left, jnp.concatenate(picked, axis=0)

    upcoming = operands(0)
    for index, (which, row) in enumerate(items):
        left, right = upcoming
        if index + 1 < len(items):
            upcoming = operands(index + 1)
        result = jnp.dot(left, right, preferred_element_type=jnp.float32)
        outs[which][role, row * BLK : (row + 2) * BLK] = result.astype(jnp.bfloat16)


def choose(flag, first, second, target):
    @pl.when(flag == 1)
    def _():
        target[...] = first[...]

    @pl.when(flag != 1)
    def _():
        target[...] = second[...]


def forward_kernel(rows, slots, scale, cols, bases, flags, *rest):
    turning = scale is not None
    start, moved = rest[:2]
    rest = rest[2:]
    if turning:
        goal, rest = rest[0], rest[1:]
    pieces, rest = rest[0], rest[1:]
    if turning:
        stash, loss_grad, final, held, parts, sums, arrived, lows, highs, back = rest
    else:
        final, held, parts, sums, arrived = rest
    start_loads(pieces, held, arrived, (0, 1))
    choose(flags[1], start, moved, final)
    wait = functools.partial(wait_load, pieces, held, arrived)

    def run_forward(layer, carry):
        if turning:
            stash[layer] = final[...]
        forward_layer(layer, wait, cols, bases, final, held, parts, sums, rows, slots)
        return carry

    lax.fori_loop(0, 2, run_forward, 0)
    if not turning:
        return
    tokens, feats = final.shape

    def residue(pair, carry):
        lanes = tile(pair)
        gap = final[:, lanes].astype(jnp.float32) - goal[:, lanes].astype(jnp.float32)
        loss_grad[:, lanes] = (gap * scale).astype(jnp.bfloat16)
        return carry

    over_pairs(feats, residue, 0)
    final[...] = loss_grad[...]

    def run_back(turn, carry):
        layer = 1 - turn
        spread(final, lows, highs)
        input_grad_layer(
            layer,
            lambda *_: None,
            cols,
            bases,
            stash.at[layer],
            final,
            final,
            held,
            lows,
            highs,
            back,
            rows,
            slots,
        )
        return carry

    lax.fori_loop(0, 2, run_back, 0)


def state_of(tokens, feats):
    return jax.ShapeDtypeStruct((tokens, feats), jnp.bfloat16)


def forward_pass(start, moved, goal, scale, pieces, meta, rows, slots):
    tokens, feats = start.shape
    blocks = feats // BLK
    units = pieces.shape[1]
    stack = jax.ShapeDtypeStruct((2, tokens, feats), jnp.bfloat16)
    scratch = [
        pltpu.VMEM(pieces.shape, jnp.bfloat16),
        pltpu.VMEM((blocks, tokens, LANES), jnp.bfloat16),
        pltpu.VMEM((blocks, tokens, LANES), jnp.float32),
        pltpu.SemaphoreType.DMA((2, units)),
    ]
    outs = [state_of(tokens, feats)]
    ins = [start, moved]
    if goal is not None:
        ins.append(goal)
        outs = [stack, state_of(tokens, feats)] + outs
        scratch += [
            pltpu.VMEM((blocks, tokens, LANES), jnp.bfloat16),
            pltpu.VMEM((blocks, tokens, LANES), jnp.bfloat16),
            pltpu.VMEM((blocks // 2, tokens, LANES), jnp.float32),
        ]
    return pl.pallas_call(
        functools.partial(forward_kernel, rows, slots, None if goal is None else scale),
        in_specs=[IN_SMEM] * 3 + [IN_VMEM] * len(ins) + [IN_HBM],
        out_specs=[IN_VMEM] * len(outs),
        out_shape=outs,
        scratch_shapes=scratch,
        compiler_params=pltpu.CompilerParams(vmem_limit_bytes=VMEM_LIMIT),
        cost_estimate=about(8 if goal is None else 14),
        name="forward_layers" if goal is None else "turning_layers",
    )(*meta, *ins, pieces)


def backward_kernel(
    rows, slots, depth, cols, bases, flags, stash, loss_grad, moved, pieces, outs, held, lows, highs, back, arrived
):
    if depth == 1:
        first, second = outs.at[1], outs.at[0]
    else:
        first = second = outs
    start_loads(pieces, held, arrived, (1,) if depth == 1 else (1, 0))
    choose(flags[2], loss_grad, moved, first)
    wait = functools.partial(wait_load, pieces, held, arrived)

    def run_back(layer):
        spread(first, lows, highs)
        input_grad_layer(
            layer, wait, cols, bases, stash.at[layer], first, second, held, lows, highs, back, rows, slots
        )

    run_back(1)
    if depth == 2:
        run_back(0)


def backward_pass(stash, loss_grad, moved, pieces, meta, rows, slots, depth):
    _, tokens, feats = stash.shape
    blocks = feats // BLK
    units = pieces.shape[1]
    if depth == 1:
        out = jax.ShapeDtypeStruct((2, tokens, feats), jnp.bfloat16)
    else:
        out = state_of(tokens, feats)
    return pl.pallas_call(
        functools.partial(backward_kernel, rows, slots, depth),
        in_specs=[IN_SMEM] * 3 + [IN_VMEM] * 3 + [IN_HBM],
        out_specs=IN_VMEM,
        out_shape=out,
        scratch_shapes=[
            pltpu.VMEM(pieces.shape, jnp.bfloat16),
            pltpu.VMEM((blocks, tokens, LANES), jnp.bfloat16),
            pltpu.VMEM((blocks, tokens, LANES), jnp.bfloat16),
            pltpu.VMEM((blocks // 2, tokens, LANES), jnp.float32),
            pltpu.SemaphoreType.DMA((2, units)),
        ],
        compiler_params=pltpu.CompilerParams(vmem_limit_bytes=VMEM_LIMIT),
        cost_estimate=about(4 * depth),
        name="backward_layers",
    )(*meta, stash, loss_grad, moved, pieces)


def join_tokens(sources, joined, arrived):
    copies = []
    begin = 0
    for index, source in enumerate(sources):
        span = pl.ds(begin, source.shape[1])
        copies.append(pltpu.make_async_copy(source, joined.at[:, span], arrived.at[index]))
        begin += source.shape[1]
    for copy in copies:
        copy.start()
    for copy in copies:
        copy.wait()


def flip_kernel(*refs):
    *sources, flipped, joined, arrived = refs
    join_tokens(sources, joined, arrived)

    def run(layer, carry):
        hidden = joined.at[layer]
        inv_rms = inv_rms_of(hidden)

        def visit(pair, carry):
            turned = (hidden[:, tile(pair)].astype(jnp.float32) * inv_rms).T.astype(jnp.bfloat16)
            flipped[layer, 2 * pair] = turned[:BLK]
            flipped[layer, 2 * pair + 1] = turned[BLK:]
            return carry

        over_pairs(hidden.shape[1], visit, 0)
        return carry

    lax.fori_loop(0, 2, run, 0)


def flip_pass(stashes):
    tokens = sum(stash.shape[1] for stash in stashes)
    feats = stashes[0].shape[2]
    return pl.pallas_call(
        flip_kernel,
        in_specs=[IN_HBM] * len(stashes),
        out_specs=IN_VMEM,
        out_shape=jax.ShapeDtypeStruct((2, feats // BLK, BLK, tokens), jnp.bfloat16),
        scratch_shapes=[
            pltpu.VMEM((2, tokens, feats), jnp.bfloat16),
            pltpu.SemaphoreType.DMA((len(stashes),)),
        ],
        compiler_params=pltpu.CompilerParams(vmem_limit_bytes=VMEM_LIMIT),
        cost_estimate=about(4),
        name="flip_rows",
    )(*stashes)


def grad_shape(rows, slots):
    return jax.ShapeDtypeStruct((2, rows * BLK, slots * BLK), jnp.bfloat16)


def block_grad_kernel(rows, slots, chosen, units, parts, cols, spots, flags, turned, *rest):
    sources, rest = rest[:parts], rest[parts:]
    outs = rest[: len(chosen)]
    joined, flipped, lows, highs, arrived, fetched = rest[len(chosen) :]
    fetches = [
        pltpu.make_async_copy(
            turned.at[:, pl.ds(spots[unit] * rows, rows)],
            flipped.at[:, pl.ds(which * rows, rows)],
            fetched.at[which],
        )
        for which, unit in enumerate(chosen)
    ]
    for fetch in fetches:
        fetch.start()
    join_tokens(sources, joined, arrived)
    for fetch in fetches:
        fetch.wait()

    def run(layer, carry):
        spread(joined.at[layer], lows, highs)
        role = 1 - jnp.abs(layer - flags[0])
        block_grad_layer(
            layer, role, cols, spots, flipped, lows, highs, outs, chosen, units, rows, slots
        )
        return carry

    lax.fori_loop(0, 2, run, 0)


def block_grad_pass(turned, cotangents, meta, spots, rows, slots, chosen):
    _, blocks, _, tokens = turned.shape
    feats = blocks * BLK
    cols, _, flags = meta
    return pl.pallas_call(
        functools.partial(
            block_grad_kernel, rows, slots, tuple(chosen), spots.shape[0], len(cotangents)
        ),
        in_specs=[IN_SMEM] * 3 + [IN_HBM] * (1 + len(cotangents)),
        out_specs=[IN_VMEM] * len(chosen),
        out_shape=[grad_shape(rows, slots) for _ in chosen],
        scratch_shapes=[
            pltpu.VMEM((2, tokens, feats), jnp.bfloat16),
            pltpu.VMEM((2, len(chosen) * rows, BLK, tokens), jnp.bfloat16),
            pltpu.VMEM((blocks, tokens, LANES), jnp.bfloat16),
            pltpu.VMEM((blocks, tokens, LANES), jnp.bfloat16),
            pltpu.SemaphoreType.DMA((len(cotangents),)),
            pltpu.SemaphoreType.DMA((len(chosen),)),
        ],
        compiler_params=pltpu.CompilerParams(vmem_limit_bytes=VMEM_LIMIT),
        cost_estimate=about(2 + len(chosen)),
        name="block_grads",
    )(cols, spots, flags, turned, *cotangents)


def to_rows(blocks):
    rows, slots, _ = blocks.shape
    split = blocks.reshape(rows, slots, BLK, BLK)
    return split.transpose(0, 2, 1, 3).reshape(rows * BLK, slots * BLK)


def from_rows(matrix, slots):
    rows = matrix.shape[0] // BLK
    split = matrix.reshape(rows, BLK, slots, BLK)
    return split.transpose(0, 2, 1, 3).reshape(rows, slots, BLK * BLK)


def token_cuts(tokens):
    if tokens % 16 or tokens < 32:
        return [(0, tokens)]
    first = -(-tokens // 32) * 16
    return [(0, first), (first, tokens)]


def folded(count):
    return list(range(0, 1)) + list(range(1, count, 2)) + list(range(2, count, 2))[::-1]


def body(inputs, target, blocks, columns, counts):
    stage, stages = lax.axis_index("stage"), lax.axis_size("stage")
    side, sides = lax.axis_index("side"), lax.axis_size("side")
    dp_id, dp_count = lax.axis_index("dp"), lax.axis_size("dp")
    mb_count, tok_local, feats = inputs.shape
    rows, slots = columns.shape[1:]
    loss_scale = (mb_count * tok_local * dp_count) ** (-0.5)
    places = dp_count // 2
    place = dp_id // 2
    core = dp_id % 2
    share = mb_count * tok_local // sides

    around = folded(places)
    ranks = [around.index(spot) for spot in range(places)]
    rank = jnp.array(ranks, jnp.int32)[place]
    hops = [
        (2 * around[i] + half, 2 * around[(i + 1) % places] + half)
        for i in range(places)
        for half in range(2)
    ]

    def ring(array):
        return lax.ppermute(array, "dp", hops)

    def sibling(array):
        return lax.ppermute(array, "dp", [(i, i ^ 1) for i in range(dp_count)])

    def partner(array):
        return lax.ppermute(array, "side", [(i, sides - 1 - i) for i in range(sides)])

    live = jnp.arange(slots, dtype=jnp.int32)[None, :] < counts[0][:, None]
    kept = jnp.where(live[:, :, None], blocks[0], jnp.zeros_like(blocks[0]))
    listed = columns[0].reshape(1, rows * slots).astype(jnp.bfloat16)
    tail = jnp.pad(listed, ((0, TAIL - 1), (0, slots * BLK - rows * slots)))
    own = jnp.concatenate([to_rows(kept), tail], axis=0)

    pieces = lax.all_gather(own, ("side", "dp"), axis=0, tiled=False)
    pieces = pieces.reshape((sides, dp_count) + own.shape)
    listed = pieces[:, :, rows * BLK, : rows * slots].reshape(sides * dp_count, rows * slots)
    cols = jnp.pad(listed.astype(jnp.int32), ((0, 0), (0, -(rows * slots) % LANES)))
    bases = jnp.arange(dp_count, dtype=jnp.int32) * rows
    flags = jnp.stack([side, stage == 0, stage == stages - 1]).astype(jnp.int32)
    meta = (cols, bases, flags)
    turns = jnp.array(around, jnp.int32)[(rank - jnp.arange(places)) % places]
    spots = jnp.concatenate([turns * 2 + core, turns * 2 + 1 - core]).astype(jnp.int32)

    def my_rows(array):
        flat = array.reshape(mb_count * tok_local, feats)
        return lax.dynamic_slice_in_dim(flat, side * share, share, 0)

    def hop(array, distance):
        route = [(i, i + distance) for i in range(stages) if 0 <= i + distance < stages]
        return lax.ppermute(array, "stage", route)

    cuts = token_cuts(share)
    ways = range(len(cuts))
    whole_start, whole_goal = my_rows(inputs), my_rows(target)
    start = [whole_start[begin:end] for begin, end in cuts]
    goal = [whole_goal[begin:end] for begin, end in cuts]
    moved = list(start)
    for step in range(stages - 1):
        final = [
            forward_pass(start[i], moved[i], None, None, pieces, meta, rows, slots)[0] for i in ways
        ]
        moved = [hop(final[i], 1) for i in ways]
    turned = [
        forward_pass(start[i], moved[i], goal[i], loss_scale, pieces, meta, rows, slots) for i in ways
    ]
    stashes, loss_grads, result = [list(column) for column in zip(*turned)]
    moved = loss_grads
    for step in range(stages - 1):
        if step:
            result = [
                backward_pass(stashes[i], loss_grads[i], moved[i], pieces, meta, rows, slots, 2)
                for i in ways
            ]
        moved = [hop(result[i], -1) for i in ways]
    flipped = flip_pass(stashes)
    cotangents = [
        backward_pass(stashes[i], loss_grads[i], moved[i], pieces, meta, rows, slots, 1) for i in ways
    ]

    order = list(range(1, places)) + [0]

    def grads_of(slot, cotangents):
        chosen = [slot, places + slot]
        near, far = block_grad_pass(flipped, cotangents, meta, spots, rows, slots, chosen)
        far = sibling(far)
        return add_rounded(near[0], far[0]), (near[1], far[1])

    outgoing, kept = grads_of(order[0], cotangents)
    travelling = None
    for index in range(places):
        moving = {"coming": partner(outgoing)}
        if travelling is not None:
            moving["passed"] = ring(travelling)
        if index + 1 < places:
            cotangents, moving = lax.optimization_barrier((cotangents, outgoing))[0], moving
            moving["next"] = grads_of(order[index + 1], cotangents)
        moving = lax.optimization_barrier(moving)
        total = kept[0].astype(jnp.float32) + kept[1].astype(jnp.float32)
        total = total + moving["coming"].astype(jnp.float32)
        if travelling is not None:
            total = total + moving["passed"].astype(jnp.float32)
        travelling = total.astype(jnp.bfloat16)
        if index + 1 < places:
            outgoing, kept = moving["next"]
    result = from_rows(travelling, slots)
    return jnp.where(live[:, :, None], result, jnp.zeros_like(result))[None]


def add_rounded(left, right):
    return (left.astype(jnp.float32) + right.astype(jnp.float32)).astype(jnp.bfloat16)


def solution(mesh):
    sections, width = mesh.devices.shape
    split = jax.sharding.Mesh(mesh.devices.reshape(sections // 2, 2, width), ("stage", "side", "dp"))
    section = ("stage", "side")
    return jax.shard_map(
        body,
        mesh=split,
        in_specs=(
            P(None, "dp", None),
            P(None, "dp", None),
            P(section, "dp", None, None),
            P(section, "dp", None),
            P(section, "dp"),
        ),
        out_specs=P(section, "dp", None, None),
        check_vma=False,
    )
```

```python
import functools

import jax
import jax.numpy as jnp
from jax import lax
from jax.experimental import pallas as pl
from jax.experimental.pallas import tpu as pltpu
from jax.sharding import PartitionSpec as P

BLK = 64
LANES = 128
EPSILON = 1e-05
VMEM_LIMIT = 44 * 1024 * 1024
STEP_ROWS = 8

TAIL = 16

IN_VMEM = pl.BlockSpec(memory_space=pltpu.VMEM)
IN_SMEM = pl.BlockSpec(memory_space=pltpu.SMEM)
IN_HBM = pl.BlockSpec(memory_space=pl.ANY)


def about(microseconds):
    return pl.CostEstimate(
        flops=int(microseconds * 1.1e9), bytes_accessed=1 << 20, transcendentals=0
    )


def step_units(units, rows):
    size = max(1, STEP_ROWS // rows)
    while units % size:
        size -= 1
    return size


def low_half(rows):
    return lax.broadcasted_iota(jnp.int32, (rows, LANES), 1) < BLK


def tile(pair):
    return pl.ds(pl.multiple_of(pair * LANES, LANES), LANES)


def over_pairs(feats, visit, carry):
    return lax.fori_loop(0, feats // LANES, visit, carry, unroll=4)


def inv_rms_of(ref):
    tokens, feats = ref.shape

    def visit(pair, total):
        values = ref[:, tile(pair)].astype(jnp.float32)
        return total + values * values

    total = over_pairs(feats, visit, jnp.zeros((tokens, LANES), jnp.float32))
    return lax.rsqrt(jnp.sum(total, axis=-1, keepdims=True) / feats + EPSILON)


def start_loads(pieces, held, arrived, roles):
    units = held.shape[1]
    for unit in range(units):
        for role in roles:
            pltpu.make_async_copy(
                pieces[2 * unit + role], held.at[role, unit], arrived.at[role, unit]
            ).start()


def wait_load(pieces, held, arrived, role, unit):
    pltpu.make_async_copy(pieces[0], held.at[role, unit], arrived.at[role, unit]).wait()


def forward_layer(role, wait, cols, bases, current, held, parts, sums, rows, slots):
    tokens, feats = current.shape
    units = held.shape[1]
    per_step = step_units(units, rows)
    half = tokens // 2
    low = low_half(tokens)
    low_packed = low_half(half)
    inv_rms = inv_rms_of(current)

    def normalise(pair, carry):
        unit_rows = current[:, tile(pair)].astype(jnp.float32) * inv_rms
        parts[2 * pair] = jnp.where(low, unit_rows, 0.0).astype(jnp.bfloat16)
        parts[2 * pair + 1] = jnp.where(low, 0.0, unit_rows).astype(jnp.bfloat16)
        sums[2 * pair] = jnp.zeros((half, LANES), jnp.float32)
        sums[2 * pair + 1] = jnp.zeros((half, LANES), jnp.float32)
        return carry

    over_pairs(feats, normalise, 0)

    def run_step(step, carry):
        for inner in range(per_step):
            wait(role, step * per_step + inner)
        items = [(inner, row) for inner in range(per_step) for row in range(0, rows, 2)]

        def product_of(index):
            inner, row = items[index]
            unit = step * per_step + inner
            place = bases[unit] + row
            left = jnp.concatenate([parts[place], parts[place + 1]], axis=0)
            right = held[role, unit, row * BLK : (row + 2) * BLK]
            return jnp.dot(left, right, preferred_element_type=jnp.float32)

        upcoming = product_of(0)
        for index, (inner, row) in enumerate(items):
            product = upcoming
            if index + 1 < len(items):
                upcoming = product_of(index + 1)
            line = role * units + step * per_step + inner
            for which in range(2):
                at = [cols[line, (row + which) * slots + slot] for slot in range(slots)]
                added = []
                for begin in range(0, slots, 2):
                    lanes = slice(begin * BLK, begin * BLK + LANES)
                    first = product[which * tokens : which * tokens + half, lanes]
                    second = product[which * tokens + half : (which + 1) * tokens, lanes]
                    even = jnp.where(low_packed, first, pltpu.roll(second, BLK, 1))
                    odd = jnp.where(low_packed, pltpu.roll(first, BLK, 1), second)
                    added.append(sums[at[begin]] + even)
                    added.append(sums[at[begin + 1]] + odd)
                for slot in range(slots):
                    sums[at[slot]] = added[slot]
        return carry

    lax.fori_loop(0, units // per_step, run_step, 0)

    def finish(pair, carry):
        lanes = tile(pair)
        first, second = sums[2 * pair], sums[2 * pair + 1]
        top = jnp.where(low_packed, first, pltpu.roll(second, BLK, 1))
        bottom = jnp.where(low_packed, pltpu.roll(first, BLK, 1), second)
        branch = jnp.concatenate([top, bottom], axis=0)
        current[:, lanes] = (current[:, lanes].astype(jnp.float32) + branch).astype(jnp.bfloat16)
        return carry

    over_pairs(feats, finish, 0)


def spread(source, lows, highs):
    tokens, feats = source.shape
    low = low_half(tokens)

    def visit(pair, carry):
        both = source[:, tile(pair)].astype(jnp.float32)
        moved = pltpu.roll(both, BLK, 1)
        lows[2 * pair] = jnp.where(low, both, 0.0).astype(jnp.bfloat16)
        highs[2 * pair] = jnp.where(low, 0.0, moved).astype(jnp.bfloat16)
        lows[2 * pair + 1] = jnp.where(low, moved, 0.0).astype(jnp.bfloat16)
        highs[2 * pair + 1] = jnp.where(low, 0.0, both).astype(jnp.bfloat16)
        return carry

    over_pairs(feats, visit, 0)


def pick_columns(lows, highs, cols, line, flat, slots):
    return jnp.concatenate(
        [
            lows[cols[line, flat + 2 * half]] + highs[cols[line, flat + 2 * half + 1]]
            for half in range(slots // 2)
        ],
        axis=1,
    )


def input_grad_layer(role, wait, cols, bases, hidden, cotangent, out, held, lows, highs, back, rows, slots):
    tokens, feats = cotangent.shape
    units = held.shape[1]
    per_step = step_units(units, rows)
    low = low_half(tokens)

    def run_step(step, carry):
        for inner in range(per_step):
            wait(role, step * per_step + inner)
        items = [(inner, row) for inner in range(per_step) for row in range(0, rows, 2)]

        def picked_at(index):
            inner, row = items[index]
            line = role * units + step * per_step + inner
            return jnp.concatenate(
                [
                    pick_columns(lows, highs, cols, line, (row + which) * slots, slots)
                    for which in range(2)
                ],
                axis=0,
            )

        upcoming = picked_at(0)
        for index, (inner, row) in enumerate(items):
            unit = step * per_step + inner
            picked = upcoming
            if index + 1 < len(items):
                upcoming = picked_at(index + 1)
            result = jnp.dot(
                picked,
                held[role, unit, :, row * BLK : (row + 2) * BLK],
                preferred_element_type=jnp.float32,
            )
            back[(bases[unit] + row) // 2] = jnp.where(low, result[:tokens], result[tokens:])
        return carry

    lax.fori_loop(0, units // per_step, run_step, 0)
    inv_rms = inv_rms_of(hidden)

    def correlate(pair, total):
        unit_rows = hidden[:, tile(pair)].astype(jnp.float32) * inv_rms
        return total + back[pair] * unit_rows

    total = over_pairs(feats, correlate, jnp.zeros((tokens, LANES), jnp.float32))
    mean = jnp.sum(total, axis=-1, keepdims=True) / feats

    def finish(pair, carry):
        lanes = tile(pair)
        unit_rows = hidden[:, lanes].astype(jnp.float32) * inv_rms
        centred = back[pair] - unit_rows * mean
        out[:, lanes] = (cotangent[:, lanes].astype(jnp.float32) + inv_rms * centred).astype(jnp.bfloat16)
        return carry

    over_pairs(feats, finish, 0)


def block_grad_layer(layer, role, cols, flipped, lows, highs, out, chosen, units, rows, slots):
    items = [(which, row) for which in range(len(chosen)) for row in range(rows)]

    def operands(index):
        which, row = items[index]
        picked = pick_columns(lows, highs, cols, role * units + chosen[which], row * slots, slots)
        return flipped[layer, which * rows + row], picked

    upcoming = operands(0)
    for index, (which, row) in enumerate(items):
        left, right = upcoming
        if index + 1 < len(items):
            upcoming = operands(index + 1)
        result = jnp.dot(left, right, preferred_element_type=jnp.float32)
        out[which][row * BLK : (row + 1) * BLK] = result.astype(jnp.bfloat16)


def choose(flag, first, second, target):
    @pl.when(flag == 1)
    def _():
        target[...] = first[...]

    @pl.when(flag != 1)
    def _():
        target[...] = second[...]


def forward_kernel(rows, slots, count, scale, cols, bases, flags, *rest):
    turning = scale is not None
    start, moved = rest[:2]
    rest = rest[2:]
    if turning:
        goal, rest = rest[0], rest[1:]
    straight, rest = rest[:count], rest[count:]
    if turning:
        across, rest = rest[:count], rest[count:]
        stash, loss_grad, final, held, parts, sums, arrived, crossed, lows, highs, back, landed = rest
    else:
        final, held, parts, sums, arrived = rest
    start_loads(straight, held, arrived, (0, 1))
    if turning:
        start_loads(across, crossed, landed, (0, 1))
    choose(flags[1], start, moved, final)
    wait = functools.partial(wait_load, straight, held, arrived)

    def run_forward(layer, carry):
        if turning:
            stash[layer] = final[...]
        role = jnp.abs(layer - flags[0])
        forward_layer(role, wait, cols, bases, final, held, parts, sums, rows, slots)
        return carry

    lax.fori_loop(0, 2, run_forward, 0)
    if not turning:
        return
    tokens, feats = final.shape

    def residue(pair, carry):
        lanes = tile(pair)
        gap = final[:, lanes].astype(jnp.float32) - goal[:, lanes].astype(jnp.float32)
        loss_grad[:, lanes] = (gap * scale).astype(jnp.bfloat16)
        return carry

    over_pairs(feats, residue, 0)
    final[...] = loss_grad[...]
    wait_across = functools.partial(wait_load, across, crossed, landed)

    def run_back(turn, carry):
        layer = 1 - turn
        role = jnp.abs(layer - flags[0])
        hidden = stash.at[layer]
        spread(final, lows, highs)
        input_grad_layer(
            role, wait_across, cols, bases, hidden, final, final, crossed, lows, highs, back, rows, slots
        )
        return carry

    lax.fori_loop(0, 2, run_back, 0)


def state_of(tokens, feats):
    return jax.ShapeDtypeStruct((tokens, feats), jnp.bfloat16)


def unit_scratch(pieces):
    units = len(pieces) // 2
    return [pltpu.VMEM((2, units) + pieces[0].shape, jnp.bfloat16), pltpu.SemaphoreType.DMA((2, units))]


def forward_pass(start, moved, goal, scale, straight, across, meta, rows, slots):
    tokens, feats = start.shape
    blocks = feats // BLK
    stack = jax.ShapeDtypeStruct((2, tokens, feats), jnp.bfloat16)
    held, arrived = unit_scratch(straight)
    scratch = [
        held,
        pltpu.VMEM((blocks, tokens, LANES), jnp.bfloat16),
        pltpu.VMEM((blocks, tokens // 2, LANES), jnp.float32),
        arrived,
    ]
    outs = [state_of(tokens, feats)]
    ins = [start, moved]
    pieces = list(straight)
    if goal is not None:
        ins.append(goal)
        pieces += across
        outs = [stack, state_of(tokens, feats)] + outs
        crossed, landed = unit_scratch(across)
        scratch += [
            crossed,
            pltpu.VMEM((blocks, tokens, LANES), jnp.bfloat16),
            pltpu.VMEM((blocks, tokens, LANES), jnp.bfloat16),
            pltpu.VMEM((blocks // 2, tokens, LANES), jnp.float32),
            landed,
        ]
    return pl.pallas_call(
        functools.partial(forward_kernel, rows, slots, len(straight), None if goal is None else scale),
        in_specs=[IN_SMEM] * 3 + [IN_VMEM] * len(ins) + [IN_HBM] * len(pieces),
        out_specs=[IN_VMEM] * len(outs),
        out_shape=outs,
        scratch_shapes=scratch,
        compiler_params=pltpu.CompilerParams(vmem_limit_bytes=VMEM_LIMIT),
        cost_estimate=about(8 if goal is None else 14),
        name="forward_layers" if goal is None else "turning_layers",
    )(*meta, *ins, *pieces)


def backward_kernel(rows, slots, count, depth, cols, bases, flags, stash, loss_grad, moved, *rest):
    across, rest = rest[:count], rest[count:]
    outs, crossed, lows, highs, back, landed = rest
    if depth == 1:
        first, second = outs.at[1], outs.at[0]
    else:
        first = second = outs
    top = 1 - flags[0]

    @pl.when(top == 0)
    def _():
        start_loads(across, crossed, landed, (0,) if depth == 1 else (0, 1))

    @pl.when(top == 1)
    def _():
        start_loads(across, crossed, landed, (1,) if depth == 1 else (1, 0))

    choose(flags[2], loss_grad, moved, first)
    wait = functools.partial(wait_load, across, crossed, landed)

    def run_back(layer):
        spread(first, lows, highs)
        role = jnp.abs(layer - flags[0])
        input_grad_layer(
            role, wait, cols, bases, stash.at[layer], first, second, crossed, lows, highs, back, rows, slots
        )

    run_back(1)
    if depth == 2:
        run_back(0)


def backward_pass(stash, loss_grad, moved, across, meta, rows, slots, depth):
    _, tokens, feats = stash.shape
    blocks = feats // BLK
    crossed, landed = unit_scratch(across)
    if depth == 1:
        out = jax.ShapeDtypeStruct((2, tokens, feats), jnp.bfloat16)
    else:
        out = state_of(tokens, feats)
    return pl.pallas_call(
        functools.partial(backward_kernel, rows, slots, len(across), depth),
        in_specs=[IN_SMEM] * 3 + [IN_VMEM] * 3 + [IN_HBM] * len(across),
        out_specs=IN_VMEM,
        out_shape=out,
        scratch_shapes=[
            crossed,
            pltpu.VMEM((blocks, tokens, LANES), jnp.bfloat16),
            pltpu.VMEM((blocks, tokens, LANES), jnp.bfloat16),
            pltpu.VMEM((blocks // 2, tokens, LANES), jnp.float32),
            landed,
        ],
        compiler_params=pltpu.CompilerParams(vmem_limit_bytes=VMEM_LIMIT),
        cost_estimate=about(4 * depth),
        name="backward_layers",
    )(*meta, stash, loss_grad, moved, *across)


def join_tokens(sources, joined, arrived):
    copies = []
    begin = 0
    for index, source in enumerate(sources):
        span = pl.ds(begin, source.shape[1])
        copies.append(pltpu.make_async_copy(source, joined.at[:, span], arrived.at[index]))
        begin += source.shape[1]
    for copy in copies:
        copy.start()
    for copy in copies:
        copy.wait()


def flip_kernel(rows, chosen, bases, *refs):
    *sources, flipped, joined, arrived = refs
    join_tokens(sources, joined, arrived)

    def run(layer, carry):
        hidden = joined.at[layer]
        inv_rms = inv_rms_of(hidden)
        for unit in range(chosen):

            def visit(step, carry):
                lanes = tile(bases[unit] // 2 + step)
                turned = (hidden[:, lanes].astype(jnp.float32) * inv_rms).T.astype(jnp.bfloat16)
                flipped[layer, unit * rows + 2 * step] = turned[:BLK]
                flipped[layer, unit * rows + 2 * step + 1] = turned[BLK:]
                return carry

            lax.fori_loop(0, rows // 2, visit, 0, unroll=True)
        return carry

    lax.fori_loop(0, 2, run, 0)


def flip_pass(stashes, bases, rows, chosen):
    tokens = sum(stash.shape[1] for stash in stashes)
    feats = stashes[0].shape[2]
    return pl.pallas_call(
        functools.partial(flip_kernel, rows, chosen),
        in_specs=[IN_SMEM] + [IN_HBM] * len(stashes),
        out_specs=IN_VMEM,
        out_shape=jax.ShapeDtypeStruct((2, chosen * rows, BLK, tokens), jnp.bfloat16),
        scratch_shapes=[
            pltpu.VMEM((2, tokens, feats), jnp.bfloat16),
            pltpu.SemaphoreType.DMA((len(stashes),)),
        ],
        compiler_params=pltpu.CompilerParams(vmem_limit_bytes=VMEM_LIMIT),
        cost_estimate=about(4),
        name="flip_rows",
    )(bases, *stashes)


def block_grad_kernel(rows, slots, chosen, units, parts, cols, flags, turned, *rest):
    sources, rest = rest[:parts], rest[parts:]
    outs = rest[: 2 * len(chosen)]
    joined, flipped, lows, highs, arrived, fetched = rest[2 * len(chosen) :]
    fetches = [
        pltpu.make_async_copy(
            turned.at[:, pl.ds(unit * rows, rows)],
            flipped.at[:, pl.ds(which * rows, rows)],
            fetched.at[which],
        )
        for which, unit in enumerate(chosen)
    ]
    for fetch in fetches:
        fetch.start()
    join_tokens(sources, joined, arrived)
    for fetch in fetches:
        fetch.wait()
    for role in (1, 0):
        layer = jnp.abs(role - flags[0])
        spread(joined.at[layer], lows, highs)
        block_grad_layer(
            layer, role, cols, flipped, lows, highs, outs[role::2], chosen, units, rows, slots
        )


def block_grad_pass(turned, cotangents, meta, rows, slots, chosen):
    tokens = turned.shape[3]
    feats = cotangents[0].shape[2]
    blocks = feats // BLK
    cols, bases, flags = meta
    out = jax.ShapeDtypeStruct((rows * BLK, slots * BLK), jnp.bfloat16)
    return pl.pallas_call(
        functools.partial(
            block_grad_kernel, rows, slots, tuple(chosen), bases.shape[0], len(cotangents)
        ),
        in_specs=[IN_SMEM] * 2 + [IN_HBM] * (1 + len(cotangents)),
        out_specs=[IN_VMEM] * (2 * len(chosen)),
        out_shape=[out] * (2 * len(chosen)),
        scratch_shapes=[
            pltpu.VMEM((2, tokens, feats), jnp.bfloat16),
            pltpu.VMEM((2, len(chosen) * rows, BLK, tokens), jnp.bfloat16),
            pltpu.VMEM((blocks, tokens, LANES), jnp.bfloat16),
            pltpu.VMEM((blocks, tokens, LANES), jnp.bfloat16),
            pltpu.SemaphoreType.DMA((len(cotangents),)),
            pltpu.SemaphoreType.DMA((len(chosen),)),
        ],
        compiler_params=pltpu.CompilerParams(vmem_limit_bytes=VMEM_LIMIT),
        cost_estimate=about(4 + len(chosen)),
        name="block_grads",
    )(cols, flags, turned, *cotangents)


def arrange_kernel(rows, count, *refs):
    pieces, outs = refs[:count], refs[count:]
    listed = outs[-1]
    for i, piece in enumerate(pieces):
        straight, across = outs[2 * i], outs[2 * i + 1]
        straight[...] = piece[: rows * BLK]
        step = min(rows * BLK, LANES)
        for begin in range(0, rows * BLK, step):
            across[:, begin : begin + step] = piece[begin : begin + step].T
        line = piece[rows * BLK :].astype(jnp.float32)[:1, : listed.shape[1]]
        listed[i : i + 1] = line.astype(jnp.int32)


def arrange_pass(pieces, rows, slots):
    width = slots * BLK
    lines = -(-rows * slots // LANES) * LANES
    outs = []
    for _ in pieces:
        outs.append(jax.ShapeDtypeStruct((rows * BLK, width), jnp.bfloat16))
        outs.append(jax.ShapeDtypeStruct((width, rows * BLK), jnp.bfloat16))
    outs.append(jax.ShapeDtypeStruct((len(pieces), lines), jnp.int32))
    arranged = pl.pallas_call(
        functools.partial(arrange_kernel, rows, len(pieces)),
        in_specs=[IN_VMEM] * len(pieces),
        out_specs=[IN_VMEM] * len(outs),
        out_shape=outs,
        compiler_params=pltpu.CompilerParams(vmem_limit_bytes=VMEM_LIMIT),
        cost_estimate=about(1 + len(pieces)),
        name="arrange_units",
    )(*pieces)
    return list(zip(arranged[:-1:2], arranged[1:-1:2])), arranged[-1]


def to_rows(blocks):
    rows, slots, _ = blocks.shape
    split = blocks.reshape(rows, slots, BLK, BLK)
    return split.transpose(0, 2, 1, 3).reshape(rows * BLK, slots * BLK)


def from_rows(matrix, slots):
    rows = matrix.shape[0] // BLK
    split = matrix.reshape(rows, BLK, slots, BLK)
    return split.transpose(0, 2, 1, 3).reshape(rows, slots, BLK * BLK)


def token_cuts(tokens):
    if tokens % 16 or tokens < 32:
        return [(0, tokens)]
    first = -(-tokens // 32) * 16
    return [(0, first), (first, tokens)]


def folded(count):
    return list(range(0, 1)) + list(range(1, count, 2)) + list(range(2, count, 2))[::-1]


def body(inputs, target, blocks, columns, counts):
    stage, stages = lax.axis_index("stage"), lax.axis_size("stage")
    side, sides = lax.axis_index("side"), lax.axis_size("side")
    dp_id, dp_count = lax.axis_index("dp"), lax.axis_size("dp")
    mb_count, tok_local, feats = inputs.shape
    rows, slots = columns.shape[1:]
    loss_scale = (mb_count * tok_local * dp_count) ** (-0.5)
    places = dp_count // 2
    place = dp_id // 2
    core = dp_id % 2
    share = mb_count * tok_local // sides

    around = folded(places)
    ranks = [around.index(spot) for spot in range(places)]
    rank = jnp.array(ranks, jnp.int32)[place]
    hops = [
        (2 * around[i] + half, 2 * around[(i + 1) % places] + half)
        for i in range(places)
        for half in range(2)
    ]

    def ring(array):
        return lax.ppermute(array, "dp", hops)

    def sibling(array):
        return lax.ppermute(array, "dp", [(i, i ^ 1) for i in range(dp_count)])

    def partner(array):
        return lax.ppermute(array, "side", [(i, sides - 1 - i) for i in range(sides)])

    live = jnp.arange(slots, dtype=jnp.int32)[None, :] < counts[0][:, None]
    kept = jnp.where(live[:, :, None], blocks[0], jnp.zeros_like(blocks[0]))
    listed = columns[0].reshape(1, rows * slots).astype(jnp.bfloat16)
    tail = jnp.pad(listed, ((0, TAIL - 1), (0, slots * BLK - rows * slots)))
    own = jnp.concatenate([to_rows(kept), tail], axis=0)

    ready = {}

    def arrange(names, arrays):
        pairs, lines = arrange_pass(arrays, rows, slots)
        return [(name, pair, lines[i : i + 1]) for i, (name, pair) in enumerate(zip(names, pairs))]

    fresh = {(0, 0): own}
    newest = own
    last_other = None
    for slot in range(places):
        names = list(fresh)
        moving = {"other": partner(newest), "far_own": sibling(newest)}
        if slot + 1 < places:
            moving["own"] = ring(newest)
        if slot:
            moving["far_other"] = sibling(last_other)
        moving["ready"] = [
            (pair, line) for _, pair, line in arrange(names, [fresh[name] for name in names])
        ]
        moving = lax.optimization_barrier(moving)
        ready.update(zip(names, moving["ready"]))
        fresh = {(1, slot): moving["other"], (0, places + slot): moving["far_own"]}
        if slot + 1 < places:
            newest = moving["own"]
            fresh[0, slot + 1] = newest
        if slot:
            fresh[1, places + slot - 1] = moving["far_other"]
        last_other = moving["other"]
    fresh[1, 2 * places - 1] = sibling(last_other)
    names = list(fresh)
    for name, pair, line in arrange(names, [fresh[name] for name in names]):
        ready[name] = (pair, line)
    units = [(role, unit) for unit in range(2 * places) for role in range(2)]
    straight = [ready[name][0][0] for name in units]
    across = [ready[name][0][1] for name in units]
    cols = jnp.concatenate(
        [ready[role, unit][1] for role in range(2) for unit in range(2 * places)], axis=0
    )
    turns = jnp.array(around, jnp.int32)[(rank - jnp.arange(places)) % places]
    bases = jnp.concatenate([turns * 2 + core, turns * 2 + 1 - core]).astype(jnp.int32) * rows
    flags = jnp.stack([side, stage == 0, stage == stages - 1]).astype(jnp.int32)
    meta = (cols, bases, flags)

    def my_rows(array):
        flat = array.reshape(mb_count * tok_local, feats)
        return lax.dynamic_slice_in_dim(flat, side * share, share, 0)

    def hop(array, distance):
        route = [(i, i + distance) for i in range(stages) if 0 <= i + distance < stages]
        return lax.ppermute(array, "stage", route)

    cuts = token_cuts(share)
    ways = range(len(cuts))
    whole_start, whole_goal = my_rows(inputs), my_rows(target)
    start = [whole_start[begin:end] for begin, end in cuts]
    goal = [whole_goal[begin:end] for begin, end in cuts]
    moved = list(start)
    for step in range(stages - 1):
        final = [
            forward_pass(start[i], moved[i], None, None, straight, across, meta, rows, slots)[0]
            for i in ways
        ]
        moved = [hop(final[i], 1) for i in ways]
    turned = [
        forward_pass(start[i], moved[i], goal[i], loss_scale, straight, across, meta, rows, slots)
        for i in ways
    ]
    stashes, loss_grads, result = [list(column) for column in zip(*turned)]
    moved = loss_grads
    for step in range(stages - 1):
        if step:
            result = [
                backward_pass(stashes[i], loss_grads[i], moved[i], across, meta, rows, slots, 2)
                for i in ways
            ]
        moved = [hop(result[i], -1) for i in ways]
    flipped = flip_pass(stashes + [sibling(stash) for stash in stashes], bases, rows, places)
    cotangents = [
        backward_pass(stashes[i], loss_grads[i], moved[i], across, meta, rows, slots, 1) for i in ways
    ]

    order = list(range(1, places)) + [0]

    cotangents = cotangents + [sibling(part) for part in cotangents]
    kept, outgoing = block_grad_pass(flipped, cotangents, meta, rows, slots, order[:1])
    cotangents, tied = lax.optimization_barrier((cotangents, outgoing))
    late = block_grad_pass(flipped, cotangents, meta, rows, slots, order[1:])
    coming, late = lax.optimization_barrier((partner(tied), late))
    travelling = add_rounded(kept, coming)
    for index in range(places - 1):
        kept, outgoing = late[2 * index], late[2 * index + 1]
        passed, coming = lax.optimization_barrier((ring(travelling), partner(outgoing)))
        total = kept.astype(jnp.float32) + coming.astype(jnp.float32) + passed.astype(jnp.float32)
        travelling = total.astype(jnp.bfloat16)
    result = from_rows(travelling, slots)
    return jnp.where(live[:, :, None], result, jnp.zeros_like(result))[None]


def add_rounded(left, right):
    return (left.astype(jnp.float32) + right.astype(jnp.float32)).astype(jnp.bfloat16)


def solution(mesh):
    sections, width = mesh.devices.shape
    split = jax.sharding.Mesh(mesh.devices.reshape(sections // 2, 2, width), ("stage", "side", "dp"))
    section = ("stage", "side")
    return jax.shard_map(
        body,
        mesh=split,
        in_specs=(
            P(None, "dp", None),
            P(None, "dp", None),
            P(section, "dp", None, None),
            P(section, "dp", None),
            P(section, "dp"),
        ),
        out_specs=P(section, "dp", None, None),
        check_vma=False,
    )
```

```python
import functools

import jax
import jax.numpy as jnp
from jax import lax
from jax.experimental import pallas as pl
from jax.experimental.pallas import tpu as pltpu
from jax.sharding import PartitionSpec as P

BLK = 64
LANES = 128
EPSILON = 1e-05
VMEM_LIMIT = 58 * 1024 * 1024
STEP_ROWS = 8

TAIL = 16
DEPTH = 4

IN_VMEM = pl.BlockSpec(memory_space=pltpu.VMEM)
IN_SMEM = pl.BlockSpec(memory_space=pltpu.SMEM)
IN_HBM = pl.BlockSpec(memory_space=pl.ANY)


def about(microseconds):
    return pl.CostEstimate(
        flops=int(microseconds * 1.1e9), bytes_accessed=1 << 20, transcendentals=0
    )


def step_units(units, rows):
    size = max(1, STEP_ROWS // rows)
    while units % size:
        size -= 1
    return size


def low_half(rows):
    return lax.broadcasted_iota(jnp.int32, (rows, LANES), 1) < BLK


def tile(pair):
    return pl.ds(pl.multiple_of(pair * LANES, LANES), LANES)


def over_pairs(feats, visit, carry):
    return lax.fori_loop(0, feats // LANES, visit, carry, unroll=4)


def inv_rms_of(ref):
    tokens, feats = ref.shape

    def visit(pair, total):
        values = ref[:, tile(pair)].astype(jnp.float32)
        return total + values * values

    total = over_pairs(feats, visit, jnp.zeros((tokens, LANES), jnp.float32))
    return lax.rsqrt(jnp.sum(total, axis=-1, keepdims=True) / feats + EPSILON)


class UnitStream:
    def __init__(self, source, held, arrived, order, length):
        self.source, self.held, self.arrived = source, held, arrived
        self.order, self.length = order, length

    def copy(self, index):
        role, unit = self.order(index)
        slot = index % DEPTH
        return pltpu.make_async_copy(
            self.source.at[role, unit], self.held.at[slot], self.arrived.at[slot]
        )

    def begin(self, ahead):
        self.ahead = ahead
        for index in range(min(ahead, self.length)):
            self.copy(jnp.int32(index)).start()

    def take(self, index):
        later = index + self.ahead

        @pl.when(later < self.length)
        def _():
            self.copy(later).start()

        self.copy(index).wait()
        return index % DEPTH


def forward_layer(role, first, stream, cols, bases, current, parts, sums, rows, slots):
    tokens, feats = current.shape
    units = bases.shape[0]
    per_step = step_units(units, rows)
    low = low_half(tokens)
    inv_rms = inv_rms_of(current)

    def normalise(pair, carry):
        lanes = tile(pair)
        unit_rows = current[:, lanes].astype(jnp.float32) * inv_rms
        parts[2 * pair] = jnp.where(low, unit_rows, 0.0).astype(jnp.bfloat16)
        parts[2 * pair + 1] = jnp.where(low, 0.0, unit_rows).astype(jnp.bfloat16)
        sums[2 * pair] = jnp.zeros((tokens, LANES), jnp.float32)
        sums[2 * pair + 1] = jnp.zeros((tokens, LANES), jnp.float32)
        return carry

    over_pairs(feats, normalise, 0)

    def run_step(step, carry):
        places = [stream.take(first + step * per_step + inner) for inner in range(per_step)]
        items = [(inner, row) for inner in range(per_step) for row in range(0, rows, 2)]

        def product_of(index):
            inner, row = items[index]
            unit = step * per_step + inner
            spot = bases[unit] + row
            left = jnp.concatenate([parts[spot], parts[spot + 1]], axis=0)
            right = stream.held[places[inner], row * BLK : (row + 2) * BLK]
            return jnp.dot(left, right, preferred_element_type=jnp.float32)

        upcoming = product_of(0)
        for index, (inner, row) in enumerate(items):
            product = upcoming
            if index + 1 < len(items):
                upcoming = product_of(index + 1)
            for which in range(2):
                line = role * units + step * per_step + inner
                flat = (row + which) * slots
                for begin in range(0, slots, 4):
                    at = [cols[line, flat + slot] for slot in range(begin, min(begin + 4, slots))]
                    added = []
                    for offset in range(len(at)):
                        slot = begin + offset
                        lanes = slice((slot // 2) * LANES, (slot // 2 + 1) * LANES)
                        piece = product[which * tokens : (which + 1) * tokens, lanes]
                        piece = jnp.where(low, piece, 0.0) if slot % 2 == 0 else jnp.where(low, 0.0, piece)
                        added.append(sums[at[offset]] + piece)
                    for offset in range(len(at)):
                        sums[at[offset]] = added[offset]
        return carry

    lax.fori_loop(0, units // per_step, run_step, 0)

    def finish(pair, carry):
        lanes = tile(pair)
        first, second = sums[2 * pair], sums[2 * pair + 1]
        branch = jnp.where(low, first, second) + pltpu.roll(jnp.where(low, second, first), BLK, 1)
        current[:, lanes] = (current[:, lanes].astype(jnp.float32) + branch).astype(jnp.bfloat16)
        return carry

    over_pairs(feats, finish, 0)


def spread(source, lows, highs):
    tokens, feats = source.shape
    low = low_half(tokens)

    def visit(pair, carry):
        both = source[:, tile(pair)].astype(jnp.float32)
        moved = pltpu.roll(both, BLK, 1)
        lows[2 * pair] = jnp.where(low, both, 0.0).astype(jnp.bfloat16)
        highs[2 * pair] = jnp.where(low, 0.0, moved).astype(jnp.bfloat16)
        lows[2 * pair + 1] = jnp.where(low, moved, 0.0).astype(jnp.bfloat16)
        highs[2 * pair + 1] = jnp.where(low, 0.0, both).astype(jnp.bfloat16)
        return carry

    over_pairs(feats, visit, 0)


def pick_columns(lows, highs, cols, line, flat, slots):
    return jnp.concatenate(
        [
            lows[cols[line, flat + 2 * half]] + highs[cols[line, flat + 2 * half + 1]]
            for half in range(slots // 2)
        ],
        axis=1,
    )


def input_grad_layer(
    role, begin, stream, cols, bases, hidden, cotangent, out, lows, highs, back, rows, slots
):
    tokens, feats = cotangent.shape
    units = bases.shape[0]
    per_step = step_units(units, rows)
    low = low_half(tokens)

    def run_step(step, carry):
        places = [stream.take(begin + step * per_step + inner) for inner in range(per_step)]
        items = [(inner, row) for inner in range(per_step) for row in range(0, rows, 2)]

        def picked_at(index):
            inner, row = items[index]
            line = role * units + step * per_step + inner
            return jnp.concatenate(
                [
                    pick_columns(lows, highs, cols, line, (row + which) * slots, slots)
                    for which in range(2)
                ],
                axis=0,
            )

        upcoming = picked_at(0)
        for index, (inner, row) in enumerate(items):
            unit = step * per_step + inner
            picked = upcoming
            if index + 1 < len(items):
                upcoming = picked_at(index + 1)
            result = lax.dot_general(
                picked,
                stream.held[places[inner], row * BLK : (row + 2) * BLK],
                (((1,), (1,)), ((), ())),
                preferred_element_type=jnp.float32,
            )
            back[(bases[unit] + row) // 2] = jnp.where(low, result[:tokens], result[tokens:])
        return carry

    lax.fori_loop(0, units // per_step, run_step, 0)
    inv_rms = inv_rms_of(hidden)

    def correlate(pair, total):
        unit_rows = hidden[:, tile(pair)].astype(jnp.float32) * inv_rms
        return total + back[pair] * unit_rows

    total = over_pairs(feats, correlate, jnp.zeros((tokens, LANES), jnp.float32))
    mean = jnp.sum(total, axis=-1, keepdims=True) / feats

    def finish(pair, carry):
        lanes = tile(pair)
        unit_rows = hidden[:, lanes].astype(jnp.float32) * inv_rms
        centred = back[pair] - unit_rows * mean
        out[:, lanes] = (cotangent[:, lanes].astype(jnp.float32) + inv_rms * centred).astype(jnp.bfloat16)
        return carry

    over_pairs(feats, finish, 0)


def block_grad_layer(layer, role, cols, flipped, lows, highs, out, chosen, units, rows, slots):
    items = [(which, row) for which in range(len(chosen)) for row in range(rows)]

    def operands(index):
        which, row = items[index]
        picked = pick_columns(lows, highs, cols, role * units + chosen[which], row * slots, slots)
        return flipped[layer, which * rows + row], picked

    upcoming = operands(0)
    for index, (which, row) in enumerate(items):
        left, right = upcoming
        if index + 1 < len(items):
            upcoming = operands(index + 1)
        result = jnp.dot(left, right, preferred_element_type=jnp.float32)
        out[which][row * BLK : (row + 1) * BLK] = result.astype(jnp.bfloat16)


def fetch_chosen(flag, first, second, target, arrived):
    @pl.when(flag == 1)
    def _():
        pltpu.make_async_copy(first, target, arrived).start()

    @pl.when(flag != 1)
    def _():
        pltpu.make_async_copy(second, target, arrived).start()

    return pltpu.make_async_copy(first, target, arrived)


def stream_ahead(units, rows):
    return DEPTH - step_units(units, rows)


def forward_kernel(rows, slots, scale, cols, bases, flags, *rest):
    turning = scale is not None
    start, moved = rest[:2]
    rest = rest[2:]
    units = bases.shape[0]
    side = flags[0]
    if turning:
        goal, source, stash_out, loss_out, final_out, held, current, parts, sums, arrived, moving = rest[:11]
        stash, wanted, lows, highs, back = rest[11:]
    else:
        source, final_out, held, current, parts, sums, arrived, moving = rest

    def order(index):
        turn = index // units
        layer = jnp.where(turn < 2, turn, 3 - turn) if turning else turn
        return jnp.abs(layer - side), index % units

    stream = UnitStream(source, held, arrived, order, (4 if turning else 2) * units)
    entry = fetch_chosen(flags[1], start, moved, current, moving.at[0])
    stream.begin(stream_ahead(units, rows))
    if turning:
        target = pltpu.make_async_copy(goal, wanted, moving.at[1])
        target.start()
    entry.wait()

    def run_forward(layer, carry):
        if turning:
            stash[layer] = current[...]
            pltpu.make_async_copy(stash.at[layer], stash_out.at[layer], moving.at[2 + layer]).start()
        role = jnp.abs(layer - side)
        forward_layer(role, layer * units, stream, cols, bases, current, parts, sums, rows, slots)
        return carry

    lax.fori_loop(0, 2, run_forward, 0)
    if turning:
        target.wait()
        tokens, feats = current.shape

        def residue(pair, carry):
            lanes = tile(pair)
            gap = current[:, lanes].astype(jnp.float32) - wanted[:, lanes].astype(jnp.float32)
            current[:, lanes] = (gap * scale).astype(jnp.bfloat16)
            return carry

        over_pairs(feats, residue, 0)
        wanted[...] = current[...]
        kept = pltpu.make_async_copy(wanted, loss_out, moving.at[4])
        kept.start()

        def run_back(turn, carry):
            layer = 1 - turn
            spread(current, lows, highs)
            input_grad_layer(
                jnp.abs(layer - side),
                (2 + turn) * units,
                stream,
                cols,
                bases,
                stash.at[layer],
                current,
                current,
                lows,
                highs,
                back,
                rows,
                slots,
            )
            return carry

        lax.fori_loop(0, 2, run_back, 0)
    leaving = pltpu.make_async_copy(current, final_out, moving.at[0])
    leaving.start()
    if turning:
        for layer in range(2):
            pltpu.make_async_copy(stash.at[layer], stash_out.at[layer], moving.at[2 + layer]).wait()
        kept.wait()
    leaving.wait()


def state_of(tokens, feats):
    return jax.ShapeDtypeStruct((tokens, feats), jnp.bfloat16)


def forward_pass(start, moved, goal, scale, source, meta, rows, slots):
    tokens, feats = start.shape
    blocks = feats // BLK
    scratch = [
        pltpu.VMEM((DEPTH,) + source.shape[2:], jnp.bfloat16),
        pltpu.VMEM((tokens, feats), jnp.bfloat16),
        pltpu.VMEM((blocks, tokens, LANES), jnp.bfloat16),
        pltpu.VMEM((blocks, tokens, LANES), jnp.float32),
        pltpu.SemaphoreType.DMA((DEPTH,)),
        pltpu.SemaphoreType.DMA((5,)),
    ]
    outs = [state_of(tokens, feats)]
    ins = [start, moved]
    if goal is not None:
        ins.append(goal)
        stack = jax.ShapeDtypeStruct((2, tokens, feats), jnp.bfloat16)
        outs = [stack, state_of(tokens, feats)] + outs
        scratch += [
            pltpu.VMEM((2, tokens, feats), jnp.bfloat16),
            pltpu.VMEM((tokens, feats), jnp.bfloat16),
            pltpu.VMEM((blocks, tokens, LANES), jnp.bfloat16),
            pltpu.VMEM((blocks, tokens, LANES), jnp.bfloat16),
            pltpu.VMEM((blocks // 2, tokens, LANES), jnp.float32),
        ]
    return pl.pallas_call(
        functools.partial(forward_kernel, rows, slots, None if goal is None else scale),
        in_specs=[IN_SMEM] * 3 + [IN_HBM] * (len(ins) + 1),
        out_specs=[IN_HBM] * len(outs),
        out_shape=outs,
        scratch_shapes=scratch,
        compiler_params=pltpu.CompilerParams(vmem_limit_bytes=VMEM_LIMIT),
        cost_estimate=about(8 if goal is None else 14),
        name="forward_layers" if goal is None else "turning_layers",
    )(*meta, *ins, source)


def backward_kernel(
    rows,
    slots,
    depth,
    cols,
    bases,
    flags,
    stash,
    loss_grad,
    moved,
    source,
    outs,
    held,
    hidden,
    first,
    second,
    lows,
    highs,
    back,
    arrived,
    moving,
):
    units = bases.shape[0]
    side = flags[0]

    def order(index):
        return jnp.abs(1 - index // units - side), index % units

    stream = UnitStream(source, held, arrived, order, depth * units)
    entry = fetch_chosen(flags[2], loss_grad, moved, first, moving.at[0])
    stream.begin(stream_ahead(units, rows))
    loads = [
        pltpu.make_async_copy(stash.at[1 - turn], hidden.at[turn], moving.at[1 + turn])
        for turn in range(depth)
    ]
    for load in loads:
        load.start()
    entry.wait()
    if depth == 1:
        early = pltpu.make_async_copy(first, outs.at[1], moving.at[0])
        early.start()
    for turn in range(depth):
        read = first if turn == 0 else second
        spread(read, lows, highs)
        loads[turn].wait()
        input_grad_layer(
            jnp.abs(1 - turn - side),
            turn * units,
            stream,
            cols,
            bases,
            hidden.at[turn],
            read,
            second,
            lows,
            highs,
            back,
            rows,
            slots,
        )
    late = pltpu.make_async_copy(second, outs.at[0] if depth == 1 else outs, moving.at[3])
    late.start()
    if depth == 1:
        early.wait()
    late.wait()


def backward_pass(stash, loss_grad, moved, source, meta, rows, slots, depth):
    _, tokens, feats = stash.shape
    blocks = feats // BLK
    if depth == 1:
        out = jax.ShapeDtypeStruct((2, tokens, feats), jnp.bfloat16)
    else:
        out = state_of(tokens, feats)
    return pl.pallas_call(
        functools.partial(backward_kernel, rows, slots, depth),
        in_specs=[IN_SMEM] * 3 + [IN_HBM] * 4,
        out_specs=IN_HBM,
        out_shape=out,
        scratch_shapes=[
            pltpu.VMEM((DEPTH,) + source.shape[2:], jnp.bfloat16),
            pltpu.VMEM((depth, tokens, feats), jnp.bfloat16),
            pltpu.VMEM((tokens, feats), jnp.bfloat16),
            pltpu.VMEM((tokens, feats), jnp.bfloat16),
            pltpu.VMEM((blocks, tokens, LANES), jnp.bfloat16),
            pltpu.VMEM((blocks, tokens, LANES), jnp.bfloat16),
            pltpu.VMEM((blocks // 2, tokens, LANES), jnp.float32),
            pltpu.SemaphoreType.DMA((DEPTH,)),
            pltpu.SemaphoreType.DMA((4,)),
        ],
        compiler_params=pltpu.CompilerParams(vmem_limit_bytes=VMEM_LIMIT),
        cost_estimate=about(4 * depth),
        name="backward_layers",
    )(*meta, stash, loss_grad, moved, source)


def join_tokens(sources, joined, arrived, layer):
    copies = []
    begin = 0
    for index, source in enumerate(sources):
        span = pl.ds(begin, source.shape[1])
        copies.append(
            pltpu.make_async_copy(source.at[layer], joined.at[layer, span], arrived.at[layer, index])
        )
        begin += source.shape[1]
    for copy in copies:
        copy.start()
    return copies


def flip_kernel(rows, chosen, bases, *refs):
    *sources, flipped, joined, arrived = refs
    loads = [join_tokens(sources, joined, arrived, layer) for layer in range(2)]
    for load in loads[0] + loads[1]:
        load.wait()

    def run(layer, carry):
        hidden = joined.at[layer]
        inv_rms = inv_rms_of(hidden)
        for unit in range(chosen):

            def visit(step, carry):
                lanes = tile(bases[unit] // 2 + step)
                turned = (hidden[:, lanes].astype(jnp.float32) * inv_rms).T.astype(jnp.bfloat16)
                flipped[layer, unit * rows + 2 * step] = turned[:BLK]
                flipped[layer, unit * rows + 2 * step + 1] = turned[BLK:]
                return carry

            lax.fori_loop(0, rows // 2, visit, 0, unroll=True)
        return carry

    lax.fori_loop(0, 2, run, 0)


def flip_pass(stashes, bases, rows, chosen):
    tokens = sum(stash.shape[1] for stash in stashes)
    feats = stashes[0].shape[2]
    return pl.pallas_call(
        functools.partial(flip_kernel, rows, chosen),
        in_specs=[IN_SMEM] + [IN_HBM] * len(stashes),
        out_specs=IN_VMEM,
        out_shape=jax.ShapeDtypeStruct((2, chosen * rows, BLK, tokens), jnp.bfloat16),
        scratch_shapes=[
            pltpu.VMEM((2, tokens, feats), jnp.bfloat16),
            pltpu.SemaphoreType.DMA((2, len(stashes))),
        ],
        compiler_params=pltpu.CompilerParams(vmem_limit_bytes=VMEM_LIMIT),
        cost_estimate=about(4),
        name="flip_rows",
    )(bases, *stashes)


def block_grad_kernel(rows, slots, chosen, units, parts, cols, flags, turned, *rest):
    sources, rest = rest[:parts], rest[parts:]
    outs = rest[: 2 * len(chosen)]
    joined, flipped, lows, highs, arrived, fetched = rest[2 * len(chosen) :]
    fetches = [
        pltpu.make_async_copy(
            turned.at[:, pl.ds(unit * rows, rows)],
            flipped.at[:, pl.ds(which * rows, rows)],
            fetched.at[which],
        )
        for which, unit in enumerate(chosen)
    ]
    for fetch in fetches:
        fetch.start()
    layers = [jnp.abs(role - flags[0]) for role in (1, 0)]
    loads = [join_tokens(sources, joined, arrived, layer) for layer in layers]
    for turn, role in enumerate((1, 0)):
        layer = layers[turn]
        for load in loads[turn] + (fetches if turn == 0 else []):
            load.wait()
        spread(joined.at[layer], lows, highs)
        block_grad_layer(
            layer, role, cols, flipped, lows, highs, outs[role::2], chosen, units, rows, slots
        )


def block_grad_pass(turned, cotangents, meta, rows, slots, chosen):
    tokens = turned.shape[3]
    feats = cotangents[0].shape[2]
    blocks = feats // BLK
    cols, bases, flags = meta
    out = jax.ShapeDtypeStruct((rows * BLK, slots * BLK), jnp.bfloat16)
    return pl.pallas_call(
        functools.partial(
            block_grad_kernel, rows, slots, tuple(chosen), bases.shape[0], len(cotangents)
        ),
        in_specs=[IN_SMEM] * 2 + [IN_HBM] * (1 + len(cotangents)),
        out_specs=[IN_VMEM] * (2 * len(chosen)),
        out_shape=[out] * (2 * len(chosen)),
        scratch_shapes=[
            pltpu.VMEM((2, tokens, feats), jnp.bfloat16),
            pltpu.VMEM((2, len(chosen) * rows, BLK, tokens), jnp.bfloat16),
            pltpu.VMEM((blocks, tokens, LANES), jnp.bfloat16),
            pltpu.VMEM((blocks, tokens, LANES), jnp.bfloat16),
            pltpu.SemaphoreType.DMA((2, len(cotangents))),
            pltpu.SemaphoreType.DMA((len(chosen),)),
        ],
        compiler_params=pltpu.CompilerParams(vmem_limit_bytes=VMEM_LIMIT),
        cost_estimate=about(4 + len(chosen)),
        name="block_grads",
    )(cols, flags, turned, *cotangents)


def store_kernel(rows, names, grown, *refs):
    count = len(names)
    pieces = refs[2 : 2 + count] if grown else refs[:count]
    weights, lists, tails, lines, arrived, moved, listed = refs[-7:]
    heads = [
        pltpu.make_async_copy(piece.at[pl.ds(rows * BLK, TAIL)], tails.at[i], arrived.at[i])
        for i, piece in enumerate(pieces)
    ]
    bodies = [
        pltpu.make_async_copy(
            piece.at[pl.ds(0, rows * BLK)], weights.at[role, unit], moved.at[i]
        )
        for i, (piece, (role, unit)) in enumerate(zip(pieces, names))
    ]
    for copy in heads + bodies:
        copy.start()
    writes = []
    for i, (role, unit) in enumerate(names):
        heads[i].wait()
        line = tails[i].astype(jnp.float32)[:8, : lines.shape[2]]
        lines[i] = line.astype(jnp.int32)
        writes.append(pltpu.make_async_copy(lines.at[i], lists.at[role, unit], listed.at[i]))
        writes[-1].start()
    for copy in bodies + writes:
        copy.wait()


def store_units(grown, names, pieces, rows, slots, units):
    width = slots * BLK
    lanes = -(-rows * slots // LANES) * LANES
    outs = [
        jax.ShapeDtypeStruct((2, units, rows * BLK, width), jnp.bfloat16),
        jax.ShapeDtypeStruct((2, units, 8, lanes), jnp.int32),
    ]
    grown = list(grown or ())
    count = len(pieces)
    return pl.pallas_call(
        functools.partial(store_kernel, rows, tuple(names), bool(grown)),
        in_specs=[IN_HBM] * (len(grown) + count),
        out_specs=[IN_HBM] * 2,
        out_shape=outs,
        input_output_aliases={0: 0, 1: 1} if grown else {},
        scratch_shapes=[
            pltpu.VMEM((count, TAIL, width), jnp.bfloat16),
            pltpu.VMEM((count, 8, lanes), jnp.int32),
            pltpu.SemaphoreType.DMA((count,)),
            pltpu.SemaphoreType.DMA((count,)),
            pltpu.SemaphoreType.DMA((count,)),
        ],
        compiler_params=pltpu.CompilerParams(vmem_limit_bytes=VMEM_LIMIT),
        cost_estimate=about(1 + count),
        name="store_units",
    )(*grown, *pieces)


def to_rows(blocks):
    rows, slots, _ = blocks.shape
    split = blocks.reshape(rows, slots, BLK, BLK)
    return split.transpose(0, 2, 1, 3).reshape(rows * BLK, slots * BLK)


def from_rows(matrix, slots):
    rows = matrix.shape[0] // BLK
    split = matrix.reshape(rows, BLK, slots, BLK)
    return split.transpose(0, 2, 1, 3).reshape(rows, slots, BLK * BLK)


def token_cuts(tokens):
    if tokens % 16 or tokens < 32:
        return [(0, tokens)]
    first = -(-tokens // 32) * 16
    return [(0, first), (first, tokens)]


def folded(count):
    return list(range(0, 1)) + list(range(1, count, 2)) + list(range(2, count, 2))[::-1]


def body(inputs, target, blocks, columns, counts):
    stage, stages = lax.axis_index("stage"), lax.axis_size("stage")
    side, sides = lax.axis_index("side"), lax.axis_size("side")
    dp_id, dp_count = lax.axis_index("dp"), lax.axis_size("dp")
    mb_count, tok_local, feats = inputs.shape
    rows, slots = columns.shape[1:]
    loss_scale = (mb_count * tok_local * dp_count) ** (-0.5)
    places = dp_count // 2
    place = dp_id // 2
    core = dp_id % 2
    share = mb_count * tok_local // sides

    around = folded(places)
    ranks = [around.index(spot) for spot in range(places)]
    rank = jnp.array(ranks, jnp.int32)[place]
    hops = [
        (2 * around[i] + half, 2 * around[(i + 1) % places] + half)
        for i in range(places)
        for half in range(2)
    ]

    def ring(array):
        return lax.ppermute(array, "dp", hops)

    def sibling(array):
        return lax.ppermute(array, "dp", [(i, i ^ 1) for i in range(dp_count)])

    def partner(array):
        return lax.ppermute(array, "side", [(i, sides - 1 - i) for i in range(sides)])

    live = jnp.arange(slots, dtype=jnp.int32)[None, :] < counts[0][:, None]
    kept = jnp.where(live[:, :, None], blocks[0], jnp.zeros_like(blocks[0]))
    listed = columns[0].reshape(1, rows * slots).astype(jnp.bfloat16)
    tail = jnp.pad(listed, ((0, TAIL - 1), (0, slots * BLK - rows * slots)))
    own = jnp.concatenate([to_rows(kept), tail], axis=0)

    units = 2 * places
    grown = None
    fresh = {(0, 0): own}
    newest = own
    last_other = None
    for slot in range(places):
        moving = {"other": partner(newest), "far_own": sibling(newest)}
        if slot + 1 < places:
            moving["own"] = ring(newest)
        if slot:
            moving["far_other"] = sibling(last_other)
        moving["grown"] = store_units(grown, list(fresh), list(fresh.values()), rows, slots, units)
        moving = lax.optimization_barrier(moving)
        grown = moving["grown"]
        fresh = {(1, slot): moving["other"], (0, places + slot): moving["far_own"]}
        if slot + 1 < places:
            newest = moving["own"]
            fresh[0, slot + 1] = newest
        if slot:
            fresh[1, places + slot - 1] = moving["far_other"]
        last_other = moving["other"]
    fresh[1, units - 1] = sibling(last_other)
    weights, lists = store_units(grown, list(fresh), list(fresh.values()), rows, slots, units)
    cols = lists[:, :, 0].reshape(2 * units, -1)
    turns = jnp.array(around, jnp.int32)[(rank - jnp.arange(places)) % places]
    bases = jnp.concatenate([turns * 2 + core, turns * 2 + 1 - core]).astype(jnp.int32) * rows
    flags = jnp.stack([side, stage == 0, stage == stages - 1]).astype(jnp.int32)
    meta = (cols, bases, flags)

    def my_rows(array):
        flat = array.reshape(mb_count * tok_local, feats)
        return lax.dynamic_slice_in_dim(flat, side * share, share, 0)

    def hop(array, distance):
        route = [(i, i + distance) for i in range(stages) if 0 <= i + distance < stages]
        return lax.ppermute(array, "stage", route)

    cuts = token_cuts(share)
    ways = range(len(cuts))
    whole_start, whole_goal = my_rows(inputs), my_rows(target)
    start = [whole_start[begin:end] for begin, end in cuts]
    goal = [whole_goal[begin:end] for begin, end in cuts]
    moved = list(start)
    for step in range(stages - 1):
        final = [
            forward_pass(start[i], moved[i], None, None, weights, meta, rows, slots)[0]
            for i in ways
        ]
        moved = [hop(final[i], 1) for i in ways]
    turned = [
        forward_pass(start[i], moved[i], goal[i], loss_scale, weights, meta, rows, slots)
        for i in ways
    ]
    stashes, loss_grads, result = [list(column) for column in zip(*turned)]
    moved = loss_grads
    for step in range(stages - 1):
        if step:
            result = [
                backward_pass(stashes[i], loss_grads[i], moved[i], weights, meta, rows, slots, 2)
                for i in ways
            ]
        moved = [hop(result[i], -1) for i in ways]
    flipped = flip_pass(stashes + [sibling(stash) for stash in stashes], bases, rows, places)
    cotangents = [
        backward_pass(stashes[i], loss_grads[i], moved[i], weights, meta, rows, slots, 1) for i in ways
    ]

    order = list(range(1, places)) + [0]

    cotangents = cotangents + [sibling(part) for part in cotangents]
    kept, outgoing = block_grad_pass(flipped, cotangents, meta, rows, slots, order[:1])
    cotangents, tied = lax.optimization_barrier((cotangents, outgoing))
    late = block_grad_pass(flipped, cotangents, meta, rows, slots, order[1:])
    coming, late = lax.optimization_barrier((partner(tied), late))
    travelling = add_rounded(kept, coming)
    for index in range(places - 1):
        kept, outgoing = late[2 * index], late[2 * index + 1]
        passed, coming = lax.optimization_barrier((ring(travelling), partner(outgoing)))
        total = kept.astype(jnp.float32) + coming.astype(jnp.float32) + passed.astype(jnp.float32)
        travelling = total.astype(jnp.bfloat16)
    result = from_rows(travelling, slots)
    return jnp.where(live[:, :, None], result, jnp.zeros_like(result))[None]


def add_rounded(left, right):
    return (left.astype(jnp.float32) + right.astype(jnp.float32)).astype(jnp.bfloat16)


def solution(mesh):
    sections, width = mesh.devices.shape
    split = jax.sharding.Mesh(mesh.devices.reshape(sections // 2, 2, width), ("stage", "side", "dp"))
    section = ("stage", "side")
    return jax.shard_map(
        body,
        mesh=split,
        in_specs=(
            P(None, "dp", None),
            P(None, "dp", None),
            P(section, "dp", None, None),
            P(section, "dp", None),
            P(section, "dp"),
        ),
        out_specs=P(section, "dp", None, None),
        check_vma=False,
    )
```

```python
import functools

import jax
import jax.numpy as jnp
from jax import lax
from jax.experimental import pallas as pl
from jax.experimental.pallas import tpu as pltpu
from jax.sharding import PartitionSpec as P

BLK = 64
LANES = 128
EPSILON = 1e-05
VMEM_LIMIT = 54 * 1024 * 1024
STEP_ROWS = 8

TAIL = 16

IN_VMEM = pl.BlockSpec(memory_space=pltpu.VMEM)
IN_SMEM = pl.BlockSpec(memory_space=pltpu.SMEM)
IN_HBM = pl.BlockSpec(memory_space=pl.ANY)


def about(microseconds):
    return pl.CostEstimate(
        flops=int(microseconds * 1.1e9), bytes_accessed=1 << 20, transcendentals=0
    )


def step_units(units, rows):
    size = max(1, STEP_ROWS // rows)
    while units % size:
        size -= 1
    return size


def low_half(rows):
    return lax.broadcasted_iota(jnp.int32, (rows, LANES), 1) < BLK


def tile(pair):
    return pl.ds(pl.multiple_of(pair * LANES, LANES), LANES)


def over_pairs(feats, visit, carry):
    return lax.fori_loop(0, feats // LANES, visit, carry, unroll=4)


def inv_rms_of(ref):
    tokens, feats = ref.shape

    def visit(pair, total):
        values = ref[:, tile(pair)].astype(jnp.float32)
        return total + values * values

    total = over_pairs(feats, visit, jnp.zeros((tokens, LANES), jnp.float32))
    return lax.rsqrt(jnp.sum(total, axis=-1, keepdims=True) / feats + EPSILON)


def start_loads(pieces, held, arrived, roles):
    units = held.shape[1]
    for role in roles:
        for unit in range(units):
            pltpu.make_async_copy(
                pieces[2 * unit + role], held.at[role, unit], arrived.at[role, unit]
            ).start()


def start_loads_in_order(side, pieces, held, arrived, layers):
    for value in range(2):
        pl.when(side == value)(
            functools.partial(
                start_loads, pieces, held, arrived, [abs(layer - value) for layer in layers]
            )
        )


def wait_load(pieces, held, arrived, role, unit):
    pltpu.make_async_copy(pieces[0], held.at[role, unit], arrived.at[role, unit]).wait()


def forward_layer(role, wait, cols, bases, current, held, parts, sums, rows, slots):
    tokens, feats = current.shape
    units = held.shape[1]
    per_step = step_units(units, rows)
    low = low_half(tokens)
    inv_rms = inv_rms_of(current)

    def normalise(pair, carry):
        lanes = tile(pair)
        unit_rows = current[:, lanes].astype(jnp.float32) * inv_rms
        parts[2 * pair] = jnp.where(low, unit_rows, 0.0).astype(jnp.bfloat16)
        parts[2 * pair + 1] = jnp.where(low, 0.0, unit_rows).astype(jnp.bfloat16)
        sums[2 * pair] = jnp.zeros((tokens, LANES), jnp.float32)
        sums[2 * pair + 1] = jnp.zeros((tokens, LANES), jnp.float32)
        return carry

    over_pairs(feats, normalise, 0)

    def run_step(step, carry):
        for inner in range(per_step):
            wait(role, step * per_step + inner)
        items = [(inner, row) for inner in range(per_step) for row in range(0, rows, 2)]

        def product_of(index):
            inner, row = items[index]
            unit = step * per_step + inner
            place = bases[unit] + row
            left = jnp.concatenate([parts[place], parts[place + 1]], axis=0)
            right = held[role, unit, row * BLK : (row + 2) * BLK]
            return jnp.dot(left, right, preferred_element_type=jnp.float32)

        upcoming = product_of(0)
        for index, (inner, row) in enumerate(items):
            product = upcoming
            if index + 1 < len(items):
                upcoming = product_of(index + 1)
            for which in range(2):
                line = role * units + step * per_step + inner
                flat = (row + which) * slots
                for begin in range(0, slots, 4):
                    at = [cols[line, flat + slot] for slot in range(begin, min(begin + 4, slots))]
                    added = []
                    for offset in range(len(at)):
                        slot = begin + offset
                        lanes = slice((slot // 2) * LANES, (slot // 2 + 1) * LANES)
                        piece = product[which * tokens : (which + 1) * tokens, lanes]
                        piece = jnp.where(low, piece, 0.0) if slot % 2 == 0 else jnp.where(low, 0.0, piece)
                        added.append(sums[at[offset]] + piece)
                    for offset in range(len(at)):
                        sums[at[offset]] = added[offset]
        return carry

    lax.fori_loop(0, units // per_step, run_step, 0)

    def finish(pair, carry):
        lanes = tile(pair)
        first, second = sums[2 * pair], sums[2 * pair + 1]
        branch = jnp.where(low, first, second) + pltpu.roll(jnp.where(low, second, first), BLK, 1)
        current[:, lanes] = (current[:, lanes].astype(jnp.float32) + branch).astype(jnp.bfloat16)
        return carry

    over_pairs(feats, finish, 0)


def spread(source, lows, highs):
    tokens, feats = source.shape
    low = low_half(tokens)

    def visit(pair, carry):
        both = source[:, tile(pair)].astype(jnp.float32)
        moved = pltpu.roll(both, BLK, 1)
        lows[2 * pair] = jnp.where(low, both, 0.0).astype(jnp.bfloat16)
        highs[2 * pair] = jnp.where(low, 0.0, moved).astype(jnp.bfloat16)
        lows[2 * pair + 1] = jnp.where(low, moved, 0.0).astype(jnp.bfloat16)
        highs[2 * pair + 1] = jnp.where(low, 0.0, both).astype(jnp.bfloat16)
        return carry

    over_pairs(feats, visit, 0)


def pick_columns(lows, highs, cols, line, flat, slots):
    return jnp.concatenate(
        [
            lows[cols[line, flat + 2 * half]] + highs[cols[line, flat + 2 * half + 1]]
            for half in range(slots // 2)
        ],
        axis=1,
    )


def input_grad_layer(role, wait, cols, bases, hidden, cotangent, out, held, lows, highs, back, rows, slots):
    tokens, feats = cotangent.shape
    units = held.shape[1]
    per_step = step_units(units, rows)
    low = low_half(tokens)

    def run_step(step, carry):
        for inner in range(per_step):
            wait(role, step * per_step + inner)
        items = [(inner, row) for inner in range(per_step) for row in range(0, rows, 2)]

        def picked_at(index):
            inner, row = items[index]
            line = role * units + step * per_step + inner
            return jnp.concatenate(
                [
                    pick_columns(lows, highs, cols, line, (row + which) * slots, slots)
                    for which in range(2)
                ],
                axis=0,
            )

        upcoming = picked_at(0)
        for index, (inner, row) in enumerate(items):
            unit = step * per_step + inner
            picked = upcoming
            if index + 1 < len(items):
                upcoming = picked_at(index + 1)
            result = lax.dot_general(
                picked,
                held[role, unit, row * BLK : (row + 2) * BLK],
                (((1,), (1,)), ((), ())),
                preferred_element_type=jnp.float32,
            )
            place = (bases[unit] + row) // 2
            back[place] = jnp.where(low, result[:tokens], result[tokens:])
        return carry

    lax.fori_loop(0, units // per_step, run_step, 0)
    inv_rms = inv_rms_of(hidden)

    def correlate(pair, total):
        unit_rows = hidden[:, tile(pair)].astype(jnp.float32) * inv_rms
        return total + back[pair] * unit_rows

    total = over_pairs(feats, correlate, jnp.zeros((tokens, LANES), jnp.float32))
    mean = jnp.sum(total, axis=-1, keepdims=True) / feats

    def finish(pair, carry):
        lanes = tile(pair)
        unit_rows = hidden[:, lanes].astype(jnp.float32) * inv_rms
        centred = back[pair] - unit_rows * mean
        out[:, lanes] = (cotangent[:, lanes].astype(jnp.float32) + inv_rms * centred).astype(jnp.bfloat16)
        return carry

    over_pairs(feats, finish, 0)


def block_grad_layer(layer, role, cols, flipped, lows, highs, out, chosen, units, rows, slots):
    items = [(which, row) for which in range(len(chosen)) for row in range(rows)]

    def operands(index):
        which, row = items[index]
        picked = pick_columns(lows, highs, cols, role * units + chosen[which], row * slots, slots)
        return flipped[layer, which * rows + row], picked

    upcoming = operands(0)
    for index, (which, row) in enumerate(items):
        left, right = upcoming
        if index + 1 < len(items):
            upcoming = operands(index + 1)
        result = jnp.dot(left, right, preferred_element_type=jnp.float32)
        out[which][row * BLK : (row + 1) * BLK] = result.astype(jnp.bfloat16)


def choose(flag, first, second, target):
    @pl.when(flag == 1)
    def _():
        target[...] = first[...]

    @pl.when(flag != 1)
    def _():
        target[...] = second[...]


def forward_kernel(rows, slots, count, scale, cols, bases, flags, *rest):
    turning = scale is not None
    start, moved = rest[:2]
    rest = rest[2:]
    if turning:
        goal, rest = rest[0], rest[1:]
    straight, rest = rest[:count], rest[count:]
    if turning:
        stash, loss_grad, final, held, parts, sums, arrived, lows, highs, back = rest
    else:
        final, held, parts, sums, arrived = rest
    start_loads_in_order(flags[0], straight, held, arrived, (0, 1))
    choose(flags[1], start, moved, final)
    wait = functools.partial(wait_load, straight, held, arrived)

    def run_forward(layer, carry):
        if turning:
            stash[layer] = final[...]
        role = jnp.abs(layer - flags[0])
        forward_layer(role, wait, cols, bases, final, held, parts, sums, rows, slots)
        return carry

    lax.fori_loop(0, 2, run_forward, 0)
    if not turning:
        return
    tokens, feats = final.shape

    def residue(pair, carry):
        lanes = tile(pair)
        gap = final[:, lanes].astype(jnp.float32) - goal[:, lanes].astype(jnp.float32)
        loss_grad[:, lanes] = (gap * scale).astype(jnp.bfloat16)
        return carry

    over_pairs(feats, residue, 0)
    final[...] = loss_grad[...]
    def run_back(turn, carry):
        layer = 1 - turn
        role = jnp.abs(layer - flags[0])
        hidden = stash.at[layer]
        spread(final, lows, highs)
        input_grad_layer(
            role, nothing, cols, bases, hidden, final, final, held, lows, highs, back, rows, slots
        )
        return carry

    lax.fori_loop(0, 2, run_back, 0)


def nothing(*_):
    return None


def state_of(tokens, feats):
    return jax.ShapeDtypeStruct((tokens, feats), jnp.bfloat16)


def unit_scratch(pieces):
    units = len(pieces) // 2
    return [pltpu.VMEM((2, units) + pieces[0].shape, jnp.bfloat16), pltpu.SemaphoreType.DMA((2, units))]


def forward_pass(start, moved, goal, scale, straight, meta, rows, slots):
    tokens, feats = start.shape
    blocks = feats // BLK
    stack = jax.ShapeDtypeStruct((2, tokens, feats), jnp.bfloat16)
    held, arrived = unit_scratch(straight)
    scratch = [
        held,
        pltpu.VMEM((blocks, tokens, LANES), jnp.bfloat16),
        pltpu.VMEM((blocks, tokens, LANES), jnp.float32),
        arrived,
    ]
    outs = [state_of(tokens, feats)]
    ins = [start, moved]
    pieces = list(straight)
    if goal is not None:
        ins.append(goal)
        outs = [stack, state_of(tokens, feats)] + outs
        scratch += [
            pltpu.VMEM((blocks, tokens, LANES), jnp.bfloat16),
            pltpu.VMEM((blocks, tokens, LANES), jnp.bfloat16),
            pltpu.VMEM((blocks // 2, tokens, LANES), jnp.float32),
        ]
    return pl.pallas_call(
        functools.partial(forward_kernel, rows, slots, len(straight), None if goal is None else scale),
        in_specs=[IN_SMEM] * 3 + [IN_VMEM] * len(ins) + [IN_HBM] * len(pieces),
        out_specs=[IN_VMEM] * len(outs),
        out_shape=outs,
        scratch_shapes=scratch,
        compiler_params=pltpu.CompilerParams(vmem_limit_bytes=VMEM_LIMIT),
        cost_estimate=about(8 if goal is None else 14),
        name="forward_layers" if goal is None else "turning_layers",
    )(*meta, *ins, *pieces)


def backward_kernel(rows, slots, count, depth, cols, bases, flags, stash, loss_grad, moved, *rest):
    across, rest = rest[:count], rest[count:]
    outs, crossed, lows, highs, back, landed = rest
    if depth == 1:
        first, second = outs.at[1], outs.at[0]
    else:
        first = second = outs
    start_loads_in_order(flags[0], across, crossed, landed, (1,) if depth == 1 else (1, 0))
    choose(flags[2], loss_grad, moved, first)
    wait = functools.partial(wait_load, across, crossed, landed)

    def run_back(layer):
        spread(first, lows, highs)
        role = jnp.abs(layer - flags[0])
        input_grad_layer(
            role, wait, cols, bases, stash.at[layer], first, second, crossed, lows, highs, back, rows, slots
        )

    run_back(1)
    if depth == 2:
        run_back(0)


def backward_pass(stash, loss_grad, moved, across, meta, rows, slots, depth):
    _, tokens, feats = stash.shape
    blocks = feats // BLK
    crossed, landed = unit_scratch(across)
    if depth == 1:
        out = jax.ShapeDtypeStruct((2, tokens, feats), jnp.bfloat16)
    else:
        out = state_of(tokens, feats)
    return pl.pallas_call(
        functools.partial(backward_kernel, rows, slots, len(across), depth),
        in_specs=[IN_SMEM] * 3 + [IN_VMEM] * 3 + [IN_HBM] * len(across),
        out_specs=IN_VMEM,
        out_shape=out,
        scratch_shapes=[
            crossed,
            pltpu.VMEM((blocks, tokens, LANES), jnp.bfloat16),
            pltpu.VMEM((blocks, tokens, LANES), jnp.bfloat16),
            pltpu.VMEM((blocks // 2, tokens, LANES), jnp.float32),
            landed,
        ],
        compiler_params=pltpu.CompilerParams(vmem_limit_bytes=VMEM_LIMIT),
        cost_estimate=about(4 * depth),
        name="backward_layers",
    )(*meta, stash, loss_grad, moved, *across)


def join_tokens(sources, joined, arrived):
    copies = []
    begin = 0
    for index, source in enumerate(sources):
        span = pl.ds(begin, source.shape[1])
        copies.append(pltpu.make_async_copy(source, joined.at[:, span], arrived.at[index]))
        begin += source.shape[1]
    for copy in copies:
        copy.start()
    for copy in copies:
        copy.wait()


def flip_kernel(rows, chosen, bases, *refs):
    *sources, flipped, joined, arrived = refs
    join_tokens(sources, joined, arrived)

    def run(layer, carry):
        hidden = joined.at[layer]
        inv_rms = inv_rms_of(hidden)
        for unit in range(chosen):

            def visit(step, carry):
                lanes = tile(bases[unit] // 2 + step)
                turned = (hidden[:, lanes].astype(jnp.float32) * inv_rms).T.astype(jnp.bfloat16)
                flipped[layer, unit * rows + 2 * step] = turned[:BLK]
                flipped[layer, unit * rows + 2 * step + 1] = turned[BLK:]
                return carry

            lax.fori_loop(0, rows // 2, visit, 0, unroll=True)
        return carry

    lax.fori_loop(0, 2, run, 0)


def flip_pass(stashes, bases, rows, chosen):
    tokens = sum(stash.shape[1] for stash in stashes)
    feats = stashes[0].shape[2]
    return pl.pallas_call(
        functools.partial(flip_kernel, rows, chosen),
        in_specs=[IN_SMEM] + [IN_HBM] * len(stashes),
        out_specs=IN_VMEM,
        out_shape=jax.ShapeDtypeStruct((2, chosen * rows, BLK, tokens), jnp.bfloat16),
        scratch_shapes=[
            pltpu.VMEM((2, tokens, feats), jnp.bfloat16),
            pltpu.SemaphoreType.DMA((len(stashes),)),
        ],
        compiler_params=pltpu.CompilerParams(vmem_limit_bytes=VMEM_LIMIT),
        cost_estimate=about(4),
        name="flip_rows",
    )(bases, *stashes)


def block_grad_kernel(rows, slots, chosen, units, parts, cols, flags, turned, *rest):
    sources, rest = rest[:parts], rest[parts:]
    outs = rest[: 2 * len(chosen)]
    joined, flipped, lows, highs, arrived, fetched = rest[2 * len(chosen) :]
    fetches = [
        pltpu.make_async_copy(
            turned.at[:, pl.ds(unit * rows, rows)],
            flipped.at[:, pl.ds(which * rows, rows)],
            fetched.at[which],
        )
        for which, unit in enumerate(chosen)
    ]
    for fetch in fetches:
        fetch.start()
    join_tokens(sources, joined, arrived)
    for fetch in fetches:
        fetch.wait()
    for role in (1, 0):
        layer = jnp.abs(role - flags[0])
        spread(joined.at[layer], lows, highs)
        block_grad_layer(
            layer, role, cols, flipped, lows, highs, outs[role::2], chosen, units, rows, slots
        )


def block_grad_pass(turned, cotangents, meta, rows, slots, chosen):
    tokens = turned.shape[3]
    feats = cotangents[0].shape[2]
    blocks = feats // BLK
    cols, bases, flags = meta
    out = jax.ShapeDtypeStruct((rows * BLK, slots * BLK), jnp.bfloat16)
    return pl.pallas_call(
        functools.partial(
            block_grad_kernel, rows, slots, tuple(chosen), bases.shape[0], len(cotangents)
        ),
        in_specs=[IN_SMEM] * 2 + [IN_HBM] * (1 + len(cotangents)),
        out_specs=[IN_VMEM] * (2 * len(chosen)),
        out_shape=[out] * (2 * len(chosen)),
        scratch_shapes=[
            pltpu.VMEM((2, tokens, feats), jnp.bfloat16),
            pltpu.VMEM((2, len(chosen) * rows, BLK, tokens), jnp.bfloat16),
            pltpu.VMEM((blocks, tokens, LANES), jnp.bfloat16),
            pltpu.VMEM((blocks, tokens, LANES), jnp.bfloat16),
            pltpu.SemaphoreType.DMA((len(cotangents),)),
            pltpu.SemaphoreType.DMA((len(chosen),)),
        ],
        compiler_params=pltpu.CompilerParams(vmem_limit_bytes=VMEM_LIMIT),
        cost_estimate=about(4 + len(chosen)),
        name="block_grads",
    )(cols, flags, turned, *cotangents)


def list_kernel(rows, pieces_count, *refs):
    pieces, (listed, tails, arrived) = refs[:pieces_count], refs[pieces_count:]
    copies = [
        pltpu.make_async_copy(piece.at[pl.ds(rows * BLK, TAIL)], tails.at[i], arrived.at[i])
        for i, piece in enumerate(pieces)
    ]
    for copy in copies:
        copy.start()
    for i, copy in enumerate(copies):
        copy.wait()
        line = tails[i].astype(jnp.float32)[:1, : listed.shape[1]]
        listed[i : i + 1] = line.astype(jnp.int32)


def list_pass(pieces, rows, slots):
    count = len(pieces)
    lanes = -(-rows * slots // LANES) * LANES
    return pl.pallas_call(
        functools.partial(list_kernel, rows, count),
        in_specs=[IN_HBM] * count,
        out_specs=IN_VMEM,
        out_shape=jax.ShapeDtypeStruct((count, lanes), jnp.int32),
        scratch_shapes=[
            pltpu.VMEM((count, TAIL, slots * BLK), jnp.bfloat16),
            pltpu.SemaphoreType.DMA((count,)),
        ],
        compiler_params=pltpu.CompilerParams(vmem_limit_bytes=VMEM_LIMIT),
        cost_estimate=about(2),
        name="list_columns",
    )(*pieces)


def to_rows(blocks):
    rows, slots, _ = blocks.shape
    split = blocks.reshape(rows, slots, BLK, BLK)
    return split.transpose(0, 2, 1, 3).reshape(rows * BLK, slots * BLK)


def from_rows(matrix, slots):
    rows = matrix.shape[0] // BLK
    split = matrix.reshape(rows, BLK, slots, BLK)
    return split.transpose(0, 2, 1, 3).reshape(rows, slots, BLK * BLK)


def token_cuts(tokens):
    if tokens % 16 or tokens < 32:
        return [(0, tokens)]
    first = -(-tokens // 32) * 16
    return [(0, first), (first, tokens)]


def folded(count):
    return list(range(0, 1)) + list(range(1, count, 2)) + list(range(2, count, 2))[::-1]


def body(inputs, target, blocks, columns, counts):
    stage, stages = lax.axis_index("stage"), lax.axis_size("stage")
    side, sides = lax.axis_index("side"), lax.axis_size("side")
    dp_id, dp_count = lax.axis_index("dp"), lax.axis_size("dp")
    mb_count, tok_local, feats = inputs.shape
    rows, slots = columns.shape[1:]
    loss_scale = (mb_count * tok_local * dp_count) ** (-0.5)
    places = dp_count // 2
    place = dp_id // 2
    core = dp_id % 2
    share = mb_count * tok_local // sides

    around = folded(places)
    ranks = [around.index(spot) for spot in range(places)]
    rank = jnp.array(ranks, jnp.int32)[place]
    hops = [
        (2 * around[i] + half, 2 * around[(i + 1) % places] + half)
        for i in range(places)
        for half in range(2)
    ]

    def ring(array):
        return lax.ppermute(array, "dp", hops)

    def sibling(array):
        return lax.ppermute(array, "dp", [(i, i ^ 1) for i in range(dp_count)])

    def partner(array):
        return lax.ppermute(array, "side", [(i, sides - 1 - i) for i in range(sides)])

    live = jnp.arange(slots, dtype=jnp.int32)[None, :] < counts[0][:, None]
    kept = jnp.where(live[:, :, None], blocks[0], jnp.zeros_like(blocks[0]))
    listed = columns[0].reshape(1, rows * slots).astype(jnp.bfloat16)
    tail = jnp.pad(listed, ((0, TAIL - 1), (0, slots * BLK - rows * slots)))
    own = jnp.concatenate([to_rows(kept), tail], axis=0)

    owns, others, far_owns, far_others = [own], [], [], []
    for slot in range(places):
        moving = {"other": partner(owns[slot]), "far_own": sibling(owns[slot])}
        if slot + 1 < places:
            moving["own"] = ring(owns[slot])
        if slot:
            moving["far_other"] = sibling(others[slot - 1])
        moving = lax.optimization_barrier(moving)
        others.append(moving["other"])
        far_owns.append(moving["far_own"])
        if slot + 1 < places:
            owns.append(moving["own"])
        if slot:
            far_others.append(moving["far_other"])
    far_others.append(sibling(others[-1]))
    own_units, other_units = owns + far_owns, others + far_others
    pieces = [piece for pair in zip(own_units, other_units) for piece in pair]
    cols = list_pass(own_units + other_units, rows, slots)
    turns = jnp.array(around, jnp.int32)[(rank - jnp.arange(places)) % places]
    bases = jnp.concatenate([turns * 2 + core, turns * 2 + 1 - core]).astype(jnp.int32) * rows
    flags = jnp.stack([side, stage == 0, stage == stages - 1]).astype(jnp.int32)
    meta = (cols, bases, flags)

    def my_rows(array):
        flat = array.reshape(mb_count * tok_local, feats)
        return lax.dynamic_slice_in_dim(flat, side * share, share, 0)

    def hop(array, distance):
        route = [(i, i + distance) for i in range(stages) if 0 <= i + distance < stages]
        return lax.ppermute(array, "stage", route)

    cuts = token_cuts(share)
    ways = range(len(cuts))
    whole_start, whole_goal = my_rows(inputs), my_rows(target)
    start = [whole_start[begin:end] for begin, end in cuts]
    goal = [whole_goal[begin:end] for begin, end in cuts]
    moved = list(start)
    for step in range(stages - 1):
        final = [
            forward_pass(start[i], moved[i], None, None, pieces, meta, rows, slots)[0]
            for i in ways
        ]
        moved = [hop(final[i], 1) for i in ways]
    turned = [
        forward_pass(start[i], moved[i], goal[i], loss_scale, pieces, meta, rows, slots)
        for i in ways
    ]
    stashes, loss_grads, result = [list(column) for column in zip(*turned)]
    moved = loss_grads
    for step in range(stages - 1):
        if step:
            result = [
                backward_pass(stashes[i], loss_grads[i], moved[i], pieces, meta, rows, slots, 2)
                for i in ways
            ]
        moved = [hop(result[i], -1) for i in ways]
    flipped = flip_pass(stashes + [sibling(stash) for stash in stashes], bases, rows, places)
    cotangents = [
        backward_pass(stashes[i], loss_grads[i], moved[i], pieces, meta, rows, slots, 1) for i in ways
    ]

    order = list(range(1, places)) + [0]

    cotangents = cotangents + [sibling(part) for part in cotangents]
    kept, outgoing = block_grad_pass(flipped, cotangents, meta, rows, slots, order[:1])
    cotangents, tied = lax.optimization_barrier((cotangents, outgoing))
    late = block_grad_pass(flipped, cotangents, meta, rows, slots, order[1:])
    coming, late = lax.optimization_barrier((partner(tied), late))
    travelling = add_rounded(kept, coming)
    for index in range(places - 1):
        kept, outgoing = late[2 * index], late[2 * index + 1]
        passed, coming = lax.optimization_barrier((ring(travelling), partner(outgoing)))
        total = kept.astype(jnp.float32) + coming.astype(jnp.float32) + passed.astype(jnp.float32)
        travelling = total.astype(jnp.bfloat16)
    result = from_rows(travelling, slots)
    return jnp.where(live[:, :, None], result, jnp.zeros_like(result))[None]


def add_rounded(left, right):
    return (left.astype(jnp.float32) + right.astype(jnp.float32)).astype(jnp.bfloat16)


def solution(mesh):
    sections, width = mesh.devices.shape
    split = jax.sharding.Mesh(mesh.devices.reshape(sections // 2, 2, width), ("stage", "side", "dp"))
    section = ("stage", "side")
    return jax.shard_map(
        body,
        mesh=split,
        in_specs=(
            P(None, "dp", None),
            P(None, "dp", None),
            P(section, "dp", None, None),
            P(section, "dp", None),
            P(section, "dp"),
        ),
        out_specs=P(section, "dp", None, None),
        check_vma=False,
    )
```

```python
import functools

import jax
import jax.numpy as jnp
from jax import lax
from jax.experimental import pallas as pl
from jax.experimental.pallas import tpu as pltpu
from jax.sharding import PartitionSpec as P

BLK = 64
LANES = 128
EPSILON = 1e-05
MIB = 1024 * 1024
STEP_ROWS = 8

TAIL = 16

IN_VMEM = pl.BlockSpec(memory_space=pltpu.VMEM)
IN_SMEM = pl.BlockSpec(memory_space=pltpu.SMEM)
IN_HBM = pl.BlockSpec(memory_space=pl.ANY)


def about(microseconds):
    return pl.CostEstimate(
        flops=int(microseconds * 1.1e9), bytes_accessed=1 << 20, transcendentals=0
    )


def step_units(units, rows):
    size = max(1, STEP_ROWS // rows)
    while units % size:
        size -= 1
    return size


def low_half(rows):
    return lax.broadcasted_iota(jnp.int32, (rows, LANES), 1) < BLK


def tile(pair):
    return pl.ds(pl.multiple_of(pair * LANES, LANES), LANES)


def over_pairs(feats, visit, carry):
    return lax.fori_loop(0, feats // LANES, visit, carry, unroll=4)


def inv_rms_of(ref):
    tokens, feats = ref.shape

    def visit(pair, total):
        values = ref[:, tile(pair)].astype(jnp.float32)
        return total + values * values

    total = over_pairs(feats, visit, jnp.zeros((tokens, LANES), jnp.float32))
    return lax.rsqrt(jnp.sum(total, axis=-1, keepdims=True) / feats + EPSILON)


def start_loads(pieces, held, arrived, roles):
    units = held.shape[1]
    for role in roles:
        for unit in range(units):
            pltpu.make_async_copy(
                pieces[2 * unit + role], held.at[role, unit], arrived.at[role, unit]
            ).start()


def start_loads_in_order(side, pieces, held, arrived, layers):
    for value in range(2):
        pl.when(side == value)(
            functools.partial(
                start_loads, pieces, held, arrived, [abs(layer - value) for layer in layers]
            )
        )


def wait_load(pieces, held, arrived, role, unit):
    pltpu.make_async_copy(pieces[0], held.at[role, unit], arrived.at[role, unit]).wait()


def forward_layer(role, wait, cols, bases, current, held, parts, sums, rows, slots):
    tokens, feats = current.shape
    units = held.shape[1]
    per_step = step_units(units, rows)
    low = low_half(tokens)
    inv_rms = inv_rms_of(current)

    def normalise(pair, carry):
        lanes = tile(pair)
        unit_rows = current[:, lanes].astype(jnp.float32) * inv_rms
        parts[2 * pair] = jnp.where(low, unit_rows, 0.0).astype(jnp.bfloat16)
        parts[2 * pair + 1] = jnp.where(low, 0.0, unit_rows).astype(jnp.bfloat16)
        sums[2 * pair] = jnp.zeros((tokens, LANES), jnp.float32)
        sums[2 * pair + 1] = jnp.zeros((tokens, LANES), jnp.float32)
        return carry

    over_pairs(feats, normalise, 0)

    def run_step(step, carry):
        for inner in range(per_step):
            wait(role, step * per_step + inner)
        items = [(inner, row) for inner in range(per_step) for row in range(0, rows, 2)]

        def product_of(index):
            inner, row = items[index]
            unit = step * per_step + inner
            place = bases[unit] + row
            left = jnp.concatenate([parts[place], parts[place + 1]], axis=0)
            right = held[role, unit, row * BLK : (row + 2) * BLK]
            return jnp.dot(left, right, preferred_element_type=jnp.float32)

        upcoming = product_of(0)
        for index, (inner, row) in enumerate(items):
            product = upcoming
            if index + 1 < len(items):
                upcoming = product_of(index + 1)
            for which in range(2):
                line = role * units + step * per_step + inner
                flat = (row + which) * slots
                for begin in range(0, slots, 4):
                    at = [cols[line, flat + slot] for slot in range(begin, min(begin + 4, slots))]
                    added = []
                    for offset in range(len(at)):
                        slot = begin + offset
                        lanes = slice((slot // 2) * LANES, (slot // 2 + 1) * LANES)
                        piece = product[which * tokens : (which + 1) * tokens, lanes]
                        piece = jnp.where(low, piece, 0.0) if slot % 2 == 0 else jnp.where(low, 0.0, piece)
                        added.append(sums[at[offset]] + piece)
                    for offset in range(len(at)):
                        sums[at[offset]] = added[offset]
        return carry

    lax.fori_loop(0, units // per_step, run_step, 0)

    def finish(pair, carry):
        lanes = tile(pair)
        first, second = sums[2 * pair], sums[2 * pair + 1]
        branch = jnp.where(low, first, second) + pltpu.roll(jnp.where(low, second, first), BLK, 1)
        current[:, lanes] = (current[:, lanes].astype(jnp.float32) + branch).astype(jnp.bfloat16)
        return carry

    over_pairs(feats, finish, 0)


def spread(source, lows, highs):
    tokens, feats = source.shape
    low = low_half(tokens)

    def visit(pair, carry):
        both = source[:, tile(pair)].astype(jnp.float32)
        moved = pltpu.roll(both, BLK, 1)
        lows[2 * pair] = jnp.where(low, both, 0.0).astype(jnp.bfloat16)
        highs[2 * pair] = jnp.where(low, 0.0, moved).astype(jnp.bfloat16)
        lows[2 * pair + 1] = jnp.where(low, moved, 0.0).astype(jnp.bfloat16)
        highs[2 * pair + 1] = jnp.where(low, 0.0, both).astype(jnp.bfloat16)
        return carry

    over_pairs(feats, visit, 0)


def pick_columns(lows, highs, cols, line, flat, slots):
    return jnp.concatenate(
        [
            lows[cols[line, flat + 2 * half]] + highs[cols[line, flat + 2 * half + 1]]
            for half in range(slots // 2)
        ],
        axis=1,
    )


def input_grad_layer(role, wait, cols, bases, hidden, cotangent, out, held, lows, highs, back, rows, slots):
    tokens, feats = cotangent.shape
    units = held.shape[1]
    per_step = step_units(units, rows)
    low = low_half(tokens)

    def run_step(step, carry):
        for inner in range(per_step):
            wait(role, step * per_step + inner)
        items = [(inner, row) for inner in range(per_step) for row in range(0, rows, 2)]

        def picked_at(index):
            inner, row = items[index]
            line = role * units + step * per_step + inner
            return jnp.concatenate(
                [
                    pick_columns(lows, highs, cols, line, (row + which) * slots, slots)
                    for which in range(2)
                ],
                axis=0,
            )

        upcoming = picked_at(0)
        for index, (inner, row) in enumerate(items):
            unit = step * per_step + inner
            picked = upcoming
            if index + 1 < len(items):
                upcoming = picked_at(index + 1)
            result = lax.dot_general(
                picked,
                held[role, unit, row * BLK : (row + 2) * BLK],
                (((1,), (1,)), ((), ())),
                preferred_element_type=jnp.float32,
            )
            place = (bases[unit] + row) // 2
            back[place] = jnp.where(low, result[:tokens], result[tokens:])
        return carry

    lax.fori_loop(0, units // per_step, run_step, 0)
    inv_rms = inv_rms_of(hidden)

    def correlate(pair, total):
        unit_rows = hidden[:, tile(pair)].astype(jnp.float32) * inv_rms
        return total + back[pair] * unit_rows

    total = over_pairs(feats, correlate, jnp.zeros((tokens, LANES), jnp.float32))
    mean = jnp.sum(total, axis=-1, keepdims=True) / feats

    def finish(pair, carry):
        lanes = tile(pair)
        unit_rows = hidden[:, lanes].astype(jnp.float32) * inv_rms
        centred = back[pair] - unit_rows * mean
        out[:, lanes] = (cotangent[:, lanes].astype(jnp.float32) + inv_rms * centred).astype(jnp.bfloat16)
        return carry

    over_pairs(feats, finish, 0)


def block_grad_layer(layer, role, cols, flipped, lows, highs, out, chosen, units, rows, slots):
    items = [(which, row) for which in range(len(chosen)) for row in range(rows)]

    def operands(index):
        which, row = items[index]
        picked = pick_columns(lows, highs, cols, role * units + chosen[which], row * slots, slots)
        return flipped[layer, which * rows + row], picked

    upcoming = operands(0)
    for index, (which, row) in enumerate(items):
        left, right = upcoming
        if index + 1 < len(items):
            upcoming = operands(index + 1)
        result = jnp.dot(left, right, preferred_element_type=jnp.float32)
        out[which][row * BLK : (row + 1) * BLK] = result.astype(jnp.bfloat16)


def choose(flag, first, second, target):
    @pl.when(flag == 1)
    def _():
        target[...] = first[...]

    @pl.when(flag != 1)
    def _():
        target[...] = second[...]


def forward_kernel(rows, slots, count, scale, cols, bases, flags, *rest):
    turning = scale is not None
    start, moved = rest[:2]
    rest = rest[2:]
    if turning:
        goal, rest = rest[0], rest[1:]
    straight, rest = rest[:count], rest[count:]
    if turning:
        stash, loss_grad, final, held, parts, sums, arrived, lows, highs, back = rest
    else:
        final, held, parts, sums, arrived = rest
    start_loads_in_order(flags[0], straight, held, arrived, (0, 1))
    choose(flags[1], start, moved, final)
    wait = functools.partial(wait_load, straight, held, arrived)

    def run_forward(layer, carry):
        if turning:
            stash[layer] = final[...]
        role = jnp.abs(layer - flags[0])
        forward_layer(role, wait, cols, bases, final, held, parts, sums, rows, slots)
        return carry

    lax.fori_loop(0, 2, run_forward, 0)
    if not turning:
        return
    tokens, feats = final.shape

    def residue(pair, carry):
        lanes = tile(pair)
        gap = final[:, lanes].astype(jnp.float32) - goal[:, lanes].astype(jnp.float32)
        loss_grad[:, lanes] = (gap * scale).astype(jnp.bfloat16)
        return carry

    over_pairs(feats, residue, 0)
    final[...] = loss_grad[...]
    def run_back(turn, carry):
        layer = 1 - turn
        role = jnp.abs(layer - flags[0])
        hidden = stash.at[layer]
        spread(final, lows, highs)
        input_grad_layer(
            role, nothing, cols, bases, hidden, final, final, held, lows, highs, back, rows, slots
        )
        return carry

    lax.fori_loop(0, 2, run_back, 0)


def nothing(*_):
    return None


def state_of(tokens, feats):
    return jax.ShapeDtypeStruct((tokens, feats), jnp.bfloat16)


def unit_scratch(pieces):
    units = len(pieces) // 2
    return [pltpu.VMEM((2, units) + pieces[0].shape, jnp.bfloat16), pltpu.SemaphoreType.DMA((2, units))]


def forward_pass(start, moved, goal, scale, straight, meta, rows, slots):
    tokens, feats = start.shape
    blocks = feats // BLK
    stack = jax.ShapeDtypeStruct((2, tokens, feats), jnp.bfloat16)
    held, arrived = unit_scratch(straight)
    scratch = [
        held,
        pltpu.VMEM((blocks, tokens, LANES), jnp.bfloat16),
        pltpu.VMEM((blocks, tokens, LANES), jnp.float32),
        arrived,
    ]
    outs = [state_of(tokens, feats)]
    ins = [start, moved]
    pieces = list(straight)
    if goal is not None:
        ins.append(goal)
        outs = [stack, state_of(tokens, feats)] + outs
        scratch += [
            pltpu.VMEM((blocks, tokens, LANES), jnp.bfloat16),
            pltpu.VMEM((blocks, tokens, LANES), jnp.bfloat16),
            pltpu.VMEM((blocks // 2, tokens, LANES), jnp.float32),
        ]
    return pl.pallas_call(
        functools.partial(forward_kernel, rows, slots, len(straight), None if goal is None else scale),
        in_specs=[IN_SMEM] * 3 + [IN_VMEM] * len(ins) + [IN_HBM] * len(pieces),
        out_specs=[IN_VMEM] * len(outs),
        out_shape=outs,
        scratch_shapes=scratch,
        compiler_params=pltpu.CompilerParams(vmem_limit_bytes=(16 if goal is None else 20) * MIB),
        cost_estimate=about(8 if goal is None else 14),
        name="forward_layers" if goal is None else "turning_layers",
    )(*meta, *ins, *pieces)


def backward_kernel(rows, slots, count, depth, cols, bases, flags, stash, loss_grad, moved, *rest):
    across, rest = rest[:count], rest[count:]
    outs, crossed, lows, highs, back, landed = rest
    if depth == 1:
        first, second = outs.at[1], outs.at[0]
    else:
        first = second = outs
    start_loads_in_order(flags[0], across, crossed, landed, (1,) if depth == 1 else (1, 0))
    choose(flags[2], loss_grad, moved, first)
    wait = functools.partial(wait_load, across, crossed, landed)

    def run_back(layer):
        spread(first, lows, highs)
        role = jnp.abs(layer - flags[0])
        input_grad_layer(
            role, wait, cols, bases, stash.at[layer], first, second, crossed, lows, highs, back, rows, slots
        )

    run_back(1)
    if depth == 2:
        run_back(0)


def backward_pass(stash, loss_grad, moved, across, meta, rows, slots, depth):
    _, tokens, feats = stash.shape
    blocks = feats // BLK
    crossed, landed = unit_scratch(across)
    if depth == 1:
        out = jax.ShapeDtypeStruct((2, tokens, feats), jnp.bfloat16)
    else:
        out = state_of(tokens, feats)
    return pl.pallas_call(
        functools.partial(backward_kernel, rows, slots, len(across), depth),
        in_specs=[IN_SMEM] * 3 + [IN_VMEM] * 3 + [IN_HBM] * len(across),
        out_specs=IN_VMEM,
        out_shape=out,
        scratch_shapes=[
            crossed,
            pltpu.VMEM((blocks, tokens, LANES), jnp.bfloat16),
            pltpu.VMEM((blocks, tokens, LANES), jnp.bfloat16),
            pltpu.VMEM((blocks // 2, tokens, LANES), jnp.float32),
            landed,
        ],
        compiler_params=pltpu.CompilerParams(vmem_limit_bytes=18 * MIB),
        cost_estimate=about(4 * depth),
        name="backward_layers",
    )(*meta, stash, loss_grad, moved, *across)


def join_tokens(sources, joined, arrived):
    copies = []
    begin = 0
    for index, source in enumerate(sources):
        span = pl.ds(begin, source.shape[1])
        copies.append(pltpu.make_async_copy(source, joined.at[:, span], arrived.at[index]))
        begin += source.shape[1]
    for copy in copies:
        copy.start()
    for copy in copies:
        copy.wait()


def flip_kernel(rows, chosen, bases, *refs):
    *sources, flipped, joined, arrived = refs
    join_tokens(sources, joined, arrived)

    def run(layer, carry):
        hidden = joined.at[layer]
        inv_rms = inv_rms_of(hidden)
        for unit in range(chosen):

            def visit(step, carry):
                lanes = tile(bases[unit] // 2 + step)
                turned = (hidden[:, lanes].astype(jnp.float32) * inv_rms).T.astype(jnp.bfloat16)
                flipped[layer, unit * rows + 2 * step] = turned[:BLK]
                flipped[layer, unit * rows + 2 * step + 1] = turned[BLK:]
                return carry

            lax.fori_loop(0, rows // 2, visit, 0, unroll=True)
        return carry

    lax.fori_loop(0, 2, run, 0)


def flip_pass(stashes, bases, rows, chosen):
    tokens = sum(stash.shape[1] for stash in stashes)
    feats = stashes[0].shape[2]
    return pl.pallas_call(
        functools.partial(flip_kernel, rows, chosen),
        in_specs=[IN_SMEM] + [IN_HBM] * len(stashes),
        out_specs=IN_VMEM,
        out_shape=jax.ShapeDtypeStruct((2, chosen * rows, BLK, tokens), jnp.bfloat16),
        scratch_shapes=[
            pltpu.VMEM((2, tokens, feats), jnp.bfloat16),
            pltpu.SemaphoreType.DMA((len(stashes),)),
        ],
        compiler_params=pltpu.CompilerParams(vmem_limit_bytes=12 * MIB),
        cost_estimate=about(4),
        name="flip_rows",
    )(bases, *stashes)


def block_grad_kernel(rows, slots, chosen, units, parts, cols, flags, turned, *rest):
    sources, rest = rest[:parts], rest[parts:]
    outs = rest[: 2 * len(chosen)]
    joined, flipped, lows, highs, arrived, fetched = rest[2 * len(chosen) :]
    fetches = [
        pltpu.make_async_copy(
            turned.at[:, pl.ds(unit * rows, rows)],
            flipped.at[:, pl.ds(which * rows, rows)],
            fetched.at[which],
        )
        for which, unit in enumerate(chosen)
    ]
    for fetch in fetches:
        fetch.start()
    join_tokens(sources, joined, arrived)
    for fetch in fetches:
        fetch.wait()
    for role in (1, 0):
        layer = jnp.abs(role - flags[0])
        spread(joined.at[layer], lows, highs)
        block_grad_layer(
            layer, role, cols, flipped, lows, highs, outs[role::2], chosen, units, rows, slots
        )


def block_grad_pass(turned, cotangents, meta, rows, slots, chosen):
    tokens = turned.shape[3]
    feats = cotangents[0].shape[2]
    blocks = feats // BLK
    cols, bases, flags = meta
    out = jax.ShapeDtypeStruct((rows * BLK, slots * BLK), jnp.bfloat16)
    return pl.pallas_call(
        functools.partial(
            block_grad_kernel, rows, slots, tuple(chosen), bases.shape[0], len(cotangents)
        ),
        in_specs=[IN_SMEM] * 2 + [IN_HBM] * (1 + len(cotangents)),
        out_specs=[IN_VMEM] * (2 * len(chosen)),
        out_shape=[out] * (2 * len(chosen)),
        scratch_shapes=[
            pltpu.VMEM((2, tokens, feats), jnp.bfloat16),
            pltpu.VMEM((2, len(chosen) * rows, BLK, tokens), jnp.bfloat16),
            pltpu.VMEM((blocks, tokens, LANES), jnp.bfloat16),
            pltpu.VMEM((blocks, tokens, LANES), jnp.bfloat16),
            pltpu.SemaphoreType.DMA((len(cotangents),)),
            pltpu.SemaphoreType.DMA((len(chosen),)),
        ],
        compiler_params=pltpu.CompilerParams(vmem_limit_bytes=18 * MIB),
        cost_estimate=about(4 + len(chosen)),
        name="block_grads",
    )(cols, flags, turned, *cotangents)


def list_kernel(rows, pieces_count, *refs):
    pieces, (listed, tails, arrived) = refs[:pieces_count], refs[pieces_count:]
    copies = [
        pltpu.make_async_copy(piece.at[pl.ds(rows * BLK, TAIL)], tails.at[i], arrived.at[i])
        for i, piece in enumerate(pieces)
    ]
    for copy in copies:
        copy.start()
    for i, copy in enumerate(copies):
        copy.wait()
        line = tails[i].astype(jnp.float32)[:1, : listed.shape[1]]
        listed[i : i + 1] = line.astype(jnp.int32)


def list_pass(pieces, rows, slots):
    count = len(pieces)
    lanes = -(-rows * slots // LANES) * LANES
    return pl.pallas_call(
        functools.partial(list_kernel, rows, count),
        in_specs=[IN_HBM] * count,
        out_specs=IN_VMEM,
        out_shape=jax.ShapeDtypeStruct((count, lanes), jnp.int32),
        scratch_shapes=[
            pltpu.VMEM((count, TAIL, slots * BLK), jnp.bfloat16),
            pltpu.SemaphoreType.DMA((count,)),
        ],
        compiler_params=pltpu.CompilerParams(vmem_limit_bytes=4 * MIB),
        cost_estimate=about(2),
        name="list_columns",
    )(*pieces)


def to_rows(blocks):
    rows, slots, _ = blocks.shape
    split = blocks.reshape(rows, slots, BLK, BLK)
    return split.transpose(0, 2, 1, 3).reshape(rows * BLK, slots * BLK)


def from_rows(matrix, slots):
    rows = matrix.shape[0] // BLK
    split = matrix.reshape(rows, BLK, slots, BLK)
    return split.transpose(0, 2, 1, 3).reshape(rows, slots, BLK * BLK)


def token_cuts(tokens):
    if tokens % 16 or tokens < 32:
        return [(0, tokens)]
    first = -(-tokens // 32) * 16
    return [(0, first), (first, tokens)]


def folded(count):
    return list(range(0, 1)) + list(range(1, count, 2)) + list(range(2, count, 2))[::-1]


def body(inputs, target, blocks, columns, counts):
    stage, stages = lax.axis_index("stage"), lax.axis_size("stage")
    side, sides = lax.axis_index("side"), lax.axis_size("side")
    dp_id, dp_count = lax.axis_index("dp"), lax.axis_size("dp")
    mb_count, tok_local, feats = inputs.shape
    rows, slots = columns.shape[1:]
    loss_scale = (mb_count * tok_local * dp_count) ** (-0.5)
    places = dp_count // 2
    place = dp_id // 2
    core = dp_id % 2
    share = mb_count * tok_local // sides

    around = folded(places)
    ranks = [around.index(spot) for spot in range(places)]
    rank = jnp.array(ranks, jnp.int32)[place]
    hops = [
        (2 * around[i] + half, 2 * around[(i + 1) % places] + half)
        for i in range(places)
        for half in range(2)
    ]

    def ring(array):
        return lax.ppermute(array, "dp", hops)

    def sibling(array):
        return lax.ppermute(array, "dp", [(i, i ^ 1) for i in range(dp_count)])

    def partner(array):
        return lax.ppermute(array, "side", [(i, sides - 1 - i) for i in range(sides)])

    live = jnp.arange(slots, dtype=jnp.int32)[None, :] < counts[0][:, None]
    kept = jnp.where(live[:, :, None], blocks[0], jnp.zeros_like(blocks[0]))
    listed = columns[0].reshape(1, rows * slots).astype(jnp.bfloat16)
    tail = jnp.pad(listed, ((0, TAIL - 1), (0, slots * BLK - rows * slots)))
    own = jnp.concatenate([to_rows(kept), tail], axis=0)

    owns, others, far_owns, far_others = [own], [], [], []
    for slot in range(places):
        moving = {"other": partner(owns[slot]), "far_own": sibling(owns[slot])}
        if slot + 1 < places:
            moving["own"] = ring(owns[slot])
        if slot:
            moving["far_other"] = sibling(others[slot - 1])
        moving = lax.optimization_barrier(moving)
        others.append(moving["other"])
        far_owns.append(moving["far_own"])
        if slot + 1 < places:
            owns.append(moving["own"])
        if slot:
            far_others.append(moving["far_other"])
    far_others.append(sibling(others[-1]))
    own_units, other_units = owns + far_owns, others + far_others
    pieces = [piece for pair in zip(own_units, other_units) for piece in pair]
    cols = list_pass(own_units + other_units, rows, slots)
    turns = jnp.array(around, jnp.int32)[(rank - jnp.arange(places)) % places]
    bases = jnp.concatenate([turns * 2 + core, turns * 2 + 1 - core]).astype(jnp.int32) * rows
    flags = jnp.stack([side, stage == 0, stage == stages - 1]).astype(jnp.int32)
    meta = (cols, bases, flags)

    def my_rows(array):
        flat = array.reshape(mb_count * tok_local, feats)
        return lax.dynamic_slice_in_dim(flat, side * share, share, 0)

    def hop(array, distance):
        route = [(i, i + distance) for i in range(stages) if 0 <= i + distance < stages]
        return lax.ppermute(array, "stage", route)

    cuts = token_cuts(share)
    ways = range(len(cuts))
    whole_start, whole_goal = my_rows(inputs), my_rows(target)
    start = [whole_start[begin:end] for begin, end in cuts]
    goal = [whole_goal[begin:end] for begin, end in cuts]
    moved = list(start)
    for step in range(stages - 1):
        final = [
            forward_pass(start[i], moved[i], None, None, pieces, meta, rows, slots)[0]
            for i in ways
        ]
        moved = [hop(final[i], 1) for i in ways]
    turned = [
        forward_pass(start[i], moved[i], goal[i], loss_scale, pieces, meta, rows, slots)
        for i in ways
    ]
    stashes, loss_grads, result = [list(column) for column in zip(*turned)]
    moved = loss_grads
    for step in range(stages - 1):
        if step:
            result = [
                backward_pass(stashes[i], loss_grads[i], moved[i], pieces, meta, rows, slots, 2)
                for i in ways
            ]
        moved = [hop(result[i], -1) for i in ways]
    flipped = flip_pass(stashes + [sibling(stash) for stash in stashes], bases, rows, places)
    cotangents = [
        backward_pass(stashes[i], loss_grads[i], moved[i], pieces, meta, rows, slots, 1) for i in ways
    ]

    order = list(range(1, places)) + [0]

    cotangents = cotangents + [sibling(part) for part in cotangents]
    kept, outgoing = block_grad_pass(flipped, cotangents, meta, rows, slots, order[:1])
    cotangents, tied = lax.optimization_barrier((cotangents, outgoing))
    late = block_grad_pass(flipped, cotangents, meta, rows, slots, order[1:])
    coming, late = lax.optimization_barrier((partner(tied), late))
    travelling = add_rounded(kept, coming)
    for index in range(places - 1):
        kept, outgoing = late[2 * index], late[2 * index + 1]
        passed, coming = lax.optimization_barrier((ring(travelling), partner(outgoing)))
        total = kept.astype(jnp.float32) + coming.astype(jnp.float32) + passed.astype(jnp.float32)
        travelling = total.astype(jnp.bfloat16)
    result = from_rows(travelling, slots)
    return jnp.where(live[:, :, None], result, jnp.zeros_like(result))[None]


def add_rounded(left, right):
    return (left.astype(jnp.float32) + right.astype(jnp.float32)).astype(jnp.bfloat16)


def solution(mesh):
    sections, width = mesh.devices.shape
    split = jax.sharding.Mesh(mesh.devices.reshape(sections // 2, 2, width), ("stage", "side", "dp"))
    section = ("stage", "side")
    return jax.shard_map(
        body,
        mesh=split,
        in_specs=(
            P(None, "dp", None),
            P(None, "dp", None),
            P(section, "dp", None, None),
            P(section, "dp", None),
            P(section, "dp"),
        ),
        out_specs=P(section, "dp", None, None),
        check_vma=False,
    )
```

```python
import functools

import jax
import jax.numpy as jnp
from jax import lax
from jax.experimental import pallas as pl
from jax.experimental.pallas import tpu as pltpu
from jax.sharding import PartitionSpec as P

BLK = 64
LANES = 128
EPSILON = 1e-05
MIB = 1024 * 1024
STEP_ROWS = 8

TAIL = 16

IN_VMEM = pl.BlockSpec(memory_space=pltpu.VMEM)
IN_SMEM = pl.BlockSpec(memory_space=pltpu.SMEM)
IN_HBM = pl.BlockSpec(memory_space=pl.ANY)


def about(microseconds):
    return pl.CostEstimate(
        flops=int(microseconds * 1.1e9), bytes_accessed=1 << 20, transcendentals=0
    )


def step_units(units, rows):
    size = max(1, STEP_ROWS // rows)
    while units % size:
        size -= 1
    return size


def low_half(rows):
    return lax.broadcasted_iota(jnp.int32, (rows, LANES), 1) < BLK


def tile(pair):
    return pl.ds(pl.multiple_of(pair * LANES, LANES), LANES)


def over_pairs(feats, visit, carry):
    return lax.fori_loop(0, feats // LANES, visit, carry, unroll=4)


def inv_rms_of(ref):
    tokens, feats = ref.shape

    def visit(pair, total):
        values = ref[:, tile(pair)].astype(jnp.float32)
        return total + values * values

    total = over_pairs(feats, visit, jnp.zeros((tokens, LANES), jnp.float32))
    return lax.rsqrt(jnp.sum(total, axis=-1, keepdims=True) / feats + EPSILON)


def start_loads(pieces, held, arrived, roles):
    units = held.shape[1]
    for role in roles:
        for unit in range(units):
            pltpu.make_async_copy(
                pieces[2 * unit + role], held.at[role, unit], arrived.at[role, unit]
            ).start()


def start_loads_in_order(side, pieces, held, arrived, layers):
    for value in range(2):
        pl.when(side == value)(
            functools.partial(
                start_loads, pieces, held, arrived, [abs(layer - value) for layer in layers]
            )
        )


def wait_load(pieces, held, arrived, role, unit):
    pltpu.make_async_copy(pieces[0], held.at[role, unit], arrived.at[role, unit]).wait()


def forward_layer(role, wait, cols, bases, current, held, parts, sums, rows, slots):
    tokens, feats = current.shape
    units = held.shape[1]
    per_step = step_units(units, rows)
    low = low_half(tokens)
    inv_rms = inv_rms_of(current)

    def normalise(pair, carry):
        lanes = tile(pair)
        unit_rows = current[:, lanes].astype(jnp.float32) * inv_rms
        parts[2 * pair] = jnp.where(low, unit_rows, 0.0).astype(jnp.bfloat16)
        parts[2 * pair + 1] = jnp.where(low, 0.0, unit_rows).astype(jnp.bfloat16)
        sums[2 * pair] = jnp.zeros((tokens, LANES), jnp.float32)
        sums[2 * pair + 1] = jnp.zeros((tokens, LANES), jnp.float32)
        return carry

    over_pairs(feats, normalise, 0)

    def run_step(step, carry):
        for inner in range(per_step):
            wait(role, step * per_step + inner)
        items = [(inner, row) for inner in range(per_step) for row in range(0, rows, 2)]

        def product_of(index):
            inner, row = items[index]
            unit = step * per_step + inner
            place = bases[unit] + row
            left = jnp.concatenate([parts[place], parts[place + 1]], axis=0)
            right = held[role, unit, row * BLK : (row + 2) * BLK]
            return jnp.dot(left, right, preferred_element_type=jnp.float32)

        def columns_of(index):
            inner, row = items[index]
            line = role * units + step * per_step + inner
            return [cols[line, row * slots + place] for place in range(2 * slots)]

        upcoming = product_of(0)
        ahead = columns_of(0)
        for index, (inner, row) in enumerate(items):
            product, listed = upcoming, ahead
            if index + 1 < len(items):
                upcoming = product_of(index + 1)
                ahead = columns_of(index + 1)
            for which in range(2):
                for begin in range(0, slots, 4):
                    at = listed[which * slots + begin : which * slots + min(begin + 4, slots)]
                    added = []
                    for offset in range(len(at)):
                        slot = begin + offset
                        lanes = slice((slot // 2) * LANES, (slot // 2 + 1) * LANES)
                        piece = product[which * tokens : (which + 1) * tokens, lanes]
                        piece = jnp.where(low, piece, 0.0) if slot % 2 == 0 else jnp.where(low, 0.0, piece)
                        added.append(sums[at[offset]] + piece)
                    for offset in range(len(at)):
                        sums[at[offset]] = added[offset]
        return carry

    lax.fori_loop(0, units // per_step, run_step, 0)

    def finish(pair, carry):
        lanes = tile(pair)
        first, second = sums[2 * pair], sums[2 * pair + 1]
        branch = jnp.where(low, first, second) + pltpu.roll(jnp.where(low, second, first), BLK, 1)
        current[:, lanes] = (current[:, lanes].astype(jnp.float32) + branch).astype(jnp.bfloat16)
        return carry

    over_pairs(feats, finish, 0)


def spread(source, lows, highs):
    tokens, feats = source.shape
    low = low_half(tokens)

    def visit(pair, carry):
        both = source[:, tile(pair)].astype(jnp.float32)
        moved = pltpu.roll(both, BLK, 1)
        lows[2 * pair] = jnp.where(low, both, 0.0).astype(jnp.bfloat16)
        highs[2 * pair] = jnp.where(low, 0.0, moved).astype(jnp.bfloat16)
        lows[2 * pair + 1] = jnp.where(low, moved, 0.0).astype(jnp.bfloat16)
        highs[2 * pair + 1] = jnp.where(low, 0.0, both).astype(jnp.bfloat16)
        return carry

    over_pairs(feats, visit, 0)


def pick_columns(lows, highs, cols, line, flat, slots):
    return jnp.concatenate(
        [
            lows[cols[line, flat + 2 * half]] + highs[cols[line, flat + 2 * half + 1]]
            for half in range(slots // 2)
        ],
        axis=1,
    )


def input_grad_layer(role, wait, cols, bases, hidden, cotangent, out, held, lows, highs, back, rows, slots):
    tokens, feats = cotangent.shape
    units = held.shape[1]
    per_step = step_units(units, rows)
    low = low_half(tokens)

    def run_step(step, carry):
        for inner in range(per_step):
            wait(role, step * per_step + inner)
        items = [(inner, row) for inner in range(per_step) for row in range(0, rows, 2)]

        def picked_at(index):
            inner, row = items[index]
            line = role * units + step * per_step + inner
            return jnp.concatenate(
                [
                    pick_columns(lows, highs, cols, line, (row + which) * slots, slots)
                    for which in range(2)
                ],
                axis=0,
            )

        upcoming = picked_at(0)
        for index, (inner, row) in enumerate(items):
            unit = step * per_step + inner
            picked = upcoming
            if index + 1 < len(items):
                upcoming = picked_at(index + 1)
            result = lax.dot_general(
                picked,
                held[role, unit, row * BLK : (row + 2) * BLK],
                (((1,), (1,)), ((), ())),
                preferred_element_type=jnp.float32,
            )
            place = (bases[unit] + row) // 2
            back[place] = jnp.where(low, result[:tokens], result[tokens:])
        return carry

    lax.fori_loop(0, units // per_step, run_step, 0)
    inv_rms = inv_rms_of(hidden)

    def correlate(pair, total):
        unit_rows = hidden[:, tile(pair)].astype(jnp.float32) * inv_rms
        return total + back[pair] * unit_rows

    total = over_pairs(feats, correlate, jnp.zeros((tokens, LANES), jnp.float32))
    mean = jnp.sum(total, axis=-1, keepdims=True) / feats

    def finish(pair, carry):
        lanes = tile(pair)
        unit_rows = hidden[:, lanes].astype(jnp.float32) * inv_rms
        centred = back[pair] - unit_rows * mean
        out[:, lanes] = (cotangent[:, lanes].astype(jnp.float32) + inv_rms * centred).astype(jnp.bfloat16)
        return carry

    over_pairs(feats, finish, 0)


def block_grad_layer(begin, role, cols, flipped, lows, highs, out, chosen, units, rows, slots):
    items = [(which, row) for which in range(len(chosen)) for row in range(rows)]

    def operands(index):
        which, row = items[index]
        picked = pick_columns(lows, highs, cols, role * units + chosen[which], row * slots, slots)
        return flipped[begin + which * rows + row], picked

    upcoming = operands(0)
    for index, (which, row) in enumerate(items):
        left, right = upcoming
        if index + 1 < len(items):
            upcoming = operands(index + 1)
        result = jnp.dot(left, right, preferred_element_type=jnp.float32)
        out[which][row * BLK : (row + 1) * BLK] = result.astype(jnp.bfloat16)


def choose(flag, first, second, target):
    @pl.when(flag == 1)
    def _():
        target[...] = first[...]

    @pl.when(flag != 1)
    def _():
        target[...] = second[...]


def forward_kernel(rows, slots, count, scale, cols, bases, flags, *rest):
    turning = scale is not None
    start, moved = rest[:2]
    rest = rest[2:]
    if turning:
        goal, rest = rest[0], rest[1:]
    straight, rest = rest[:count], rest[count:]
    if turning:
        stash, loss_grad, final, held, parts, sums, arrived, lows, highs, back = rest
    else:
        final, held, parts, sums, arrived = rest
    start_loads_in_order(flags[0], straight, held, arrived, (0, 1))
    choose(flags[1], start, moved, final)
    wait = functools.partial(wait_load, straight, held, arrived)

    def run_forward(layer, carry):
        if turning:
            stash[layer] = final[...]
        role = jnp.abs(layer - flags[0])
        forward_layer(role, wait, cols, bases, final, held, parts, sums, rows, slots)
        return carry

    lax.fori_loop(0, 2, run_forward, 0)
    if not turning:
        return
    tokens, feats = final.shape

    def residue(pair, carry):
        lanes = tile(pair)
        gap = final[:, lanes].astype(jnp.float32) - goal[:, lanes].astype(jnp.float32)
        loss_grad[:, lanes] = (gap * scale).astype(jnp.bfloat16)
        return carry

    over_pairs(feats, residue, 0)
    final[...] = loss_grad[...]
    def run_back(turn, carry):
        layer = 1 - turn
        role = jnp.abs(layer - flags[0])
        hidden = stash.at[layer]
        spread(final, lows, highs)
        input_grad_layer(
            role, nothing, cols, bases, hidden, final, final, held, lows, highs, back, rows, slots
        )
        return carry

    lax.fori_loop(0, 2, run_back, 0)


def nothing(*_):
    return None


def state_of(tokens, feats):
    return jax.ShapeDtypeStruct((tokens, feats), jnp.bfloat16)


def unit_scratch(pieces):
    units = len(pieces) // 2
    return [pltpu.VMEM((2, units) + pieces[0].shape, jnp.bfloat16), pltpu.SemaphoreType.DMA((2, units))]


def forward_pass(start, moved, goal, scale, straight, meta, rows, slots):
    tokens, feats = start.shape
    blocks = feats // BLK
    stack = jax.ShapeDtypeStruct((2, tokens, feats), jnp.bfloat16)
    held, arrived = unit_scratch(straight)
    scratch = [
        held,
        pltpu.VMEM((blocks, tokens, LANES), jnp.bfloat16),
        pltpu.VMEM((blocks, tokens, LANES), jnp.float32),
        arrived,
    ]
    outs = [state_of(tokens, feats)]
    ins = [start, moved]
    pieces = list(straight)
    if goal is not None:
        ins.append(goal)
        outs = [stack, state_of(tokens, feats)] + outs
        scratch += [
            pltpu.VMEM((blocks, tokens, LANES), jnp.bfloat16),
            pltpu.VMEM((blocks, tokens, LANES), jnp.bfloat16),
            pltpu.VMEM((blocks // 2, tokens, LANES), jnp.float32),
        ]
    return pl.pallas_call(
        functools.partial(forward_kernel, rows, slots, len(straight), None if goal is None else scale),
        in_specs=[IN_SMEM] * 3 + [IN_VMEM] * len(ins) + [IN_HBM] * len(pieces),
        out_specs=[IN_VMEM] * len(outs),
        out_shape=outs,
        scratch_shapes=scratch,
        compiler_params=pltpu.CompilerParams(vmem_limit_bytes=(16 if goal is None else 20) * MIB),
        cost_estimate=about(8 if goal is None else 14),
        name="forward_layers" if goal is None else "turning_layers",
    )(*meta, *ins, *pieces)


def backward_kernel(rows, slots, count, depth, cols, bases, flags, stash, loss_grad, moved, *rest):
    across, rest = rest[:count], rest[count:]
    outs, crossed, lows, highs, back, landed = rest
    if depth == 1:
        first, second = outs.at[1], outs.at[0]
    else:
        first = second = outs
    start_loads_in_order(flags[0], across, crossed, landed, (1,) if depth == 1 else (1, 0))
    choose(flags[2], loss_grad, moved, first)
    wait = functools.partial(wait_load, across, crossed, landed)

    def run_back(layer):
        spread(first, lows, highs)
        role = jnp.abs(layer - flags[0])
        input_grad_layer(
            role, wait, cols, bases, stash.at[layer], first, second, crossed, lows, highs, back, rows, slots
        )

    run_back(1)
    if depth == 2:
        run_back(0)


def backward_pass(stash, loss_grad, moved, across, meta, rows, slots, depth):
    _, tokens, feats = stash.shape
    blocks = feats // BLK
    crossed, landed = unit_scratch(across)
    if depth == 1:
        out = jax.ShapeDtypeStruct((2, tokens, feats), jnp.bfloat16)
    else:
        out = state_of(tokens, feats)
    return pl.pallas_call(
        functools.partial(backward_kernel, rows, slots, len(across), depth),
        in_specs=[IN_SMEM] * 3 + [IN_VMEM] * 3 + [IN_HBM] * len(across),
        out_specs=IN_VMEM,
        out_shape=out,
        scratch_shapes=[
            crossed,
            pltpu.VMEM((blocks, tokens, LANES), jnp.bfloat16),
            pltpu.VMEM((blocks, tokens, LANES), jnp.bfloat16),
            pltpu.VMEM((blocks // 2, tokens, LANES), jnp.float32),
            landed,
        ],
        compiler_params=pltpu.CompilerParams(vmem_limit_bytes=18 * MIB),
        cost_estimate=about(4 * depth),
        name="backward_layers",
    )(*meta, stash, loss_grad, moved, *across)


def join_tokens(sources, joined, arrived, layer):
    copies = []
    begin = 0
    for index, source in enumerate(sources):
        span = pl.ds(begin, source.shape[1])
        copies.append(
            pltpu.make_async_copy(source.at[layer], joined.at[layer, span], arrived.at[layer, index])
        )
        begin += source.shape[1]
    for copy in copies:
        copy.start()
    return copies


def flip_kernel(rows, chosen, bases, *refs):
    *sources, flipped, joined, arrived = refs
    loads = [join_tokens(sources, joined, arrived, layer) for layer in range(2)]
    for load in loads[0] + loads[1]:
        load.wait()

    def run(layer, carry):
        hidden = joined.at[layer]
        inv_rms = inv_rms_of(hidden)
        for unit in range(chosen):

            def visit(step, carry):
                lanes = tile(bases[unit] // 2 + step)
                turned = (hidden[:, lanes].astype(jnp.float32) * inv_rms).T.astype(jnp.bfloat16)
                flipped[layer, unit * rows + 2 * step] = turned[:BLK]
                flipped[layer, unit * rows + 2 * step + 1] = turned[BLK:]
                return carry

            lax.fori_loop(0, rows // 2, visit, 0, unroll=True)
        return carry

    lax.fori_loop(0, 2, run, 0)


def flip_pass(stashes, bases, rows, chosen):
    tokens = sum(stash.shape[1] for stash in stashes)
    feats = stashes[0].shape[2]
    return pl.pallas_call(
        functools.partial(flip_kernel, rows, chosen),
        in_specs=[IN_SMEM] + [IN_HBM] * len(stashes),
        out_specs=IN_VMEM,
        out_shape=jax.ShapeDtypeStruct((2, chosen * rows, BLK, tokens), jnp.bfloat16),
        scratch_shapes=[
            pltpu.VMEM((2, tokens, feats), jnp.bfloat16),
            pltpu.SemaphoreType.DMA((2, len(stashes))),
        ],
        compiler_params=pltpu.CompilerParams(vmem_limit_bytes=12 * MIB),
        cost_estimate=about(4),
        name="flip_rows",
    )(bases, *stashes)


def block_grad_kernel(rows, slots, jobs, units, parts, cols, flags, turned, *rest):
    sources, rest = rest[:parts], rest[parts:]
    total = sum(len(chosen) for _, chosen in jobs)
    outs = rest[:total]
    joined, flipped, lows, highs, arrived, fetched = rest[total:]
    layers = [jnp.abs(role - flags[0]) for role, _ in jobs]
    fetches = []
    begin = 0
    for layer, (_, chosen) in zip(layers, jobs):
        fetches.append(join_tokens(sources, joined, arrived, layer))
        for which, unit in enumerate(chosen):
            copy = pltpu.make_async_copy(
                turned.at[layer, pl.ds(unit * rows, rows)],
                flipped.at[pl.ds((begin + which) * rows, rows)],
                fetched.at[begin + which],
            )
            copy.start()
            fetches[-1].append(copy)
        begin += len(chosen)
    begin = 0
    for turn, (role, chosen) in enumerate(jobs):
        for fetch in fetches[turn]:
            fetch.wait()
        spread(joined.at[layers[turn]], lows, highs)
        block_grad_layer(
            begin * rows, role, cols, flipped, lows, highs, outs[begin:], chosen, units, rows, slots
        )
        begin += len(chosen)


def block_grad_pass(turned, cotangents, meta, rows, slots, jobs):
    tokens = turned.shape[3]
    feats = cotangents[0].shape[2]
    blocks = feats // BLK
    cols, bases, flags = meta
    total = sum(len(chosen) for _, chosen in jobs)
    out = jax.ShapeDtypeStruct((rows * BLK, slots * BLK), jnp.bfloat16)
    return pl.pallas_call(
        functools.partial(block_grad_kernel, rows, slots, jobs, bases.shape[0], len(cotangents)),
        in_specs=[IN_SMEM] * 2 + [IN_HBM] * (1 + len(cotangents)),
        out_specs=[IN_VMEM] * total,
        out_shape=[out] * total,
        scratch_shapes=[
            pltpu.VMEM((2, tokens, feats), jnp.bfloat16),
            pltpu.VMEM((total * rows, BLK, tokens), jnp.bfloat16),
            pltpu.VMEM((blocks, tokens, LANES), jnp.bfloat16),
            pltpu.VMEM((blocks, tokens, LANES), jnp.bfloat16),
            pltpu.SemaphoreType.DMA((2, len(cotangents))),
            pltpu.SemaphoreType.DMA((total,)),
        ],
        compiler_params=pltpu.CompilerParams(vmem_limit_bytes=18 * MIB),
        cost_estimate=about(3 + total // 2),
        name="block_grads",
    )(cols, flags, turned, *cotangents)


def list_kernel(rows, pieces_count, *refs):
    pieces, (listed, tails, arrived) = refs[:pieces_count], refs[pieces_count:]
    copies = [
        pltpu.make_async_copy(piece.at[pl.ds(rows * BLK, TAIL)], tails.at[i], arrived.at[i])
        for i, piece in enumerate(pieces)
    ]
    for copy in copies:
        copy.start()
    for i, copy in enumerate(copies):
        copy.wait()
        line = tails[i].astype(jnp.float32)[:1, : listed.shape[1]]
        listed[i : i + 1] = line.astype(jnp.int32)


def list_pass(pieces, rows, slots):
    count = len(pieces)
    lanes = -(-rows * slots // LANES) * LANES
    return pl.pallas_call(
        functools.partial(list_kernel, rows, count),
        in_specs=[IN_HBM] * count,
        out_specs=IN_VMEM,
        out_shape=jax.ShapeDtypeStruct((count, lanes), jnp.int32),
        scratch_shapes=[
            pltpu.VMEM((count, TAIL, slots * BLK), jnp.bfloat16),
            pltpu.SemaphoreType.DMA((count,)),
        ],
        compiler_params=pltpu.CompilerParams(vmem_limit_bytes=4 * MIB),
        cost_estimate=about(2),
        name="list_columns",
    )(*pieces)


def to_rows(blocks):
    rows, slots, _ = blocks.shape
    split = blocks.reshape(rows, slots, BLK, BLK)
    return split.transpose(0, 2, 1, 3).reshape(rows * BLK, slots * BLK)


def from_rows(matrix, slots):
    rows = matrix.shape[0] // BLK
    split = matrix.reshape(rows, BLK, slots, BLK)
    return split.transpose(0, 2, 1, 3).reshape(rows, slots, BLK * BLK)


def token_cuts(tokens):
    if tokens % 16 or tokens < 32:
        return [(0, tokens)]
    first = -(-tokens // 32) * 16
    return [(0, first), (first, tokens)]


def folded(count):
    return list(range(0, 1)) + list(range(1, count, 2)) + list(range(2, count, 2))[::-1]


def body(inputs, target, blocks, columns, counts):
    stage, stages = lax.axis_index("stage"), lax.axis_size("stage")
    side, sides = lax.axis_index("side"), lax.axis_size("side")
    dp_id, dp_count = lax.axis_index("dp"), lax.axis_size("dp")
    mb_count, tok_local, feats = inputs.shape
    rows, slots = columns.shape[1:]
    loss_scale = (mb_count * tok_local * dp_count) ** (-0.5)
    places = dp_count // 2
    place = dp_id // 2
    core = dp_id % 2
    share = mb_count * tok_local // sides

    around = folded(places)
    ranks = [around.index(spot) for spot in range(places)]
    rank = jnp.array(ranks, jnp.int32)[place]
    hops = [
        (2 * around[i] + half, 2 * around[(i + 1) % places] + half)
        for i in range(places)
        for half in range(2)
    ]

    def ring(array):
        return lax.ppermute(array, "dp", hops)

    def sibling(array):
        return lax.ppermute(array, "dp", [(i, i ^ 1) for i in range(dp_count)])

    def partner(array):
        return lax.ppermute(array, "side", [(i, sides - 1 - i) for i in range(sides)])

    live = jnp.arange(slots, dtype=jnp.int32)[None, :] < counts[0][:, None]
    kept = jnp.where(live[:, :, None], blocks[0], jnp.zeros_like(blocks[0]))
    listed = columns[0].reshape(1, rows * slots).astype(jnp.bfloat16)
    tail = jnp.pad(listed, ((0, TAIL - 1), (0, slots * BLK - rows * slots)))
    own = jnp.concatenate([to_rows(kept), tail], axis=0)

    owns, others, far_owns, far_others = [own], [], [], []
    for slot in range(places):
        moving = {}
        if slot + 1 < places:
            moving["a_own"] = ring(owns[slot])
        moving["b_other"] = partner(owns[slot])
        if slot:
            moving["c_far_other"] = sibling(others[slot - 1])
        moving["d_far_own"] = sibling(owns[slot])
        moving = lax.optimization_barrier(moving)
        others.append(moving["b_other"])
        far_owns.append(moving["d_far_own"])
        if slot + 1 < places:
            owns.append(moving["a_own"])
        if slot:
            far_others.append(moving["c_far_other"])
    far_others.append(sibling(others[-1]))
    own_units, other_units = owns + far_owns, others + far_others
    pieces = [piece for pair in zip(own_units, other_units) for piece in pair]
    cols = list_pass(own_units + other_units, rows, slots)
    turns = jnp.array(around, jnp.int32)[(rank - jnp.arange(places)) % places]
    bases = jnp.concatenate([turns * 2 + core, turns * 2 + 1 - core]).astype(jnp.int32) * rows
    flags = jnp.stack([side, stage == 0, stage == stages - 1]).astype(jnp.int32)
    meta = (cols, bases, flags)

    def my_rows(array):
        flat = array.reshape(mb_count * tok_local, feats)
        return lax.dynamic_slice_in_dim(flat, side * share, share, 0)

    def hop(array, distance):
        route = [(i, i + distance) for i in range(stages) if 0 <= i + distance < stages]
        return lax.ppermute(array, "stage", route)

    cuts = token_cuts(share)
    ways = range(len(cuts))
    whole_start, whole_goal = my_rows(inputs), my_rows(target)
    start = [whole_start[begin:end] for begin, end in cuts]
    goal = [whole_goal[begin:end] for begin, end in cuts]
    moved = list(start)
    for step in range(stages - 1):
        final = [
            forward_pass(start[i], moved[i], None, None, pieces, meta, rows, slots)[0]
            for i in ways
        ]
        moved = [hop(final[i], 1) for i in ways]
    turned = [
        forward_pass(start[i], moved[i], goal[i], loss_scale, pieces, meta, rows, slots)
        for i in ways
    ]
    stashes, loss_grads, result = [list(column) for column in zip(*turned)]
    moved = loss_grads
    for step in range(stages - 1):
        if step:
            result = [
                backward_pass(stashes[i], loss_grads[i], moved[i], pieces, meta, rows, slots, 2)
                for i in ways
            ]
        moved = [hop(result[i], -1) for i in ways]
    flipped = flip_pass(stashes + [sibling(stash) for stash in stashes], bases, rows, places)
    stashes[-1], flipped = lax.optimization_barrier((stashes[-1], flipped))
    cotangents = [
        backward_pass(stashes[i], loss_grads[i], moved[i], pieces, meta, rows, slots, 1) for i in ways
    ]

    order = list(range(1, places)) + [0]

    cotangents = cotangents + [sibling(part) for part in cotangents]
    early, late = order[:1], order[1:]
    (outgoing,) = block_grad_pass(flipped, cotangents, meta, rows, slots, ((1, tuple(early)),))
    cotangents, outgoing = lax.optimization_barrier((cotangents, outgoing))
    jobs = ((1, tuple(late)), (0, tuple(order)))
    grads = block_grad_pass(flipped, cotangents, meta, rows, slots, jobs)
    coming, grads = lax.optimization_barrier((partner(outgoing), grads))
    leaving, staying = grads[: len(late)], grads[len(late) :]
    kept = staying[0]
    travelling = add_rounded(kept, coming)
    for index in range(places - 1):
        kept, outgoing = staying[index + 1], leaving[index]
        passed, coming = lax.optimization_barrier((ring(travelling), partner(outgoing)))
        total = kept.astype(jnp.float32) + coming.astype(jnp.float32) + passed.astype(jnp.float32)
        travelling = total.astype(jnp.bfloat16)
    result = from_rows(travelling, slots)
    return jnp.where(live[:, :, None], result, jnp.zeros_like(result))[None]


def add_rounded(left, right):
    return (left.astype(jnp.float32) + right.astype(jnp.float32)).astype(jnp.bfloat16)


def solution(mesh):
    sections, width = mesh.devices.shape
    split = jax.sharding.Mesh(mesh.devices.reshape(sections // 2, 2, width), ("stage", "side", "dp"))
    section = ("stage", "side")
    return jax.shard_map(
        body,
        mesh=split,
        in_specs=(
            P(None, "dp", None),
            P(None, "dp", None),
            P(section, "dp", None, None),
            P(section, "dp", None),
            P(section, "dp"),
        ),
        out_specs=P(section, "dp", None, None),
        check_vma=False,
    )
```

```python
import functools

import jax
import jax.numpy as jnp
from jax import lax
from jax.experimental import pallas as pl
from jax.experimental.pallas import tpu as pltpu
from jax.sharding import PartitionSpec as P

BLK = 64
LANES = 128
EPSILON = 1e-05
MIB = 1024 * 1024
STEP_ROWS = 8

TAIL = 16

IN_VMEM = pl.BlockSpec(memory_space=pltpu.VMEM)
IN_SMEM = pl.BlockSpec(memory_space=pltpu.SMEM)
IN_HBM = pl.BlockSpec(memory_space=pl.ANY)


def about(microseconds):
    return pl.CostEstimate(
        flops=int(microseconds * 1.1e9), bytes_accessed=1 << 20, transcendentals=0
    )


def step_units(units, rows):
    size = max(1, STEP_ROWS // rows)
    while units % size:
        size -= 1
    return size


def low_half(rows):
    return lax.broadcasted_iota(jnp.int32, (rows, LANES), 1) < BLK


def half_masks(rows):
    lanes = lax.broadcasted_iota(jnp.int32, (rows, LANES), 1)
    low = jnp.where(lanes < BLK, 1.0, 0.0).astype(jnp.bfloat16)
    return low, jnp.where(lanes < BLK, 0.0, 1.0).astype(jnp.bfloat16)


def tile(pair):
    return pl.ds(pl.multiple_of(pair * LANES, LANES), LANES)


def over_pairs(feats, visit, carry):
    return lax.fori_loop(0, feats // LANES, visit, carry, unroll=4)


def inv_rms_from(total, feats):
    return lax.rsqrt(jnp.sum(total, axis=-1, keepdims=True) / feats + EPSILON)


def squares_of(ref):
    tokens, feats = ref.shape

    def visit(pair, total):
        values = ref[:, tile(pair)].astype(jnp.float32)
        return total + values * values

    return over_pairs(feats, visit, jnp.zeros((tokens, LANES), jnp.float32))


def inv_rms_of(ref):
    return inv_rms_from(squares_of(ref), ref.shape[1])


def start_loads(pieces, held, arrived, roles):
    units = held.shape[1]
    for role in roles:
        for unit in range(units):
            pltpu.make_async_copy(
                pieces[2 * unit + role], held.at[role, unit], arrived.at[role, unit]
            ).start()


def start_loads_in_order(side, pieces, held, arrived, layers):
    for value in range(2):
        pl.when(side == value)(
            functools.partial(
                start_loads, pieces, held, arrived, [abs(layer - value) for layer in layers]
            )
        )


def wait_load(pieces, held, arrived, role, unit):
    pltpu.make_async_copy(pieces[0], held.at[role, unit], arrived.at[role, unit]).wait()


def forward_layer(role, wait, cols, bases, current, inv_rms, held, parts, sums, rows, slots):
    tokens, feats = current.shape
    units = held.shape[1]
    per_step = step_units(units, rows)
    low = low_half(tokens)
    keep_low, keep_high = half_masks(tokens)

    def normalise(pair, carry):
        unit_rows = (current[:, tile(pair)].astype(jnp.float32) * inv_rms).astype(jnp.bfloat16)
        parts[2 * pair] = unit_rows * keep_low
        parts[2 * pair + 1] = unit_rows * keep_high
        sums[2 * pair] = jnp.zeros((tokens, LANES), jnp.float32)
        sums[2 * pair + 1] = jnp.zeros((tokens, LANES), jnp.float32)
        return carry

    over_pairs(feats, normalise, 0)

    def run_step(step, carry):
        for inner in range(per_step):
            wait(role, step * per_step + inner)
        items = [(inner, row) for inner in range(per_step) for row in range(0, rows, 2)]

        def product_of(index):
            inner, row = items[index]
            unit = step * per_step + inner
            place = bases[unit] + row
            left = jnp.concatenate([parts[place], parts[place + 1]], axis=0)
            right = held[role, unit, row * BLK : (row + 2) * BLK]
            return jnp.dot(left, right, preferred_element_type=jnp.float32)

        def columns_of(index):
            inner, row = items[index]
            line = role * units + step * per_step + inner
            return [cols[line, row * slots + place] for place in range(2 * slots)]

        upcoming = product_of(0)
        ahead = columns_of(0)
        for index, (inner, row) in enumerate(items):
            product, listed = upcoming, ahead
            if index + 1 < len(items):
                upcoming = product_of(index + 1)
                ahead = columns_of(index + 1)
            for which in range(2):
                for begin in range(0, slots, 4):
                    at = listed[which * slots + begin : which * slots + min(begin + 4, slots)]
                    added = []
                    for offset in range(len(at)):
                        slot = begin + offset
                        lanes = slice((slot // 2) * LANES, (slot // 2 + 1) * LANES)
                        piece = product[which * tokens : (which + 1) * tokens, lanes]
                        piece = jnp.where(low, piece, 0.0) if slot % 2 == 0 else jnp.where(low, 0.0, piece)
                        added.append(sums[at[offset]] + piece)
                    for offset in range(len(at)):
                        sums[at[offset]] = added[offset]
        return carry

    lax.fori_loop(0, units // per_step, run_step, 0)

    def finish(pair, total):
        lanes = tile(pair)
        first, second = sums[2 * pair], sums[2 * pair + 1]
        branch = jnp.where(low, first, second) + pltpu.roll(jnp.where(low, second, first), BLK, 1)
        added = (current[:, lanes].astype(jnp.float32) + branch).astype(jnp.bfloat16)
        current[:, lanes] = added
        widened = added.astype(jnp.float32)
        return total + widened * widened

    return over_pairs(feats, finish, jnp.zeros((tokens, LANES), jnp.float32))


def spread(source, lows, highs):
    tokens, feats = source.shape
    keep_low, keep_high = half_masks(tokens)

    def visit(pair, carry):
        both = source[:, tile(pair)]
        moved = pltpu.roll(both.astype(jnp.float32), BLK, 1).astype(jnp.bfloat16)
        lows[2 * pair] = both * keep_low
        highs[2 * pair] = moved * keep_high
        lows[2 * pair + 1] = moved * keep_low
        highs[2 * pair + 1] = both * keep_high
        return carry

    over_pairs(feats, visit, 0)


def pick_columns(lows, highs, cols, line, flat, slots):
    return jnp.concatenate(
        [
            lows[cols[line, flat + 2 * half]] + highs[cols[line, flat + 2 * half + 1]]
            for half in range(slots // 2)
        ],
        axis=1,
    )


def input_grad_layer(
    role, wait, cols, bases, hidden, inv_rms, cotangent, out, held, lows, highs, back, rows, slots
):
    tokens, feats = cotangent.shape
    units = held.shape[1]
    per_step = step_units(units, rows)
    low = low_half(tokens)

    def run_step(step, carry):
        for inner in range(per_step):
            wait(role, step * per_step + inner)
        items = [(inner, row) for inner in range(per_step) for row in range(0, rows, 2)]

        def picked_at(index):
            inner, row = items[index]
            line = role * units + step * per_step + inner
            return jnp.concatenate(
                [
                    pick_columns(lows, highs, cols, line, (row + which) * slots, slots)
                    for which in range(2)
                ],
                axis=0,
            )

        upcoming = picked_at(0)
        for index, (inner, row) in enumerate(items):
            unit = step * per_step + inner
            picked = upcoming
            if index + 1 < len(items):
                upcoming = picked_at(index + 1)
            result = lax.dot_general(
                picked,
                held[role, unit, row * BLK : (row + 2) * BLK],
                (((1,), (1,)), ((), ())),
                preferred_element_type=jnp.float32,
            )
            place = (bases[unit] + row) // 2
            back[place] = jnp.where(low, result[:tokens], result[tokens:])
        return carry

    lax.fori_loop(0, units // per_step, run_step, 0)

    def correlate(pair, total):
        return total + back[pair] * hidden[:, tile(pair)].astype(jnp.float32)

    total = over_pairs(feats, correlate, jnp.zeros((tokens, LANES), jnp.float32))
    mean = jnp.sum(total, axis=-1, keepdims=True) / feats * inv_rms
    along = inv_rms * inv_rms * mean

    def finish(pair, carry):
        lanes = tile(pair)
        grown = cotangent[:, lanes].astype(jnp.float32) + inv_rms * back[pair]
        out[:, lanes] = (grown - along * hidden[:, lanes].astype(jnp.float32)).astype(jnp.bfloat16)
        return carry

    over_pairs(feats, finish, 0)


def block_grad_layer(begin, role, cols, flipped, lows, highs, out, chosen, units, rows, slots):
    items = [(which, row) for which in range(len(chosen)) for row in range(rows)]

    def operands(index):
        which, row = items[index]
        picked = pick_columns(lows, highs, cols, role * units + chosen[which], row * slots, slots)
        return flipped[begin + which * rows + row], picked

    upcoming = operands(0)
    for index, (which, row) in enumerate(items):
        left, right = upcoming
        if index + 1 < len(items):
            upcoming = operands(index + 1)
        result = jnp.dot(left, right, preferred_element_type=jnp.float32)
        out[which][row * BLK : (row + 1) * BLK] = result.astype(jnp.bfloat16)


def choose(flag, first, second, target):
    @pl.when(flag == 1)
    def _():
        target[...] = first[...]

    @pl.when(flag != 1)
    def _():
        target[...] = second[...]


def forward_kernel(rows, slots, count, scale, cols, bases, flags, *rest):
    turning = scale is not None
    start, moved = rest[:2]
    rest = rest[2:]
    if turning:
        goal, rest = rest[0], rest[1:]
    straight, rest = rest[:count], rest[count:]
    if turning:
        stash, loss_grad, final, held, parts, sums, arrived, lows, highs, back, scales = rest
    else:
        final, held, parts, sums, arrived = rest
    start_loads_in_order(flags[0], straight, held, arrived, (0, 1))
    choose(flags[1], start, moved, final)
    wait = functools.partial(wait_load, straight, held, arrived)

    tokens, feats = final.shape

    def run_forward(layer, total):
        inv_rms = inv_rms_from(total, feats)
        if turning:
            stash[layer] = final[...]
            scales[layer] = jnp.broadcast_to(inv_rms, (tokens, LANES))
        role = jnp.abs(layer - flags[0])
        return forward_layer(
            role, wait, cols, bases, final, inv_rms, held, parts, sums, rows, slots
        )

    lax.fori_loop(0, 2, run_forward, squares_of(final))
    if not turning:
        return

    def residue(pair, carry):
        lanes = tile(pair)
        gap = final[:, lanes].astype(jnp.float32) - goal[:, lanes].astype(jnp.float32)
        loss_grad[:, lanes] = (gap * scale).astype(jnp.bfloat16)
        return carry

    over_pairs(feats, residue, 0)
    final[...] = loss_grad[...]
    def run_back(turn, carry):
        layer = 1 - turn
        role = jnp.abs(layer - flags[0])
        hidden = stash.at[layer]
        spread(final, lows, highs)
        input_grad_layer(
            role,
            nothing,
            cols,
            bases,
            hidden,
            scales[layer][:, :1],
            final,
            final,
            held,
            lows,
            highs,
            back,
            rows,
            slots,
        )
        return carry

    lax.fori_loop(0, 2, run_back, 0)


def nothing(*_):
    return None


def state_of(tokens, feats):
    return jax.ShapeDtypeStruct((tokens, feats), jnp.bfloat16)


def unit_scratch(pieces):
    units = len(pieces) // 2
    return [pltpu.VMEM((2, units) + pieces[0].shape, jnp.bfloat16), pltpu.SemaphoreType.DMA((2, units))]


def forward_pass(start, moved, goal, scale, straight, meta, rows, slots):
    tokens, feats = start.shape
    blocks = feats // BLK
    stack = jax.ShapeDtypeStruct((2, tokens, feats), jnp.bfloat16)
    held, arrived = unit_scratch(straight)
    scratch = [
        held,
        pltpu.VMEM((blocks, tokens, LANES), jnp.bfloat16),
        pltpu.VMEM((blocks, tokens, LANES), jnp.float32),
        arrived,
    ]
    outs = [state_of(tokens, feats)]
    ins = [start, moved]
    pieces = list(straight)
    if goal is not None:
        ins.append(goal)
        outs = [stack, state_of(tokens, feats)] + outs
        scratch += [
            pltpu.VMEM((blocks, tokens, LANES), jnp.bfloat16),
            pltpu.VMEM((blocks, tokens, LANES), jnp.bfloat16),
            pltpu.VMEM((blocks // 2, tokens, LANES), jnp.float32),
            pltpu.VMEM((2, tokens, LANES), jnp.float32),
        ]
    return pl.pallas_call(
        functools.partial(forward_kernel, rows, slots, len(straight), None if goal is None else scale),
        in_specs=[IN_SMEM] * 3 + [IN_VMEM] * len(ins) + [IN_HBM] * len(pieces),
        out_specs=[IN_VMEM] * len(outs),
        out_shape=outs,
        scratch_shapes=scratch,
        compiler_params=pltpu.CompilerParams(vmem_limit_bytes=(16 if goal is None else 20) * MIB),
        cost_estimate=about(8 if goal is None else 14),
        name="forward_layers" if goal is None else "turning_layers",
    )(*meta, *ins, *pieces)


def backward_kernel(rows, slots, count, depth, cols, bases, flags, stash, loss_grad, moved, *rest):
    across, rest = rest[:count], rest[count:]
    outs, crossed, lows, highs, back, landed = rest
    if depth == 1:
        first, second = outs.at[1], outs.at[0]
    else:
        first = second = outs
    start_loads_in_order(flags[0], across, crossed, landed, (1,) if depth == 1 else (1, 0))
    choose(flags[2], loss_grad, moved, first)
    wait = functools.partial(wait_load, across, crossed, landed)

    def run_back(layer):
        spread(first, lows, highs)
        role = jnp.abs(layer - flags[0])
        input_grad_layer(
            role,
            wait,
            cols,
            bases,
            stash.at[layer],
            inv_rms_of(stash.at[layer]),
            first,
            second,
            crossed,
            lows,
            highs,
            back,
            rows,
            slots,
        )

    run_back(1)
    if depth == 2:
        run_back(0)


def backward_pass(stash, loss_grad, moved, across, meta, rows, slots, depth):
    _, tokens, feats = stash.shape
    blocks = feats // BLK
    crossed, landed = unit_scratch(across)
    if depth == 1:
        out = jax.ShapeDtypeStruct((2, tokens, feats), jnp.bfloat16)
    else:
        out = state_of(tokens, feats)
    return pl.pallas_call(
        functools.partial(backward_kernel, rows, slots, len(across), depth),
        in_specs=[IN_SMEM] * 3 + [IN_VMEM] * 3 + [IN_HBM] * len(across),
        out_specs=IN_VMEM,
        out_shape=out,
        scratch_shapes=[
            crossed,
            pltpu.VMEM((blocks, tokens, LANES), jnp.bfloat16),
            pltpu.VMEM((blocks, tokens, LANES), jnp.bfloat16),
            pltpu.VMEM((blocks // 2, tokens, LANES), jnp.float32),
            landed,
        ],
        compiler_params=pltpu.CompilerParams(vmem_limit_bytes=18 * MIB),
        cost_estimate=about(4 * depth),
        name="backward_layers",
    )(*meta, stash, loss_grad, moved, *across)


def join_tokens(sources, joined, arrived, layer):
    copies = []
    begin = 0
    for index, source in enumerate(sources):
        span = pl.ds(begin, source.shape[1])
        copies.append(
            pltpu.make_async_copy(source.at[layer], joined.at[layer, span], arrived.at[layer, index])
        )
        begin += source.shape[1]
    for copy in copies:
        copy.start()
    return copies


def flip_kernel(rows, chosen, bases, *refs):
    *sources, flipped, joined, arrived = refs
    loads = [join_tokens(sources, joined, arrived, layer) for layer in range(2)]
    for load in loads[0] + loads[1]:
        load.wait()

    def run(layer, carry):
        hidden = joined.at[layer]
        inv_rms = inv_rms_of(hidden)
        for unit in range(chosen):

            def visit(step, carry):
                lanes = tile(bases[unit] // 2 + step)
                turned = (hidden[:, lanes].astype(jnp.float32) * inv_rms).T.astype(jnp.bfloat16)
                flipped[layer, unit * rows + 2 * step] = turned[:BLK]
                flipped[layer, unit * rows + 2 * step + 1] = turned[BLK:]
                return carry

            lax.fori_loop(0, rows // 2, visit, 0, unroll=True)
        return carry

    lax.fori_loop(0, 2, run, 0)


def flip_pass(stashes, bases, rows, chosen):
    tokens = sum(stash.shape[1] for stash in stashes)
    feats = stashes[0].shape[2]
    return pl.pallas_call(
        functools.partial(flip_kernel, rows, chosen),
        in_specs=[IN_SMEM] + [IN_HBM] * len(stashes),
        out_specs=IN_VMEM,
        out_shape=jax.ShapeDtypeStruct((2, chosen * rows, BLK, tokens), jnp.bfloat16),
        scratch_shapes=[
            pltpu.VMEM((2, tokens, feats), jnp.bfloat16),
            pltpu.SemaphoreType.DMA((2, len(stashes))),
        ],
        compiler_params=pltpu.CompilerParams(vmem_limit_bytes=12 * MIB),
        cost_estimate=about(4),
        name="flip_rows",
    )(bases, *stashes)


def block_grad_kernel(rows, slots, jobs, units, parts, cols, flags, turned, *rest):
    sources, rest = rest[:parts], rest[parts:]
    total = sum(len(chosen) for _, chosen in jobs)
    outs = rest[:total]
    joined, flipped, lows, highs, arrived, fetched = rest[total:]
    layers = [jnp.abs(role - flags[0]) for role, _ in jobs]
    fetches = []
    begin = 0
    for layer, (_, chosen) in zip(layers, jobs):
        fetches.append(join_tokens(sources, joined, arrived, layer))
        for which, unit in enumerate(chosen):
            copy = pltpu.make_async_copy(
                turned.at[layer, pl.ds(unit * rows, rows)],
                flipped.at[pl.ds((begin + which) * rows, rows)],
                fetched.at[begin + which],
            )
            copy.start()
            fetches[-1].append(copy)
        begin += len(chosen)
    begin = 0
    for turn, (role, chosen) in enumerate(jobs):
        for fetch in fetches[turn]:
            fetch.wait()
        spread(joined.at[layers[turn]], lows, highs)
        block_grad_layer(
            begin * rows, role, cols, flipped, lows, highs, outs[begin:], chosen, units, rows, slots
        )
        begin += len(chosen)


def block_grad_pass(turned, cotangents, meta, rows, slots, jobs):
    tokens = turned.shape[3]
    feats = cotangents[0].shape[2]
    blocks = feats // BLK
    cols, bases, flags = meta
    total = sum(len(chosen) for _, chosen in jobs)
    out = jax.ShapeDtypeStruct((rows * BLK, slots * BLK), jnp.bfloat16)
    return pl.pallas_call(
        functools.partial(block_grad_kernel, rows, slots, jobs, bases.shape[0], len(cotangents)),
        in_specs=[IN_SMEM] * 2 + [IN_HBM] * (1 + len(cotangents)),
        out_specs=[IN_VMEM] * total,
        out_shape=[out] * total,
        scratch_shapes=[
            pltpu.VMEM((2, tokens, feats), jnp.bfloat16),
            pltpu.VMEM((total * rows, BLK, tokens), jnp.bfloat16),
            pltpu.VMEM((blocks, tokens, LANES), jnp.bfloat16),
            pltpu.VMEM((blocks, tokens, LANES), jnp.bfloat16),
            pltpu.SemaphoreType.DMA((2, len(cotangents))),
            pltpu.SemaphoreType.DMA((total,)),
        ],
        compiler_params=pltpu.CompilerParams(vmem_limit_bytes=18 * MIB),
        cost_estimate=about(3 + total // 2),
        name="block_grads",
    )(cols, flags, turned, *cotangents)


def list_kernel(rows, pieces_count, *refs):
    pieces, (listed, tails, arrived) = refs[:pieces_count], refs[pieces_count:]
    copies = [
        pltpu.make_async_copy(piece.at[pl.ds(rows * BLK, TAIL)], tails.at[i], arrived.at[i])
        for i, piece in enumerate(pieces)
    ]
    for copy in copies:
        copy.start()
    for i, copy in enumerate(copies):
        copy.wait()
        line = tails[i].astype(jnp.float32)[:1, : listed.shape[1]]
        listed[i : i + 1] = line.astype(jnp.int32)


def list_pass(pieces, rows, slots):
    count = len(pieces)
    lanes = -(-rows * slots // LANES) * LANES
    return pl.pallas_call(
        functools.partial(list_kernel, rows, count),
        in_specs=[IN_HBM] * count,
        out_specs=IN_VMEM,
        out_shape=jax.ShapeDtypeStruct((count, lanes), jnp.int32),
        scratch_shapes=[
            pltpu.VMEM((count, TAIL, slots * BLK), jnp.bfloat16),
            pltpu.SemaphoreType.DMA((count,)),
        ],
        compiler_params=pltpu.CompilerParams(vmem_limit_bytes=4 * MIB),
        cost_estimate=about(2),
        name="list_columns",
    )(*pieces)


def to_rows(blocks):
    rows, slots, _ = blocks.shape
    split = blocks.reshape(rows, slots, BLK, BLK)
    return split.transpose(0, 2, 1, 3).reshape(rows * BLK, slots * BLK)


def from_rows(matrix, slots):
    rows = matrix.shape[0] // BLK
    split = matrix.reshape(rows, BLK, slots, BLK)
    return split.transpose(0, 2, 1, 3).reshape(rows, slots, BLK * BLK)


def token_cuts(tokens):
    if tokens % 16 or tokens < 32:
        return [(0, tokens)]
    first = -(-tokens // 32) * 16
    return [(0, first), (first, tokens)]


def folded(count):
    return list(range(0, 1)) + list(range(1, count, 2)) + list(range(2, count, 2))[::-1]


def body(inputs, target, blocks, columns, counts):
    stage, stages = lax.axis_index("stage"), lax.axis_size("stage")
    side, sides = lax.axis_index("side"), lax.axis_size("side")
    dp_id, dp_count = lax.axis_index("dp"), lax.axis_size("dp")
    mb_count, tok_local, feats = inputs.shape
    rows, slots = columns.shape[1:]
    loss_scale = (mb_count * tok_local * dp_count) ** (-0.5)
    places = dp_count // 2
    place = dp_id // 2
    core = dp_id % 2
    share = mb_count * tok_local // sides

    around = folded(places)
    ranks = [around.index(spot) for spot in range(places)]
    rank = jnp.array(ranks, jnp.int32)[place]
    hops = [
        (2 * around[i] + half, 2 * around[(i + 1) % places] + half)
        for i in range(places)
        for half in range(2)
    ]

    def ring(array):
        return lax.ppermute(array, "dp", hops)

    def sibling(array):
        return lax.ppermute(array, "dp", [(i, i ^ 1) for i in range(dp_count)])

    def partner(array):
        return lax.ppermute(array, "side", [(i, sides - 1 - i) for i in range(sides)])

    slot_of = lax.broadcasted_iota(jnp.int32, (rows, BLK, slots * BLK), 2) // BLK
    live = (slot_of < counts[0][:, None, None]).reshape(rows * BLK, slots * BLK)
    listed = columns[0].reshape(1, rows * slots).astype(jnp.bfloat16)
    tail = jnp.pad(listed, ((0, TAIL - 1), (0, slots * BLK - rows * slots)))
    straight = to_rows(blocks[0])
    own = jnp.concatenate([jnp.where(live, straight, jnp.zeros_like(straight)), tail], axis=0)

    owns, others, far_owns, far_others = [own], [], [], []
    for slot in range(places):
        moving = {}
        if slot + 1 < places:
            moving["a_own"] = ring(owns[slot])
        moving["b_other"] = partner(owns[slot])
        if slot:
            moving["c_far_other"] = sibling(others[slot - 1])
        moving["d_far_own"] = sibling(owns[slot])
        moving = lax.optimization_barrier(moving)
        others.append(moving["b_other"])
        far_owns.append(moving["d_far_own"])
        if slot + 1 < places:
            owns.append(moving["a_own"])
        if slot:
            far_others.append(moving["c_far_other"])
    far_others.append(sibling(others[-1]))
    own_units, other_units = owns + far_owns, others + far_others
    pieces = [piece for pair in zip(own_units, other_units) for piece in pair]
    cols = list_pass(own_units + other_units, rows, slots)
    turns = jnp.array(around, jnp.int32)[(rank - jnp.arange(places)) % places]
    bases = jnp.concatenate([turns * 2 + core, turns * 2 + 1 - core]).astype(jnp.int32) * rows
    flags = jnp.stack([side, stage == 0, stage == stages - 1]).astype(jnp.int32)
    meta = (cols, bases, flags)

    def my_rows(array):
        flat = array.reshape(mb_count * tok_local, feats)
        return lax.dynamic_slice_in_dim(flat, side * share, share, 0)

    def hop(array, distance):
        route = [(i, i + distance) for i in range(stages) if 0 <= i + distance < stages]
        return lax.ppermute(array, "stage", route)

    cuts = token_cuts(share)
    ways = range(len(cuts))
    whole_start, whole_goal = my_rows(inputs), my_rows(target)
    start = [whole_start[begin:end] for begin, end in cuts]
    goal = [whole_goal[begin:end] for begin, end in cuts]
    moved = list(start)
    for step in range(stages - 1):
        final = [
            forward_pass(start[i], moved[i], None, None, pieces, meta, rows, slots)[0]
            for i in ways
        ]
        moved = [hop(final[i], 1) for i in ways]
    turned = [
        forward_pass(start[i], moved[i], goal[i], loss_scale, pieces, meta, rows, slots)
        for i in ways
    ]
    stashes, loss_grads, result = [list(column) for column in zip(*turned)]
    moved = loss_grads
    for step in range(stages - 1):
        if step:
            result = [
                backward_pass(stashes[i], loss_grads[i], moved[i], pieces, meta, rows, slots, 2)
                for i in ways
            ]
        moved = [hop(result[i], -1) for i in ways]
    flipped = flip_pass(stashes + [sibling(stash) for stash in stashes], bases, rows, places)
    stashes[-1], flipped = lax.optimization_barrier((stashes[-1], flipped))
    cotangents = [
        backward_pass(stashes[i], loss_grads[i], moved[i], pieces, meta, rows, slots, 1) for i in ways
    ]

    order = list(range(1, places)) + [0]

    cotangents = cotangents + [sibling(part) for part in cotangents]
    early, late = order[:1], order[1:]
    (outgoing,) = block_grad_pass(flipped, cotangents, meta, rows, slots, ((1, tuple(early)),))
    cotangents, outgoing = lax.optimization_barrier((cotangents, outgoing))
    jobs = ((1, tuple(late)), (0, tuple(order)))
    grads = block_grad_pass(flipped, cotangents, meta, rows, slots, jobs)
    coming, grads = lax.optimization_barrier((partner(outgoing), grads))
    leaving, staying = grads[: len(late)], grads[len(late) :]
    kept = staying[0]
    travelling = add_rounded(kept, coming)
    for index in range(places - 1):
        kept, outgoing = staying[index + 1], leaving[index]
        passed, coming, leaving = lax.optimization_barrier(
            (ring(travelling), partner(outgoing), leaving)
        )
        total = kept.astype(jnp.float32) + coming.astype(jnp.float32) + passed.astype(jnp.float32)
        travelling = total.astype(jnp.bfloat16)
    travelling = jnp.where(live, travelling, jnp.zeros_like(travelling))
    return from_rows(travelling, slots)[None]


def add_rounded(left, right):
    return (left.astype(jnp.float32) + right.astype(jnp.float32)).astype(jnp.bfloat16)


def solution(mesh):
    sections, width = mesh.devices.shape
    split = jax.sharding.Mesh(mesh.devices.reshape(sections // 2, 2, width), ("stage", "side", "dp"))
    section = ("stage", "side")
    return jax.shard_map(
        body,
        mesh=split,
        in_specs=(
            P(None, "dp", None),
            P(None, "dp", None),
            P(section, "dp", None, None),
            P(section, "dp", None),
            P(section, "dp"),
        ),
        out_specs=P(section, "dp", None, None),
        check_vma=False,
    )
```

```python
import functools

import jax
import jax.numpy as jnp
from jax import lax
from jax.experimental import pallas as pl
from jax.experimental.pallas import tpu as pltpu
from jax.sharding import PartitionSpec as P

BLK = 64
LANES = 128
EPSILON = 1e-05
MIB = 1024 * 1024
STEP_ROWS = 8

TAIL = 16

IN_VMEM = pl.BlockSpec(memory_space=pltpu.VMEM)
IN_SMEM = pl.BlockSpec(memory_space=pltpu.SMEM)
IN_HBM = pl.BlockSpec(memory_space=pl.ANY)


def about(microseconds):
    return pl.CostEstimate(
        flops=int(microseconds * 1.1e9), bytes_accessed=1 << 20, transcendentals=0
    )


def step_units(units, rows):
    size = max(1, STEP_ROWS // rows)
    while units % size:
        size -= 1
    return size


def low_half(rows):
    return lax.broadcasted_iota(jnp.int32, (rows, LANES), 1) < BLK


def tile(pair):
    return pl.ds(pl.multiple_of(pair * LANES, LANES), LANES)


def over_pairs(feats, visit, carry):
    return lax.fori_loop(0, feats // LANES, visit, carry, unroll=4)


def inv_rms_of(ref):
    tokens, feats = ref.shape

    def visit(pair, total):
        values = ref[:, tile(pair)].astype(jnp.float32)
        return total + values * values

    total = over_pairs(feats, visit, jnp.zeros((tokens, LANES), jnp.float32))
    return lax.rsqrt(jnp.sum(total, axis=-1, keepdims=True) / feats + EPSILON)


def start_loads(pieces, held, arrived, roles, layout):
    for role in roles:
        for unit, parts in enumerate(layout[role]):
            for index, begin in parts:
                piece = pieces[index]
                pltpu.make_async_copy(
                    piece,
                    held.at[role, unit, pl.ds(begin, piece.shape[0])],
                    arrived.at[role, unit],
                ).start()


def start_loads_in_order(side, pieces, held, arrived, layers, layout):
    for value in range(2):
        pl.when(side == value)(
            functools.partial(
                start_loads, pieces, held, arrived, [abs(layer - value) for layer in layers], layout
            )
        )


def wait_load(held, arrived, role, unit):
    whole = held.at[role, unit]
    pltpu.make_async_copy(whole, whole, arrived.at[role, unit]).wait()


def forward_layer(role, wait, cols, bases, current, held, parts, sums, rows, slots):
    tokens, feats = current.shape
    units = held.shape[1]
    per_step = step_units(units, rows)
    low = low_half(tokens)
    inv_rms = inv_rms_of(current)

    def normalise(pair, carry):
        lanes = tile(pair)
        unit_rows = current[:, lanes].astype(jnp.float32) * inv_rms
        parts[2 * pair] = jnp.where(low, unit_rows, 0.0).astype(jnp.bfloat16)
        parts[2 * pair + 1] = jnp.where(low, 0.0, unit_rows).astype(jnp.bfloat16)
        sums[2 * pair] = jnp.zeros((tokens, LANES), jnp.float32)
        sums[2 * pair + 1] = jnp.zeros((tokens, LANES), jnp.float32)
        return carry

    over_pairs(feats, normalise, 0)

    def run_step(step, carry):
        for inner in range(per_step):
            wait(role, step * per_step + inner)
        items = [(inner, row) for inner in range(per_step) for row in range(0, rows, 2)]

        def product_of(index):
            inner, row = items[index]
            unit = step * per_step + inner
            place = bases[unit] + row
            left = jnp.concatenate([parts[place], parts[place + 1]], axis=0)
            right = held[role, unit, row * BLK : (row + 2) * BLK]
            return jnp.dot(left, right, preferred_element_type=jnp.float32)

        def columns_of(index):
            inner, row = items[index]
            line = role * units + step * per_step + inner
            return [cols[line, row * slots + place] for place in range(2 * slots)]

        upcoming = product_of(0)
        ahead = columns_of(0)
        for index, (inner, row) in enumerate(items):
            product, listed = upcoming, ahead
            if index + 1 < len(items):
                upcoming = product_of(index + 1)
                ahead = columns_of(index + 1)
            for which in range(2):
                for begin in range(0, slots, 4):
                    at = listed[which * slots + begin : which * slots + min(begin + 4, slots)]
                    added = []
                    for offset in range(len(at)):
                        slot = begin + offset
                        lanes = slice((slot // 2) * LANES, (slot // 2 + 1) * LANES)
                        piece = product[which * tokens : (which + 1) * tokens, lanes]
                        piece = jnp.where(low, piece, 0.0) if slot % 2 == 0 else jnp.where(low, 0.0, piece)
                        added.append(sums[at[offset]] + piece)
                    for offset in range(len(at)):
                        sums[at[offset]] = added[offset]
        return carry

    lax.fori_loop(0, units // per_step, run_step, 0)

    def finish(pair, carry):
        lanes = tile(pair)
        first, second = sums[2 * pair], sums[2 * pair + 1]
        branch = jnp.where(low, first, second) + pltpu.roll(jnp.where(low, second, first), BLK, 1)
        current[:, lanes] = (current[:, lanes].astype(jnp.float32) + branch).astype(jnp.bfloat16)
        return carry

    over_pairs(feats, finish, 0)


def spread(source, lows, highs):
    tokens, feats = source.shape
    low = low_half(tokens)

    def visit(pair, carry):
        both = source[:, tile(pair)].astype(jnp.float32)
        moved = pltpu.roll(both, BLK, 1)
        lows[2 * pair] = jnp.where(low, both, 0.0).astype(jnp.bfloat16)
        highs[2 * pair] = jnp.where(low, 0.0, moved).astype(jnp.bfloat16)
        lows[2 * pair + 1] = jnp.where(low, moved, 0.0).astype(jnp.bfloat16)
        highs[2 * pair + 1] = jnp.where(low, 0.0, both).astype(jnp.bfloat16)
        return carry

    over_pairs(feats, visit, 0)


def pick_columns(lows, highs, cols, line, flat, slots):
    return jnp.concatenate(
        [
            lows[cols[line, flat + 2 * half]] + highs[cols[line, flat + 2 * half + 1]]
            for half in range(slots // 2)
        ],
        axis=1,
    )


def input_grad_layer(role, wait, cols, bases, hidden, cotangent, out, held, lows, highs, back, rows, slots):
    tokens, feats = cotangent.shape
    units = held.shape[1]
    per_step = step_units(units, rows)
    low = low_half(tokens)

    def run_step(step, carry):
        for inner in range(per_step):
            wait(role, step * per_step + inner)
        items = [(inner, row) for inner in range(per_step) for row in range(0, rows, 2)]

        def picked_at(index):
            inner, row = items[index]
            line = role * units + step * per_step + inner
            return jnp.concatenate(
                [
                    pick_columns(lows, highs, cols, line, (row + which) * slots, slots)
                    for which in range(2)
                ],
                axis=0,
            )

        upcoming = picked_at(0)
        for index, (inner, row) in enumerate(items):
            unit = step * per_step + inner
            picked = upcoming
            if index + 1 < len(items):
                upcoming = picked_at(index + 1)
            result = lax.dot_general(
                picked,
                held[role, unit, row * BLK : (row + 2) * BLK],
                (((1,), (1,)), ((), ())),
                preferred_element_type=jnp.float32,
            )
            place = (bases[unit] + row) // 2
            back[place] = jnp.where(low, result[:tokens], result[tokens:])
        return carry

    lax.fori_loop(0, units // per_step, run_step, 0)
    inv_rms = inv_rms_of(hidden)

    def correlate(pair, total):
        unit_rows = hidden[:, tile(pair)].astype(jnp.float32) * inv_rms
        return total + back[pair] * unit_rows

    total = over_pairs(feats, correlate, jnp.zeros((tokens, LANES), jnp.float32))
    mean = jnp.sum(total, axis=-1, keepdims=True) / feats

    def finish(pair, carry):
        lanes = tile(pair)
        unit_rows = hidden[:, lanes].astype(jnp.float32) * inv_rms
        centred = back[pair] - unit_rows * mean
        out[:, lanes] = (cotangent[:, lanes].astype(jnp.float32) + inv_rms * centred).astype(jnp.bfloat16)
        return carry

    over_pairs(feats, finish, 0)


def block_grad_layer(begin, role, cols, flipped, lows, highs, out, chosen, units, rows, slots):
    items = [(which, row) for which in range(len(chosen)) for row in range(rows)]

    def operands(index):
        which, row = items[index]
        picked = pick_columns(lows, highs, cols, role * units + chosen[which], row * slots, slots)
        return flipped[begin + which * rows + row], picked

    upcoming = operands(0)
    for index, (which, row) in enumerate(items):
        left, right = upcoming
        if index + 1 < len(items):
            upcoming = operands(index + 1)
        result = jnp.dot(left, right, preferred_element_type=jnp.float32).astype(jnp.bfloat16)
        target = out[which]
        if isinstance(target, tuple):
            target, row = target[row // (rows // 2)], row % (rows // 2)
        target[row * BLK : (row + 1) * BLK] = result


def choose(flag, first, second, target):
    @pl.when(flag == 1)
    def _():
        target[...] = first[...]

    @pl.when(flag != 1)
    def _():
        target[...] = second[...]


def forward_kernel(rows, slots, count, layout, scale, cols, bases, flags, *rest):
    turning = scale is not None
    start, moved = rest[:2]
    rest = rest[2:]
    if turning:
        goal, rest = rest[0], rest[1:]
    straight, rest = rest[:count], rest[count:]
    if turning:
        stash, loss_grad, final, held, parts, sums, arrived, lows, highs, back = rest
    else:
        final, held, parts, sums, arrived = rest
    start_loads_in_order(flags[0], straight, held, arrived, (0, 1), layout)
    choose(flags[1], start, moved, final)
    wait = functools.partial(wait_load, held, arrived)

    def run_forward(layer, carry):
        if turning:
            stash[layer] = final[...]
        role = jnp.abs(layer - flags[0])
        forward_layer(role, wait, cols, bases, final, held, parts, sums, rows, slots)
        return carry

    lax.fori_loop(0, 2, run_forward, 0)
    if not turning:
        return
    tokens, feats = final.shape

    def residue(pair, carry):
        lanes = tile(pair)
        gap = final[:, lanes].astype(jnp.float32) - goal[:, lanes].astype(jnp.float32)
        loss_grad[:, lanes] = (gap * scale).astype(jnp.bfloat16)
        return carry

    over_pairs(feats, residue, 0)
    final[...] = loss_grad[...]
    def run_back(turn, carry):
        layer = 1 - turn
        role = jnp.abs(layer - flags[0])
        hidden = stash.at[layer]
        spread(final, lows, highs)
        input_grad_layer(
            role, nothing, cols, bases, hidden, final, final, held, lows, highs, back, rows, slots
        )
        return carry

    lax.fori_loop(0, 2, run_back, 0)


def nothing(*_):
    return None


def state_of(tokens, feats):
    return jax.ShapeDtypeStruct((tokens, feats), jnp.bfloat16)


def unit_scratch(layout, rows, slots):
    units = len(layout[0])
    shape = (2, units, rows * BLK + TAIL, slots * BLK)
    return [pltpu.VMEM(shape, jnp.bfloat16), pltpu.SemaphoreType.DMA((2, units))]


def forward_pass(start, moved, goal, scale, weights, meta, rows, slots):
    straight, layout = weights
    tokens, feats = start.shape
    blocks = feats // BLK
    stack = jax.ShapeDtypeStruct((2, tokens, feats), jnp.bfloat16)
    held, arrived = unit_scratch(layout, rows, slots)
    scratch = [
        held,
        pltpu.VMEM((blocks, tokens, LANES), jnp.bfloat16),
        pltpu.VMEM((blocks, tokens, LANES), jnp.float32),
        arrived,
    ]
    outs = [state_of(tokens, feats)]
    ins = [start, moved]
    pieces = list(straight)
    if goal is not None:
        ins.append(goal)
        outs = [stack, state_of(tokens, feats)] + outs
        scratch += [
            pltpu.VMEM((blocks, tokens, LANES), jnp.bfloat16),
            pltpu.VMEM((blocks, tokens, LANES), jnp.bfloat16),
            pltpu.VMEM((blocks // 2, tokens, LANES), jnp.float32),
        ]
    return pl.pallas_call(
        functools.partial(
            forward_kernel, rows, slots, len(straight), layout, None if goal is None else scale
        ),
        in_specs=[IN_SMEM] * 3 + [IN_VMEM] * len(ins) + [IN_HBM] * len(pieces),
        out_specs=[IN_VMEM] * len(outs),
        out_shape=outs,
        scratch_shapes=scratch,
        compiler_params=pltpu.CompilerParams(vmem_limit_bytes=(16 if goal is None else 20) * MIB),
        cost_estimate=about(8 if goal is None else 14),
        name="forward_layers" if goal is None else "turning_layers",
    )(*meta, *ins, *pieces)


def backward_kernel(rows, slots, count, layout, depth, cols, bases, flags, stash, loss_grad, moved, *rest):
    across, rest = rest[:count], rest[count:]
    outs, crossed, lows, highs, back, landed = rest
    if depth == 1:
        first, second = outs.at[1], outs.at[0]
    else:
        first = second = outs
    order = (1,) if depth == 1 else (1, 0)
    start_loads_in_order(flags[0], across, crossed, landed, order, layout)
    choose(flags[2], loss_grad, moved, first)
    wait = functools.partial(wait_load, crossed, landed)

    def run_back(layer):
        spread(first, lows, highs)
        role = jnp.abs(layer - flags[0])
        input_grad_layer(
            role, wait, cols, bases, stash.at[layer], first, second, crossed, lows, highs, back, rows, slots
        )

    run_back(1)
    if depth == 2:
        run_back(0)


def backward_pass(stash, loss_grad, moved, weights, meta, rows, slots, depth):
    across, layout = weights
    _, tokens, feats = stash.shape
    blocks = feats // BLK
    crossed, landed = unit_scratch(layout, rows, slots)
    if depth == 1:
        out = jax.ShapeDtypeStruct((2, tokens, feats), jnp.bfloat16)
    else:
        out = state_of(tokens, feats)
    return pl.pallas_call(
        functools.partial(backward_kernel, rows, slots, len(across), layout, depth),
        in_specs=[IN_SMEM] * 3 + [IN_VMEM] * 3 + [IN_HBM] * len(across),
        out_specs=IN_VMEM,
        out_shape=out,
        scratch_shapes=[
            crossed,
            pltpu.VMEM((blocks, tokens, LANES), jnp.bfloat16),
            pltpu.VMEM((blocks, tokens, LANES), jnp.bfloat16),
            pltpu.VMEM((blocks // 2, tokens, LANES), jnp.float32),
            landed,
        ],
        compiler_params=pltpu.CompilerParams(vmem_limit_bytes=18 * MIB),
        cost_estimate=about(4 * depth),
        name="backward_layers",
    )(*meta, stash, loss_grad, moved, *across)


def join_tokens(sources, joined, arrived, layer):
    copies = []
    begin = 0
    for index, source in enumerate(sources):
        span = pl.ds(begin, source.shape[1])
        copies.append(
            pltpu.make_async_copy(source.at[layer], joined.at[layer, span], arrived.at[layer, index])
        )
        begin += source.shape[1]
    for copy in copies:
        copy.start()
    return copies


def flip_kernel(rows, chosen, bases, *refs):
    *sources, flipped, joined, arrived = refs
    loads = [join_tokens(sources, joined, arrived, layer) for layer in range(2)]
    for load in loads[0] + loads[1]:
        load.wait()

    def run(layer, carry):
        hidden = joined.at[layer]
        inv_rms = inv_rms_of(hidden)
        for unit in range(chosen):

            def visit(step, carry):
                lanes = tile(bases[unit] // 2 + step)
                turned = (hidden[:, lanes].astype(jnp.float32) * inv_rms).T.astype(jnp.bfloat16)
                flipped[layer, unit * rows + 2 * step] = turned[:BLK]
                flipped[layer, unit * rows + 2 * step + 1] = turned[BLK:]
                return carry

            lax.fori_loop(0, rows // 2, visit, 0, unroll=True)
        return carry

    lax.fori_loop(0, 2, run, 0)


def flip_pass(stashes, bases, rows, chosen):
    tokens = sum(stash.shape[1] for stash in stashes)
    feats = stashes[0].shape[2]
    return pl.pallas_call(
        functools.partial(flip_kernel, rows, chosen),
        in_specs=[IN_SMEM] + [IN_HBM] * len(stashes),
        out_specs=IN_VMEM,
        out_shape=jax.ShapeDtypeStruct((2, chosen * rows, BLK, tokens), jnp.bfloat16),
        scratch_shapes=[
            pltpu.VMEM((2, tokens, feats), jnp.bfloat16),
            pltpu.SemaphoreType.DMA((2, len(stashes))),
        ],
        compiler_params=pltpu.CompilerParams(vmem_limit_bytes=12 * MIB),
        cost_estimate=about(4),
        name="flip_rows",
    )(bases, *stashes)


def block_grad_kernel(rows, slots, jobs, halved, units, parts, cols, flags, turned, *rest):
    sources, rest = rest[:parts], rest[parts:]
    total = sum(len(chosen) for _, chosen in jobs)
    outs = [tuple(rest[:2])] if halved else rest[:total]
    joined, flipped, lows, highs, arrived, fetched = rest[-6:]
    layers = [jnp.abs(role - flags[0]) for role, _ in jobs]
    fetches = []
    begin = 0
    for layer, (_, chosen) in zip(layers, jobs):
        fetches.append(join_tokens(sources, joined, arrived, layer))
        for which, unit in enumerate(chosen):
            copy = pltpu.make_async_copy(
                turned.at[layer, pl.ds(unit * rows, rows)],
                flipped.at[pl.ds((begin + which) * rows, rows)],
                fetched.at[begin + which],
            )
            copy.start()
            fetches[-1].append(copy)
        begin += len(chosen)
    begin = 0
    for turn, (role, chosen) in enumerate(jobs):
        for fetch in fetches[turn]:
            fetch.wait()
        spread(joined.at[layers[turn]], lows, highs)
        block_grad_layer(
            begin * rows, role, cols, flipped, lows, highs, outs[begin:], chosen, units, rows, slots
        )
        begin += len(chosen)


def block_grad_pass(turned, cotangents, meta, rows, slots, jobs, halved=False):
    tokens = turned.shape[3]
    feats = cotangents[0].shape[2]
    blocks = feats // BLK
    cols, bases, flags = meta
    total = sum(len(chosen) for _, chosen in jobs)
    tall = rows // 2 * BLK if halved else rows * BLK
    outs = [jax.ShapeDtypeStruct((tall, slots * BLK), jnp.bfloat16)] * (2 if halved else total)
    return pl.pallas_call(
        functools.partial(
            block_grad_kernel, rows, slots, jobs, halved, bases.shape[0], len(cotangents)
        ),
        in_specs=[IN_SMEM] * 2 + [IN_HBM] * (1 + len(cotangents)),
        out_specs=[IN_VMEM] * len(outs),
        out_shape=outs,
        scratch_shapes=[
            pltpu.VMEM((2, tokens, feats), jnp.bfloat16),
            pltpu.VMEM((total * rows, BLK, tokens), jnp.bfloat16),
            pltpu.VMEM((blocks, tokens, LANES), jnp.bfloat16),
            pltpu.VMEM((blocks, tokens, LANES), jnp.bfloat16),
            pltpu.SemaphoreType.DMA((2, len(cotangents))),
            pltpu.SemaphoreType.DMA((total,)),
        ],
        compiler_params=pltpu.CompilerParams(vmem_limit_bytes=18 * MIB),
        cost_estimate=about(3 + total // 2),
        name="block_grads",
    )(cols, flags, turned, *cotangents)


def list_kernel(tail_pieces, *refs):
    pieces, (listed, tails, arrived) = refs[:-3], refs[-3:]
    copies = []
    for line, index in enumerate(tail_pieces):
        piece = pieces[index]
        last = piece.at[pl.ds(piece.shape[0] - TAIL, TAIL)]
        copies.append(pltpu.make_async_copy(last, tails.at[line], arrived.at[line]))
    for copy in copies:
        copy.start()
    for line, copy in enumerate(copies):
        copy.wait()
        entry = tails[line].astype(jnp.float32)[:1, : listed.shape[1]]
        listed[line : line + 1] = entry.astype(jnp.int32)


def list_pass(weights, rows, slots):
    pieces, layout = weights
    tail_pieces = tuple(parts[-1][0] for role in range(2) for parts in layout[role])
    count = len(tail_pieces)
    lanes = -(-rows * slots // LANES) * LANES
    return pl.pallas_call(
        functools.partial(list_kernel, tail_pieces),
        in_specs=[IN_HBM] * len(pieces),
        out_specs=IN_VMEM,
        out_shape=jax.ShapeDtypeStruct((count, lanes), jnp.int32),
        scratch_shapes=[
            pltpu.VMEM((count, TAIL, slots * BLK), jnp.bfloat16),
            pltpu.SemaphoreType.DMA((count,)),
        ],
        compiler_params=pltpu.CompilerParams(vmem_limit_bytes=4 * MIB),
        cost_estimate=about(2),
        name="list_columns",
    )(*pieces)


def to_rows(blocks):
    rows, slots, _ = blocks.shape
    split = blocks.reshape(rows, slots, BLK, BLK)
    return split.transpose(0, 2, 1, 3).reshape(rows * BLK, slots * BLK)


def from_rows(matrix, slots):
    rows = matrix.shape[0] // BLK
    split = matrix.reshape(rows, BLK, slots, BLK)
    return split.transpose(0, 2, 1, 3).reshape(rows, slots, BLK * BLK)


def token_cuts(tokens):
    if tokens % 16 or tokens < 32:
        return [(0, tokens)]
    first = -(-tokens // 32) * 16
    return [(0, first), (first, tokens)]


def folded(count):
    return list(range(0, 1)) + list(range(1, count, 2)) + list(range(2, count, 2))[::-1]


def body(inputs, target, blocks, columns, counts):
    stage, stages = lax.axis_index("stage"), lax.axis_size("stage")
    side, sides = lax.axis_index("side"), lax.axis_size("side")
    dp_id, dp_count = lax.axis_index("dp"), lax.axis_size("dp")
    mb_count, tok_local, feats = inputs.shape
    rows, slots = columns.shape[1:]
    loss_scale = (mb_count * tok_local * dp_count) ** (-0.5)
    places = dp_count // 2
    place = dp_id // 2
    core = dp_id % 2
    share = mb_count * tok_local // sides

    around = folded(places)
    ranks = [around.index(spot) for spot in range(places)]
    rank = jnp.array(ranks, jnp.int32)[place]
    hops = [
        (2 * around[i] + half, 2 * around[(i + 1) % places] + half)
        for i in range(places)
        for half in range(2)
    ]

    def ring(array):
        return lax.ppermute(array, "dp", hops)

    def sibling(array):
        return lax.ppermute(array, "dp", [(i, i ^ 1) for i in range(dp_count)])

    def partner(array):
        return lax.ppermute(array, "side", [(i, sides - 1 - i) for i in range(sides)])

    slot_of = lax.broadcasted_iota(jnp.int32, (rows, BLK, slots * BLK), 2) // BLK
    live = (slot_of < counts[0][:, None, None]).reshape(rows * BLK, slots * BLK)
    listed = columns[0].reshape(1, rows * slots).astype(jnp.bfloat16)
    tail = jnp.pad(listed, ((0, TAIL - 1), (0, slots * BLK - rows * slots)))
    straight = to_rows(blocks[0])
    own = jnp.concatenate([jnp.where(live, straight, jnp.zeros_like(straight)), tail], axis=0)

    half = rows // 2 * BLK
    owns, others, far_owns, far_others = [own], [], [], []
    for slot in range(places):
        last = slot + 1 == places
        moving = {}
        if not last:
            moving["a_own"] = ring(owns[slot])
            moving["b_other"] = [partner(owns[slot])]
        elif slot:
            moving["b_other"] = [ring(others[-1][0][:half]), partner(owns[slot][half:])]
        else:
            moving["b_other"] = [partner(owns[slot])]
        if slot:
            moving["c_far_other"] = [sibling(part) for part in others[-1]]
        moving["d_far_own"] = sibling(owns[slot])
        moving = lax.optimization_barrier(moving)
        others.append(moving["b_other"])
        far_owns.append(moving["d_far_own"])
        if not last:
            owns.append(moving["a_own"])
        if slot:
            far_others.append(moving["c_far_other"])
    far_others.append([sibling(part) for part in others[-1]])
    pieces, layout = [], []
    for units in ([[piece] for piece in owns + far_owns], others + far_others):
        layout.append([])
        for parts in units:
            begin = 0
            layout[-1].append([])
            for part in parts:
                layout[-1][-1].append((len(pieces), begin))
                pieces.append(part)
                begin += part.shape[0]
    weights = (pieces, layout)
    cols = list_pass(weights, rows, slots)
    turns = jnp.array(around, jnp.int32)[(rank - jnp.arange(places)) % places]
    bases = jnp.concatenate([turns * 2 + core, turns * 2 + 1 - core]).astype(jnp.int32) * rows
    flags = jnp.stack([side, stage == 0, stage == stages - 1]).astype(jnp.int32)
    meta = (cols, bases, flags)

    def my_rows(array):
        flat = array.reshape(mb_count * tok_local, feats)
        return lax.dynamic_slice_in_dim(flat, side * share, share, 0)

    def hop(array, distance):
        route = [(i, i + distance) for i in range(stages) if 0 <= i + distance < stages]
        return lax.ppermute(array, "stage", route)

    cuts = token_cuts(share)
    ways = range(len(cuts))
    whole_start, whole_goal = my_rows(inputs), my_rows(target)
    start = [whole_start[begin:end] for begin, end in cuts]
    goal = [whole_goal[begin:end] for begin, end in cuts]
    moved = list(start)
    for step in range(stages - 1):
        final = [
            forward_pass(start[i], moved[i], None, None, weights, meta, rows, slots)[0]
            for i in ways
        ]
        moved = [hop(final[i], 1) for i in ways]
    turned = [
        forward_pass(start[i], moved[i], goal[i], loss_scale, weights, meta, rows, slots)
        for i in ways
    ]
    stashes, loss_grads, result = [list(column) for column in zip(*turned)]
    moved = loss_grads
    for step in range(stages - 1):
        if step:
            result = [
                backward_pass(stashes[i], loss_grads[i], moved[i], weights, meta, rows, slots, 2)
                for i in ways
            ]
        moved = [hop(result[i], -1) for i in ways]
    flipped = flip_pass(stashes + [sibling(stash) for stash in stashes], bases, rows, places)
    stashes[-1], flipped = lax.optimization_barrier((stashes[-1], flipped))
    cotangents = [
        backward_pass(stashes[i], loss_grads[i], moved[i], weights, meta, rows, slots, 1) for i in ways
    ]

    order = list(range(1, places)) + [0]

    cotangents = cotangents + [sibling(part) for part in cotangents]
    early, late = order[:1], order[1:]
    first = block_grad_pass(flipped, cotangents, meta, rows, slots, ((1, tuple(early)),), True)
    cotangents, first = lax.optimization_barrier((cotangents, first))
    jobs = ((1, tuple(late)), (0, tuple(order)))
    grads = block_grad_pass(flipped, cotangents, meta, rows, slots, jobs)
    if places > 1:
        moving = lax.optimization_barrier((ring(first[1]), partner(first[0]), grads))
    else:
        moving = lax.optimization_barrier((partner(first[1]), partner(first[0]), grads))
    lower, upper, grads = moving
    leaving, staying = list(grads[: len(late)]), grads[len(late) :]
    if places > 1:
        upper = jnp.concatenate([upper, jnp.zeros_like(lower)], axis=0)
        travelling = add_rounded(staying[0], upper)
        leaving[0] = add_rounded(leaving[0], jnp.concatenate([jnp.zeros_like(lower), lower], axis=0))
    else:
        travelling = add_rounded(staying[0], jnp.concatenate([upper, lower], axis=0))
    for index in range(places - 1):
        kept, outgoing = staying[index + 1], leaving[index]
        passed, coming, leaving = lax.optimization_barrier(
            (ring(travelling), partner(outgoing), leaving)
        )
        total = kept.astype(jnp.float32) + coming.astype(jnp.float32) + passed.astype(jnp.float32)
        travelling = total.astype(jnp.bfloat16)
    travelling = jnp.where(live, travelling, jnp.zeros_like(travelling))
    return from_rows(travelling, slots)[None]


def add_rounded(left, right):
    return (left.astype(jnp.float32) + right.astype(jnp.float32)).astype(jnp.bfloat16)


def solution(mesh):
    sections, width = mesh.devices.shape
    split = jax.sharding.Mesh(mesh.devices.reshape(sections // 2, 2, width), ("stage", "side", "dp"))
    section = ("stage", "side")
    return jax.shard_map(
        body,
        mesh=split,
        in_specs=(
            P(None, "dp", None),
            P(None, "dp", None),
            P(section, "dp", None, None),
            P(section, "dp", None),
            P(section, "dp"),
        ),
        out_specs=P(section, "dp", None, None),
        check_vma=False,
    )
```

```python
import functools

import jax
import jax.numpy as jnp
from jax import lax
from jax.experimental import pallas as pl
from jax.experimental.pallas import tpu as pltpu
from jax.sharding import PartitionSpec as P

BLK = 64
LANES = 128
EPSILON = 1e-05
MIB = 1024 * 1024
STEP_ROWS = 8

TAIL = 16

IN_VMEM = pl.BlockSpec(memory_space=pltpu.VMEM)
IN_SMEM = pl.BlockSpec(memory_space=pltpu.SMEM)
IN_HBM = pl.BlockSpec(memory_space=pl.ANY)


def about(microseconds):
    return pl.CostEstimate(
        flops=int(microseconds * 1.1e9), bytes_accessed=1 << 20, transcendentals=0
    )


def step_units(units, rows):
    size = max(1, STEP_ROWS // rows)
    while units % size:
        size -= 1
    return size


def low_half(rows):
    return lax.broadcasted_iota(jnp.int32, (rows, LANES), 1) < BLK


def tile(pair):
    return pl.ds(pl.multiple_of(pair * LANES, LANES), LANES)


def over_pairs(feats, visit, carry):
    return lax.fori_loop(0, feats // LANES, visit, carry, unroll=4)


def inv_rms_of(ref):
    tokens, feats = ref.shape

    def visit(pair, total):
        values = ref[:, tile(pair)].astype(jnp.float32)
        return total + values * values

    total = over_pairs(feats, visit, jnp.zeros((tokens, LANES), jnp.float32))
    return lax.rsqrt(jnp.sum(total, axis=-1, keepdims=True) / feats + EPSILON)


def start_loads(pieces, held, arrived, roles, layout):
    for role in roles:
        for unit, parts in enumerate(layout[role]):
            for index, begin in parts:
                piece = pieces[index]
                pltpu.make_async_copy(
                    piece,
                    held.at[role, unit, pl.ds(begin, piece.shape[0])],
                    arrived.at[role, unit],
                ).start()


def start_loads_in_order(side, pieces, held, arrived, layers, layout):
    for value in range(2):
        pl.when(side == value)(
            functools.partial(
                start_loads, pieces, held, arrived, [abs(layer - value) for layer in layers], layout
            )
        )


def wait_load(held, arrived, role, unit):
    whole = held.at[role, unit]
    pltpu.make_async_copy(whole, whole, arrived.at[role, unit]).wait()


def forward_layer(role, wait, cols, bases, current, held, parts, sums, rows, slots):
    tokens, feats = current.shape
    units = held.shape[1]
    per_step = step_units(units, rows)
    low = low_half(tokens)
    inv_rms = inv_rms_of(current)

    def normalise(pair, carry):
        lanes = tile(pair)
        unit_rows = current[:, lanes].astype(jnp.float32) * inv_rms
        parts[2 * pair] = jnp.where(low, unit_rows, 0.0).astype(jnp.bfloat16)
        parts[2 * pair + 1] = jnp.where(low, 0.0, unit_rows).astype(jnp.bfloat16)
        sums[2 * pair] = jnp.zeros((tokens, LANES), jnp.float32)
        sums[2 * pair + 1] = jnp.zeros((tokens, LANES), jnp.float32)
        return carry

    over_pairs(feats, normalise, 0)

    def run_step(step, carry):
        for inner in range(per_step):
            wait(role, step * per_step + inner)
        items = [(inner, row) for inner in range(per_step) for row in range(0, rows, 2)]

        def product_of(index):
            inner, row = items[index]
            unit = step * per_step + inner
            place = bases[unit] + row
            left = jnp.concatenate([parts[place], parts[place + 1]], axis=0)
            right = held[role, unit, row * BLK : (row + 2) * BLK]
            return jnp.dot(left, right, preferred_element_type=jnp.float32)

        def columns_of(index):
            inner, row = items[index]
            line = role * units + step * per_step + inner
            return [cols[line, row * slots + place] for place in range(2 * slots)]

        upcoming = product_of(0)
        ahead = columns_of(0)
        for index, (inner, row) in enumerate(items):
            product, listed = upcoming, ahead
            if index + 1 < len(items):
                upcoming = product_of(index + 1)
                ahead = columns_of(index + 1)
            for which in range(2):
                for begin in range(0, slots, 4):
                    at = listed[which * slots + begin : which * slots + min(begin + 4, slots)]
                    added = []
                    for offset in range(len(at)):
                        slot = begin + offset
                        lanes = slice((slot // 2) * LANES, (slot // 2 + 1) * LANES)
                        piece = product[which * tokens : (which + 1) * tokens, lanes]
                        piece = jnp.where(low, piece, 0.0) if slot % 2 == 0 else jnp.where(low, 0.0, piece)
                        added.append(sums[at[offset]] + piece)
                    for offset in range(len(at)):
                        sums[at[offset]] = added[offset]
        return carry

    lax.fori_loop(0, units // per_step, run_step, 0)

    def finish(pair, carry):
        lanes = tile(pair)
        first, second = sums[2 * pair], sums[2 * pair + 1]
        branch = jnp.where(low, first, second) + pltpu.roll(jnp.where(low, second, first), BLK, 1)
        current[:, lanes] = (current[:, lanes].astype(jnp.float32) + branch).astype(jnp.bfloat16)
        return carry

    over_pairs(feats, finish, 0)


def spread(source, lows, highs):
    tokens, feats = source.shape
    low = low_half(tokens)

    def visit(pair, carry):
        both = source[:, tile(pair)].astype(jnp.float32)
        moved = pltpu.roll(both, BLK, 1)
        lows[2 * pair] = jnp.where(low, both, 0.0).astype(jnp.bfloat16)
        highs[2 * pair] = jnp.where(low, 0.0, moved).astype(jnp.bfloat16)
        lows[2 * pair + 1] = jnp.where(low, moved, 0.0).astype(jnp.bfloat16)
        highs[2 * pair + 1] = jnp.where(low, 0.0, both).astype(jnp.bfloat16)
        return carry

    over_pairs(feats, visit, 0)


def pick_columns(lows, highs, cols, line, flat, slots):
    return jnp.concatenate(
        [
            lows[cols[line, flat + 2 * half]] + highs[cols[line, flat + 2 * half + 1]]
            for half in range(slots // 2)
        ],
        axis=1,
    )


def input_grad_layer(role, wait, cols, bases, hidden, cotangent, out, held, lows, highs, back, rows, slots):
    tokens, feats = cotangent.shape
    units = held.shape[1]
    per_step = step_units(units, rows)
    low = low_half(tokens)

    def run_step(step, carry):
        for inner in range(per_step):
            wait(role, step * per_step + inner)
        items = [(inner, row) for inner in range(per_step) for row in range(0, rows, 2)]

        def picked_at(index):
            inner, row = items[index]
            line = role * units + step * per_step + inner
            return jnp.concatenate(
                [
                    pick_columns(lows, highs, cols, line, (row + which) * slots, slots)
                    for which in range(2)
                ],
                axis=0,
            )

        upcoming = picked_at(0)
        for index, (inner, row) in enumerate(items):
            unit = step * per_step + inner
            picked = upcoming
            if index + 1 < len(items):
                upcoming = picked_at(index + 1)
            result = lax.dot_general(
                picked,
                held[role, unit, row * BLK : (row + 2) * BLK],
                (((1,), (1,)), ((), ())),
                preferred_element_type=jnp.float32,
            )
            place = (bases[unit] + row) // 2
            back[place] = jnp.where(low, result[:tokens], result[tokens:])
        return carry

    lax.fori_loop(0, units // per_step, run_step, 0)
    inv_rms = inv_rms_of(hidden)

    def correlate(pair, total):
        unit_rows = hidden[:, tile(pair)].astype(jnp.float32) * inv_rms
        return total + back[pair] * unit_rows

    total = over_pairs(feats, correlate, jnp.zeros((tokens, LANES), jnp.float32))
    mean = jnp.sum(total, axis=-1, keepdims=True) / feats

    def finish(pair, carry):
        lanes = tile(pair)
        unit_rows = hidden[:, lanes].astype(jnp.float32) * inv_rms
        centred = back[pair] - unit_rows * mean
        out[:, lanes] = (cotangent[:, lanes].astype(jnp.float32) + inv_rms * centred).astype(jnp.bfloat16)
        return carry

    over_pairs(feats, finish, 0)


def block_grad_layer(begin, role, cols, flipped, lows, highs, out, chosen, units, rows, slots):
    items = [(which, row) for which in range(len(chosen)) for row in range(rows)]

    def operands(index):
        which, row = items[index]
        picked = pick_columns(lows, highs, cols, role * units + chosen[which], row * slots, slots)
        return flipped[begin + which * rows + row], picked

    upcoming = operands(0)
    for index, (which, row) in enumerate(items):
        left, right = upcoming
        if index + 1 < len(items):
            upcoming = operands(index + 1)
        result = jnp.dot(left, right, preferred_element_type=jnp.float32).astype(jnp.bfloat16)
        target = out[which]
        if isinstance(target, tuple):
            target, row = target[row // (rows // 2)], row % (rows // 2)
        target[row * BLK : (row + 1) * BLK] = result


def choose(flag, first, second, target):
    @pl.when(flag == 1)
    def _():
        target[...] = first[...]

    @pl.when(flag != 1)
    def _():
        target[...] = second[...]


def forward_kernel(rows, slots, count, layout, scale, cols, bases, flags, *rest):
    turning = scale is not None
    start, moved = rest[:2]
    rest = rest[2:]
    if turning:
        goal, rest = rest[0], rest[1:]
    straight, rest = rest[:count], rest[count:]
    if turning:
        stash, loss_grad, final, held, parts, sums, arrived, lows, highs, back = rest
    else:
        final, held, parts, sums, arrived = rest
    start_loads_in_order(flags[0], straight, held, arrived, (0, 1), layout)
    choose(flags[1], start, moved, final)
    wait = functools.partial(wait_load, held, arrived)

    def run_forward(layer, carry):
        if turning:
            stash[layer] = final[...]
        role = jnp.abs(layer - flags[0])
        forward_layer(role, wait, cols, bases, final, held, parts, sums, rows, slots)
        return carry

    lax.fori_loop(0, 2, run_forward, 0)
    if not turning:
        return
    tokens, feats = final.shape

    def residue(pair, carry):
        lanes = tile(pair)
        gap = final[:, lanes].astype(jnp.float32) - goal[:, lanes].astype(jnp.float32)
        loss_grad[:, lanes] = (gap * scale).astype(jnp.bfloat16)
        return carry

    over_pairs(feats, residue, 0)
    final[...] = loss_grad[...]
    def run_back(turn, carry):
        layer = 1 - turn
        role = jnp.abs(layer - flags[0])
        hidden = stash.at[layer]
        spread(final, lows, highs)
        input_grad_layer(
            role, nothing, cols, bases, hidden, final, final, held, lows, highs, back, rows, slots
        )
        return carry

    lax.fori_loop(0, 2, run_back, 0)


def nothing(*_):
    return None


def state_of(tokens, feats):
    return jax.ShapeDtypeStruct((tokens, feats), jnp.bfloat16)


def unit_scratch(layout, rows, slots):
    units = len(layout[0])
    shape = (2, units, rows * BLK + TAIL, slots * BLK)
    return [pltpu.VMEM(shape, jnp.bfloat16), pltpu.SemaphoreType.DMA((2, units))]


def forward_pass(start, moved, goal, scale, weights, meta, rows, slots):
    straight, layout = weights
    tokens, feats = start.shape
    blocks = feats // BLK
    stack = jax.ShapeDtypeStruct((2, tokens, feats), jnp.bfloat16)
    held, arrived = unit_scratch(layout, rows, slots)
    scratch = [
        held,
        pltpu.VMEM((blocks, tokens, LANES), jnp.bfloat16),
        pltpu.VMEM((blocks, tokens, LANES), jnp.float32),
        arrived,
    ]
    outs = [state_of(tokens, feats)]
    ins = [start, moved]
    pieces = list(straight)
    if goal is not None:
        ins.append(goal)
        outs = [stack, state_of(tokens, feats)] + outs
        scratch += [
            pltpu.VMEM((blocks, tokens, LANES), jnp.bfloat16),
            pltpu.VMEM((blocks, tokens, LANES), jnp.bfloat16),
            pltpu.VMEM((blocks // 2, tokens, LANES), jnp.float32),
        ]
    return pl.pallas_call(
        functools.partial(
            forward_kernel, rows, slots, len(straight), layout, None if goal is None else scale
        ),
        in_specs=[IN_SMEM] * 3 + [IN_VMEM] * len(ins) + [IN_HBM] * len(pieces),
        out_specs=[IN_VMEM] * len(outs),
        out_shape=outs,
        scratch_shapes=scratch,
        compiler_params=pltpu.CompilerParams(vmem_limit_bytes=(16 if goal is None else 20) * MIB),
        cost_estimate=about(8 if goal is None else 14),
        name="forward_layers" if goal is None else "turning_layers",
    )(*meta, *ins, *pieces)


def backward_kernel(rows, slots, count, layout, depth, cols, bases, flags, stash, loss_grad, moved, *rest):
    across, rest = rest[:count], rest[count:]
    outs, crossed, lows, highs, back, landed = rest
    if depth == 1:
        first, second = outs.at[1], outs.at[0]
    else:
        first = second = outs
    order = (1,) if depth == 1 else (1, 0)
    start_loads_in_order(flags[0], across, crossed, landed, order, layout)
    choose(flags[2], loss_grad, moved, first)
    wait = functools.partial(wait_load, crossed, landed)

    def run_back(layer):
        spread(first, lows, highs)
        role = jnp.abs(layer - flags[0])
        input_grad_layer(
            role, wait, cols, bases, stash.at[layer], first, second, crossed, lows, highs, back, rows, slots
        )

    run_back(1)
    if depth == 2:
        run_back(0)


def backward_pass(stash, loss_grad, moved, weights, meta, rows, slots, depth):
    across, layout = weights
    _, tokens, feats = stash.shape
    blocks = feats // BLK
    crossed, landed = unit_scratch(layout, rows, slots)
    if depth == 1:
        out = jax.ShapeDtypeStruct((2, tokens, feats), jnp.bfloat16)
    else:
        out = state_of(tokens, feats)
    return pl.pallas_call(
        functools.partial(backward_kernel, rows, slots, len(across), layout, depth),
        in_specs=[IN_SMEM] * 3 + [IN_VMEM] * 3 + [IN_HBM] * len(across),
        out_specs=IN_VMEM,
        out_shape=out,
        scratch_shapes=[
            crossed,
            pltpu.VMEM((blocks, tokens, LANES), jnp.bfloat16),
            pltpu.VMEM((blocks, tokens, LANES), jnp.bfloat16),
            pltpu.VMEM((blocks // 2, tokens, LANES), jnp.float32),
            landed,
        ],
        compiler_params=pltpu.CompilerParams(vmem_limit_bytes=18 * MIB),
        cost_estimate=about(4 * depth),
        name="backward_layers",
    )(*meta, stash, loss_grad, moved, *across)


def join_tokens(sources, joined, arrived, layer):
    copies = []
    begin = 0
    for index, source in enumerate(sources):
        span = pl.ds(begin, source.shape[1])
        copies.append(
            pltpu.make_async_copy(source.at[layer], joined.at[layer, span], arrived.at[layer, index])
        )
        begin += source.shape[1]
    for copy in copies:
        copy.start()
    return copies


def flip_kernel(rows, chosen, bases, *refs):
    *sources, flipped, joined, arrived = refs
    loads = [join_tokens(sources, joined, arrived, layer) for layer in range(2)]
    for load in loads[0] + loads[1]:
        load.wait()

    def run(layer, carry):
        hidden = joined.at[layer]
        inv_rms = inv_rms_of(hidden)
        for unit in range(chosen):

            def visit(step, carry):
                lanes = tile(bases[unit] // 2 + step)
                turned = (hidden[:, lanes].astype(jnp.float32) * inv_rms).T.astype(jnp.bfloat16)
                flipped[layer, unit * rows + 2 * step] = turned[:BLK]
                flipped[layer, unit * rows + 2 * step + 1] = turned[BLK:]
                return carry

            lax.fori_loop(0, rows // 2, visit, 0, unroll=True)
        return carry

    lax.fori_loop(0, 2, run, 0)


def flip_pass(stashes, bases, rows, chosen):
    tokens = sum(stash.shape[1] for stash in stashes)
    feats = stashes[0].shape[2]
    return pl.pallas_call(
        functools.partial(flip_kernel, rows, chosen),
        in_specs=[IN_SMEM] + [IN_HBM] * len(stashes),
        out_specs=IN_VMEM,
        out_shape=jax.ShapeDtypeStruct((2, chosen * rows, BLK, tokens), jnp.bfloat16),
        scratch_shapes=[
            pltpu.VMEM((2, tokens, feats), jnp.bfloat16),
            pltpu.SemaphoreType.DMA((2, len(stashes))),
        ],
        compiler_params=pltpu.CompilerParams(vmem_limit_bytes=12 * MIB),
        cost_estimate=about(4),
        name="flip_rows",
    )(bases, *stashes)


def block_grad_kernel(rows, slots, jobs, halved, units, parts, cols, flags, turned, *rest):
    sources, rest = rest[:parts], rest[parts:]
    total = sum(len(chosen) for _, chosen in jobs)
    outs = [tuple(rest[:2])] if halved else rest[:total]
    joined, flipped, lows, highs, arrived, fetched = rest[-6:]
    layers = [jnp.abs(role - flags[0]) for role, _ in jobs]
    fetches = []
    begin = 0
    for layer, (_, chosen) in zip(layers, jobs):
        fetches.append(join_tokens(sources, joined, arrived, layer))
        for which, unit in enumerate(chosen):
            copy = pltpu.make_async_copy(
                turned.at[layer, pl.ds(unit * rows, rows)],
                flipped.at[pl.ds((begin + which) * rows, rows)],
                fetched.at[begin + which],
            )
            copy.start()
            fetches[-1].append(copy)
        begin += len(chosen)
    begin = 0
    for turn, (role, chosen) in enumerate(jobs):
        for fetch in fetches[turn]:
            fetch.wait()
        spread(joined.at[layers[turn]], lows, highs)
        block_grad_layer(
            begin * rows, role, cols, flipped, lows, highs, outs[begin:], chosen, units, rows, slots
        )
        begin += len(chosen)


def block_grad_pass(turned, cotangents, meta, rows, slots, jobs, halved=False):
    tokens = turned.shape[3]
    feats = cotangents[0].shape[2]
    blocks = feats // BLK
    cols, bases, flags = meta
    total = sum(len(chosen) for _, chosen in jobs)
    tall = rows // 2 * BLK if halved else rows * BLK
    outs = [jax.ShapeDtypeStruct((tall, slots * BLK), jnp.bfloat16)] * (2 if halved else total)
    return pl.pallas_call(
        functools.partial(
            block_grad_kernel, rows, slots, jobs, halved, bases.shape[0], len(cotangents)
        ),
        in_specs=[IN_SMEM] * 2 + [IN_HBM] * (1 + len(cotangents)),
        out_specs=[IN_VMEM] * len(outs),
        out_shape=outs,
        scratch_shapes=[
            pltpu.VMEM((2, tokens, feats), jnp.bfloat16),
            pltpu.VMEM((total * rows, BLK, tokens), jnp.bfloat16),
            pltpu.VMEM((blocks, tokens, LANES), jnp.bfloat16),
            pltpu.VMEM((blocks, tokens, LANES), jnp.bfloat16),
            pltpu.SemaphoreType.DMA((2, len(cotangents))),
            pltpu.SemaphoreType.DMA((total,)),
        ],
        compiler_params=pltpu.CompilerParams(vmem_limit_bytes=18 * MIB),
        cost_estimate=about(3 + total // 2),
        name="block_grads",
    )(cols, flags, turned, *cotangents)


def list_kernel(tail_pieces, *refs):
    pieces, (listed, tails, arrived) = refs[:-3], refs[-3:]
    copies = []
    for line, index in enumerate(tail_pieces):
        piece = pieces[index]
        last = piece.at[pl.ds(piece.shape[0] - TAIL, TAIL)]
        copies.append(pltpu.make_async_copy(last, tails.at[line], arrived.at[line]))
    for copy in copies:
        copy.start()
    for line, copy in enumerate(copies):
        copy.wait()
        entry = tails[line].astype(jnp.float32)[:1, : listed.shape[1]]
        listed[line : line + 1] = entry.astype(jnp.int32)


def list_pass(weights, rows, slots):
    pieces, layout = weights
    tail_pieces = tuple(parts[-1][0] for role in range(2) for parts in layout[role])
    count = len(tail_pieces)
    lanes = -(-rows * slots // LANES) * LANES
    return pl.pallas_call(
        functools.partial(list_kernel, tail_pieces),
        in_specs=[IN_HBM] * len(pieces),
        out_specs=IN_VMEM,
        out_shape=jax.ShapeDtypeStruct((count, lanes), jnp.int32),
        scratch_shapes=[
            pltpu.VMEM((count, TAIL, slots * BLK), jnp.bfloat16),
            pltpu.SemaphoreType.DMA((count,)),
        ],
        compiler_params=pltpu.CompilerParams(vmem_limit_bytes=4 * MIB),
        cost_estimate=about(2),
        name="list_columns",
    )(*pieces)


def to_rows(blocks):
    rows, slots, _ = blocks.shape
    split = blocks.reshape(rows, slots, BLK, BLK)
    return split.transpose(0, 2, 1, 3).reshape(rows * BLK, slots * BLK)


def from_rows(matrix, slots):
    rows = matrix.shape[0] // BLK
    split = matrix.reshape(rows, BLK, slots, BLK)
    return split.transpose(0, 2, 1, 3).reshape(rows, slots, BLK * BLK)


def token_cuts(tokens):
    if tokens % 16 or tokens < 32:
        return [(0, tokens)]
    first = -(-tokens // 32) * 16
    return [(0, first), (first, tokens)]


def folded(count):
    return list(range(0, 1)) + list(range(1, count, 2)) + list(range(2, count, 2))[::-1]


def body(inputs, target, blocks, columns, counts):
    stage, stages = lax.axis_index("stage"), lax.axis_size("stage")
    side, sides = lax.axis_index("side"), lax.axis_size("side")
    dp_id, dp_count = lax.axis_index("dp"), lax.axis_size("dp")
    mb_count, tok_local, feats = inputs.shape
    rows, slots = columns.shape[1:]
    loss_scale = (mb_count * tok_local * dp_count) ** (-0.5)
    places = dp_count // 2
    place = dp_id // 2
    core = dp_id % 2
    share = mb_count * tok_local // sides

    around = folded(places)
    ranks = [around.index(spot) for spot in range(places)]
    rank = jnp.array(ranks, jnp.int32)[place]
    hops = [
        (2 * around[i] + half, 2 * around[(i + 1) % places] + half)
        for i in range(places)
        for half in range(2)
    ]

    def ring(array):
        return lax.ppermute(array, "dp", hops)

    def sibling(array):
        return lax.ppermute(array, "dp", [(i, i ^ 1) for i in range(dp_count)])

    def partner(array):
        return lax.ppermute(array, "side", [(i, sides - 1 - i) for i in range(sides)])

    slot_of = lax.broadcasted_iota(jnp.int32, (rows, BLK, slots * BLK), 2) // BLK
    live = (slot_of < counts[0][:, None, None]).reshape(rows * BLK, slots * BLK)
    listed = columns[0].reshape(1, rows * slots).astype(jnp.bfloat16)
    tail = jnp.pad(listed, ((0, TAIL - 1), (0, slots * BLK - rows * slots)))
    straight = to_rows(blocks[0])
    own = jnp.concatenate([jnp.where(live, straight, jnp.zeros_like(straight)), tail], axis=0)

    owns, others, far_owns, far_others = [own], [], [], []
    for slot in range(places):
        last = slot + 1 == places
        moving = {}
        if not last:
            moving["a_own"] = ring(owns[slot])
        moving["b_other"] = [partner(owns[slot])]
        if slot:
            moving["c_far_other"] = [sibling(part) for part in others[-1]]
        moving["d_far_own"] = sibling(owns[slot])
        moving = lax.optimization_barrier(moving)
        others.append(moving["b_other"])
        far_owns.append(moving["d_far_own"])
        if not last:
            owns.append(moving["a_own"])
        if slot:
            far_others.append(moving["c_far_other"])
    far_others.append([sibling(part) for part in others[-1]])
    pieces, layout = [], []
    for units in ([[piece] for piece in owns + far_owns], others + far_others):
        layout.append([])
        for parts in units:
            begin = 0
            layout[-1].append([])
            for part in parts:
                layout[-1][-1].append((len(pieces), begin))
                pieces.append(part)
                begin += part.shape[0]
    weights = (pieces, layout)
    cols = list_pass(weights, rows, slots)
    turns = jnp.array(around, jnp.int32)[(rank - jnp.arange(places)) % places]
    bases = jnp.concatenate([turns * 2 + core, turns * 2 + 1 - core]).astype(jnp.int32) * rows
    flags = jnp.stack([side, stage == 0, stage == stages - 1]).astype(jnp.int32)
    meta = (cols, bases, flags)

    def my_rows(array):
        flat = array.reshape(mb_count * tok_local, feats)
        return lax.dynamic_slice_in_dim(flat, side * share, share, 0)

    def hop(array, distance):
        route = [(i, i + distance) for i in range(stages) if 0 <= i + distance < stages]
        return lax.ppermute(array, "stage", route)

    cuts = token_cuts(share)
    ways = range(len(cuts))
    whole_start, whole_goal = my_rows(inputs), my_rows(target)
    start = [whole_start[begin:end] for begin, end in cuts]
    goal = [whole_goal[begin:end] for begin, end in cuts]
    moved = list(start)
    for step in range(stages - 1):
        final = [
            forward_pass(start[i], moved[i], None, None, weights, meta, rows, slots)[0]
            for i in ways
        ]
        moved = [hop(final[i], 1) for i in ways]
    turned = [
        forward_pass(start[i], moved[i], goal[i], loss_scale, weights, meta, rows, slots)
        for i in ways
    ]
    stashes, loss_grads, result = [list(column) for column in zip(*turned)]
    moved = loss_grads
    for step in range(stages - 1):
        if step:
            result = [
                backward_pass(stashes[i], loss_grads[i], moved[i], weights, meta, rows, slots, 2)
                for i in ways
            ]
        moved = [hop(result[i], -1) for i in ways]
    flipped = flip_pass(stashes + [sibling(stash) for stash in stashes], bases, rows, places)
    stashes[-1], flipped = lax.optimization_barrier((stashes[-1], flipped))
    cotangents = [
        backward_pass(stashes[i], loss_grads[i], moved[i], weights, meta, rows, slots, 1) for i in ways
    ]

    order = list(range(1, places)) + [0]

    cotangents = cotangents + [sibling(part) for part in cotangents]
    early, late = order[:1], order[1:]
    first = block_grad_pass(flipped, cotangents, meta, rows, slots, ((1, tuple(early)),), True)
    cotangents, first = lax.optimization_barrier((cotangents, first))
    jobs = ((1, tuple(late)), (0, tuple(order)))
    grads = block_grad_pass(flipped, cotangents, meta, rows, slots, jobs)
    if places > 1:
        moving = lax.optimization_barrier((ring(first[1]), partner(first[0]), grads))
    else:
        moving = lax.optimization_barrier((partner(first[1]), partner(first[0]), grads))
    lower, upper, grads = moving
    leaving, staying = list(grads[: len(late)]), grads[len(late) :]
    if places > 1:
        upper = jnp.concatenate([upper, jnp.zeros_like(lower)], axis=0)
        travelling = add_rounded(staying[0], upper)
        leaving[0] = add_rounded(leaving[0], jnp.concatenate([jnp.zeros_like(lower), lower], axis=0))
    else:
        travelling = add_rounded(staying[0], jnp.concatenate([upper, lower], axis=0))
    for index in range(places - 1):
        kept, outgoing = staying[index + 1], leaving[index]
        passed, coming, leaving = lax.optimization_barrier(
            (ring(travelling), partner(outgoing), leaving)
        )
        total = kept.astype(jnp.float32) + coming.astype(jnp.float32) + passed.astype(jnp.float32)
        travelling = total.astype(jnp.bfloat16)
    travelling = jnp.where(live, travelling, jnp.zeros_like(travelling))
    return from_rows(travelling, slots)[None]


def add_rounded(left, right):
    return (left.astype(jnp.float32) + right.astype(jnp.float32)).astype(jnp.bfloat16)


def solution(mesh):
    sections, width = mesh.devices.shape
    split = jax.sharding.Mesh(mesh.devices.reshape(sections // 2, 2, width), ("stage", "side", "dp"))
    section = ("stage", "side")
    return jax.shard_map(
        body,
        mesh=split,
        in_specs=(
            P(None, "dp", None),
            P(None, "dp", None),
            P(section, "dp", None, None),
            P(section, "dp", None),
            P(section, "dp"),
        ),
        out_specs=P(section, "dp", None, None),
        check_vma=False,
    )
```

```python
import functools

import jax
import jax.numpy as jnp
from jax import lax
from jax.experimental import pallas as pl
from jax.experimental.pallas import tpu as pltpu
from jax.sharding import PartitionSpec as P

BLK = 64
LANES = 128
EPSILON = 1e-05
MIB = 1024 * 1024
STEP_ROWS = 8

TAIL = 16

IN_VMEM = pl.BlockSpec(memory_space=pltpu.VMEM)
IN_SMEM = pl.BlockSpec(memory_space=pltpu.SMEM)
IN_HBM = pl.BlockSpec(memory_space=pl.ANY)


def about(microseconds):
    return pl.CostEstimate(
        flops=int(microseconds * 1.1e9), bytes_accessed=1 << 20, transcendentals=0
    )


def step_units(units, rows):
    size = max(1, STEP_ROWS // rows)
    while units % size:
        size -= 1
    return size


def low_half(rows):
    return lax.broadcasted_iota(jnp.int32, (rows, LANES), 1) < BLK


def tile(pair):
    return pl.ds(pl.multiple_of(pair * LANES, LANES), LANES)


def over_pairs(feats, visit, carry):
    return lax.fori_loop(0, feats // LANES, visit, carry, unroll=4)


def inv_rms_of(ref):
    tokens, feats = ref.shape

    def visit(pair, total):
        values = ref[:, tile(pair)].astype(jnp.float32)
        return total + values * values

    total = over_pairs(feats, visit, jnp.zeros((tokens, LANES), jnp.float32))
    return lax.rsqrt(jnp.sum(total, axis=-1, keepdims=True) / feats + EPSILON)


def start_loads(pieces, held, arrived, roles, layout):
    for role in roles:
        for unit, parts in enumerate(layout[role]):
            for index, begin in parts:
                piece = pieces[index]
                pltpu.make_async_copy(
                    piece,
                    held.at[role, unit, pl.ds(begin, piece.shape[0])],
                    arrived.at[role, unit],
                ).start()


def start_loads_in_order(side, pieces, held, arrived, layers, layout):
    for value in range(2):
        pl.when(side == value)(
            functools.partial(
                start_loads, pieces, held, arrived, [abs(layer - value) for layer in layers], layout
            )
        )


def wait_load(held, arrived, role, unit):
    whole = held.at[role, unit]
    pltpu.make_async_copy(whole, whole, arrived.at[role, unit]).wait()


def forward_layer(role, wait, cols, bases, current, held, parts, sums, rows, slots):
    tokens, feats = current.shape
    units = held.shape[1]
    per_step = step_units(units, rows)
    low = low_half(tokens)
    inv_rms = inv_rms_of(current)

    def normalise(pair, carry):
        lanes = tile(pair)
        unit_rows = current[:, lanes].astype(jnp.float32) * inv_rms
        parts[2 * pair] = jnp.where(low, unit_rows, 0.0).astype(jnp.bfloat16)
        parts[2 * pair + 1] = jnp.where(low, 0.0, unit_rows).astype(jnp.bfloat16)
        sums[2 * pair] = jnp.zeros((tokens, LANES), jnp.float32)
        sums[2 * pair + 1] = jnp.zeros((tokens, LANES), jnp.float32)
        return carry

    over_pairs(feats, normalise, 0)

    def run_step(step, carry):
        for inner in range(per_step):
            wait(role, step * per_step + inner)
        items = [(inner, row) for inner in range(per_step) for row in range(0, rows, 2)]

        def product_of(index):
            inner, row = items[index]
            unit = step * per_step + inner
            place = bases[unit] + row
            left = jnp.concatenate([parts[place], parts[place + 1]], axis=0)
            right = held[role, unit, row * BLK : (row + 2) * BLK]
            return jnp.dot(left, right, preferred_element_type=jnp.float32)

        def columns_of(index):
            inner, row = items[index]
            line = role * units + step * per_step + inner
            return [cols[line, row * slots + place] for place in range(2 * slots)]

        upcoming = product_of(0)
        ahead = columns_of(0)
        for index, (inner, row) in enumerate(items):
            product, listed = upcoming, ahead
            if index + 1 < len(items):
                upcoming = product_of(index + 1)
                ahead = columns_of(index + 1)
            for which in range(2):
                for begin in range(0, slots, 4):
                    at = listed[which * slots + begin : which * slots + min(begin + 4, slots)]
                    added = []
                    for offset in range(len(at)):
                        slot = begin + offset
                        lanes = slice((slot // 2) * LANES, (slot // 2 + 1) * LANES)
                        piece = product[which * tokens : (which + 1) * tokens, lanes]
                        piece = jnp.where(low, piece, 0.0) if slot % 2 == 0 else jnp.where(low, 0.0, piece)
                        added.append(sums[at[offset]] + piece)
                    for offset in range(len(at)):
                        sums[at[offset]] = added[offset]
        return carry

    lax.fori_loop(0, units // per_step, run_step, 0)

    def finish(pair, carry):
        lanes = tile(pair)
        first, second = sums[2 * pair], sums[2 * pair + 1]
        branch = jnp.where(low, first, second) + pltpu.roll(jnp.where(low, second, first), BLK, 1)
        current[:, lanes] = (current[:, lanes].astype(jnp.float32) + branch).astype(jnp.bfloat16)
        return carry

    over_pairs(feats, finish, 0)


def spread(source, lows, highs):
    tokens, feats = source.shape
    low = low_half(tokens)

    def visit(pair, carry):
        both = source[:, tile(pair)].astype(jnp.float32)
        moved = pltpu.roll(both, BLK, 1)
        lows[2 * pair] = jnp.where(low, both, 0.0).astype(jnp.bfloat16)
        highs[2 * pair] = jnp.where(low, 0.0, moved).astype(jnp.bfloat16)
        lows[2 * pair + 1] = jnp.where(low, moved, 0.0).astype(jnp.bfloat16)
        highs[2 * pair + 1] = jnp.where(low, 0.0, both).astype(jnp.bfloat16)
        return carry

    over_pairs(feats, visit, 0)


def pick_columns(lows, highs, cols, line, flat, slots):
    return jnp.concatenate(
        [
            lows[cols[line, flat + 2 * half]] + highs[cols[line, flat + 2 * half + 1]]
            for half in range(slots // 2)
        ],
        axis=1,
    )


def input_grad_layer(role, wait, cols, bases, hidden, cotangent, out, held, lows, highs, back, rows, slots):
    tokens, feats = cotangent.shape
    units = held.shape[1]
    per_step = step_units(units, rows)
    low = low_half(tokens)

    def run_step(step, carry):
        for inner in range(per_step):
            wait(role, step * per_step + inner)
        items = [(inner, row) for inner in range(per_step) for row in range(0, rows, 2)]

        def picked_at(index):
            inner, row = items[index]
            line = role * units + step * per_step + inner
            return jnp.concatenate(
                [
                    pick_columns(lows, highs, cols, line, (row + which) * slots, slots)
                    for which in range(2)
                ],
                axis=0,
            )

        upcoming = picked_at(0)
        for index, (inner, row) in enumerate(items):
            unit = step * per_step + inner
            picked = upcoming
            if index + 1 < len(items):
                upcoming = picked_at(index + 1)
            result = lax.dot_general(
                picked,
                held[role, unit, row * BLK : (row + 2) * BLK],
                (((1,), (1,)), ((), ())),
                preferred_element_type=jnp.float32,
            )
            place = (bases[unit] + row) // 2
            back[place] = jnp.where(low, result[:tokens], result[tokens:])
        return carry

    lax.fori_loop(0, units // per_step, run_step, 0)
    inv_rms = inv_rms_of(hidden)

    def correlate(pair, total):
        unit_rows = hidden[:, tile(pair)].astype(jnp.float32) * inv_rms
        return total + back[pair] * unit_rows

    total = over_pairs(feats, correlate, jnp.zeros((tokens, LANES), jnp.float32))
    mean = jnp.sum(total, axis=-1, keepdims=True) / feats

    def finish(pair, carry):
        lanes = tile(pair)
        unit_rows = hidden[:, lanes].astype(jnp.float32) * inv_rms
        centred = back[pair] - unit_rows * mean
        out[:, lanes] = (cotangent[:, lanes].astype(jnp.float32) + inv_rms * centred).astype(jnp.bfloat16)
        return carry

    over_pairs(feats, finish, 0)


def block_grad_layer(begin, role, cols, flipped, lows, highs, out, chosen, units, rows, slots):
    items = [(which, row) for which in range(len(chosen)) for row in range(rows)]

    def operands(index):
        which, row = items[index]
        picked = pick_columns(lows, highs, cols, role * units + chosen[which], row * slots, slots)
        return flipped[begin + which * rows + row], picked

    upcoming = operands(0)
    for index, (which, row) in enumerate(items):
        left, right = upcoming
        if index + 1 < len(items):
            upcoming = operands(index + 1)
        result = jnp.dot(left, right, preferred_element_type=jnp.float32).astype(jnp.bfloat16)
        target = out[which]
        if isinstance(target, tuple):
            target, row = target[row // (rows // 2)], row % (rows // 2)
        target[row * BLK : (row + 1) * BLK] = result


def choose(flag, first, second, target):
    @pl.when(flag == 1)
    def _():
        target[...] = first[...]

    @pl.when(flag != 1)
    def _():
        target[...] = second[...]


def forward_kernel(rows, slots, count, layout, scale, cols, bases, flags, *rest):
    turning = scale is not None
    start, moved = rest[:2]
    rest = rest[2:]
    if turning:
        goal, rest = rest[0], rest[1:]
    straight, rest = rest[:count], rest[count:]
    if turning:
        stash, loss_grad, final, held, parts, sums, arrived, lows, highs, back = rest
    else:
        final, held, parts, sums, arrived = rest
    start_loads_in_order(flags[0], straight, held, arrived, (0, 1), layout)
    choose(flags[1], start, moved, final)
    wait = functools.partial(wait_load, held, arrived)

    def run_forward(layer, carry):
        if turning:
            stash[layer] = final[...]
        role = jnp.abs(layer - flags[0])
        forward_layer(role, wait, cols, bases, final, held, parts, sums, rows, slots)
        return carry

    lax.fori_loop(0, 2, run_forward, 0)
    if not turning:
        return
    tokens, feats = final.shape

    def residue(pair, carry):
        lanes = tile(pair)
        gap = final[:, lanes].astype(jnp.float32) - goal[:, lanes].astype(jnp.float32)
        loss_grad[:, lanes] = (gap * scale).astype(jnp.bfloat16)
        return carry

    over_pairs(feats, residue, 0)
    final[...] = loss_grad[...]
    def run_back(turn, carry):
        layer = 1 - turn
        role = jnp.abs(layer - flags[0])
        hidden = stash.at[layer]
        spread(final, lows, highs)
        input_grad_layer(
            role, nothing, cols, bases, hidden, final, final, held, lows, highs, back, rows, slots
        )
        return carry

    lax.fori_loop(0, 2, run_back, 0)


def nothing(*_):
    return None


def state_of(tokens, feats):
    return jax.ShapeDtypeStruct((tokens, feats), jnp.bfloat16)


def unit_scratch(layout, rows, slots):
    units = len(layout[0])
    shape = (2, units, rows * BLK + TAIL, slots * BLK)
    return [pltpu.VMEM(shape, jnp.bfloat16), pltpu.SemaphoreType.DMA((2, units))]


def forward_pass(start, moved, goal, scale, weights, meta, rows, slots):
    straight, layout = weights
    tokens, feats = start.shape
    blocks = feats // BLK
    stack = jax.ShapeDtypeStruct((2, tokens, feats), jnp.bfloat16)
    held, arrived = unit_scratch(layout, rows, slots)
    scratch = [
        held,
        pltpu.VMEM((blocks, tokens, LANES), jnp.bfloat16),
        pltpu.VMEM((blocks, tokens, LANES), jnp.float32),
        arrived,
    ]
    outs = [state_of(tokens, feats)]
    ins = [start, moved]
    pieces = list(straight)
    if goal is not None:
        ins.append(goal)
        outs = [stack, state_of(tokens, feats)] + outs
        scratch += [
            pltpu.VMEM((blocks, tokens, LANES), jnp.bfloat16),
            pltpu.VMEM((blocks, tokens, LANES), jnp.bfloat16),
            pltpu.VMEM((blocks // 2, tokens, LANES), jnp.float32),
        ]
    return pl.pallas_call(
        functools.partial(
            forward_kernel, rows, slots, len(straight), layout, None if goal is None else scale
        ),
        in_specs=[IN_SMEM] * 3 + [IN_VMEM] * len(ins) + [IN_HBM] * len(pieces),
        out_specs=[IN_VMEM] * len(outs),
        out_shape=outs,
        scratch_shapes=scratch,
        compiler_params=pltpu.CompilerParams(vmem_limit_bytes=(16 if goal is None else 20) * MIB),
        cost_estimate=about(8 if goal is None else 14),
        name="forward_layers" if goal is None else "turning_layers",
    )(*meta, *ins, *pieces)


def backward_kernel(rows, slots, count, layout, depth, cols, bases, flags, stash, loss_grad, moved, *rest):
    across, rest = rest[:count], rest[count:]
    outs, crossed, lows, highs, back, landed = rest
    if depth == 1:
        first, second = outs.at[1], outs.at[0]
    else:
        first = second = outs
    order = (1,) if depth == 1 else (1, 0)
    start_loads_in_order(flags[0], across, crossed, landed, order, layout)
    choose(flags[2], loss_grad, moved, first)
    wait = functools.partial(wait_load, crossed, landed)

    def run_back(layer):
        spread(first, lows, highs)
        role = jnp.abs(layer - flags[0])
        input_grad_layer(
            role, wait, cols, bases, stash.at[layer], first, second, crossed, lows, highs, back, rows, slots
        )

    run_back(1)
    if depth == 2:
        run_back(0)


def backward_pass(stash, loss_grad, moved, weights, meta, rows, slots, depth):
    across, layout = weights
    _, tokens, feats = stash.shape
    blocks = feats // BLK
    crossed, landed = unit_scratch(layout, rows, slots)
    if depth == 1:
        out = jax.ShapeDtypeStruct((2, tokens, feats), jnp.bfloat16)
    else:
        out = state_of(tokens, feats)
    return pl.pallas_call(
        functools.partial(backward_kernel, rows, slots, len(across), layout, depth),
        in_specs=[IN_SMEM] * 3 + [IN_VMEM] * 3 + [IN_HBM] * len(across),
        out_specs=IN_VMEM,
        out_shape=out,
        scratch_shapes=[
            crossed,
            pltpu.VMEM((blocks, tokens, LANES), jnp.bfloat16),
            pltpu.VMEM((blocks, tokens, LANES), jnp.bfloat16),
            pltpu.VMEM((blocks // 2, tokens, LANES), jnp.float32),
            landed,
        ],
        compiler_params=pltpu.CompilerParams(vmem_limit_bytes=18 * MIB),
        cost_estimate=about(4 * depth),
        name="backward_layers",
    )(*meta, stash, loss_grad, moved, *across)


def join_tokens(sources, joined, arrived, layer):
    copies = []
    begin = 0
    for index, source in enumerate(sources):
        span = pl.ds(begin, source.shape[1])
        copies.append(
            pltpu.make_async_copy(source.at[layer], joined.at[layer, span], arrived.at[layer, index])
        )
        begin += source.shape[1]
    for copy in copies:
        copy.start()
    return copies


def flip_kernel(rows, chosen, bases, *refs):
    *sources, flipped, joined, arrived = refs
    loads = [join_tokens(sources, joined, arrived, layer) for layer in range(2)]
    for load in loads[0] + loads[1]:
        load.wait()

    def run(layer, carry):
        hidden = joined.at[layer]
        inv_rms = inv_rms_of(hidden)
        for unit in range(chosen):

            def visit(step, carry):
                lanes = tile(bases[unit] // 2 + step)
                turned = (hidden[:, lanes].astype(jnp.float32) * inv_rms).T.astype(jnp.bfloat16)
                flipped[layer, unit * rows + 2 * step] = turned[:BLK]
                flipped[layer, unit * rows + 2 * step + 1] = turned[BLK:]
                return carry

            lax.fori_loop(0, rows // 2, visit, 0, unroll=True)
        return carry

    lax.fori_loop(0, 2, run, 0)


def flip_pass(stashes, bases, rows, chosen):
    tokens = sum(stash.shape[1] for stash in stashes)
    feats = stashes[0].shape[2]
    return pl.pallas_call(
        functools.partial(flip_kernel, rows, chosen),
        in_specs=[IN_SMEM] + [IN_HBM] * len(stashes),
        out_specs=IN_VMEM,
        out_shape=jax.ShapeDtypeStruct((2, chosen * rows, BLK, tokens), jnp.bfloat16),
        scratch_shapes=[
            pltpu.VMEM((2, tokens, feats), jnp.bfloat16),
            pltpu.SemaphoreType.DMA((2, len(stashes))),
        ],
        compiler_params=pltpu.CompilerParams(vmem_limit_bytes=12 * MIB),
        cost_estimate=about(4),
        name="flip_rows",
    )(bases, *stashes)


def block_grad_kernel(rows, slots, jobs, halved, units, parts, cols, flags, turned, *rest):
    sources, rest = rest[:parts], rest[parts:]
    total = sum(len(chosen) for _, chosen in jobs)
    outs = [tuple(rest[:2])] if halved else rest[:total]
    joined, flipped, lows, highs, arrived, fetched = rest[-6:]
    layers = [jnp.abs(role - flags[0]) for role, _ in jobs]
    fetches = []
    begin = 0
    for layer, (_, chosen) in zip(layers, jobs):
        fetches.append(join_tokens(sources, joined, arrived, layer))
        for which, unit in enumerate(chosen):
            copy = pltpu.make_async_copy(
                turned.at[layer, pl.ds(unit * rows, rows)],
                flipped.at[pl.ds((begin + which) * rows, rows)],
                fetched.at[begin + which],
            )
            copy.start()
            fetches[-1].append(copy)
        begin += len(chosen)
    begin = 0
    for turn, (role, chosen) in enumerate(jobs):
        for fetch in fetches[turn]:
            fetch.wait()
        spread(joined.at[layers[turn]], lows, highs)
        block_grad_layer(
            begin * rows, role, cols, flipped, lows, highs, outs[begin:], chosen, units, rows, slots
        )
        begin += len(chosen)


def block_grad_pass(turned, cotangents, meta, rows, slots, jobs, halved=False):
    tokens = turned.shape[3]
    feats = cotangents[0].shape[2]
    blocks = feats // BLK
    cols, bases, flags = meta
    total = sum(len(chosen) for _, chosen in jobs)
    tall = rows // 2 * BLK if halved else rows * BLK
    outs = [jax.ShapeDtypeStruct((tall, slots * BLK), jnp.bfloat16)] * (2 if halved else total)
    return pl.pallas_call(
        functools.partial(
            block_grad_kernel, rows, slots, jobs, halved, bases.shape[0], len(cotangents)
        ),
        in_specs=[IN_SMEM] * 2 + [IN_HBM] * (1 + len(cotangents)),
        out_specs=[IN_VMEM] * len(outs),
        out_shape=outs,
        scratch_shapes=[
            pltpu.VMEM((2, tokens, feats), jnp.bfloat16),
            pltpu.VMEM((total * rows, BLK, tokens), jnp.bfloat16),
            pltpu.VMEM((blocks, tokens, LANES), jnp.bfloat16),
            pltpu.VMEM((blocks, tokens, LANES), jnp.bfloat16),
            pltpu.SemaphoreType.DMA((2, len(cotangents))),
            pltpu.SemaphoreType.DMA((total,)),
        ],
        compiler_params=pltpu.CompilerParams(vmem_limit_bytes=18 * MIB),
        cost_estimate=about(3 + total // 2),
        name="block_grads",
    )(cols, flags, turned, *cotangents)


def list_kernel(tail_pieces, *refs):
    pieces, (listed, tails, arrived) = refs[:-3], refs[-3:]
    copies = []
    for line, index in enumerate(tail_pieces):
        piece = pieces[index]
        last = piece.at[pl.ds(piece.shape[0] - TAIL, TAIL)]
        copies.append(pltpu.make_async_copy(last, tails.at[line], arrived.at[line]))
    for copy in copies:
        copy.start()
    for line, copy in enumerate(copies):
        copy.wait()
        entry = tails[line].astype(jnp.float32)[:1, : listed.shape[1]]
        listed[line : line + 1] = entry.astype(jnp.int32)


def list_pass(weights, rows, slots):
    pieces, layout = weights
    tail_pieces = tuple(parts[-1][0] for role in range(2) for parts in layout[role])
    count = len(tail_pieces)
    lanes = -(-rows * slots // LANES) * LANES
    return pl.pallas_call(
        functools.partial(list_kernel, tail_pieces),
        in_specs=[IN_HBM] * len(pieces),
        out_specs=IN_VMEM,
        out_shape=jax.ShapeDtypeStruct((count, lanes), jnp.int32),
        scratch_shapes=[
            pltpu.VMEM((count, TAIL, slots * BLK), jnp.bfloat16),
            pltpu.SemaphoreType.DMA((count,)),
        ],
        compiler_params=pltpu.CompilerParams(vmem_limit_bytes=4 * MIB),
        cost_estimate=about(2),
        name="list_columns",
    )(*pieces)


def to_rows(blocks):
    rows, slots, _ = blocks.shape
    split = blocks.reshape(rows, slots, BLK, BLK)
    return split.transpose(0, 2, 1, 3).reshape(rows * BLK, slots * BLK)


def from_rows(matrix, slots):
    rows = matrix.shape[0] // BLK
    split = matrix.reshape(rows, BLK, slots, BLK)
    return split.transpose(0, 2, 1, 3).reshape(rows, slots, BLK * BLK)


def token_cuts(tokens):
    if tokens % 16 or tokens < 32:
        return [(0, tokens)]
    first = -(-tokens // 32) * 16
    return [(0, first), (first, tokens)]


def folded(count):
    return list(range(0, 1)) + list(range(1, count, 2)) + list(range(2, count, 2))[::-1]


def body(inputs, target, blocks, columns, counts):
    stage, stages = lax.axis_index("stage"), lax.axis_size("stage")
    side, sides = lax.axis_index("side"), lax.axis_size("side")
    dp_id, dp_count = lax.axis_index("dp"), lax.axis_size("dp")
    mb_count, tok_local, feats = inputs.shape
    rows, slots = columns.shape[1:]
    loss_scale = (mb_count * tok_local * dp_count) ** (-0.5)
    places = dp_count // 2
    place = dp_id // 2
    core = dp_id % 2
    share = mb_count * tok_local // sides

    around = folded(places)
    ranks = [around.index(spot) for spot in range(places)]
    rank = jnp.array(ranks, jnp.int32)[place]
    hops = [
        (2 * around[i] + half, 2 * around[(i + 1) % places] + half)
        for i in range(places)
        for half in range(2)
    ]

    def ring(array):
        return lax.ppermute(array, "dp", hops)

    def sibling(array):
        return lax.ppermute(array, "dp", [(i, i ^ 1) for i in range(dp_count)])

    def partner(array):
        return lax.ppermute(array, "side", [(i, sides - 1 - i) for i in range(sides)])

    slot_of = lax.broadcasted_iota(jnp.int32, (rows, BLK, slots * BLK), 2) // BLK
    live = (slot_of < counts[0][:, None, None]).reshape(rows * BLK, slots * BLK)
    listed = columns[0].reshape(1, rows * slots).astype(jnp.bfloat16)
    tail = jnp.pad(listed, ((0, TAIL - 1), (0, slots * BLK - rows * slots)))
    straight = to_rows(blocks[0])
    own = jnp.concatenate([jnp.where(live, straight, jnp.zeros_like(straight)), tail], axis=0)

    owns, others, far_owns, far_others = [own], [], [], []
    for slot in range(places):
        last = slot + 1 == places
        moving = {}
        if not last:
            moving["a_own"] = ring(owns[slot])
        moving["b_other"] = [partner(owns[slot])]
        if slot:
            moving["c_far_other"] = [sibling(part) for part in others[-1]]
        moving["d_far_own"] = sibling(owns[slot])
        moving = lax.optimization_barrier(moving)
        others.append(moving["b_other"])
        far_owns.append(moving["d_far_own"])
        if not last:
            owns.append(moving["a_own"])
        if slot:
            far_others.append(moving["c_far_other"])
    far_others.append([sibling(part) for part in others[-1]])
    pieces, layout = [], []
    for units in ([[piece] for piece in owns + far_owns], others + far_others):
        layout.append([])
        for parts in units:
            begin = 0
            layout[-1].append([])
            for part in parts:
                layout[-1][-1].append((len(pieces), begin))
                pieces.append(part)
                begin += part.shape[0]
    weights = (pieces, layout)
    cols = list_pass(weights, rows, slots)
    turns = jnp.array(around, jnp.int32)[(rank - jnp.arange(places)) % places]
    bases = jnp.concatenate([turns * 2 + core, turns * 2 + 1 - core]).astype(jnp.int32) * rows
    flags = jnp.stack([side, stage == 0, stage == stages - 1]).astype(jnp.int32)
    meta = (cols, bases, flags)

    def my_rows(array):
        flat = array.reshape(mb_count * tok_local, feats)
        return lax.dynamic_slice_in_dim(flat, side * share, share, 0)

    def hop(array, distance):
        route = [(i, i + distance) for i in range(stages) if 0 <= i + distance < stages]
        return lax.ppermute(array, "stage", route)

    cuts = token_cuts(share)
    ways = range(len(cuts))
    whole_start, whole_goal = my_rows(inputs), my_rows(target)
    start = [whole_start[begin:end] for begin, end in cuts]
    goal = [whole_goal[begin:end] for begin, end in cuts]
    moved = list(start)
    for step in range(stages - 1):
        final = [
            forward_pass(start[i], moved[i], None, None, weights, meta, rows, slots)[0]
            for i in ways
        ]
        moved = [hop(final[i], 1) for i in ways]
    turned = [
        forward_pass(start[i], moved[i], goal[i], loss_scale, weights, meta, rows, slots)
        for i in ways
    ]
    stashes, loss_grads, result = [list(column) for column in zip(*turned)]
    moved = loss_grads
    for step in range(stages - 1):
        if step:
            result = [
                backward_pass(stashes[i], loss_grads[i], moved[i], weights, meta, rows, slots, 2)
                for i in ways
            ]
        moved = [hop(result[i], -1) for i in ways]
    flipped = flip_pass(stashes + [sibling(stash) for stash in stashes], bases, rows, places)
    stashes[-1], flipped = lax.optimization_barrier((stashes[-1], flipped))
    cotangents = [
        backward_pass(stashes[i], loss_grads[i], moved[i], weights, meta, rows, slots, 1) for i in ways
    ]

    order = list(range(1, places)) + [0]

    cotangents = cotangents + [sibling(part) for part in cotangents]
    early, late = order[:1], order[1:]
    first = block_grad_pass(flipped, cotangents, meta, rows, slots, ((1, tuple(early)),), True)
    cotangents, first = lax.optimization_barrier((cotangents, first))
    jobs = tuple((role, chosen) for role, chosen in ((1, tuple(late[:1])), (0, tuple(early))) if chosen)
    grads = block_grad_pass(flipped, cotangents, meta, rows, slots, jobs)
    if places > 1:
        moving = lax.optimization_barrier((ring(first[1]), partner(first[0]), grads))
    else:
        moving = lax.optimization_barrier((partner(first[1]), partner(first[0]), grads))
    lower, upper, grads = moving
    leaving, staying = list(grads[: len(late[:1])]), [grads[-1]]
    if places > 1:
        cotangents, lower, upper = lax.optimization_barrier((cotangents, lower, upper))
        jobs = tuple((role, chosen) for role, chosen in ((1, tuple(late[1:])), (0, tuple(late))) if chosen)
        grads = block_grad_pass(flipped, cotangents, meta, rows, slots, jobs)
        leaving += grads[: len(late[1:])]
        staying += grads[len(late[1:]) :]
    if places > 1:
        upper = jnp.concatenate([upper, jnp.zeros_like(lower)], axis=0)
        travelling = add_rounded(staying[0], upper)
        leaving[0] = add_rounded(leaving[0], jnp.concatenate([jnp.zeros_like(lower), lower], axis=0))
    else:
        travelling = add_rounded(staying[0], jnp.concatenate([upper, lower], axis=0))
    for index in range(places - 1):
        kept, outgoing = staying[index + 1], leaving[index]
        passed, coming = lax.optimization_barrier((ring(travelling), partner(outgoing)))
        total = kept.astype(jnp.float32) + coming.astype(jnp.float32) + passed.astype(jnp.float32)
        travelling = total.astype(jnp.bfloat16)
    travelling = jnp.where(live, travelling, jnp.zeros_like(travelling))
    return from_rows(travelling, slots)[None]


def add_rounded(left, right):
    return (left.astype(jnp.float32) + right.astype(jnp.float32)).astype(jnp.bfloat16)


def solution(mesh):
    sections, width = mesh.devices.shape
    split = jax.sharding.Mesh(mesh.devices.reshape(sections // 2, 2, width), ("stage", "side", "dp"))
    section = ("stage", "side")
    return jax.shard_map(
        body,
        mesh=split,
        in_specs=(
            P(None, "dp", None),
            P(None, "dp", None),
            P(section, "dp", None, None),
            P(section, "dp", None),
            P(section, "dp"),
        ),
        out_specs=P(section, "dp", None, None),
        check_vma=False,
    )
```

```python
import functools

import jax
import jax.numpy as jnp
from jax import lax
from jax.experimental import pallas as pl
from jax.experimental.pallas import tpu as pltpu
from jax.sharding import PartitionSpec as P

BLK = 64
LANES = 128
EPSILON = 1e-05
MIB = 1024 * 1024
STEP_ROWS = 16

TAIL = 16

IN_VMEM = pl.BlockSpec(memory_space=pltpu.VMEM)
IN_SMEM = pl.BlockSpec(memory_space=pltpu.SMEM)
IN_HBM = pl.BlockSpec(memory_space=pl.ANY)


def about(microseconds):
    return pl.CostEstimate(
        flops=int(microseconds * 1.1e9), bytes_accessed=1 << 20, transcendentals=0
    )


def step_units(units, rows):
    size = max(1, STEP_ROWS // rows)
    while units % size:
        size -= 1
    return size


def low_half(rows):
    return lax.broadcasted_iota(jnp.int32, (rows, LANES), 1) < BLK


def tile(pair):
    return pl.ds(pl.multiple_of(pair * LANES, LANES), LANES)


def over_pairs(feats, visit, carry):
    return lax.fori_loop(0, feats // LANES, visit, carry, unroll=4)


def inv_rms_of(ref):
    tokens, feats = ref.shape

    def visit(pair, total):
        values = ref[:, tile(pair)].astype(jnp.float32)
        return total + values * values

    total = over_pairs(feats, visit, jnp.zeros((tokens, LANES), jnp.float32))
    return lax.rsqrt(jnp.sum(total, axis=-1, keepdims=True) / feats + EPSILON)


def start_loads(pieces, held, arrived, roles, layout):
    for role in roles:
        for unit, parts in enumerate(layout[role]):
            for index, begin in parts:
                piece = pieces[index]
                pltpu.make_async_copy(
                    piece,
                    held.at[role, unit, pl.ds(begin, piece.shape[0])],
                    arrived.at[role, unit],
                ).start()


def start_loads_in_order(side, pieces, held, arrived, layers, layout):
    for value in range(2):
        pl.when(side == value)(
            functools.partial(
                start_loads, pieces, held, arrived, [abs(layer - value) for layer in layers], layout
            )
        )


def wait_load(held, arrived, role, unit):
    whole = held.at[role, unit]
    pltpu.make_async_copy(whole, whole, arrived.at[role, unit]).wait()


def forward_layer(role, wait, cols, bases, current, held, parts, sums, rows, slots):
    tokens, feats = current.shape
    units = held.shape[1]
    per_step = step_units(units, rows)
    low = low_half(tokens)
    inv_rms = inv_rms_of(current)

    def normalise(pair, carry):
        lanes = tile(pair)
        unit_rows = current[:, lanes].astype(jnp.float32) * inv_rms
        parts[2 * pair] = jnp.where(low, unit_rows, 0.0).astype(jnp.bfloat16)
        parts[2 * pair + 1] = jnp.where(low, 0.0, unit_rows).astype(jnp.bfloat16)
        sums[2 * pair] = jnp.zeros((tokens, LANES), jnp.float32)
        sums[2 * pair + 1] = jnp.zeros((tokens, LANES), jnp.float32)
        return carry

    over_pairs(feats, normalise, 0)

    def run_step(step, carry):
        for inner in range(per_step):
            wait(role, step * per_step + inner)
        items = [(inner, row) for inner in range(per_step) for row in range(0, rows, 2)]

        def product_of(index):
            inner, row = items[index]
            unit = step * per_step + inner
            place = bases[unit] + row
            left = jnp.concatenate([parts[place], parts[place + 1]], axis=0)
            right = held[role, unit, row * BLK : (row + 2) * BLK]
            return jnp.dot(left, right, preferred_element_type=jnp.float32)

        def columns_of(index):
            inner, row = items[index]
            line = role * units + step * per_step + inner
            return [cols[line, row * slots + place] for place in range(2 * slots)]

        upcoming = product_of(0)
        ahead = columns_of(0)
        for index, (inner, row) in enumerate(items):
            product, listed = upcoming, ahead
            if index + 1 < len(items):
                upcoming = product_of(index + 1)
                ahead = columns_of(index + 1)
            for which in range(2):
                for begin in range(0, slots, 4):
                    at = listed[which * slots + begin : which * slots + min(begin + 4, slots)]
                    added = []
                    for offset in range(len(at)):
                        slot = begin + offset
                        lanes = slice((slot // 2) * LANES, (slot // 2 + 1) * LANES)
                        piece = product[which * tokens : (which + 1) * tokens, lanes]
                        piece = jnp.where(low, piece, 0.0) if slot % 2 == 0 else jnp.where(low, 0.0, piece)
                        added.append(sums[at[offset]] + piece)
                    for offset in range(len(at)):
                        sums[at[offset]] = added[offset]
        return carry

    lax.fori_loop(0, units // per_step, run_step, 0)

    def finish(pair, carry):
        lanes = tile(pair)
        first, second = sums[2 * pair], sums[2 * pair + 1]
        branch = jnp.where(low, first, second) + pltpu.roll(jnp.where(low, second, first), BLK, 1)
        current[:, lanes] = (current[:, lanes].astype(jnp.float32) + branch).astype(jnp.bfloat16)
        return carry

    over_pairs(feats, finish, 0)


def spread(source, lows, highs):
    tokens, feats = source.shape
    low = low_half(tokens)

    def visit(pair, carry):
        both = source[:, tile(pair)].astype(jnp.float32)
        moved = pltpu.roll(both, BLK, 1)
        lows[2 * pair] = jnp.where(low, both, 0.0).astype(jnp.bfloat16)
        highs[2 * pair] = jnp.where(low, 0.0, moved).astype(jnp.bfloat16)
        lows[2 * pair + 1] = jnp.where(low, moved, 0.0).astype(jnp.bfloat16)
        highs[2 * pair + 1] = jnp.where(low, 0.0, both).astype(jnp.bfloat16)
        return carry

    over_pairs(feats, visit, 0)


def pick_columns(lows, highs, cols, line, flat, slots):
    return jnp.concatenate(
        [
            lows[cols[line, flat + 2 * half]] + highs[cols[line, flat + 2 * half + 1]]
            for half in range(slots // 2)
        ],
        axis=1,
    )


def input_grad_layer(role, wait, cols, bases, hidden, cotangent, out, held, lows, highs, back, rows, slots):
    tokens, feats = cotangent.shape
    units = held.shape[1]
    per_step = step_units(units, rows)
    low = low_half(tokens)

    def run_step(step, carry):
        for inner in range(per_step):
            wait(role, step * per_step + inner)
        items = [(inner, row) for inner in range(per_step) for row in range(0, rows, 2)]

        def picked_at(index):
            inner, row = items[index]
            line = role * units + step * per_step + inner
            return jnp.concatenate(
                [
                    pick_columns(lows, highs, cols, line, (row + which) * slots, slots)
                    for which in range(2)
                ],
                axis=0,
            )

        upcoming = picked_at(0)
        for index, (inner, row) in enumerate(items):
            unit = step * per_step + inner
            picked = upcoming
            if index + 1 < len(items):
                upcoming = picked_at(index + 1)
            result = lax.dot_general(
                picked,
                held[role, unit, row * BLK : (row + 2) * BLK],
                (((1,), (1,)), ((), ())),
                preferred_element_type=jnp.float32,
            )
            place = (bases[unit] + row) // 2
            back[place] = jnp.where(low, result[:tokens], result[tokens:])
        return carry

    lax.fori_loop(0, units // per_step, run_step, 0)
    inv_rms = inv_rms_of(hidden)

    def correlate(pair, total):
        unit_rows = hidden[:, tile(pair)].astype(jnp.float32) * inv_rms
        return total + back[pair] * unit_rows

    total = over_pairs(feats, correlate, jnp.zeros((tokens, LANES), jnp.float32))
    mean = jnp.sum(total, axis=-1, keepdims=True) / feats

    def finish(pair, carry):
        lanes = tile(pair)
        unit_rows = hidden[:, lanes].astype(jnp.float32) * inv_rms
        centred = back[pair] - unit_rows * mean
        out[:, lanes] = (cotangent[:, lanes].astype(jnp.float32) + inv_rms * centred).astype(jnp.bfloat16)
        return carry

    over_pairs(feats, finish, 0)


def block_grad_layer(begin, role, cols, flipped, lows, highs, out, chosen, units, rows, slots):
    items = [(which, row) for which in range(len(chosen)) for row in range(rows)]

    def operands(index):
        which, row = items[index]
        picked = pick_columns(lows, highs, cols, role * units + chosen[which], row * slots, slots)
        return flipped[begin + which * rows + row], picked

    upcoming = operands(0)
    for index, (which, row) in enumerate(items):
        left, right = upcoming
        if index + 1 < len(items):
            upcoming = operands(index + 1)
        result = jnp.dot(left, right, preferred_element_type=jnp.float32).astype(jnp.bfloat16)
        target = out[which]
        if isinstance(target, tuple):
            target, row = target[row // (rows // 2)], row % (rows // 2)
        target[row * BLK : (row + 1) * BLK] = result


def choose(flag, first, second, target):
    @pl.when(flag == 1)
    def _():
        target[...] = first[...]

    @pl.when(flag != 1)
    def _():
        target[...] = second[...]


def forward_kernel(rows, slots, count, layout, scale, cols, bases, flags, *rest):
    turning = scale is not None
    start, moved = rest[:2]
    rest = rest[2:]
    if turning:
        goal, rest = rest[0], rest[1:]
    straight, rest = rest[:count], rest[count:]
    if turning:
        stash, loss_grad, final, held, parts, sums, arrived, lows, highs, back = rest
    else:
        final, held, parts, sums, arrived = rest
    start_loads_in_order(flags[0], straight, held, arrived, (0, 1), layout)
    choose(flags[1], start, moved, final)
    wait = functools.partial(wait_load, held, arrived)

    def run_forward(layer, carry):
        if turning:
            stash[layer] = final[...]
        role = jnp.abs(layer - flags[0])
        forward_layer(role, wait, cols, bases, final, held, parts, sums, rows, slots)
        return carry

    lax.fori_loop(0, 2, run_forward, 0)
    if not turning:
        return
    tokens, feats = final.shape

    def residue(pair, carry):
        lanes = tile(pair)
        gap = final[:, lanes].astype(jnp.float32) - goal[:, lanes].astype(jnp.float32)
        loss_grad[:, lanes] = (gap * scale).astype(jnp.bfloat16)
        return carry

    over_pairs(feats, residue, 0)
    final[...] = loss_grad[...]
    def run_back(turn, carry):
        layer = 1 - turn
        role = jnp.abs(layer - flags[0])
        hidden = stash.at[layer]
        spread(final, lows, highs)
        input_grad_layer(
            role, nothing, cols, bases, hidden, final, final, held, lows, highs, back, rows, slots
        )
        return carry

    lax.fori_loop(0, 2, run_back, 0)


def nothing(*_):
    return None


def state_of(tokens, feats):
    return jax.ShapeDtypeStruct((tokens, feats), jnp.bfloat16)


def unit_scratch(layout, rows, slots):
    units = len(layout[0])
    shape = (2, units, rows * BLK + TAIL, slots * BLK)
    return [pltpu.VMEM(shape, jnp.bfloat16), pltpu.SemaphoreType.DMA((2, units))]


def forward_pass(start, moved, goal, scale, weights, meta, rows, slots):
    straight, layout = weights
    tokens, feats = start.shape
    blocks = feats // BLK
    stack = jax.ShapeDtypeStruct((2, tokens, feats), jnp.bfloat16)
    held, arrived = unit_scratch(layout, rows, slots)
    scratch = [
        held,
        pltpu.VMEM((blocks, tokens, LANES), jnp.bfloat16),
        pltpu.VMEM((blocks, tokens, LANES), jnp.float32),
        arrived,
    ]
    outs = [state_of(tokens, feats)]
    ins = [start, moved]
    pieces = list(straight)
    if goal is not None:
        ins.append(goal)
        outs = [stack, state_of(tokens, feats)] + outs
        scratch += [
            pltpu.VMEM((blocks, tokens, LANES), jnp.bfloat16),
            pltpu.VMEM((blocks, tokens, LANES), jnp.bfloat16),
            pltpu.VMEM((blocks // 2, tokens, LANES), jnp.float32),
        ]
    return pl.pallas_call(
        functools.partial(
            forward_kernel, rows, slots, len(straight), layout, None if goal is None else scale
        ),
        in_specs=[IN_SMEM] * 3 + [IN_VMEM] * len(ins) + [IN_HBM] * len(pieces),
        out_specs=[IN_VMEM] * len(outs),
        out_shape=outs,
        scratch_shapes=scratch,
        compiler_params=pltpu.CompilerParams(vmem_limit_bytes=(16 if goal is None else 20) * MIB),
        cost_estimate=about(8 if goal is None else 14),
        name="forward_layers" if goal is None else "turning_layers",
    )(*meta, *ins, *pieces)


def backward_kernel(rows, slots, count, layout, depth, cols, bases, flags, stash, loss_grad, moved, *rest):
    across, rest = rest[:count], rest[count:]
    outs, crossed, lows, highs, back, landed = rest
    if depth == 1:
        first, second = outs.at[1], outs.at[0]
    else:
        first = second = outs
    order = (1,) if depth == 1 else (1, 0)
    start_loads_in_order(flags[0], across, crossed, landed, order, layout)
    choose(flags[2], loss_grad, moved, first)
    wait = functools.partial(wait_load, crossed, landed)

    def run_back(layer):
        spread(first, lows, highs)
        role = jnp.abs(layer - flags[0])
        input_grad_layer(
            role, wait, cols, bases, stash.at[layer], first, second, crossed, lows, highs, back, rows, slots
        )

    run_back(1)
    if depth == 2:
        run_back(0)


def backward_pass(stash, loss_grad, moved, weights, meta, rows, slots, depth):
    across, layout = weights
    _, tokens, feats = stash.shape
    blocks = feats // BLK
    crossed, landed = unit_scratch(layout, rows, slots)
    if depth == 1:
        out = jax.ShapeDtypeStruct((2, tokens, feats), jnp.bfloat16)
    else:
        out = state_of(tokens, feats)
    return pl.pallas_call(
        functools.partial(backward_kernel, rows, slots, len(across), layout, depth),
        in_specs=[IN_SMEM] * 3 + [IN_VMEM] * 3 + [IN_HBM] * len(across),
        out_specs=IN_VMEM,
        out_shape=out,
        scratch_shapes=[
            crossed,
            pltpu.VMEM((blocks, tokens, LANES), jnp.bfloat16),
            pltpu.VMEM((blocks, tokens, LANES), jnp.bfloat16),
            pltpu.VMEM((blocks // 2, tokens, LANES), jnp.float32),
            landed,
        ],
        compiler_params=pltpu.CompilerParams(vmem_limit_bytes=18 * MIB),
        cost_estimate=about(4 * depth),
        name="backward_layers",
    )(*meta, stash, loss_grad, moved, *across)


def join_tokens(sources, joined, arrived, layer):
    copies = []
    begin = 0
    for index, source in enumerate(sources):
        span = pl.ds(begin, source.shape[1])
        copies.append(
            pltpu.make_async_copy(source.at[layer], joined.at[layer, span], arrived.at[layer, index])
        )
        begin += source.shape[1]
    for copy in copies:
        copy.start()
    return copies


def flip_kernel(rows, chosen, bases, *refs):
    *sources, flipped, joined, arrived = refs
    loads = [join_tokens(sources, joined, arrived, layer) for layer in range(2)]
    for load in loads[0] + loads[1]:
        load.wait()

    def run(layer, carry):
        hidden = joined.at[layer]
        inv_rms = inv_rms_of(hidden)
        for unit in range(chosen):

            def visit(step, carry):
                lanes = tile(bases[unit] // 2 + step)
                turned = (hidden[:, lanes].astype(jnp.float32) * inv_rms).T.astype(jnp.bfloat16)
                flipped[layer, unit * rows + 2 * step] = turned[:BLK]
                flipped[layer, unit * rows + 2 * step + 1] = turned[BLK:]
                return carry

            lax.fori_loop(0, rows // 2, visit, 0, unroll=True)
        return carry

    lax.fori_loop(0, 2, run, 0)


def flip_pass(stashes, bases, rows, chosen):
    tokens = sum(stash.shape[1] for stash in stashes)
    feats = stashes[0].shape[2]
    return pl.pallas_call(
        functools.partial(flip_kernel, rows, chosen),
        in_specs=[IN_SMEM] + [IN_HBM] * len(stashes),
        out_specs=IN_VMEM,
        out_shape=jax.ShapeDtypeStruct((2, chosen * rows, BLK, tokens), jnp.bfloat16),
        scratch_shapes=[
            pltpu.VMEM((2, tokens, feats), jnp.bfloat16),
            pltpu.SemaphoreType.DMA((2, len(stashes))),
        ],
        compiler_params=pltpu.CompilerParams(vmem_limit_bytes=12 * MIB),
        cost_estimate=about(4),
        name="flip_rows",
    )(bases, *stashes)


def block_grad_kernel(rows, slots, jobs, halved, units, parts, cols, flags, turned, *rest):
    sources, rest = rest[:parts], rest[parts:]
    total = sum(len(chosen) for _, chosen in jobs)
    outs = [tuple(rest[:2])] if halved else rest[:total]
    joined, flipped, lows, highs, arrived, fetched = rest[-6:]
    layers = [jnp.abs(role - flags[0]) for role, _ in jobs]
    fetches = []
    begin = 0
    for layer, (_, chosen) in zip(layers, jobs):
        fetches.append(join_tokens(sources, joined, arrived, layer))
        for which, unit in enumerate(chosen):
            copy = pltpu.make_async_copy(
                turned.at[layer, pl.ds(unit * rows, rows)],
                flipped.at[pl.ds((begin + which) * rows, rows)],
                fetched.at[begin + which],
            )
            copy.start()
            fetches[-1].append(copy)
        begin += len(chosen)
    begin = 0
    for turn, (role, chosen) in enumerate(jobs):
        for fetch in fetches[turn]:
            fetch.wait()
        spread(joined.at[layers[turn]], lows, highs)
        block_grad_layer(
            begin * rows, role, cols, flipped, lows, highs, outs[begin:], chosen, units, rows, slots
        )
        begin += len(chosen)


def block_grad_pass(turned, cotangents, meta, rows, slots, jobs, halved=False):
    tokens = turned.shape[3]
    feats = cotangents[0].shape[2]
    blocks = feats // BLK
    cols, bases, flags = meta
    total = sum(len(chosen) for _, chosen in jobs)
    tall = rows // 2 * BLK if halved else rows * BLK
    outs = [jax.ShapeDtypeStruct((tall, slots * BLK), jnp.bfloat16)] * (2 if halved else total)
    return pl.pallas_call(
        functools.partial(
            block_grad_kernel, rows, slots, jobs, halved, bases.shape[0], len(cotangents)
        ),
        in_specs=[IN_SMEM] * 2 + [IN_HBM] * (1 + len(cotangents)),
        out_specs=[IN_VMEM] * len(outs),
        out_shape=outs,
        scratch_shapes=[
            pltpu.VMEM((2, tokens, feats), jnp.bfloat16),
            pltpu.VMEM((total * rows, BLK, tokens), jnp.bfloat16),
            pltpu.VMEM((blocks, tokens, LANES), jnp.bfloat16),
            pltpu.VMEM((blocks, tokens, LANES), jnp.bfloat16),
            pltpu.SemaphoreType.DMA((2, len(cotangents))),
            pltpu.SemaphoreType.DMA((total,)),
        ],
        compiler_params=pltpu.CompilerParams(vmem_limit_bytes=18 * MIB),
        cost_estimate=about(3 + total // 2),
        name="block_grads",
    )(cols, flags, turned, *cotangents)


def list_kernel(tail_pieces, *refs):
    pieces, (listed, tails, arrived) = refs[:-3], refs[-3:]
    copies = []
    for line, index in enumerate(tail_pieces):
        piece = pieces[index]
        last = piece.at[pl.ds(piece.shape[0] - TAIL, TAIL)]
        copies.append(pltpu.make_async_copy(last, tails.at[line], arrived.at[line]))
    for copy in copies:
        copy.start()
    for line, copy in enumerate(copies):
        copy.wait()
        entry = tails[line].astype(jnp.float32)[:1, : listed.shape[1]]
        listed[line : line + 1] = entry.astype(jnp.int32)


def list_pass(weights, rows, slots):
    pieces, layout = weights
    tail_pieces = tuple(parts[-1][0] for role in range(2) for parts in layout[role])
    count = len(tail_pieces)
    lanes = -(-rows * slots // LANES) * LANES
    return pl.pallas_call(
        functools.partial(list_kernel, tail_pieces),
        in_specs=[IN_HBM] * len(pieces),
        out_specs=IN_VMEM,
        out_shape=jax.ShapeDtypeStruct((count, lanes), jnp.int32),
        scratch_shapes=[
            pltpu.VMEM((count, TAIL, slots * BLK), jnp.bfloat16),
            pltpu.SemaphoreType.DMA((count,)),
        ],
        compiler_params=pltpu.CompilerParams(vmem_limit_bytes=4 * MIB),
        cost_estimate=about(2),
        name="list_columns",
    )(*pieces)


def to_rows(blocks):
    rows, slots, _ = blocks.shape
    split = blocks.reshape(rows, slots, BLK, BLK)
    return split.transpose(0, 2, 1, 3).reshape(rows * BLK, slots * BLK)


def from_rows(matrix, slots):
    rows = matrix.shape[0] // BLK
    split = matrix.reshape(rows, BLK, slots, BLK)
    return split.transpose(0, 2, 1, 3).reshape(rows, slots, BLK * BLK)


def token_cuts(tokens):
    if tokens % 16 or tokens < 32:
        return [(0, tokens)]
    first = -(-tokens // 32) * 16
    return [(0, first), (first, tokens)]


def folded(count):
    return list(range(0, 1)) + list(range(1, count, 2)) + list(range(2, count, 2))[::-1]


def body(inputs, target, blocks, columns, counts):
    stage, stages = lax.axis_index("stage"), lax.axis_size("stage")
    side, sides = lax.axis_index("side"), lax.axis_size("side")
    dp_id, dp_count = lax.axis_index("dp"), lax.axis_size("dp")
    mb_count, tok_local, feats = inputs.shape
    rows, slots = columns.shape[1:]
    loss_scale = (mb_count * tok_local * dp_count) ** (-0.5)
    places = dp_count // 2
    place = dp_id // 2
    core = dp_id % 2
    share = mb_count * tok_local // sides

    around = folded(places)
    ranks = [around.index(spot) for spot in range(places)]
    rank = jnp.array(ranks, jnp.int32)[place]
    hops = [
        (2 * around[i] + half, 2 * around[(i + 1) % places] + half)
        for i in range(places)
        for half in range(2)
    ]

    def ring(array):
        return lax.ppermute(array, "dp", hops)

    def sibling(array):
        return lax.ppermute(array, "dp", [(i, i ^ 1) for i in range(dp_count)])

    def partner(array):
        return lax.ppermute(array, "side", [(i, sides - 1 - i) for i in range(sides)])

    slot_of = lax.broadcasted_iota(jnp.int32, (rows, BLK, slots * BLK), 2) // BLK
    live = (slot_of < counts[0][:, None, None]).reshape(rows * BLK, slots * BLK)
    listed = columns[0].reshape(1, rows * slots).astype(jnp.bfloat16)
    tail = jnp.pad(listed, ((0, TAIL - 1), (0, slots * BLK - rows * slots)))
    straight = to_rows(blocks[0])
    own = jnp.concatenate([jnp.where(live, straight, jnp.zeros_like(straight)), tail], axis=0)

    owns, others, far_owns, far_others = [own], [], [], []
    for slot in range(places):
        last = slot + 1 == places
        moving = {}
        if not last:
            moving["a_own"] = ring(owns[slot])
        moving["b_other"] = [partner(owns[slot])]
        if slot:
            moving["c_far_other"] = [sibling(part) for part in others[-1]]
        moving["d_far_own"] = sibling(owns[slot])
        moving = lax.optimization_barrier(moving)
        others.append(moving["b_other"])
        far_owns.append(moving["d_far_own"])
        if not last:
            owns.append(moving["a_own"])
        if slot:
            far_others.append(moving["c_far_other"])
    far_others.append([sibling(part) for part in others[-1]])
    pieces, layout = [], []
    for units in ([[piece] for piece in owns + far_owns], others + far_others):
        layout.append([])
        for parts in units:
            begin = 0
            layout[-1].append([])
            for part in parts:
                layout[-1][-1].append((len(pieces), begin))
                pieces.append(part)
                begin += part.shape[0]
    weights = (pieces, layout)
    cols = list_pass(weights, rows, slots)
    turns = jnp.array(around, jnp.int32)[(rank - jnp.arange(places)) % places]
    bases = jnp.concatenate([turns * 2 + core, turns * 2 + 1 - core]).astype(jnp.int32) * rows
    flags = jnp.stack([side, stage == 0, stage == stages - 1]).astype(jnp.int32)
    meta = (cols, bases, flags)

    def my_rows(array):
        flat = array.reshape(mb_count * tok_local, feats)
        return lax.dynamic_slice_in_dim(flat, side * share, share, 0)

    def hop(array, distance):
        route = [(i, i + distance) for i in range(stages) if 0 <= i + distance < stages]
        return lax.ppermute(array, "stage", route)

    cuts = token_cuts(share)
    ways = range(len(cuts))
    whole_start, whole_goal = my_rows(inputs), my_rows(target)
    start = [whole_start[begin:end] for begin, end in cuts]
    goal = [whole_goal[begin:end] for begin, end in cuts]
    moved = list(start)
    for step in range(stages - 1):
        final = [
            forward_pass(start[i], moved[i], None, None, weights, meta, rows, slots)[0]
            for i in ways
        ]
        moved = [hop(final[i], 1) for i in ways]
    turned = [
        forward_pass(start[i], moved[i], goal[i], loss_scale, weights, meta, rows, slots)
        for i in ways
    ]
    stashes, loss_grads, result = [list(column) for column in zip(*turned)]
    moved = loss_grads
    for step in range(stages - 1):
        if step:
            result = [
                backward_pass(stashes[i], loss_grads[i], moved[i], weights, meta, rows, slots, 2)
                for i in ways
            ]
        moved = [hop(result[i], -1) for i in ways]
    flipped = flip_pass(stashes + [sibling(stash) for stash in stashes], bases, rows, places)
    stashes[-1], flipped = lax.optimization_barrier((stashes[-1], flipped))
    cotangents = [
        backward_pass(stashes[i], loss_grads[i], moved[i], weights, meta, rows, slots, 1) for i in ways
    ]

    order = list(range(1, places)) + [0]

    cotangents = cotangents + [sibling(part) for part in cotangents]
    early, late = order[:1], order[1:]
    first = block_grad_pass(flipped, cotangents, meta, rows, slots, ((1, tuple(early)),), True)
    cotangents, first = lax.optimization_barrier((cotangents, first))
    jobs = tuple((role, chosen) for role, chosen in ((1, tuple(late[:1])), (0, tuple(early))) if chosen)
    grads = block_grad_pass(flipped, cotangents, meta, rows, slots, jobs)
    if places > 1:
        moving = lax.optimization_barrier((ring(first[1]), partner(first[0]), grads))
    else:
        moving = lax.optimization_barrier((partner(first[1]), partner(first[0]), grads))
    lower, upper, grads = moving
    leaving, staying = list(grads[: len(late[:1])]), [grads[-1]]
    if places > 1:
        cotangents, lower, upper = lax.optimization_barrier((cotangents, lower, upper))
        jobs = tuple((role, chosen) for role, chosen in ((1, tuple(late[1:])), (0, tuple(late))) if chosen)
        grads = block_grad_pass(flipped, cotangents, meta, rows, slots, jobs)
        leaving += grads[: len(late[1:])]
        staying += grads[len(late[1:]) :]
    if places > 1:
        upper = jnp.concatenate([upper, jnp.zeros_like(lower)], axis=0)
        travelling = add_rounded(staying[0], upper)
        leaving[0] = add_rounded(leaving[0], jnp.concatenate([jnp.zeros_like(lower), lower], axis=0))
    else:
        travelling = add_rounded(staying[0], jnp.concatenate([upper, lower], axis=0))
    for index in range(places - 1):
        kept, outgoing = staying[index + 1], leaving[index]
        passed, coming = lax.optimization_barrier((ring(travelling), partner(outgoing)))
        total = kept.astype(jnp.float32) + coming.astype(jnp.float32) + passed.astype(jnp.float32)
        travelling = total.astype(jnp.bfloat16)
    travelling = jnp.where(live, travelling, jnp.zeros_like(travelling))
    return from_rows(travelling, slots)[None]


def add_rounded(left, right):
    return (left.astype(jnp.float32) + right.astype(jnp.float32)).astype(jnp.bfloat16)


def solution(mesh):
    sections, width = mesh.devices.shape
    split = jax.sharding.Mesh(mesh.devices.reshape(sections // 2, 2, width), ("stage", "side", "dp"))
    section = ("stage", "side")
    return jax.shard_map(
        body,
        mesh=split,
        in_specs=(
            P(None, "dp", None),
            P(None, "dp", None),
            P(section, "dp", None, None),
            P(section, "dp", None),
            P(section, "dp"),
        ),
        out_specs=P(section, "dp", None, None),
        check_vma=False,
    )
```
